32 devices in a mesh: ctx: 16 (over z, x, core), ch: 2 (over y).
Axes of the slice: x: 2, y: 2, z: 4, core: 2. Of those that a mesh axis runs over, the one named last changes fastest.
Arguments:
- q_in: bfloat16 [2048, 4096], P('ctx', 'ch'), may hold values from -6 to 6
- k_in: bfloat16 [2048, 4096], P('ctx', 'ch'), may hold values from -6 to 6
- v_in: bfloat16 [2048, 4096], P('ctx', 'ch'), may hold values from -6 to 6
- grad_out: bfloat16 [2048, 4096], P('ctx', 'ch'), may hold values from -30 to 30
- short_filter: float32 [3, 4096], P(None, 'ch'), may hold values from -3 to 3
- kernel: float32 [2048, 4096], P('ctx', 'ch'), may hold values from -0.125 to 0.125
- skip: float32 [4096], P('ch'), may hold values from -3 to 3
Outputs:
- mixed: bfloat16 [2048, 4096], P('ctx', 'ch')
- grad_q: bfloat16 [2048, 4096], P('ctx', 'ch')
- grad_k: bfloat16 [2048, 4096], P('ctx', 'ch')
- grad_v: bfloat16 [2048, 4096], P('ctx', 'ch')
- grad_short: float32 [3, 4096], P(None, 'ch')
- grad_skip: float32 [4096], P('ch')
- grad_kernel: float32 [2048, 4096], P('ctx', 'ch')
The draws below stay inside these ranges and needn't reach their ends.
All inputs are finite; a program needn't handle non-finite values.
Results may differ from the reference program's by a relative error of at most 0.009.
Values may be sent and summed in bfloat16 or wider, within the bound.
No kernel may reach another device: no remote copies, remote signals or barrier semaphores. Data moves between devices by JAX's collectives and lax.ppermute only.
A program may use at most 128 MiB of HBM per device.

```python
import math
import jax
import jax.numpy as jnp
from jax import lax

D = 4096
SHORT = 3
SEQ = 2048


def draw_grad_out(key, part):
    key_base = jax.random.fold_in(key, 11)
    key_chan = jax.random.fold_in(key, 12)
    key_rows = jax.random.fold_in(key, 13)
    chan_pos = jnp.arange(D).astype(jnp.float32) / D
    chan_noise = jax.random.uniform(key_chan, (D,), jnp.float32)
    row_noise = jax.random.uniform(key_rows, (SEQ,), jnp.float32)
    base = jax.random.truncated_normal(key_base, -3.0, 3.0, (SEQ, D), jnp.float32)
    chan_trend = 0.5 * chan_pos
    log_scale = chan_trend[None, :] + 0.5 * chan_noise[None, :] + 0.5 * row_noise[:, None] - 0.75
    return (base * jnp.exp(log_scale * math.log(10.0))).astype(jnp.bfloat16)


def block_scale(own_key, dims, split, least, high):
    def one(dim, shards_of):
        heights = jax.random.uniform(jax.random.fold_in(jax.random.fold_in(own_key, 6), dim), (shards_of,), jnp.float32, least / len(split), high / len(split))
        return jnp.repeat(jnp.exp(heights), dims[dim] // shards_of).reshape((-1,) + (1,) * (len(dims) - dim - 1))

    gain = one(*split[0])
    for cut in split[1:]:
        gain = gain * one(*cut)
    return gain


def scatter_about(own_key, extent, scale, most, split=(), held_as=jnp.bfloat16):
    drawn = scale * jax.random.normal(own_key, extent, jnp.float32)
    if split:
        drawn = drawn * block_scale(own_key, extent, split, -0.22, 0.18)
    return jnp.clip(drawn, -most, most).astype(held_as)


def setup_inputs(seed: int = 0) -> dict:
    seeds = jax.random.split(jax.random.key(seed), 8)
    q_in = scatter_about(seeds[0], (SEQ, D), 1.0, 6.0, ((0, 16), (1, 2)))
    k_in = scatter_about(seeds[1], (SEQ, D), 1.0, 6.0, ((0, 16), (1, 2)))
    v_in = scatter_about(seeds[2], (SEQ, D), 1.0, 6.0, ((0, 16), (1, 2)))
    grad_out = draw_grad_out(jax.random.fold_in(seeds[7], 71), 0)
    short_filter = scatter_about(seeds[4], (SHORT, D), 0.6, 3.0, ((1, 2),), jnp.float32)
    kernel = scatter_about(seeds[5], (SEQ, D), SEQ ** -0.5, 0.125, ((0, 16), (1, 2)), jnp.float32)
    skip = scatter_about(seeds[6], (D,), 0.5, 3.0, ((0, 2),), jnp.float32)
    return dict(q_in=q_in, k_in=k_in, v_in=v_in, grad_out=grad_out, short_filter=short_filter, kernel=kernel, skip=skip)


def causal_short(signal, short_taps):
    halo_rows = short_taps.shape[0] - 1
    seq_len = signal.shape[0]
    padded = jnp.concatenate([jnp.zeros((halo_rows, signal.shape[1]), jnp.float32), signal], axis=0)
    result = short_taps[0] * padded[halo_rows:halo_rows + seq_len]
    for shift_idx in range(1, short_taps.shape[0]):
        result = result + short_taps[shift_idx] * padded[halo_rows - shift_idx:halo_rows - shift_idx + seq_len]
    return (result, padded)

def causal_adjoint(signal, short_taps):
    halo_rows = short_taps.shape[0] - 1
    seq_len = signal.shape[0]
    padded = jnp.concatenate([signal, jnp.zeros((halo_rows, signal.shape[1]), jnp.float32)], axis=0)
    result = short_taps[0] * padded[0:seq_len]
    for shift_idx in range(1, short_taps.shape[0]):
        result = result + short_taps[shift_idx] * padded[shift_idx:shift_idx + seq_len]
    return result

def channel_block(q_in, k_in, v_in, grad_out, short_taps, kernel, skip):
    seq_len = q_in.shape[0]
    halo_rows = short_taps.shape[0] - 1
    q_short, q_pad = causal_short(q_in.astype(jnp.float32), short_taps)
    k_short, k_pad = causal_short(k_in.astype(jnp.float32), short_taps)
    v_short, v_pad = causal_short(v_in.astype(jnp.float32), short_taps)
    product = lax.optimization_barrier((k_short * v_short).astype(jnp.bfloat16))
    product_wide = product.astype(jnp.float32)
    fft_len = 2 * seq_len
    spec_prod = jnp.fft.rfft(product_wide, n=fft_len, axis=0)
    spec_kernel = jnp.fft.rfft(kernel, n=fft_len, axis=0)
    conv = jnp.fft.irfft(spec_prod * spec_kernel, n=fft_len, axis=0)[:seq_len]
    filtered = conv + skip[None, :] * product_wide
    mixed = (q_short * filtered).astype(jnp.bfloat16)
    upstream = grad_out.astype(jnp.float32)
    back_q = upstream * filtered
    back_mix = upstream * q_short
    back_cast = lax.optimization_barrier(back_mix.astype(jnp.bfloat16)).astype(jnp.float32)
    spec_back = jnp.fft.rfft(back_cast, n=fft_len, axis=0)
    back_prod = jnp.fft.irfft(jnp.conj(spec_kernel) * spec_back, n=fft_len, axis=0)[:seq_len] + skip[None, :] * back_mix
    kernel_grad = jnp.fft.irfft(jnp.conj(spec_prod) * spec_back, n=fft_len, axis=0)[:seq_len]
    back_k = back_prod * v_short
    back_v = back_prod * k_short
    grad_q = causal_adjoint(back_q, short_taps).astype(jnp.bfloat16)
    grad_k = causal_adjoint(back_k, short_taps).astype(jnp.bfloat16)
    grad_v = causal_adjoint(back_v, short_taps).astype(jnp.bfloat16)
    tap_rows = []
    for shift_idx in range(short_taps.shape[0]):
        first = halo_rows - shift_idx
        tap_rows.append(lax.optimization_barrier(jnp.sum(back_q * q_pad[first:first + seq_len] + back_k * k_pad[first:first + seq_len] + back_v * v_pad[first:first + seq_len], axis=0)))
    short_grad = jnp.stack(tap_rows)
    skip_grad = lax.optimization_barrier(jnp.sum(back_mix * product_wide, axis=0))
    return (mixed, grad_q, grad_k, grad_v, short_grad, skip_grad, kernel_grad)

def run_block(pieces):
    return channel_block(*pieces)

def reference(q_in, k_in, v_in, grad_out, short_filter, kernel, skip):
    seq_len, width_all = q_in.shape
    lanes = 128
    block_count = width_all // lanes

    def split_rows(array):
        return array.reshape(seq_len, block_count, lanes).transpose(1, 0, 2)

    def join_rows(array):
        return array.transpose(1, 0, 2).reshape(seq_len, width_all)
    taps_blocks = short_filter.reshape(short_filter.shape[0], block_count, lanes).transpose(1, 0, 2)
    results = lax.map(run_block, (split_rows(q_in), split_rows(k_in), split_rows(v_in), split_rows(grad_out), taps_blocks, split_rows(kernel), skip.reshape(block_count, lanes)))
    short_grad = results[4].transpose(1, 0, 2).reshape(short_filter.shape[0], width_all)
    skip_grad = results[5].reshape(width_all)
    kernel_grad = join_rows(results[6])
    norm_sq = jnp.sum(short_grad * short_grad) + jnp.sum(skip_grad * skip_grad) + jnp.sum(kernel_grad * kernel_grad)
    clip_limit = math.sqrt(float(seq_len * width_all))
    factor = clip_limit / jnp.maximum(jnp.sqrt(norm_sq), clip_limit)
    return (join_rows(results[0]), join_rows(results[1]), join_rows(results[2]), join_rows(results[3]), factor * short_grad, factor * skip_grad, factor * kernel_grad)
```

```python
import math

import jax
import jax.numpy as jnp
import ml_dtypes
import numpy as np
from jax import lax
from jax.experimental import pallas as pl
from jax.experimental.pallas import tpu as pltpu
from jax.sharding import PartitionSpec as P

LANES = 128
SPAN = 256
CHUNK = 16
PAD = 8
VMEM_BYTES = 40 * 1024 * 1024

f32 = jnp.float32
bf16 = jnp.bfloat16


def leaf_phases(count, phase=0.25):
    if count == 1:
        return [phase]
    return leaf_phases(count // 2, phase / 2) + leaf_phases(count // 2, phase / 2 + 0.5)


def turn(re, im, phase):
    cosine = math.cos(2.0 * math.pi * phase)
    sine = math.sin(2.0 * math.pi * phase)
    if im is None:
        return re * cosine, re * (-sine)
    return re * cosine + im * sine, im * cosine - re * sine


def to_leaves(parts, phase=0.25):
    count = len(parts)
    if count == 1:
        return parts
    half = count // 2
    first = []
    second = []
    for low, high in zip(parts[:half], parts[half:]):
        high_re, high_im = turn(high[0], high[1], phase / 2)
        first.append((low[0] + high_re, high_im if low[1] is None else low[1] + high_im))
        second.append((low[0] - high_re, -high_im if low[1] is None else low[1] - high_im))
    return to_leaves(first, phase / 2) + to_leaves(second, phase / 2 + 0.5)


def from_leaves(leaves, phase=0.25, real_only=True):
    count = len(leaves)
    if count == 1:
        return leaves
    half = count // 2
    first = from_leaves(leaves[:half], phase / 2, False)
    second = from_leaves(leaves[half:], phase / 2 + 0.5, False)
    cosine = math.cos(math.pi * phase)
    sine = math.sin(math.pi * phase)
    low = []
    high = []
    for one, two in zip(first, second):
        diff_re = one[0] - two[0]
        diff_im = one[1] - two[1]
        if real_only:
            low.append((one[0] + two[0], None))
            high.append((diff_re * cosine - diff_im * sine, None))
        else:
            low.append((one[0] + two[0], one[1] + two[1]))
            high.append((diff_re * cosine - diff_im * sine, diff_im * cosine + diff_re * sine))
    return low + high


def dft_matrix():
    idx = np.arange(SPAN)
    angle = (idx[:, None] * idx[None, :] % SPAN) * (2.0 * np.pi / SPAN)
    cosine, sine = np.cos(angle), np.sin(angle)
    return np.block([[cosine, sine], [-sine, cosine]])


def twist_table(outer):
    angle = np.asarray(leaf_phases(outer))[:, None] * np.arange(SPAN)[None, :] * (2.0 * np.pi / SPAN)
    return np.stack([np.cos(angle), np.sin(angle)])


def halves(matrix):
    high = matrix.astype(ml_dtypes.bfloat16)
    low = (matrix - high.astype(np.float64)).astype(ml_dtypes.bfloat16)
    return np.concatenate([high, high, low], axis=1)


def split_store(ref, rows, lanes, value):
    high = value.astype(bf16)
    ref[pl.ds(rows, CHUNK), lanes] = high
    ref[pl.ds(2 * SPAN + rows, CHUNK), lanes] = (value - high.astype(f32)).astype(bf16)


def wide_dot(matrix_ref, split_ref, result_ref):
    split = 4 * SPAN
    width = 2 * LANES
    for start in range(0, result_ref.shape[1], width):
        lanes = slice(start, start + width)
        result_ref[:, lanes] = jnp.dot(
            matrix_ref[:, :split], split_ref[:, lanes], preferred_element_type=f32
        ) + jnp.dot(matrix_ref[:, split:], split_ref[: 2 * SPAN, lanes], preferred_element_type=f32)


def signal_spectrum(signal_ref, twist_ref, forward_ref, split_ref, spec_ref):
    outer = signal_ref.shape[0]

    def step(idx, carry):
        row = pl.multiple_of(idx * CHUNK, CHUNK)
        here = pl.ds(row, CHUNK)
        leaves = to_leaves([(signal_ref[part, here, :].astype(f32), None) for part in range(outer)])
        for leaf, (re, im) in enumerate(leaves):
            cosine = twist_ref[0, leaf, here, :]
            sine = twist_ref[1, leaf, here, :]
            lanes = slice(leaf * LANES, (leaf + 1) * LANES)
            split_store(split_ref, row, lanes, re * cosine + im * sine)
            split_store(split_ref, SPAN + row, lanes, im * cosine - re * sine)
        return carry

    lax.fori_loop(0, SPAN // CHUNK, step, 0)
    wide_dot(forward_ref, split_ref, spec_ref)


def combine(left_ref, right_ref, split_ref, conjugate):
    def step(idx, carry):
        row = pl.multiple_of(idx * CHUNK, CHUNK)
        for start in range(0, left_ref.shape[1], LANES):
            lanes = slice(start, start + LANES)
            left_re = left_ref[pl.ds(row, CHUNK), lanes]
            left_im = left_ref[pl.ds(SPAN + row, CHUNK), lanes]
            right_re = right_ref[pl.ds(row, CHUNK), lanes]
            right_im = right_ref[pl.ds(SPAN + row, CHUNK), lanes]
            if conjugate:
                re = left_re * right_re + left_im * right_im
                im = left_re * right_im - left_im * right_re
            else:
                re = left_re * right_re - left_im * right_im
                im = left_re * right_im + left_im * right_re
            split_store(split_ref, row, lanes, re)
            split_store(split_ref, SPAN + row, lanes, im)
        return carry

    lax.fori_loop(0, SPAN // CHUNK, step, 0)


def spectrum_signal(split_ref, inverse_ref, twist_ref, time_ref, signal_ref, square_ref=None):
    outer = signal_ref.shape[0]
    wide_dot(inverse_ref, split_ref, time_ref)

    def step(idx, carry):
        row = pl.multiple_of(idx * CHUNK, CHUNK)
        here = pl.ds(row, CHUNK)
        leaves = []
        for leaf in range(outer):
            cosine = twist_ref[0, leaf, here, :]
            sine = twist_ref[1, leaf, here, :]
            lanes = slice(leaf * LANES, (leaf + 1) * LANES)
            re = time_ref[here, lanes]
            im = time_ref[pl.ds(SPAN + row, CHUNK), lanes]
            leaves.append((re * cosine - im * sine, im * cosine + re * sine))
        parts = from_leaves(leaves)
        for part in range(outer):
            signal_ref[part, here, :] = parts[part][0].astype(bf16)
            if square_ref is not None:
                carry = carry + parts[part][0] * parts[part][0]
        return carry

    total = lax.fori_loop(0, SPAN // CHUNK, step, jnp.zeros((CHUNK, LANES), f32))
    if square_ref is not None:
        square_ref[...] = total


def filter_kernel(filter_ref, twist_ref, forward_ref, spec_ref, split_ref):
    signal_spectrum(filter_ref, twist_ref, forward_ref, split_ref, spec_ref)


def conv_kernel(
    product_ref, filter_spec_ref, twist_ref, forward_ref, inverse_ref,
    conv_ref, product_spec_ref, split_ref, time_ref,
):
    signal_spectrum(product_ref, twist_ref, forward_ref, split_ref, product_spec_ref)
    combine(filter_spec_ref, product_spec_ref, split_ref, False)
    spectrum_signal(split_ref, inverse_ref, twist_ref, time_ref, conv_ref)


def corr_kernel(
    cotan_ref, filter_spec_ref, product_spec_ref, twist_ref, forward_ref, inverse_ref,
    corr_ref, lag_ref, square_ref, cotan_spec_ref, split_ref, time_ref,
):
    signal_spectrum(cotan_ref, twist_ref, forward_ref, split_ref, cotan_spec_ref)
    combine(filter_spec_ref, cotan_spec_ref, split_ref, True)
    spectrum_signal(split_ref, inverse_ref, twist_ref, time_ref, corr_ref)
    combine(product_spec_ref, cotan_spec_ref, split_ref, True)
    spectrum_signal(split_ref, inverse_ref, twist_ref, time_ref, lag_ref, square_ref)


def call(kernel, outs, scratch, *args, **options):
    return pl.pallas_call(
        kernel,
        out_shape=outs,
        scratch_shapes=scratch,
        compiler_params=pltpu.CompilerParams(vmem_limit_bytes=VMEM_BYTES),
        **options,
    )(*args)


class Transforms:
    def __init__(self, seq_len):
        self.outer = seq_len // SPAN
        matrix = dft_matrix()
        self.forward = jnp.asarray(halves(matrix))
        self.inverse = jnp.asarray(halves(matrix.T / seq_len))
        twist = twist_table(self.outer).astype(np.float32)[..., None]
        self.twist = jnp.broadcast_to(jnp.asarray(twist), twist.shape[:3] + (LANES,))
        self.spec = jax.ShapeDtypeStruct((2 * SPAN, self.outer * LANES), f32)
        self.time = jax.ShapeDtypeStruct((self.outer, SPAN, LANES), bf16)
        self.square = jax.ShapeDtypeStruct((CHUNK, LANES), f32)
        self.split = pltpu.VMEM((4 * SPAN, self.outer * LANES), bf16)
        self.work = pltpu.VMEM(self.spec.shape, f32)

    def filter(self, kernel):
        return call(
            filter_kernel, self.spec, [self.split],
            kernel.reshape(self.time.shape), self.twist, self.forward,
        )

    def conv(self, product, filter_spec):
        return call(
            conv_kernel, (self.time, self.spec), [self.split, self.work],
            product.reshape(self.time.shape), filter_spec, self.twist, self.forward, self.inverse,
        )

    def corr(self, cotan, filter_spec, product_spec):
        return call(
            corr_kernel, (self.time, self.time, self.square), [self.work, self.split, self.work],
            cotan.reshape(self.time.shape), filter_spec, product_spec,
            self.twist, self.forward, self.inverse,
        )


class PlainTransforms:
    def __init__(self, seq_len):
        self.seq_len = seq_len
        self.outer = seq_len // SPAN
        idx = np.arange(SPAN)
        angle = (idx[:, None] * idx[None, :] % SPAN) * (2.0 * np.pi / SPAN)
        self.cosine = jnp.asarray(np.cos(angle), f32)
        self.sine = jnp.asarray(np.sin(angle), f32)
        self.twist = jnp.asarray(twist_table(self.outer), f32)[..., None]

    def dot(self, matrix, signal):
        return jnp.einsum("fs,tsc->tfc", matrix, signal, precision=lax.Precision.HIGHEST)

    def filter(self, signal):
        parts = signal.astype(f32).reshape(self.outer, SPAN, -1)
        leaves = to_leaves([(parts[part], None) for part in range(self.outer)])
        re = jnp.stack([leaf[0] for leaf in leaves])
        im = jnp.stack([leaf[1] for leaf in leaves])
        twist_re = re * self.twist[0] + im * self.twist[1]
        twist_im = im * self.twist[0] - re * self.twist[1]
        return (
            self.dot(self.cosine, twist_re) + self.dot(self.sine, twist_im),
            self.dot(self.cosine, twist_im) - self.dot(self.sine, twist_re),
        )

    def back(self, re, im):
        time_re = self.dot(self.cosine, re) - self.dot(self.sine, im)
        time_im = self.dot(self.cosine, im) + self.dot(self.sine, re)
        leaf_re = time_re * self.twist[0] - time_im * self.twist[1]
        leaf_im = time_im * self.twist[0] + time_re * self.twist[1]
        parts = from_leaves([(leaf_re[leaf], leaf_im[leaf]) for leaf in range(self.outer)])
        return jnp.stack([part[0] for part in parts]) * (1.0 / self.seq_len)

    def conv(self, product, filter_spec):
        spec = self.filter(product)
        re = filter_spec[0] * spec[0] - filter_spec[1] * spec[1]
        im = filter_spec[0] * spec[1] + filter_spec[1] * spec[0]
        return self.back(re, im).astype(bf16), spec

    def corr(self, cotan, filter_spec, product_spec):
        spec = self.filter(cotan)
        results = []
        for other in (filter_spec, product_spec):
            re = other[0] * spec[0] + other[1] * spec[1]
            im = other[0] * spec[1] - other[1] * spec[0]
            results.append(self.back(re, im))
        squares = jnp.sum(results[1] * results[1], axis=(0, 1))[None, :]
        return results[0].astype(bf16), results[1].astype(bf16), squares


def group(idx):
    return slice(idx * LANES, (idx + 1) * LANES)


def pack_kernel(wide_ref, packed_ref):
    for idx in range(packed_ref.shape[0]):
        packed_ref[idx] = wide_ref[:, group(idx)].astype(packed_ref.dtype)


def extend_rows(lead, rows, ext_ref):
    halo_rows = lead.shape[0]
    ext_ref[PAD - halo_rows : PAD, :] = lead.astype(f32)
    ext_ref[PAD:, :] = rows.astype(f32)


def delayed(ext_ref, by):
    return ext_ref[PAD - by : ext_ref.shape[0] - by, :]


def short_conv(ext_ref, taps):
    result = taps[0:1] * delayed(ext_ref, 0)
    for shift_idx in range(1, taps.shape[0]):
        result = result + taps[shift_idx : shift_idx + 1] * delayed(ext_ref, shift_idx)
    return result


def signals_kernel(
    q_ref, k_ref, v_ref, grad_ref, lead_ref, taps_ref, product_ref, cotan_ref, q_ext, k_ext, v_ext
):
    halo_rows = taps_ref.shape[0] - 1
    for idx in range(product_ref.shape[0]):
        lanes = group(idx)
        taps = taps_ref[:, lanes]
        for place, (ref, ext) in enumerate(((q_ref, q_ext), (k_ref, k_ext), (v_ref, v_ext))):
            extend_rows(lead_ref[place * halo_rows : (place + 1) * halo_rows, lanes], ref[:, lanes], ext)
        product_ref[idx] = (short_conv(k_ext, taps) * short_conv(v_ext, taps)).astype(bf16)
        cotan_ref[idx] = (grad_ref[:, lanes].astype(f32) * short_conv(q_ext, taps)).astype(bf16)


def finish_kernel(
    q_ref, k_ref, v_ref, grad_ref, lead_ref, taps_ref, skip_ref, conv_ref, corr_ref,
    mixed_ref, grad_q_ref, grad_k_ref, grad_v_ref, edge_ref, sums_ref,
    q_ext, k_ext, v_ext, back_ext,
):
    taps_count = taps_ref.shape[0]
    halo_rows = taps_count - 1
    rows_here = q_ref.shape[0]
    sums_ref[...] = jnp.zeros_like(sums_ref)
    back_ext[rows_here:, :] = jnp.zeros((PAD, LANES), f32)
    for idx in range(conv_ref.shape[0]):
        lanes = group(idx)
        taps = taps_ref[:, lanes]
        skip = skip_ref[:, lanes]
        exts = (q_ext, k_ext, v_ext)
        for place, (ref, ext) in enumerate(zip((q_ref, k_ref, v_ref), exts)):
            extend_rows(lead_ref[place * halo_rows : (place + 1) * halo_rows, lanes], ref[:, lanes], ext)
        q_short = short_conv(q_ext, taps)
        k_short = short_conv(k_ext, taps)
        v_short = short_conv(v_ext, taps)
        product = (k_short * v_short).astype(bf16).astype(f32)
        filtered = conv_ref[idx].astype(f32) + skip * product
        mixed_ref[:, lanes] = (q_short * filtered).astype(bf16)
        upstream = grad_ref[:, lanes].astype(f32)
        back_q = upstream * filtered
        back_mix = upstream * q_short
        back_prod = corr_ref[idx].astype(f32) + skip * back_mix
        sums_ref[idx, taps_count : taps_count + 1, :] = jnp.sum(back_mix * product, axis=0, keepdims=True)
        backs = (back_q, back_prod * v_short, back_prod * k_short)
        taps_sums = [0.0] * taps_count
        for place, (back, ext, out_ref) in enumerate(
            zip(backs, exts, (grad_q_ref, grad_k_ref, grad_v_ref))
        ):
            for shift_idx in range(taps_count):
                taps_sums[shift_idx] = taps_sums[shift_idx] + back * delayed(ext, shift_idx)
            back_ext[:rows_here, :] = back
            grad = taps[0:1] * back
            for shift_idx in range(1, taps_count):
                grad = grad + taps[shift_idx : shift_idx + 1] * back_ext[shift_idx : shift_idx + rows_here, :]
            out_ref[:, lanes] = grad.astype(bf16)
            edge_ref[place, 0:halo_rows, lanes] = back[:halo_rows]
            edge_ref[place, halo_rows : 2 * halo_rows, lanes] = grad[rows_here - halo_rows :]
        for shift_idx in range(taps_count):
            sums_ref[idx, shift_idx : shift_idx + 1, :] = jnp.sum(taps_sums[shift_idx], axis=0, keepdims=True)


def edges_kernel(edge_ref, tail_ref, taps_ref, q_ref, k_ref, v_ref, q_out, k_out, v_out, work_ref):
    taps_count = taps_ref.shape[0]
    halo_rows = taps_count - 1
    block_rows = q_ref.shape[0]
    for place, (ref, out_ref) in enumerate(((q_ref, q_out), (k_ref, k_out), (v_ref, v_out))):
        work_ref[...] = ref[...].astype(f32)
        for row in range(halo_rows):
            total = edge_ref[place, halo_rows + row : halo_rows + row + 1, :]
            for shift_idx in range(halo_rows - row, taps_count):
                source = row + shift_idx - halo_rows
                total = total + taps_ref[shift_idx : shift_idx + 1, :] * tail_ref[place, source : source + 1, :]
            at = block_rows - halo_rows + row
            work_ref[at : at + 1, :] = total
        out_ref[...] = work_ref[...].astype(bf16)


def scale_kernel(here_ref, limit, all_ref, lag_ref, taps_out, skip_out, kernel_out):
    taps_count = taps_out.shape[0]
    pieces = all_ref.shape[0]
    squares = jnp.sum(all_ref[:, :, taps_count + 1, :])
    factor = limit / jnp.maximum(jnp.sqrt(jnp.full((1, LANES), squares)), limit)
    share = all_ref.shape[-1]
    for piece in range(pieces):
        own = all_ref[piece, here_ref[0]]
        lanes = slice(piece * share, (piece + 1) * share)
        taps_out[:, lanes] = own[0:taps_count] * factor[:, :share]
        skip_out[:, lanes] = own[taps_count : taps_count + 1] * factor[:, :share]
    for idx in range(lag_ref.shape[0]):
        kernel_out[:, group(idx)] = lag_ref[idx].astype(f32) * factor


def exchange(pieces_first, axes="ctx"):
    return lax.all_to_all(pieces_first, axes, split_axis=0, concat_axis=0, tiled=True)


def to_pieces(groups, pieces):
    count, rows, lanes = groups.shape
    if count == pieces:
        return groups
    share = count * lanes // pieces
    split = groups.reshape(count, rows, lanes // share, share)
    return split.transpose(0, 2, 1, 3).reshape(pieces, rows, share)


def to_groups(parts):
    pieces, rows, share = parts.shape
    if share == LANES:
        return parts
    joined = parts.reshape(pieces * share // LANES, LANES // share, rows, share)
    return joined.transpose(0, 2, 1, 3).reshape(-1, rows, LANES)


def body(q_in, k_in, v_in, grad_out, short_filter, kernel, skip):
    pieces = lax.axis_size("ctx")
    sides = lax.axis_size("ch")
    rows_here, channels = q_in.shape
    seq_len = pieces * rows_here
    taps_count = short_filter.shape[0]
    halo_rows = taps_count - 1
    groups = channels // LANES
    share = channels // pieces
    at_once = min(groups, 4)
    steps = groups // at_once
    width = at_once * LANES
    skip_row = skip.reshape(1, channels)
    transforms = (Transforms if share == LANES else PlainTransforms)(seq_len)

    rows_spec = pl.BlockSpec((rows_here, width), lambda i: (0, i))
    group_spec = pl.BlockSpec((at_once, rows_here, LANES), lambda i: (i, 0, 0))
    lead_spec = pl.BlockSpec((3 * halo_rows, width), lambda i: (0, i))
    taps_spec = pl.BlockSpec((taps_count, width), lambda i: (0, i))
    skip_spec = pl.BlockSpec((1, width), lambda i: (0, i))
    sums_spec = pl.BlockSpec((at_once, PAD, LANES), lambda i: (i, 0, 0))
    edge_spec = pl.BlockSpec((3, 2 * halo_rows, width), lambda i: (0, 0, i))
    grouped = jax.ShapeDtypeStruct((groups, rows_here, LANES), bf16)
    flat = jax.ShapeDtypeStruct((rows_here, channels), bf16)
    ext = pltpu.VMEM((rows_here + PAD, LANES), f32)

    lead = jnp.concatenate([x[rows_here - halo_rows :] for x in (q_in, k_in, v_in)], axis=0)
    lead = lax.ppermute(lead, "ctx", [(i, i + 1) for i in range(pieces - 1)])

    packed = call(pack_kernel, grouped, [], kernel, grid=(steps,), in_specs=[rows_spec], out_specs=group_spec)
    filter_here = exchange(to_pieces(packed, pieces))
    product, cotan = call(
        signals_kernel, (grouped, grouped), [ext, ext, ext],
        q_in, k_in, v_in, grad_out, lead, short_filter,
        grid=(steps,),
        in_specs=[rows_spec] * 4 + [lead_spec, taps_spec],
        out_specs=(group_spec, group_spec),
    )
    product_here = exchange(to_pieces(product, pieces))
    cotan_here = exchange(to_pieces(cotan, pieces))

    filter_spec = transforms.filter(filter_here)
    conv, product_spec = transforms.conv(product_here, filter_spec)
    conv = to_groups(exchange(conv.reshape(pieces, rows_here, share)))
    corr, lag, lag_squares = transforms.corr(cotan_here, filter_spec, product_spec)
    corr = to_groups(exchange(corr.reshape(pieces, rows_here, share)))
    lag = to_groups(exchange(lag.reshape(pieces, rows_here, share)))

    mixed, grad_q, grad_k, grad_v, edge, sums = call(
        finish_kernel,
        (
            flat, flat, flat, flat,
            jax.ShapeDtypeStruct((3, 2 * halo_rows, channels), f32),
            jax.ShapeDtypeStruct((groups, PAD, LANES), f32),
        ),
        [ext, ext, ext, ext],
        q_in, k_in, v_in, grad_out, lead, short_filter, skip_row, conv, corr,
        grid=(steps,),
        in_specs=[rows_spec] * 4 + [lead_spec, taps_spec, skip_spec, group_spec, group_spec],
        out_specs=(rows_spec,) * 4 + (edge_spec, sums_spec),
    )

    sums_here = jnp.sum(exchange(to_pieces(sums, pieces)), axis=0)
    squares = jnp.sum(lag_squares, axis=0) + jnp.sum(sums_here * sums_here, axis=0)
    shared = jnp.concatenate([sums_here[: taps_count + 1], squares[None], sums_here[taps_count + 2 :]], axis=0)
    everyone = exchange(
        jnp.broadcast_to(shared[None], (pieces * sides,) + shared.shape), ("ctx", "ch")
    ).reshape(pieces, sides, PAD, share)

    tail = lax.ppermute(edge[:, :halo_rows], "ctx", [(i, i - 1) for i in range(1, pieces)])
    last_block = 16
    last_spec = pl.BlockSpec((last_block, channels), lambda i: (rows_here // last_block - 1, 0))
    whole = lambda *dims: pl.BlockSpec(dims, lambda i: (0,) * len(dims))
    grad_q, grad_k, grad_v = call(
        edges_kernel, (flat, flat, flat), [pltpu.VMEM((last_block, channels), f32)],
        edge, tail, short_filter, grad_q, grad_k, grad_v,
        grid=(1,),
        in_specs=[whole(*edge.shape), whole(*tail.shape), whole(*short_filter.shape)] + [last_spec] * 3,
        out_specs=(last_spec,) * 3,
        input_output_aliases={3: 0, 4: 1, 5: 2},
    )

    limit = math.sqrt(float(seq_len * channels * sides))
    grad_short, grad_skip, grad_kernel = call(
        lambda here, *refs: scale_kernel(here, limit, *refs),
        (
            jax.ShapeDtypeStruct((taps_count, channels), f32),
            jax.ShapeDtypeStruct((1, channels), f32),
            jax.ShapeDtypeStruct((rows_here, channels), f32),
        ),
        [],
        lax.axis_index("ch").reshape(1), everyone, lag,
        in_specs=[pl.BlockSpec(memory_space=pltpu.SMEM)] + [pl.BlockSpec(memory_space=pltpu.VMEM)] * 2,
        out_specs=(pl.BlockSpec(memory_space=pltpu.VMEM),) * 3,
    )
    return mixed, grad_q, grad_k, grad_v, grad_short, grad_skip.reshape(channels), grad_kernel


def solution(mesh):
    in_specs = (
        P("ctx", "ch"),
        P("ctx", "ch"),
        P("ctx", "ch"),
        P("ctx", "ch"),
        P(None, "ch"),
        P("ctx", "ch"),
        P("ch"),
    )
    out_specs = (
        P("ctx", "ch"),
        P("ctx", "ch"),
        P("ctx", "ch"),
        P("ctx", "ch"),
        P(None, "ch"),
        P("ch"),
        P("ctx", "ch"),
    )
    return jax.shard_map(body, mesh=mesh, in_specs=in_specs, out_specs=out_specs, check_vma=False)
```

```python
import math

import jax
import jax.numpy as jnp
import ml_dtypes
import numpy as np
from jax import lax
from jax.experimental import pallas as pl
from jax.experimental.pallas import tpu as pltpu
from jax.sharding import PartitionSpec as P

LANES = 128
SPAN = 256
CHUNK = 16
PAD = 8
BOTH = 2 * SPAN
VMEM_BYTES = 58 * 1024 * 1024
SMALL_VMEM_BYTES = 8 * 1024 * 1024

f32 = jnp.float32
bf16 = jnp.bfloat16


def leaf_phases(count, phase=0.25):
    if count == 1:
        return [phase]
    return leaf_phases(count // 2, phase / 2) + leaf_phases(count // 2, phase / 2 + 0.5)


def turn(re, im, phase):
    cosine = math.cos(2.0 * math.pi * phase)
    sine = math.sin(2.0 * math.pi * phase)
    if im is None:
        return re * cosine, re * (-sine)
    return re * cosine + im * sine, im * cosine - re * sine


def to_leaves(parts, phase=0.25):
    count = len(parts)
    if count == 1:
        return parts
    half = count // 2
    first = []
    second = []
    for low, high in zip(parts[:half], parts[half:]):
        high_re, high_im = turn(high[0], high[1], phase / 2)
        first.append((low[0] + high_re, high_im if low[1] is None else low[1] + high_im))
        second.append((low[0] - high_re, -high_im if low[1] is None else low[1] - high_im))
    return to_leaves(first, phase / 2) + to_leaves(second, phase / 2 + 0.5)


def from_leaves(leaves, phase=0.25, real_only=True):
    count = len(leaves)
    if count == 1:
        return leaves
    half = count // 2
    first = from_leaves(leaves[:half], phase / 2, False)
    second = from_leaves(leaves[half:], phase / 2 + 0.5, False)
    cosine = math.cos(math.pi * phase)
    sine = math.sin(math.pi * phase)
    low = []
    high = []
    for one, two in zip(first, second):
        diff_re = one[0] - two[0]
        diff_im = one[1] - two[1]
        if real_only:
            low.append((one[0] + two[0], None))
            high.append((diff_re * cosine - diff_im * sine, None))
        else:
            low.append((one[0] + two[0], one[1] + two[1]))
            high.append((diff_re * cosine - diff_im * sine, diff_im * cosine + diff_re * sine))
    return low + high


def dft_matrix():
    idx = np.arange(SPAN)
    angle = (idx[:, None] * idx[None, :] % SPAN) * (2.0 * np.pi / SPAN)
    cosine, sine = np.cos(angle), np.sin(angle)
    return np.block([[cosine, sine], [-sine, cosine]])


def twist_table(outer):
    angle = np.asarray(leaf_phases(outer))[:, None] * np.arange(SPAN)[None, :] * (2.0 * np.pi / SPAN)
    return np.stack([np.cos(angle), np.sin(angle)])


def halves(matrix):
    high = matrix.astype(ml_dtypes.bfloat16)
    low = (matrix - high.astype(np.float64)).astype(ml_dtypes.bfloat16)
    return np.stack([high, low])


def leaf_lanes(leaf):
    return slice(leaf * LANES, (leaf + 1) * LANES)


def split_store(ref, row, lanes, value):
    high = value.astype(bf16)
    low = (value - high.astype(f32)).astype(bf16)
    ref[pl.ds(row, CHUNK), lanes] = high
    ref[pl.ds(BOTH + row, CHUNK), lanes] = low
    ref[pl.ds(2 * BOTH + row, CHUNK), lanes] = high


def matrix_copies(matrix_hbm, matrix_ref, sems):
    return [
        pltpu.make_async_copy(
            matrix_hbm.at[half], matrix_ref.at[:, pl.ds(place * BOTH, BOTH)], sems.at[place]
        )
        for place, half in enumerate((0, 0, 1))
    ]


def transform(matrix_ref, split_ref, result_ref):
    for start in range(0, result_ref.shape[1], 2 * LANES):
        lanes = slice(start, start + 2 * LANES)
        result_ref[:, lanes] = jnp.dot(matrix_ref[...], split_ref[:, lanes], preferred_element_type=f32)


def spread_twist(column_ref, twist_ref):
    outer = twist_ref.shape[1]

    def step(idx, carry):
        here = pl.ds(pl.multiple_of(idx * CHUNK, CHUNK), CHUNK)
        columns = column_ref[here, :]
        for leaf in range(outer):
            for side in range(2):
                column = columns[:, side * outer + leaf : side * outer + leaf + 1]
                twist_ref[side, leaf, here, :] = jnp.broadcast_to(column, (CHUNK, LANES))
        return carry

    lax.fori_loop(0, SPAN // CHUNK, step, 0)


def over_chunks(rows_here, step, carry=0):
    for piece in range(SPAN // rows_here):

        def inner(idx, carry, piece=piece):
            row = pl.multiple_of(idx * CHUNK, CHUNK)
            return step(piece, row, pl.multiple_of(piece * rows_here + row, CHUNK), carry)

        carry = lax.fori_loop(0, rows_here // CHUNK, inner, carry)
    return carry


def leaves_of(read, rows_here, twist_ref, split_ref):
    outer = twist_ref.shape[1]
    ratio = SPAN // rows_here

    def step(piece, row, span_row, carry):
        here = pl.ds(span_row, CHUNK)
        parts = [(read(part * ratio + piece, pl.ds(row, CHUNK)).astype(f32), None) for part in range(outer)]
        for leaf, (re, im) in enumerate(to_leaves(parts)):
            cosine = twist_ref[0, leaf, here, :]
            sine = twist_ref[1, leaf, here, :]
            split_store(split_ref, span_row, leaf_lanes(leaf), re * cosine + im * sine)
            split_store(split_ref, SPAN + span_row, leaf_lanes(leaf), im * cosine - re * sine)
        return carry

    over_chunks(rows_here, step)


def combine(left_ref, right_ref, split_ref, conjugate):
    def step(idx, carry):
        row = pl.multiple_of(idx * CHUNK, CHUNK)
        for leaf in range(left_ref.shape[1] // LANES):
            lanes = leaf_lanes(leaf)
            left_re = left_ref[pl.ds(row, CHUNK), lanes]
            left_im = left_ref[pl.ds(SPAN + row, CHUNK), lanes]
            right_re = right_ref[pl.ds(row, CHUNK), lanes]
            right_im = right_ref[pl.ds(SPAN + row, CHUNK), lanes]
            if conjugate:
                re = left_re * right_re + left_im * right_im
                minus_im = left_im * right_re - left_re * right_im
            else:
                re = left_re * right_re - left_im * right_im
                minus_im = -left_re * right_im - left_im * right_re
            split_store(split_ref, row, lanes, re)
            split_store(split_ref, SPAN + row, lanes, minus_im)
        return carry

    lax.fori_loop(0, SPAN // CHUNK, step, 0)


def signal_of(time_ref, twist_ref, rows_here, write, carry=0):
    outer = twist_ref.shape[1]
    ratio = SPAN // rows_here
    scale = 1.0 / (SPAN * outer)

    def step(piece, row, span_row, carry):
        here = pl.ds(span_row, CHUNK)
        leaves = []
        for leaf in range(outer):
            cosine = twist_ref[0, leaf, here, :]
            sine = twist_ref[1, leaf, here, :]
            re = time_ref[here, leaf_lanes(leaf)]
            minus_im = time_ref[pl.ds(SPAN + span_row, CHUNK), leaf_lanes(leaf)]
            leaves.append((re * cosine + minus_im * sine, re * sine - minus_im * cosine))
        for part, (value, _) in enumerate(from_leaves(leaves)):
            carry = write(part * ratio + piece, pl.ds(row, CHUNK), value * scale, carry)
        return carry

    return over_chunks(rows_here, step, carry)


def filter_kernel(filter_ref, column_ref, matrix_hbm, spec_ref, twist_ref, matrix_ref, split_ref, sems):
    copies = matrix_copies(matrix_hbm, matrix_ref, sems)
    for copy in copies:
        copy.start()
    spread_twist(column_ref, twist_ref)
    leaves_of(lambda piece, rows: filter_ref[piece, rows, :], filter_ref.shape[1], twist_ref, split_ref)
    for copy in copies:
        copy.wait()
    transform(matrix_ref, split_ref, spec_ref)


def products_kernel(
    signals_ref, column_ref, matrix_hbm, filter_hbm, results_ref, lag_hbm,
    twist_ref, matrix_ref, split_ref, lag_split_ref, filter_ref, product_ref, cotan_ref, time_ref, sems,
):
    rows_here = signals_ref.shape[2]
    copies = matrix_copies(matrix_hbm, matrix_ref, sems)
    filter_copy = pltpu.make_async_copy(filter_hbm, filter_ref, sems.at[3])
    lag_copy = pltpu.make_async_copy(lag_split_ref, lag_hbm, sems.at[4])
    for copy in copies + [filter_copy]:
        copy.start()
    spread_twist(column_ref, twist_ref)
    leaves_of(lambda piece, rows: signals_ref[piece, 0, rows, :], rows_here, twist_ref, split_ref)
    for copy in copies:
        copy.wait()
    transform(matrix_ref, split_ref, product_ref)
    leaves_of(lambda piece, rows: signals_ref[piece, 1, rows, :], rows_here, twist_ref, split_ref)
    transform(matrix_ref, split_ref, cotan_ref)
    combine(product_ref, cotan_ref, lag_split_ref, True)
    lag_copy.start()
    filter_copy.wait()
    for place, (other_ref, conjugate) in enumerate(((product_ref, False), (cotan_ref, True))):
        combine(filter_ref, other_ref, split_ref, conjugate)
        transform(matrix_ref, split_ref, time_ref)

        def write(piece, rows, value, carry, place=place):
            results_ref[piece, place, rows, :] = value.astype(bf16)
            return carry

        signal_of(time_ref, twist_ref, rows_here, write)
    lag_copy.wait()


def lag_kernel(
    split_hbm, column_ref, matrix_hbm, lag_ref, square_ref, twist_ref, matrix_ref, split_ref, time_ref, sems
):
    copies = matrix_copies(matrix_hbm, matrix_ref, sems)
    copies.append(pltpu.make_async_copy(split_hbm, split_ref, sems.at[3]))
    for copy in copies:
        copy.start()
    spread_twist(column_ref, twist_ref)
    for copy in copies:
        copy.wait()
    transform(matrix_ref, split_ref, time_ref)

    def write(piece, rows, value, carry):
        lag_ref[piece, rows, :] = value.astype(bf16)
        return carry + value * value

    square_ref[...] = signal_of(
        time_ref, twist_ref, lag_ref.shape[1], write, jnp.zeros((CHUNK, LANES), f32)
    )


def call(kernel, outs, scratch, *args, vmem_bytes=VMEM_BYTES, **options):
    return pl.pallas_call(
        kernel,
        out_shape=outs,
        scratch_shapes=scratch,
        compiler_params=pltpu.CompilerParams(vmem_limit_bytes=vmem_bytes),
        **options,
    )(*args)


IN_VMEM = pl.BlockSpec(memory_space=pltpu.VMEM)
ANYWHERE = pl.BlockSpec(memory_space=pl.ANY)


class Transforms:
    def __init__(self, pieces, rows_here):
        outer = pieces * rows_here // SPAN
        self.matrix = jnp.asarray(halves(dft_matrix()))
        twist = twist_table(outer).astype(np.float32).reshape(2 * outer, SPAN)
        self.column = jnp.asarray(np.ascontiguousarray(twist.T))
        self.spec = jax.ShapeDtypeStruct((BOTH, outer * LANES), f32)
        self.split = jax.ShapeDtypeStruct((3 * BOTH, outer * LANES), bf16)
        self.signal = jax.ShapeDtypeStruct((pieces, rows_here, LANES), bf16)
        self.pair = jax.ShapeDtypeStruct((pieces, 2, rows_here, LANES), bf16)
        self.square = jax.ShapeDtypeStruct((CHUNK, LANES), f32)
        self.work = pltpu.VMEM(self.spec.shape, f32)
        self.split_work = pltpu.VMEM(self.split.shape, bf16)
        self.tables = [pltpu.VMEM((2, outer, SPAN, LANES), f32), pltpu.VMEM((BOTH, 3 * BOTH), bf16)]

    def filter(self, signal):
        return call(
            filter_kernel, self.spec, self.tables + [self.split_work, pltpu.SemaphoreType.DMA((3,))],
            signal, self.column, self.matrix,
            in_specs=[IN_VMEM, IN_VMEM, ANYWHERE],
            out_specs=IN_VMEM,
        )

    def products(self, signals, filter_spec):
        return call(
            products_kernel, (self.pair, self.split),
            self.tables
            + [self.split_work, self.split_work, self.work, self.work, self.work, self.work]
            + [pltpu.SemaphoreType.DMA((5,))],
            signals, self.column, self.matrix, filter_spec,
            in_specs=[IN_VMEM, IN_VMEM, ANYWHERE, ANYWHERE],
            out_specs=(IN_VMEM, ANYWHERE),
        )

    def lag(self, lag_split):
        return call(
            lag_kernel, (self.signal, self.square),
            self.tables + [self.split_work, self.work, pltpu.SemaphoreType.DMA((4,))],
            lag_split, self.column, self.matrix,
            in_specs=[ANYWHERE, IN_VMEM, ANYWHERE],
            out_specs=(IN_VMEM, IN_VMEM),
        )


class PlainTransforms:
    def __init__(self, pieces, rows_here):
        self.seq_len = pieces * rows_here
        self.pieces = pieces
        self.outer = self.seq_len // SPAN
        idx = np.arange(SPAN)
        angle = (idx[:, None] * idx[None, :] % SPAN) * (2.0 * np.pi / SPAN)
        self.cosine = jnp.asarray(np.cos(angle), f32)
        self.sine = jnp.asarray(np.sin(angle), f32)
        self.twist = jnp.asarray(twist_table(self.outer), f32)[..., None]

    def dot(self, matrix, signal):
        return jnp.einsum("fs,tsc->tfc", matrix, signal, precision=lax.Precision.HIGHEST)

    def filter(self, signal):
        parts = signal.astype(f32).reshape(self.outer, SPAN, -1)
        leaves = to_leaves([(parts[part], None) for part in range(self.outer)])
        re = jnp.stack([leaf[0] for leaf in leaves])
        im = jnp.stack([leaf[1] for leaf in leaves])
        twist_re = re * self.twist[0] + im * self.twist[1]
        twist_im = im * self.twist[0] - re * self.twist[1]
        return (
            self.dot(self.cosine, twist_re) + self.dot(self.sine, twist_im),
            self.dot(self.cosine, twist_im) - self.dot(self.sine, twist_re),
        )

    def back(self, re, im):
        time_re = self.dot(self.cosine, re) - self.dot(self.sine, im)
        time_im = self.dot(self.cosine, im) + self.dot(self.sine, re)
        leaf_re = time_re * self.twist[0] - time_im * self.twist[1]
        leaf_im = time_im * self.twist[0] + time_re * self.twist[1]
        parts = from_leaves([(leaf_re[leaf], leaf_im[leaf]) for leaf in range(self.outer)])
        signal = jnp.stack([part[0] for part in parts]) * (1.0 / self.seq_len)
        return signal.reshape(self.pieces, self.seq_len // self.pieces, -1)

    def products(self, signals, filter_spec):
        product = self.filter(signals[:, 0])
        cotan = self.filter(signals[:, 1])
        conv = self.back(
            filter_spec[0] * product[0] - filter_spec[1] * product[1],
            filter_spec[0] * product[1] + filter_spec[1] * product[0],
        )
        corr = self.back(
            filter_spec[0] * cotan[0] + filter_spec[1] * cotan[1],
            filter_spec[0] * cotan[1] - filter_spec[1] * cotan[0],
        )
        lag = (
            product[0] * cotan[0] + product[1] * cotan[1],
            product[0] * cotan[1] - product[1] * cotan[0],
        )
        return jnp.stack([conv, corr], axis=1).astype(bf16), lag

    def lag(self, lag_spec):
        lag = self.back(*lag_spec)
        return lag.astype(bf16), jnp.sum(lag * lag, axis=(0, 1))[None, :]


def group(idx):
    return slice(idx * LANES, (idx + 1) * LANES)


def pack_kernel(wide_ref, packed_ref):
    for idx in range(packed_ref.shape[0]):
        packed_ref[idx] = wide_ref[:, group(idx)].astype(packed_ref.dtype)


def extend_rows(lead, rows, ext_ref):
    halo_rows = lead.shape[0]
    ext_ref[PAD - halo_rows : PAD, :] = lead.astype(f32)
    ext_ref[PAD:, :] = rows.astype(f32)


def delayed(ext_ref, by):
    return ext_ref[PAD - by : ext_ref.shape[0] - by, :]


def short_conv(ext_ref, taps):
    result = taps[0:1] * delayed(ext_ref, 0)
    for shift_idx in range(1, taps.shape[0]):
        result = result + taps[shift_idx : shift_idx + 1] * delayed(ext_ref, shift_idx)
    return result


def signals_kernel(
    q_ref, k_ref, v_ref, grad_ref, lead_ref, taps_ref, signals_ref, short_ref, q_ext, k_ext, v_ext
):
    halo_rows = taps_ref.shape[0] - 1
    for idx in range(signals_ref.shape[0]):
        lanes = group(idx)
        taps = taps_ref[:, lanes]
        shorts = []
        for place, (ref, ext) in enumerate(((q_ref, q_ext), (k_ref, k_ext), (v_ref, v_ext))):
            extend_rows(lead_ref[place * halo_rows : (place + 1) * halo_rows, lanes], ref[:, lanes], ext)
            shorts.append(short_conv(ext, taps))
            short_ref[place, :, lanes] = shorts[place]
        signals_ref[idx, 0] = (shorts[1] * shorts[2]).astype(bf16)
        signals_ref[idx, 1] = (grad_ref[:, lanes].astype(f32) * shorts[0]).astype(bf16)


def finish_kernel(
    q_ref, k_ref, v_ref, grad_ref, short_ref, lead_ref, taps_ref, skip_ref, long_ref,
    mixed_ref, grad_q_ref, grad_k_ref, grad_v_ref, edge_ref, sums_ref,
    q_back, k_back, v_back,
):
    taps_count = taps_ref.shape[0]
    halo_rows = taps_count - 1
    rows_here = q_ref.shape[0]
    for ext in (q_back, k_back, v_back):
        ext[rows_here:, :] = jnp.zeros((PAD, LANES), f32)
    for idx in range(long_ref.shape[0]):
        lanes = group(idx)
        taps = taps_ref[:, lanes]
        skip = skip_ref[:, lanes]
        q_short = short_ref[0, :, lanes]
        k_short = short_ref[1, :, lanes]
        v_short = short_ref[2, :, lanes]
        product = (k_short * v_short).astype(bf16).astype(f32)
        filtered = long_ref[idx, 0].astype(f32) + skip * product
        mixed_ref[:, lanes] = (q_short * filtered).astype(bf16)
        upstream = grad_ref[:, lanes].astype(f32)
        back_mix = upstream * q_short
        back_prod = long_ref[idx, 1].astype(f32) + skip * back_mix
        sums_ref[taps_count : taps_count + 1, lanes] = jnp.sum(back_mix * product, axis=0, keepdims=True)
        backs = (upstream * filtered, back_prod * v_short, back_prod * k_short)
        sums = [0.0] * taps_count
        heads = [0.0] * taps_count
        for place, (back, ext, in_ref, out_ref) in enumerate(
            zip(backs, (q_back, k_back, v_back), (q_ref, k_ref, v_ref), (grad_q_ref, grad_k_ref, grad_v_ref))
        ):
            ext[:rows_here, :] = back
            signal = in_ref[:, lanes].astype(f32)
            lead = lead_ref[place * halo_rows : (place + 1) * halo_rows, lanes].astype(f32)
            sums[0] = sums[0] + back * signal
            grad = taps[0:1] * back
            for shift_idx in range(1, taps_count):
                ahead = ext[shift_idx : shift_idx + rows_here, :]
                grad = grad + taps[shift_idx : shift_idx + 1] * ahead
                sums[shift_idx] = sums[shift_idx] + ahead * signal
                heads[shift_idx] = heads[shift_idx] + jnp.sum(
                    back[:shift_idx] * lead[halo_rows - shift_idx :], axis=0, keepdims=True
                )
            out_ref[:, lanes] = grad.astype(bf16)
            edge_ref[place, 0:halo_rows, lanes] = back[:halo_rows]
            edge_ref[place, halo_rows : 2 * halo_rows, lanes] = grad[rows_here - halo_rows :]
        for shift_idx in range(taps_count):
            sums_ref[shift_idx : shift_idx + 1, lanes] = heads[shift_idx] + jnp.sum(
                sums[shift_idx], axis=0, keepdims=True
            )


def edges_kernel(edge_ref, tail_ref, taps_ref, q_ref, k_ref, v_ref, q_out, k_out, v_out, work_ref):
    taps_count = taps_ref.shape[0]
    halo_rows = taps_count - 1
    block_rows = q_ref.shape[0]
    for place, (ref, out_ref) in enumerate(((q_ref, q_out), (k_ref, k_out), (v_ref, v_out))):
        work_ref[...] = ref[...].astype(f32)
        for row in range(halo_rows):
            total = edge_ref[place, halo_rows + row : halo_rows + row + 1, :]
            for shift_idx in range(halo_rows - row, taps_count):
                source = row + shift_idx - halo_rows
                total = total + taps_ref[shift_idx : shift_idx + 1, :] * tail_ref[place, source : source + 1, :]
            at = block_rows - halo_rows + row
            work_ref[at : at + 1, :] = total
        out_ref[...] = work_ref[...].astype(bf16)


def scale_kernel(limit, totals_ref, norm_ref, lag_ref, taps_out, skip_out, kernel_out):
    taps_count = taps_out.shape[0]
    channels = taps_out.shape[1]
    factor = limit / jnp.maximum(jnp.sqrt(norm_ref[...]), limit)
    for idx in range(channels // LANES):
        taps_out[:, group(idx)] = totals_ref[0:taps_count, group(idx)] * factor
        skip_out[:, group(idx)] = totals_ref[taps_count : taps_count + 1, group(idx)] * factor
        kernel_out[:, group(idx)] = lag_ref[idx].astype(f32) * factor


def exchange(pieces_first):
    return lax.all_to_all(pieces_first, "ctx", split_axis=0, concat_axis=0, tiled=True)


def to_pieces(groups, pieces):
    count, kinds, rows, lanes = groups.shape
    if count == pieces:
        return groups
    share = count * lanes // pieces
    split = groups.reshape(count, kinds, rows, lanes // share, share)
    return split.transpose(0, 3, 1, 2, 4).reshape(pieces, kinds, rows, share)


def to_groups(parts):
    pieces, kinds, rows, share = parts.shape
    if share == LANES:
        return parts
    joined = parts.reshape(pieces * share // LANES, LANES // share, kinds, rows, share)
    return joined.transpose(0, 2, 3, 1, 4).reshape(-1, kinds, rows, LANES)


def total_over(value, axis):
    size = lax.axis_size(axis)
    step = 1
    while step < size:
        value = value + lax.ppermute(value, axis, [(i, i ^ step) for i in range(size)])
        step *= 2
    return value


def body(q_in, k_in, v_in, grad_out, short_filter, kernel, skip):
    pieces = lax.axis_size("ctx")
    sides = lax.axis_size("ch")
    rows_here, channels = q_in.shape
    seq_len = pieces * rows_here
    taps_count = short_filter.shape[0]
    halo_rows = taps_count - 1
    groups = channels // LANES
    share = channels // pieces
    at_once = min(groups, 4)
    steps = groups // at_once
    width = at_once * LANES
    transforms = (Transforms if share == LANES else PlainTransforms)(pieces, rows_here)

    rows_spec = pl.BlockSpec((rows_here, width), lambda i: (0, i))
    short_spec = pl.BlockSpec((3, rows_here, width), lambda i: (0, 0, i))
    group_spec = pl.BlockSpec((at_once, rows_here, LANES), lambda i: (i, 0, 0))
    pair_spec = pl.BlockSpec((at_once, 2, rows_here, LANES), lambda i: (i, 0, 0, 0))
    edge_spec = pl.BlockSpec((3, 2 * halo_rows, width), lambda i: (0, 0, i))

    def flat_spec(rows):
        return pl.BlockSpec((rows, width), lambda i: (0, i))

    flat = jax.ShapeDtypeStruct((rows_here, channels), bf16)
    ext = pltpu.VMEM((rows_here + PAD, LANES), f32)

    lead = jnp.concatenate([x[rows_here - halo_rows :] for x in (q_in, k_in, v_in)], axis=0)
    lead = lax.ppermute(lead, "ctx", [(i, i + 1) for i in range(pieces - 1)])

    packed = call(
        pack_kernel, jax.ShapeDtypeStruct((groups, rows_here, LANES), bf16), [], kernel,
        grid=(steps,), in_specs=[rows_spec], out_specs=group_spec,
    )
    filter_here = exchange(to_pieces(packed[:, None], pieces))[:, 0]
    signals, short = call(
        signals_kernel,
        (
            jax.ShapeDtypeStruct((groups, 2, rows_here, LANES), bf16),
            jax.ShapeDtypeStruct((3, rows_here, channels), f32),
        ),
        [ext, ext, ext],
        q_in, k_in, v_in, grad_out, lead, short_filter,
        grid=(steps,),
        in_specs=[rows_spec] * 4 + [flat_spec(3 * halo_rows), flat_spec(taps_count)],
        out_specs=(pair_spec, short_spec),
    )
    signals_here = exchange(to_pieces(signals, pieces))
    filter_spec = transforms.filter(filter_here)
    long_here, lag_spec = transforms.products(signals_here, filter_spec)
    long = to_groups(exchange(long_here))
    lag_here, lag_squares = transforms.lag(lag_spec)
    lag = to_groups(exchange(lag_here[:, None]))[:, 0]

    mixed, grad_q, grad_k, grad_v, edge, sums = call(
        finish_kernel,
        (
            flat, flat, flat, flat,
            jax.ShapeDtypeStruct((3, 2 * halo_rows, channels), f32),
            jax.ShapeDtypeStruct((taps_count + 1, channels), f32),
        ),
        [ext, ext, ext],
        q_in, k_in, v_in, grad_out, short, lead, short_filter, skip.reshape(1, channels), long,
        grid=(steps,),
        in_specs=[rows_spec] * 4
        + [short_spec, flat_spec(3 * halo_rows), flat_spec(taps_count), flat_spec(1), pair_spec],
        out_specs=(rows_spec,) * 4 + (edge_spec, flat_spec(taps_count + 1)),
    )

    extra = jnp.zeros((taps_count + 1, LANES), f32).at[0, :share].set(jnp.sum(lag_squares, axis=0))
    totals = total_over(jnp.concatenate([sums, extra], axis=1), "ctx")
    square = jnp.sum(totals[:, :channels] * totals[:, :channels]) + jnp.sum(totals[0, channels:])
    norm_sq = total_over(jnp.full((1, LANES), square), "ch")

    tail = lax.ppermute(edge[:, :halo_rows], "ctx", [(i, i - 1) for i in range(1, pieces)])
    last_block = 16
    last_spec = pl.BlockSpec((last_block, channels), lambda i: (rows_here // last_block - 1, 0))
    whole = lambda *dims: pl.BlockSpec(dims, lambda i: (0,) * len(dims))
    grad_q, grad_k, grad_v = call(
        edges_kernel, (flat, flat, flat), [pltpu.VMEM((last_block, channels), f32)],
        edge, tail, short_filter, grad_q, grad_k, grad_v,
        vmem_bytes=SMALL_VMEM_BYTES,
        grid=(1,),
        in_specs=[whole(*edge.shape), whole(*tail.shape), whole(*short_filter.shape)] + [last_spec] * 3,
        out_specs=(last_spec,) * 3,
        input_output_aliases={3: 0, 4: 1, 5: 2},
    )

    limit = math.sqrt(float(seq_len * channels * sides))
    grad_short, grad_skip, grad_kernel = call(
        lambda *refs: scale_kernel(limit, *refs),
        (
            jax.ShapeDtypeStruct((taps_count, channels), f32),
            jax.ShapeDtypeStruct((1, channels), f32),
            jax.ShapeDtypeStruct((rows_here, channels), f32),
        ),
        [],
        totals, norm_sq, lag,
        vmem_bytes=SMALL_VMEM_BYTES,
        in_specs=[IN_VMEM] * 3,
        out_specs=(IN_VMEM,) * 3,
    )
    return mixed, grad_q, grad_k, grad_v, grad_short, grad_skip.reshape(channels), grad_kernel


def solution(mesh):
    in_specs = (
        P("ctx", "ch"),
        P("ctx", "ch"),
        P("ctx", "ch"),
        P("ctx", "ch"),
        P(None, "ch"),
        P("ctx", "ch"),
        P("ch"),
    )
    out_specs = (
        P("ctx", "ch"),
        P("ctx", "ch"),
        P("ctx", "ch"),
        P("ctx", "ch"),
        P(None, "ch"),
        P("ch"),
        P("ctx", "ch"),
    )
    return jax.shard_map(body, mesh=mesh, in_specs=in_specs, out_specs=out_specs, check_vma=False)
```

```python
import functools
import math

import jax
import jax.numpy as jnp
import ml_dtypes
import numpy as np
from jax import lax
from jax.experimental import pallas as pl
from jax.experimental.pallas import tpu as pltpu
from jax.sharding import PartitionSpec as P

LANES = 128
SPAN = 256
BOTH = 2 * SPAN
CHUNK = 16
CHUNKS = SPAN // CHUNK
PAD = 8
ROWS = 32
PASSES = 2
VMEM_BYTES = 60 * 1024 * 1024
SMALL_VMEM_BYTES = 8 * 1024 * 1024

f32 = jnp.float32
bf16 = jnp.bfloat16

IN_VMEM = pl.BlockSpec(memory_space=pltpu.VMEM)
IN_SMEM = pl.BlockSpec(memory_space=pltpu.SMEM)
ANYWHERE = pl.BlockSpec(memory_space=pl.ANY)


def call(kernel, outs, scratch, *args, vmem_bytes=VMEM_BYTES, **options):
    return pl.pallas_call(
        kernel,
        out_shape=outs,
        scratch_shapes=scratch,
        compiler_params=pltpu.CompilerParams(vmem_limit_bytes=vmem_bytes),
        **options,
    )(*args)


def leaf_phases(count):
    return [(4 * leaf + 1) / (4 * count) for leaf in range(count)]


def root_times(re, im, num, den, sign):
    if num == 0:
        return re, im
    if 4 * num == den:
        return (im, -re) if sign < 0 else (-im, re)
    cosine = math.cos(2.0 * math.pi * num / den)
    sine = sign * math.sin(2.0 * math.pi * num / den)
    if 8 * num == den:
        return ((re + im) * cosine, (im - re) * cosine) if sign < 0 else ((re - im) * cosine, (re + im) * cosine)
    if 8 * num == 3 * den:
        return ((re - im) * cosine, (re + im) * cosine) if sign < 0 else ((re + im) * cosine, (im - re) * cosine)
    return re * cosine - im * sine, im * cosine + re * sine


def short_fft(values, sign):
    count = len(values)
    if count == 1:
        return values
    even = short_fft(values[0::2], sign)
    odd = short_fft(values[1::2], sign)
    first = []
    second = []
    for num in range(count // 2):
        re, im = root_times(*odd[num], num, count, sign)
        first.append((even[num][0] + re, even[num][1] + im))
        second.append((even[num][0] - re, even[num][1] - im))
    return first + second


def to_leaves(parts):
    count = len(parts)
    turned = []
    for idx, part in enumerate(parts):
        angle = 2.0 * math.pi * idx / (4 * count)
        turned.append((part * math.cos(angle), part * (-math.sin(angle))) if idx else (part, jnp.zeros_like(part)))
    return short_fft(turned, -1)


def from_leaves(leaves, scale):
    count = len(leaves)
    parts = []
    for idx, (re, im) in enumerate(short_fft(leaves, 1)):
        angle = 2.0 * math.pi * idx / (4 * count)
        if idx == 0:
            parts.append(re * scale)
        else:
            parts.append(re * (math.cos(angle) * scale) - im * (math.sin(angle) * scale))
    return parts


def dft_matrix():
    idx = np.arange(SPAN)
    angle = (idx[:, None] * idx[None, :] % SPAN) * (2.0 * np.pi / SPAN)
    cosine, sine = np.cos(angle), np.sin(angle)
    return np.block([[cosine, sine], [-sine, cosine]])


def twist_angles(outer, inner):
    return np.asarray(leaf_phases(outer))[:, None] * np.asarray(inner)[None, :] * (2.0 * np.pi / SPAN)


def matrix_blocks():
    matrix = dft_matrix()
    high = matrix.astype(ml_dtypes.bfloat16)
    low = (matrix - high.astype(np.float64)).astype(ml_dtypes.bfloat16)
    return np.concatenate([high, low, high][:PASSES], axis=1)


def leaf_place(leaf):
    return leaf // 2, slice((leaf % 2) * LANES, (leaf % 2 + 1) * LANES)


def split_store(ref, leaf, row, value):
    pair, lanes = leaf_place(leaf)
    high = value.astype(bf16)
    for block in range(PASSES):
        part = high
        if PASSES == 3 and block == 2:
            part = (value - high.astype(f32)).astype(bf16)
        ref[pair, pl.ds(block * BOTH + row, CHUNK), lanes] = part


def run(stages, matmul=None):
    tiles = matmul[2].shape[0] if matmul else 4

    def step(tile, carry):
        if matmul:
            matrix_ref, split_ref, result_ref = matmul
            result_ref[tile] = jnp.dot(matrix_ref[...], split_ref[tile], preferred_element_type=f32)
        for part in range(CHUNKS // tiles):
            for stage in stages:
                carry = stage(tile * (CHUNKS // tiles) + part, carry)
        return carry

    return step, tiles


def run_all(stages, matmul=None, carry=0):
    step, tiles = run(stages, matmul)
    return lax.fori_loop(0, tiles, step, carry)


def chunk_row(idx):
    return pl.multiple_of(idx * CHUNK, CHUNK)


def twist_stage(coarse_ref, fine_ref, twist_ref):
    outer = twist_ref.shape[1]

    def stage(idx, carry):
        here = pl.ds(chunk_row(idx), CHUNK)
        for leaf in range(outer):
            far_cosine = coarse_ref[idx, leaf]
            far_sine = coarse_ref[idx, outer + leaf]
            cosine = fine_ref[0, leaf]
            sine = fine_ref[1, leaf]
            twist_ref[0, leaf, here, :] = far_cosine * cosine - far_sine * sine
            twist_ref[1, leaf, here, :] = far_sine * cosine + far_cosine * sine
        return carry

    return stage


def piece_place(idx, part, rows_here):
    ratio = SPAN // rows_here
    in_piece = rows_here // CHUNK
    return part * ratio + idx // in_piece, pl.ds(chunk_row(idx % in_piece), CHUNK)


def leaves_stage(signals_ref, kind, twist_ref, split_ref):
    outer = twist_ref.shape[1]
    rows_here = signals_ref.shape[2]

    def stage(idx, carry):
        row = chunk_row(idx)
        parts = []
        for part in range(outer):
            piece, rows = piece_place(idx, part, rows_here)
            parts.append(signals_ref[piece, kind, rows, :].astype(f32))
        for leaf, (re, im) in enumerate(to_leaves(parts)):
            cosine = twist_ref[0, leaf, pl.ds(row, CHUNK), :]
            sine = twist_ref[1, leaf, pl.ds(row, CHUNK), :]
            split_store(split_ref, leaf, row, re * cosine + im * sine)
            split_store(split_ref, leaf, SPAN + row, im * cosine - re * sine)
        return carry

    return stage


def combine_stage(left_ref, right_ref, split_ref, conjugate):
    def stage(idx, carry):
        row = chunk_row(idx)
        for leaf in range(2 * left_ref.shape[0]):
            pair, lanes = leaf_place(leaf)
            left_re = left_ref[pair, pl.ds(row, CHUNK), lanes]
            left_im = left_ref[pair, pl.ds(SPAN + row, CHUNK), lanes]
            right_re = right_ref[pair, pl.ds(row, CHUNK), lanes]
            right_im = right_ref[pair, pl.ds(SPAN + row, CHUNK), lanes]
            if conjugate:
                re = left_re * right_re + left_im * right_im
                minus_im = left_im * right_re - left_re * right_im
            else:
                re = left_re * right_re - left_im * right_im
                minus_im = -(left_re * right_im + left_im * right_re)
            split_store(split_ref, leaf, row, re)
            split_store(split_ref, leaf, SPAN + row, minus_im)
        return carry

    return stage


def signal_stage(time_ref, twist_ref, rows_here, write):
    outer = twist_ref.shape[1]
    scale = 1.0 / (SPAN * outer)

    def stage(idx, carry):
        row = chunk_row(idx)
        leaves = []
        for leaf in range(outer):
            pair, lanes = leaf_place(leaf)
            cosine = twist_ref[0, leaf, pl.ds(row, CHUNK), :]
            sine = twist_ref[1, leaf, pl.ds(row, CHUNK), :]
            re = time_ref[pair, pl.ds(row, CHUNK), lanes]
            minus_im = time_ref[pair, pl.ds(SPAN + row, CHUNK), lanes]
            leaves.append((re * cosine + minus_im * sine, re * sine - minus_im * cosine))
        for part, value in enumerate(from_leaves(leaves, scale)):
            piece, rows = piece_place(idx, part, rows_here)
            carry = write(piece, rows, value, carry)
        return carry

    return stage


def products_kernel(
    signals_hbm, coarse_ref, fine_ref, matrix_hbm, results_hbm, lag_hbm,
    twist_ref, matrix_ref, signals_ref, results_ref, one_split, two_split, lag_split,
    filter_ref, product_ref, cotan_ref, time_ref, sems,
):
    rows_here = signals_ref.shape[2]
    arrivals = [
        pltpu.make_async_copy(signals_hbm.at[:, kind], signals_ref.at[:, kind], sems.at[kind]) for kind in range(3)
    ]
    matrix_copy = pltpu.make_async_copy(matrix_hbm, matrix_ref, sems.at[3])
    lag_copy = pltpu.make_async_copy(lag_split, lag_hbm, sems.at[4])
    returns = [
        pltpu.make_async_copy(results_ref.at[:, kind], results_hbm.at[:, kind], sems.at[5 + kind]) for kind in range(2)
    ]

    def leaves(kind, split_ref):
        return leaves_stage(signals_ref, kind, twist_ref, split_ref)

    def result(kind, from_ref):
        def write(piece, rows, value, carry):
            results_ref[piece, kind, rows, :] = value.astype(bf16)
            return carry

        return signal_stage(from_ref, twist_ref, rows_here, write)

    for copy in (arrivals[2], arrivals[0], matrix_copy, arrivals[1]):
        copy.start()
    run_all([twist_stage(coarse_ref, fine_ref, twist_ref)])
    arrivals[2].wait()
    run_all([leaves(2, one_split)])
    arrivals[0].wait()
    matrix_copy.wait()
    run_all([leaves(0, two_split)], (matrix_ref, one_split, filter_ref))
    arrivals[1].wait()
    run_all([leaves(1, one_split)], (matrix_ref, two_split, product_ref))
    run_all([combine_stage(filter_ref, product_ref, two_split, False)], (matrix_ref, one_split, cotan_ref))
    run_all([combine_stage(filter_ref, cotan_ref, one_split, True)], (matrix_ref, two_split, time_ref))
    run_all([combine_stage(product_ref, cotan_ref, lag_split, True), result(0, time_ref)], (matrix_ref, one_split, filter_ref))
    lag_copy.start()
    returns[0].start()
    run_all([result(1, filter_ref)])
    returns[1].start()
    lag_copy.wait()
    returns[0].wait()
    returns[1].wait()


def lag_kernel(
    split_hbm, coarse_ref, fine_ref, matrix_hbm, lag_ref, square_ref, twist_ref, matrix_ref, split_ref, time_ref, sems
):
    copies = [
        pltpu.make_async_copy(matrix_hbm, matrix_ref, sems.at[0]),
        pltpu.make_async_copy(split_hbm, split_ref, sems.at[1]),
    ]
    for copy in copies:
        copy.start()
    for copy in copies:
        copy.wait()
    run_all([twist_stage(coarse_ref, fine_ref, twist_ref)], (matrix_ref, split_ref, time_ref))

    def write(piece, rows, value, carry):
        lag_ref[piece, rows, :] = value.astype(bf16)
        return carry + value * value

    square_ref[...] = run_all(
        [signal_stage(time_ref, twist_ref, lag_ref.shape[1], write)], None, jnp.zeros((CHUNK, LANES), f32)
    )


class Transforms:
    def __init__(self, pieces, rows_here):
        outer = pieces * rows_here // SPAN
        pairs = outer // 2
        self.matrix = jnp.asarray(matrix_blocks())
        coarse = twist_angles(outer, CHUNK * np.arange(CHUNKS)).T
        self.coarse = jnp.asarray(np.concatenate([np.cos(coarse), np.sin(coarse)], axis=1), f32)
        fine = twist_angles(outer, np.arange(CHUNK))
        fine = jnp.asarray(np.stack([np.cos(fine), np.sin(fine)]), f32)[..., None]
        self.fine = jnp.broadcast_to(fine, fine.shape[:3] + (LANES,))
        self.split = jax.ShapeDtypeStruct((pairs, PASSES * BOTH, 2 * LANES), bf16)
        self.signal = jax.ShapeDtypeStruct((pieces, rows_here, LANES), bf16)
        self.result = jax.ShapeDtypeStruct((pieces, 2, rows_here, LANES), bf16)
        self.square = jax.ShapeDtypeStruct((CHUNK, LANES), f32)
        self.signals_work = pltpu.VMEM((pieces, 3, rows_here, LANES), bf16)
        self.results_work = pltpu.VMEM(self.result.shape, bf16)
        self.work = pltpu.VMEM((pairs, BOTH, 2 * LANES), f32)
        self.split_work = pltpu.VMEM(self.split.shape, bf16)
        self.tables = [pltpu.VMEM((2, outer, SPAN, LANES), f32), pltpu.VMEM(self.matrix.shape, bf16)]

    def products(self, signals):
        return call(
            products_kernel, (self.result, self.split),
            self.tables
            + [self.signals_work, self.results_work]
            + [self.split_work] * 3
            + [self.work] * 4
            + [pltpu.SemaphoreType.DMA((7,))],
            signals, self.coarse, self.fine, self.matrix,
            in_specs=[ANYWHERE, IN_SMEM, IN_VMEM, ANYWHERE],
            out_specs=(ANYWHERE, ANYWHERE),
        )

    def lag(self, lag_split):
        return call(
            lag_kernel, (self.signal, self.square),
            self.tables + [self.split_work, self.work, pltpu.SemaphoreType.DMA((2,))],
            lag_split, self.coarse, self.fine, self.matrix,
            in_specs=[ANYWHERE, IN_SMEM, IN_VMEM, ANYWHERE],
            out_specs=(IN_VMEM, IN_VMEM),
        )


class PlainTransforms:
    def __init__(self, pieces, rows_here):
        self.seq_len = pieces * rows_here
        self.pieces = pieces
        self.outer = self.seq_len // SPAN
        idx = np.arange(SPAN)
        angle = (idx[:, None] * idx[None, :] % SPAN) * (2.0 * np.pi / SPAN)
        self.cosine = jnp.asarray(np.cos(angle), f32)
        self.sine = jnp.asarray(np.sin(angle), f32)
        twist = twist_angles(self.outer, idx)
        self.twist = jnp.asarray(np.stack([np.cos(twist), np.sin(twist)]), f32)[..., None]

    def dot(self, matrix, signal):
        return jnp.einsum("fs,tsc->tfc", matrix, signal, precision=lax.Precision.HIGHEST)

    def spectrum(self, signal):
        parts = signal.astype(f32).reshape(self.outer, SPAN, -1)
        leaves = to_leaves([parts[part] for part in range(self.outer)])
        re = jnp.stack([leaf[0] for leaf in leaves])
        im = jnp.stack([leaf[1] for leaf in leaves])
        twist_re = re * self.twist[0] + im * self.twist[1]
        twist_im = im * self.twist[0] - re * self.twist[1]
        return (
            self.dot(self.cosine, twist_re) + self.dot(self.sine, twist_im),
            self.dot(self.cosine, twist_im) - self.dot(self.sine, twist_re),
        )

    def back(self, re, im):
        time_re = self.dot(self.cosine, re) - self.dot(self.sine, im)
        time_im = self.dot(self.cosine, im) + self.dot(self.sine, re)
        leaf_re = time_re * self.twist[0] - time_im * self.twist[1]
        leaf_im = time_im * self.twist[0] + time_re * self.twist[1]
        parts = from_leaves([(leaf_re[leaf], leaf_im[leaf]) for leaf in range(self.outer)], 1.0 / self.seq_len)
        return jnp.stack(parts).reshape(self.pieces, self.seq_len // self.pieces, -1)

    def products(self, signals):
        product, cotan, taps = (self.spectrum(signals[:, kind]) for kind in range(3))
        conv = self.back(taps[0] * product[0] - taps[1] * product[1], taps[0] * product[1] + taps[1] * product[0])
        corr = self.back(taps[0] * cotan[0] + taps[1] * cotan[1], taps[0] * cotan[1] - taps[1] * cotan[0])
        lag = (
            product[0] * cotan[0] + product[1] * cotan[1],
            product[0] * cotan[1] - product[1] * cotan[0],
        )
        return jnp.stack([conv, corr], axis=1).astype(bf16), lag

    def lag(self, lag_spec):
        lag = self.back(*lag_spec)
        return lag.astype(bf16), jnp.sum(lag * lag, axis=(0, 1))[None, :]


def group(idx):
    return pl.ds(pl.multiple_of(idx * LANES, LANES), LANES)


def streamed(work, steps, per_step, places, in_count, out_count, *refs):
    hbm = refs[: in_count + out_count]
    held = refs[in_count + out_count : 2 * (in_count + out_count)]
    scratch = refs[2 * (in_count + out_count) : -1]
    sems = refs[-1]

    def copy(place, step):
        outside = hbm[place].at[places[place][0](step)]
        inside = held[place].at[places[place][1](step)]
        ends = (outside, inside) if place < in_count else (inside, outside)
        return pltpu.make_async_copy(*ends, sems.at[place, step])

    for step in range(steps):
        for place in range(in_count):
            copy(place, step).start()
    for step in range(steps):
        for place in range(in_count):
            copy(place, step).wait()

        def one(idx, carry):
            work(idx, held[:in_count], held[in_count:], scratch)
            return carry

        lax.fori_loop(step * per_step, (step + 1) * per_step, one, 0)
        for place in range(in_count, in_count + out_count):
            copy(place, step).start()
    for step in range(steps):
        for place in range(in_count, in_count + out_count):
            copy(place, step).wait()


def stream_call(work, steps, per_step, operands, results, scratch=(), aliases=None):
    arrays = [operand[0] for operand in operands]
    shapes = [jax.ShapeDtypeStruct(array.shape, array.dtype) for array in arrays] + [result[0] for result in results]
    cuts = [entry[1] for entry in operands] + [entry[1] for entry in results]
    held = [pltpu.VMEM(entry[2] or shape.shape, shape.dtype) for entry, shape in zip(operands + results, shapes)]
    extra = list(aliases or ())
    kernel = functools.partial(streamed, work, steps, per_step, cuts, len(arrays), len(results))

    def with_aliases(*refs):
        kernel(*refs[: len(arrays)], *refs[len(arrays) + len(extra) :])

    return call(
        with_aliases,
        tuple(result[0] for result in results),
        held + list(scratch) + [pltpu.SemaphoreType.DMA((len(shapes), steps))],
        *arrays, *extra,
        in_specs=[ANYWHERE] * (len(arrays) + len(extra)),
        out_specs=(ANYWHERE,) * len(results),
        input_output_aliases={len(arrays) + idx: idx for idx in range(len(extra))},
    )


def cut_lanes(width, rank):
    def place(step):
        return (slice(None),) * (rank - 1) + (pl.ds(step * width, width),)

    return place, place


def cut_groups(per_step, kinds=None):
    def outside(step):
        here = pl.ds(step * per_step, per_step)
        return (here,) if kinds is None else (here, kinds)

    def inside(step):
        return (pl.ds(step * per_step, per_step),)

    return outside, inside


def row_blocks(rows_here):
    return [slice(start, start + ROWS) for start in range(0, rows_here, ROWS)]


def pack_work(idx, operands, results, scratch):
    results[0][idx] = operands[0][:, group(idx)].astype(bf16)


def extend_rows(lead, in_ref, lanes, ext_ref):
    ext_ref[PAD - lead.shape[0] : PAD, :] = lead
    ext_ref[PAD:, :] = in_ref[:, lanes].astype(f32)


def short_conv(ext_ref, taps, rows):
    result = None
    for shift_idx in range(taps.shape[0]):
        term = taps[shift_idx : shift_idx + 1] * ext_ref[PAD + rows.start - shift_idx : PAD + rows.stop - shift_idx, :]
        result = term if result is None else result + term
    return result


def extend_three(idx, operands, lead_ref, halo_rows, exts):
    lead = lead_ref[:, group(idx)]
    for place, ext in enumerate(exts):
        extend_rows(lead[place * halo_rows : (place + 1) * halo_rows], operands[place], group(idx), ext)


def signals_work(idx, operands, results, exts):
    q_ref, k_ref, v_ref, grad_ref, lead_ref, taps_ref = operands
    taps = taps_ref[:, group(idx)]
    extend_three(idx, operands, lead_ref, taps.shape[0] - 1, exts)
    for rows in row_blocks(q_ref.shape[0]):
        q_short, k_short, v_short = (short_conv(ext, taps, rows) for ext in exts)
        results[0][idx, 0, rows, :] = (k_short * v_short).astype(bf16)
        results[0][idx, 1, rows, :] = (grad_ref[rows, group(idx)].astype(f32) * q_short).astype(bf16)


def short_work(idx, operands, results, exts):
    q_ref, k_ref, v_ref, lead_ref, taps_ref = operands
    taps = taps_ref[:, group(idx)]
    extend_three(idx, operands, lead_ref, taps.shape[0] - 1, exts)
    for rows in row_blocks(q_ref.shape[0]):
        for place, ext in enumerate(exts):
            results[0][place, rows, group(idx)] = short_conv(ext, taps, rows)


def fold(value):
    return jnp.sum(value.reshape(-1, 8, LANES), axis=0)


def finish_work(idx, operands, results, exts):
    q_ref, k_ref, v_ref, grad_ref, short_ref, lead_ref, taps_ref, skip_ref, long_ref = operands
    mixed_ref, grad_q_ref, grad_k_ref, grad_v_ref, front_ref, back_ref, sums_ref = results
    lanes = group(idx)
    taps = taps_ref[:, lanes]
    skip = skip_ref[:, lanes]
    lead = lead_ref[:, lanes]
    taps_count = taps.shape[0]
    halo_rows = taps_count - 1
    rows_here = q_ref.shape[0]
    sums = [jnp.zeros((8, LANES), f32) for _ in range(taps_count + 1)]
    for ext in exts:
        ext[rows_here:, :] = jnp.zeros((PAD, LANES), f32)
    for rows in row_blocks(rows_here):
        q_short, k_short, v_short = (short_ref[place, rows, lanes] for place in range(3))
        product = (k_short * v_short).astype(bf16).astype(f32)
        filtered = long_ref[idx, 0, rows, :].astype(f32) + skip * product
        mixed_ref[rows, lanes] = (q_short * filtered).astype(bf16)
        upstream = grad_ref[rows, lanes].astype(f32)
        back_mix = upstream * q_short
        back_prod = long_ref[idx, 1, rows, :].astype(f32) + skip * back_mix
        sums[taps_count] = sums[taps_count] + fold(back_mix * product)
        exts[0][rows, :] = upstream * filtered
        exts[1][rows, :] = back_prod * v_short
        exts[2][rows, :] = back_prod * k_short
    for place, (ext, in_ref, out_ref) in enumerate(
        zip(exts, (q_ref, k_ref, v_ref), (grad_q_ref, grad_k_ref, grad_v_ref))
    ):
        for rows in row_blocks(rows_here):
            signal = in_ref[rows, lanes].astype(f32)
            grad = None
            for shift_idx in range(taps_count):
                ahead = ext[rows.start + shift_idx : rows.stop + shift_idx, :]
                term = taps[shift_idx : shift_idx + 1] * ahead
                grad = term if grad is None else grad + term
                sums[shift_idx] = sums[shift_idx] + fold(ahead * signal)
            out_ref[rows, lanes] = grad.astype(bf16)
        back_ref[place * halo_rows : (place + 1) * halo_rows, lanes] = grad[ROWS - halo_rows :]
        front_ref[place * halo_rows : (place + 1) * halo_rows, lanes] = ext[0:halo_rows, :]
    for shift_idx in range(taps_count + 1):
        total = jnp.sum(sums[shift_idx], axis=0, keepdims=True)
        for place in range(3 if shift_idx < taps_count else 0):
            for row in range(shift_idx):
                at = place * halo_rows + halo_rows - shift_idx + row
                total = total + lead[at : at + 1] * exts[place][row : row + 1, :]
        sums_ref[shift_idx : shift_idx + 1, lanes] = total


def lead_kernel(q_ref, k_ref, v_ref, lead_ref):
    halo_rows = lead_ref.shape[0] // 3
    for place, ref in enumerate((q_ref, k_ref, v_ref)):
        rows = ref[...].astype(f32)
        lead_ref[place * halo_rows : (place + 1) * halo_rows, :] = rows[rows.shape[0] - halo_rows :]


def edges_kernel(back_ref, tail_ref, taps_ref, q_ref, k_ref, v_ref, q_out, k_out, v_out, work_ref):
    taps_count = taps_ref.shape[0]
    halo_rows = taps_count - 1
    block_rows = q_ref.shape[0]
    for place, (ref, out_ref) in enumerate(((q_ref, q_out), (k_ref, k_out), (v_ref, v_out))):
        work_ref[...] = ref[...].astype(f32)
        first = place * halo_rows
        for row in range(halo_rows):
            total = back_ref[first + row : first + row + 1, :]
            for shift_idx in range(halo_rows - row, taps_count):
                source = first + row + shift_idx - halo_rows
                total = total + taps_ref[shift_idx : shift_idx + 1, :] * tail_ref[source : source + 1, :]
            at = block_rows - halo_rows + row
            work_ref[at : at + 1, :] = total
        out_ref[...] = work_ref[...].astype(bf16)


def norm_kernel(*refs):
    values, totals_ref, square_ref = refs[:-2], refs[-2], refs[-1]
    channels = totals_ref.shape[1] - LANES
    totals = values[0][...]
    if len(values) == 4:
        totals = (totals + values[1][...]) + (values[2][...] + values[3][...])
    totals_ref[...] = totals
    square = jnp.sum(totals[:, :channels] * totals[:, :channels]) + jnp.sum(totals[0:1, channels:])
    square_ref[...] = jnp.full(square_ref.shape, square)


def scale_kernel(limit, totals_ref, norm_ref, lag_hbm, taps_out, skip_out, kernel_out, lag_ref, sems):
    taps_count, channels = taps_out.shape
    groups = lag_ref.shape[0]
    per_step = max(groups // 4, 1)
    copies = []
    for step in range(groups // per_step):
        here = pl.ds(step * per_step, per_step)
        copies.append(pltpu.make_async_copy(lag_hbm.at[here], lag_ref.at[here], sems.at[step]))
        copies[step].start()
    factor = limit / jnp.maximum(jnp.sqrt(norm_ref[...]), limit)
    for idx in range(groups):
        lanes = slice(idx * LANES, (idx + 1) * LANES)
        taps_out[:, lanes] = totals_ref[0:taps_count, lanes] * factor
        skip_out[:, lanes] = totals_ref[taps_count : taps_count + 1, lanes] * factor
    for step, copy in enumerate(copies):
        copy.wait()
        for idx in range(step * per_step, (step + 1) * per_step):
            kernel_out[:, idx * LANES : (idx + 1) * LANES] = lag_ref[idx].astype(f32) * factor


def exchange(pieces_first):
    return lax.all_to_all(pieces_first, "ctx", split_axis=0, concat_axis=0, tiled=True)


def to_pieces(groups, pieces):
    count, kinds, rows, lanes = groups.shape
    if count == pieces:
        return groups
    share = count * lanes // pieces
    split = groups.reshape(count, kinds, rows, lanes // share, share)
    return split.transpose(0, 3, 1, 2, 4).reshape(pieces, kinds, rows, share)


def to_groups(parts):
    pieces, kinds, rows, share = parts.shape
    if share == LANES:
        return parts
    joined = parts.reshape(pieces * share // LANES, LANES // share, kinds, rows, share)
    return joined.transpose(0, 2, 3, 1, 4).reshape(-1, kinds, rows, LANES)


def partners(value, axis, steps):
    size = lax.axis_size(axis)
    return [value] + [lax.ppermute(value, axis, [(i, i ^ step) for i in range(size)]) for step in steps]


def rounds_of(size):
    rounds = []
    step = 1
    while step < size:
        rounds.append((step, 2 * step, 3 * step) if size // step >= 4 else (step,))
        step *= 4 if size // step >= 4 else 2
    return rounds


def add_up(values):
    if len(values) == 2:
        return values[0] + values[1]
    return (values[0] + values[1]) + (values[2] + values[3])


def body(q_in, k_in, v_in, grad_out, short_filter, kernel, skip):
    pieces = lax.axis_size("ctx")
    sides = lax.axis_size("ch")
    rows_here, channels = q_in.shape
    seq_len = pieces * rows_here
    taps_count = short_filter.shape[0]
    halo_rows = taps_count - 1
    groups = channels // LANES
    share = channels // pieces
    per_step = min(groups, 4)
    steps = groups // per_step
    lanes2 = cut_lanes(per_step * LANES, 2)
    lanes3 = cut_lanes(per_step * LANES, 3)
    transforms = (Transforms if share == LANES else PlainTransforms)(pieces, rows_here)
    stream = functools.partial(stream_call, steps=steps, per_step=per_step)

    flat = jax.ShapeDtypeStruct((rows_here, channels), bf16)
    halo = jax.ShapeDtypeStruct((3 * halo_rows, channels), f32)
    sent = jax.ShapeDtypeStruct((groups, 3, rows_here, LANES), bf16)
    exts = [pltpu.VMEM((rows_here + PAD, LANES), f32)] * 3
    last_block = 16
    last_spec = pl.BlockSpec((last_block, channels), lambda i: (rows_here // last_block - 1, 0))

    def whole(array):
        return pl.BlockSpec(array.shape, lambda i: (0,) * len(array.shape))

    lead = call(
        lead_kernel, halo, [], q_in, k_in, v_in,
        grid=(1,), in_specs=[last_spec] * 3, out_specs=whole(halo),
    )
    lead = lax.ppermute(lead, "ctx", [(i, i + 1) for i in range(pieces - 1)])

    (packed,) = stream(
        pack_work,
        operands=[(kernel, lanes2, None)],
        results=[(sent, cut_groups(per_step, 2), (groups, rows_here, LANES))],
    )
    (signals,) = stream(
        signals_work,
        operands=[(x, lanes2, None) for x in (q_in, k_in, v_in, grad_out, lead, short_filter)],
        results=[(sent, cut_groups(per_step, pl.ds(0, 2)), (groups, 2, rows_here, LANES))],
        scratch=exts,
        aliases=[packed],
    )
    signals_here = exchange(to_pieces(signals, pieces))
    (short,) = stream(
        short_work,
        operands=[(x, lanes2, None) for x in (q_in, k_in, v_in, lead, short_filter)],
        results=[(jax.ShapeDtypeStruct((3, rows_here, channels), f32), lanes3, None)],
        scratch=exts,
    )
    long_here, lag_spec = transforms.products(signals_here)
    long = to_groups(exchange(long_here))
    lag_here, lag_squares = transforms.lag(lag_spec)

    mixed, grad_q, grad_k, grad_v, front, back, sums = stream(
        finish_work,
        operands=[(x, lanes2, None) for x in (q_in, k_in, v_in, grad_out)]
        + [(short, lanes3, None)]
        + [(x, lanes2, None) for x in (lead, short_filter, skip.reshape(1, channels))]
        + [(long, cut_groups(per_step), None)],
        results=[(flat, lanes2, None)] * 4
        + [(halo, lanes2, None)] * 2
        + [(jax.ShapeDtypeStruct((taps_count + 1, channels), f32), lanes2, None)],
        scratch=exts,
    )
    lag = to_groups(exchange(lag_here[:, None]))[:, 0]

    extra = jnp.zeros((taps_count + 1, LANES), f32).at[0, :share].set(jnp.sum(lag_squares, axis=0))
    totals = jnp.concatenate([sums, extra], axis=1)
    rounds = rounds_of(pieces)
    for steps_of in rounds[:-1]:
        totals = add_up(partners(totals, "ctx", steps_of))
    last = partners(totals, "ctx", rounds[-1])
    if len(last) == 2:
        last = [last[0] + last[1]]
    totals, norm_sq = call(
        norm_kernel,
        (jax.ShapeDtypeStruct(totals.shape, f32), jax.ShapeDtypeStruct((1, LANES), f32)),
        [], *last,
        vmem_bytes=SMALL_VMEM_BYTES,
        in_specs=[IN_VMEM] * len(last), out_specs=(IN_VMEM, IN_VMEM),
    )
    for steps_of in rounds_of(sides):
        norm_sq = add_up(partners(norm_sq, "ch", steps_of))

    tail = lax.ppermute(front, "ctx", [(i, i - 1) for i in range(1, pieces)])
    grad_q, grad_k, grad_v = call(
        edges_kernel, (flat, flat, flat), [pltpu.VMEM((last_block, channels), f32)],
        back, tail, short_filter, grad_q, grad_k, grad_v,
        vmem_bytes=SMALL_VMEM_BYTES,
        grid=(1,),
        in_specs=[whole(back), whole(tail), whole(short_filter)] + [last_spec] * 3,
        out_specs=(last_spec,) * 3,
        input_output_aliases={3: 0, 4: 1, 5: 2},
    )

    limit = math.sqrt(float(seq_len * channels * sides))
    grad_short, grad_skip, grad_kernel = call(
        functools.partial(scale_kernel, limit),
        (
            jax.ShapeDtypeStruct((taps_count, channels), f32),
            jax.ShapeDtypeStruct((1, channels), f32),
            jax.ShapeDtypeStruct((rows_here, channels), f32),
        ),
        [pltpu.VMEM(lag.shape, bf16), pltpu.SemaphoreType.DMA((4,))],
        totals, norm_sq, lag,
        vmem_bytes=SMALL_VMEM_BYTES,
        in_specs=[IN_VMEM, IN_VMEM, ANYWHERE],
        out_specs=(IN_VMEM,) * 3,
    )
    return mixed, grad_q, grad_k, grad_v, grad_short, grad_skip.reshape(channels), grad_kernel


def solution(mesh):
    in_specs = (
        P("ctx", "ch"),
        P("ctx", "ch"),
        P("ctx", "ch"),
        P("ctx", "ch"),
        P(None, "ch"),
        P("ctx", "ch"),
        P("ch"),
    )
    out_specs = (
        P("ctx", "ch"),
        P("ctx", "ch"),
        P("ctx", "ch"),
        P("ctx", "ch"),
        P(None, "ch"),
        P("ch"),
        P("ctx", "ch"),
    )
    return jax.shard_map(body, mesh=mesh, in_specs=in_specs, out_specs=out_specs, check_vma=False)
```

```python
import functools
import math

import jax
import jax.numpy as jnp
import ml_dtypes
import numpy as np
from jax import lax
from jax.experimental import pallas as pl
from jax.experimental.pallas import tpu as pltpu
from jax.sharding import PartitionSpec as P

LANES = 128
SPAN = 256
BOTH = 2 * SPAN
CHUNK = 16
CHUNKS = SPAN // CHUNK
PAD = 8
ROWS = 32
PASSES = 2
VMEM_BYTES = 60 * 1024 * 1024
SMALL_VMEM_BYTES = 8 * 1024 * 1024

f32 = jnp.float32
bf16 = jnp.bfloat16

IN_VMEM = pl.BlockSpec(memory_space=pltpu.VMEM)
IN_SMEM = pl.BlockSpec(memory_space=pltpu.SMEM)
ANYWHERE = pl.BlockSpec(memory_space=pl.ANY)


def call(kernel, outs, scratch, *args, vmem_bytes=VMEM_BYTES, **options):
    return pl.pallas_call(
        kernel,
        out_shape=outs,
        scratch_shapes=scratch,
        compiler_params=pltpu.CompilerParams(vmem_limit_bytes=vmem_bytes),
        **options,
    )(*args)


def leaf_phases(count):
    return [(4 * leaf + 1) / (4 * count) for leaf in range(count)]


def root_times(re, im, num, den, sign):
    if num == 0:
        return re, im
    if 4 * num == den:
        return (im, -re) if sign < 0 else (-im, re)
    cosine = math.cos(2.0 * math.pi * num / den)
    sine = sign * math.sin(2.0 * math.pi * num / den)
    if 8 * num == den:
        return ((re + im) * cosine, (im - re) * cosine) if sign < 0 else ((re - im) * cosine, (re + im) * cosine)
    if 8 * num == 3 * den:
        return ((re - im) * cosine, (re + im) * cosine) if sign < 0 else ((re + im) * cosine, (im - re) * cosine)
    return re * cosine - im * sine, im * cosine + re * sine


def short_fft(values, sign):
    count = len(values)
    if count == 1:
        return values
    even = short_fft(values[0::2], sign)
    odd = short_fft(values[1::2], sign)
    first = []
    second = []
    for num in range(count // 2):
        re, im = root_times(*odd[num], num, count, sign)
        first.append((even[num][0] + re, even[num][1] + im))
        second.append((even[num][0] - re, even[num][1] - im))
    return first + second


def to_leaves(parts):
    count = len(parts)
    turned = []
    for idx, part in enumerate(parts):
        angle = 2.0 * math.pi * idx / (4 * count)
        turned.append((part * math.cos(angle), part * (-math.sin(angle))) if idx else (part, jnp.zeros_like(part)))
    return short_fft(turned, -1)


def from_leaves(leaves, scale):
    count = len(leaves)
    parts = []
    for idx, (re, im) in enumerate(short_fft(leaves, 1)):
        angle = 2.0 * math.pi * idx / (4 * count)
        if idx == 0:
            parts.append(re * scale)
        else:
            parts.append(re * (math.cos(angle) * scale) - im * (math.sin(angle) * scale))
    return parts


def dft_matrix():
    idx = np.arange(SPAN)
    angle = (idx[:, None] * idx[None, :] % SPAN) * (2.0 * np.pi / SPAN)
    cosine, sine = np.cos(angle), np.sin(angle)
    return np.block([[cosine, sine], [-sine, cosine]])


def twist_angles(outer, inner):
    return np.asarray(leaf_phases(outer))[:, None] * np.asarray(inner)[None, :] * (2.0 * np.pi / SPAN)


def matrix_blocks():
    matrix = dft_matrix()
    high = matrix.astype(ml_dtypes.bfloat16)
    low = (matrix - high.astype(np.float64)).astype(ml_dtypes.bfloat16)
    return np.concatenate([high, low, high][:PASSES], axis=1)


def leaf_place(leaf):
    return leaf // 2, slice((leaf % 2) * LANES, (leaf % 2 + 1) * LANES)


def split_store(ref, leaf, below, here, value):
    pair, lanes = leaf_place(leaf)
    high = value.astype(bf16)
    for block in range(PASSES):
        part = high
        if PASSES == 3 and block == 2:
            part = (value - high.astype(f32)).astype(bf16)
        ref[pair, shifted_rows(here, block * BOTH + below), lanes] = part


def run_all(stages, rows_here, matmul=None, carry=0):
    tiles = matmul[2].shape[0] if matmul else 4
    ratio = SPAN // rows_here
    in_part = tiles // ratio
    per_tile = CHUNKS // tiles
    for part in range(ratio):

        def step(tile, carry, part=part):
            if matmul:
                matrix_ref, split_ref, result_ref = matmul
                place = part * in_part + tile
                result_ref[place] = jnp.dot(matrix_ref[...], split_ref[place], preferred_element_type=f32)
            for chunk in range(per_tile):
                for stage in stages:
                    carry = stage(part, chunk_row(tile * per_tile + chunk), carry)
            return carry

        carry = lax.fori_loop(0, in_part, step, carry)
    return carry


def chunk_row(idx):
    return pl.multiple_of(idx * CHUNK, CHUNK)


def in_span(part, row, rows_here):
    return pl.ds(pl.multiple_of(part * rows_here + row, CHUNK), CHUNK)


def twist_stage(coarse_ref, fine_ref, twist_ref, rows_here):
    outer = twist_ref.shape[1]

    def stage(part, row, carry):
        here = in_span(part, row, rows_here)
        idx = part * (rows_here // CHUNK) + row // CHUNK
        for leaf in range(outer):
            far_cosine = coarse_ref[idx, leaf]
            far_sine = coarse_ref[idx, outer + leaf]
            cosine = fine_ref[0, leaf]
            sine = fine_ref[1, leaf]
            twist_ref[0, leaf, here, :] = far_cosine * cosine - far_sine * sine
            twist_ref[1, leaf, here, :] = far_sine * cosine + far_cosine * sine
        return carry

    return stage


def leaves_stage(signals_ref, kind, twist_ref, split_ref):
    outer = twist_ref.shape[1]
    rows_here = signals_ref.shape[2]
    ratio = SPAN // rows_here

    def stage(part, row, carry):
        here = in_span(part, row, rows_here)
        parts = [
            signals_ref[place * ratio + part, kind, pl.ds(row, CHUNK), :].astype(f32) for place in range(outer)
        ]
        for leaf, (re, im) in enumerate(to_leaves(parts)):
            cosine = twist_ref[0, leaf, here, :]
            sine = twist_ref[1, leaf, here, :]
            split_store(split_ref, leaf, 0, here, re * cosine + im * sine)
            split_store(split_ref, leaf, SPAN, here, im * cosine - re * sine)
        return carry

    return stage


def shifted_rows(here, by):
    return pl.ds(here.start + by, here.size)


def combine_stage(left_ref, right_ref, split_ref, rows_here, conjugate):
    def stage(part, row, carry):
        here = in_span(part, row, rows_here)
        below = shifted_rows(here, SPAN)
        for leaf in range(2 * left_ref.shape[0]):
            pair, lanes = leaf_place(leaf)
            left_re = left_ref[pair, here, lanes]
            left_im = left_ref[pair, below, lanes]
            right_re = right_ref[pair, here, lanes]
            right_im = right_ref[pair, below, lanes]
            if conjugate:
                re = left_re * right_re + left_im * right_im
                minus_im = left_im * right_re - left_re * right_im
            else:
                re = left_re * right_re - left_im * right_im
                minus_im = -(left_re * right_im + left_im * right_re)
            split_store(split_ref, leaf, 0, here, re)
            split_store(split_ref, leaf, SPAN, here, minus_im)
        return carry

    return stage


def signal_stage(time_ref, twist_ref, rows_here, write):
    outer = twist_ref.shape[1]
    ratio = SPAN // rows_here
    scale = 1.0 / (SPAN * outer)

    def stage(part, row, carry):
        here = in_span(part, row, rows_here)
        below = shifted_rows(here, SPAN)
        leaves = []
        for leaf in range(outer):
            pair, lanes = leaf_place(leaf)
            cosine = twist_ref[0, leaf, here, :]
            sine = twist_ref[1, leaf, here, :]
            re = time_ref[pair, here, lanes]
            minus_im = time_ref[pair, below, lanes]
            leaves.append((re * cosine + minus_im * sine, re * sine - minus_im * cosine))
        for place, value in enumerate(from_leaves(leaves, scale)):
            carry = write(place * ratio + part, pl.ds(row, CHUNK), value, carry)
        return carry

    return stage


def filter_kernel(
    filter_ref, coarse_ref, fine_ref, matrix_ref, spec_ref, twist_ref, split_ref,
):
    rows_here = filter_ref.shape[2]
    run_all([twist_stage(coarse_ref, fine_ref, twist_ref, rows_here)], rows_here)
    run_all([leaves_stage(filter_ref, 0, twist_ref, split_ref)], rows_here)
    run_all([], rows_here, (matrix_ref, split_ref, spec_ref))


def products_kernel(
    signals_hbm, filter_hbm, coarse_ref, fine_ref, matrix_hbm, results_hbm, lag_hbm,
    twist_ref, matrix_ref, signals_ref, results_ref, one_split, two_split, lag_split,
    filter_ref, product_ref, cotan_ref, time_ref, sems,
):
    rows_here = signals_ref.shape[2]
    arrivals = [
        pltpu.make_async_copy(signals_hbm.at[:, kind], signals_ref.at[:, kind], sems.at[kind]) for kind in range(2)
    ]
    matrix_copy = pltpu.make_async_copy(matrix_hbm, matrix_ref, sems.at[2])
    filter_copy = pltpu.make_async_copy(filter_hbm, filter_ref, sems.at[3])
    lag_copy = pltpu.make_async_copy(lag_split, lag_hbm, sems.at[4])
    returns = [
        pltpu.make_async_copy(results_ref.at[:, kind], results_hbm.at[:, kind], sems.at[5 + kind]) for kind in range(2)
    ]

    def leaves(kind, split_ref):
        return leaves_stage(signals_ref, kind, twist_ref, split_ref)

    def combine(left_ref, right_ref, split_ref, conjugate):
        return combine_stage(left_ref, right_ref, split_ref, rows_here, conjugate)

    def result(kind, from_ref):
        def write(piece, rows, value, carry):
            results_ref[piece, kind, rows, :] = value.astype(bf16)
            return carry

        return signal_stage(from_ref, twist_ref, rows_here, write)

    for copy in (arrivals[0], matrix_copy, arrivals[1], filter_copy):
        copy.start()
    run_all([twist_stage(coarse_ref, fine_ref, twist_ref, rows_here)], rows_here)
    arrivals[0].wait()
    run_all([leaves(0, one_split)], rows_here)
    arrivals[1].wait()
    matrix_copy.wait()
    run_all([leaves(1, two_split)], rows_here, (matrix_ref, one_split, product_ref))
    filter_copy.wait()
    run_all([combine(filter_ref, product_ref, one_split, False)], rows_here, (matrix_ref, two_split, cotan_ref))
    run_all([combine(filter_ref, cotan_ref, two_split, True)], rows_here, (matrix_ref, one_split, time_ref))
    run_all(
        [combine(product_ref, cotan_ref, lag_split, True), result(0, time_ref)],
        rows_here, (matrix_ref, two_split, filter_ref),
    )
    lag_copy.start()
    returns[0].start()
    run_all([result(1, filter_ref)], rows_here)
    returns[1].start()
    lag_copy.wait()
    returns[0].wait()
    returns[1].wait()


def lag_kernel(
    split_hbm, coarse_ref, fine_ref, matrix_hbm, lag_ref, square_ref, twist_ref, matrix_ref, split_ref, time_ref, sems
):
    rows_here = lag_ref.shape[1]
    copies = [
        pltpu.make_async_copy(matrix_hbm, matrix_ref, sems.at[0]),
        pltpu.make_async_copy(split_hbm, split_ref, sems.at[1]),
    ]
    for copy in copies:
        copy.start()
    run_all([twist_stage(coarse_ref, fine_ref, twist_ref, rows_here)], rows_here)
    for copy in copies:
        copy.wait()
    run_all([], rows_here, (matrix_ref, split_ref, time_ref))

    def write(piece, rows, value, carry):
        lag_ref[piece, rows, :] = value.astype(bf16)
        return carry + value * value

    square = run_all(
        [signal_stage(time_ref, twist_ref, rows_here, write)], rows_here, None, jnp.zeros((CHUNK, LANES), f32)
    )
    square_ref[...] = jnp.sum(square, axis=0, keepdims=True)


class Transforms:
    def __init__(self, pieces, rows_here):
        outer = pieces * rows_here // SPAN
        pairs = outer // 2
        coarse = twist_angles(outer, CHUNK * np.arange(CHUNKS)).T
        fine = twist_angles(outer, np.arange(CHUNK))[..., None] * np.ones(LANES)
        self.tables = [
            jnp.asarray(np.concatenate([np.cos(coarse), np.sin(coarse)], axis=1).astype(np.float32)),
            jnp.asarray(np.stack([np.cos(fine), np.sin(fine)]).astype(np.float32)),
            jnp.asarray(matrix_blocks()),
        ]
        self.spec = jax.ShapeDtypeStruct((pairs, BOTH, 2 * LANES), f32)
        self.split = jax.ShapeDtypeStruct((pairs, PASSES * BOTH, 2 * LANES), bf16)
        self.signal = jax.ShapeDtypeStruct((pieces, rows_here, LANES), bf16)
        self.result = jax.ShapeDtypeStruct((pieces, 2, rows_here, LANES), bf16)
        self.square = jax.ShapeDtypeStruct((1, LANES), f32)
        self.pair_work = pltpu.VMEM(self.result.shape, bf16)
        self.work = pltpu.VMEM(self.spec.shape, f32)
        self.split_work = pltpu.VMEM(self.split.shape, bf16)
        self.twist_work = pltpu.VMEM((2, outer, SPAN, LANES), f32)
        self.matrix_work = pltpu.VMEM(self.tables[2].shape, bf16)

    def filter(self, signal):
        return call(
            filter_kernel, self.spec, [self.twist_work, self.split_work],
            signal, *self.tables,
            in_specs=[IN_VMEM, IN_SMEM, IN_VMEM, IN_VMEM],
            out_specs=IN_VMEM,
        )

    def products(self, signals, filter_spec):
        return call(
            products_kernel, (self.result, self.split),
            [self.twist_work, self.matrix_work, self.pair_work, self.pair_work]
            + [self.split_work] * 3
            + [self.work] * 4
            + [pltpu.SemaphoreType.DMA((7,))],
            signals, filter_spec, *self.tables,
            in_specs=[ANYWHERE, ANYWHERE, IN_SMEM, IN_VMEM, ANYWHERE],
            out_specs=(ANYWHERE, ANYWHERE),
        )

    def lag(self, lag_split):
        return call(
            lag_kernel, (self.signal, self.square),
            [self.twist_work, self.matrix_work, self.split_work, self.work, pltpu.SemaphoreType.DMA((2,))],
            lag_split, *self.tables,
            in_specs=[ANYWHERE, IN_SMEM, IN_VMEM, ANYWHERE],
            out_specs=(IN_VMEM, IN_VMEM),
        )


class PlainTransforms:
    def __init__(self, pieces, rows_here):
        self.seq_len = pieces * rows_here
        self.pieces = pieces
        self.outer = self.seq_len // SPAN
        idx = np.arange(SPAN)
        angle = (idx[:, None] * idx[None, :] % SPAN) * (2.0 * np.pi / SPAN)
        self.cosine = jnp.asarray(np.cos(angle), f32)
        self.sine = jnp.asarray(np.sin(angle), f32)
        twist = twist_angles(self.outer, idx)
        self.twist = jnp.asarray(np.stack([np.cos(twist), np.sin(twist)]), f32)[..., None]

    def dot(self, matrix, signal):
        return jnp.einsum("fs,tsc->tfc", matrix, signal, precision=lax.Precision.HIGHEST)

    def spectrum(self, signal):
        parts = signal.astype(f32).reshape(self.outer, SPAN, -1)
        leaves = to_leaves([parts[part] for part in range(self.outer)])
        re = jnp.stack([leaf[0] for leaf in leaves])
        im = jnp.stack([leaf[1] for leaf in leaves])
        twist_re = re * self.twist[0] + im * self.twist[1]
        twist_im = im * self.twist[0] - re * self.twist[1]
        return (
            self.dot(self.cosine, twist_re) + self.dot(self.sine, twist_im),
            self.dot(self.cosine, twist_im) - self.dot(self.sine, twist_re),
        )

    def back(self, re, im):
        time_re = self.dot(self.cosine, re) - self.dot(self.sine, im)
        time_im = self.dot(self.cosine, im) + self.dot(self.sine, re)
        leaf_re = time_re * self.twist[0] - time_im * self.twist[1]
        leaf_im = time_im * self.twist[0] + time_re * self.twist[1]
        parts = from_leaves([(leaf_re[leaf], leaf_im[leaf]) for leaf in range(self.outer)], 1.0 / self.seq_len)
        return jnp.stack(parts).reshape(self.pieces, self.seq_len // self.pieces, -1)

    def filter(self, signal):
        return self.spectrum(signal[:, 0])

    def products(self, signals, taps):
        product, cotan = (self.spectrum(signals[:, kind]) for kind in range(2))
        conv = self.back(taps[0] * product[0] - taps[1] * product[1], taps[0] * product[1] + taps[1] * product[0])
        corr = self.back(taps[0] * cotan[0] + taps[1] * cotan[1], taps[0] * cotan[1] - taps[1] * cotan[0])
        lag = (
            product[0] * cotan[0] + product[1] * cotan[1],
            product[0] * cotan[1] - product[1] * cotan[0],
        )
        return jnp.stack([conv, corr], axis=1).astype(bf16), lag

    def lag(self, lag_spec):
        lag = self.back(*lag_spec)
        squares = jnp.sum(lag * lag, axis=(0, 1))
        return lag.astype(bf16), jnp.zeros((1, LANES), f32).at[0, : squares.shape[0]].set(squares)


def group(idx):
    return pl.ds(pl.multiple_of(idx * LANES, LANES), LANES)


def streamed(work, steps, per_step, places, in_count, out_count, kept, *refs):
    moved = in_count + out_count
    hbm = refs[:moved]
    kept_refs = refs[moved : moved + kept]
    held = refs[moved + kept : 2 * moved + kept]
    scratch = refs[2 * moved + kept : -1]
    sems = refs[-1]

    def copy(place, step):
        outside = hbm[place].at[places[place][0](step)]
        inside = held[place].at[places[place][1](step)]
        ends = (outside, inside) if place < in_count else (inside, outside)
        return pltpu.make_async_copy(*ends, sems.at[place, step])

    def arrivals(step):
        return [copy(place, step) for place in range(in_count) if places[place][0](step) is not None]

    for step in range(steps):
        for arrival in arrivals(step):
            arrival.start()
    for step in range(steps):
        for arrival in arrivals(step):
            arrival.wait()

        def one(idx, carry):
            work(idx, held[:in_count], held[in_count:] + kept_refs, scratch)
            return carry

        lax.fori_loop(step * per_step, (step + 1) * per_step, one, 0)
        for place in range(in_count, moved):
            copy(place, step).start()
    for step in range(steps):
        for place in range(in_count, moved):
            copy(place, step).wait()


def stream_call(work, steps, per_step, operands, results, scratch=(), aliases=(), kept=()):
    arrays = [operand[0] for operand in operands]
    shapes = [jax.ShapeDtypeStruct(array.shape, array.dtype) for array in arrays] + [result[0] for result in results]
    cuts = [entry[1] for entry in operands] + [entry[1] for entry in results]
    held = [pltpu.VMEM(entry[2] or shape.shape, shape.dtype) for entry, shape in zip(operands + results, shapes)]
    extra = list(aliases)
    kernel = functools.partial(streamed, work, steps, per_step, cuts, len(arrays), len(results), len(kept))

    def with_aliases(*refs):
        kernel(*refs[: len(arrays)], *refs[len(arrays) + len(extra) :])

    return call(
        with_aliases,
        tuple(result[0] for result in results) + tuple(kept),
        held + list(scratch) + [pltpu.SemaphoreType.DMA((len(shapes), steps))],
        *arrays, *extra,
        in_specs=[ANYWHERE] * (len(arrays) + len(extra)),
        out_specs=(ANYWHERE,) * len(results) + (IN_VMEM,) * len(kept),
        input_output_aliases={len(arrays) + idx: idx for idx in range(len(extra))},
    )


def cut_lanes(width, rank):
    def place(step):
        return (slice(None),) * (rank - 1) + (pl.ds(step * width, width),)

    return place, place


def cut_groups(per_step):
    def place(step):
        return (pl.ds(step * per_step, per_step),)

    return place, place


def cut_none(step):
    return None if step else (slice(None),)


def row_blocks(rows_here):
    return [slice(start, start + ROWS) for start in range(0, rows_here, ROWS)]


def pack_work(idx, operands, results, scratch):
    results[0][idx, 0] = operands[0][:, group(idx)].astype(bf16)


def extend_rows(lead, in_ref, lanes, ext_ref):
    ext_ref[PAD - lead.shape[0] : PAD, :] = lead
    ext_ref[PAD:, :] = in_ref[:, lanes].astype(f32)


def short_conv(ext_ref, taps, rows):
    result = None
    for shift_idx in range(taps.shape[0]):
        term = taps[shift_idx : shift_idx + 1] * ext_ref[PAD + rows.start - shift_idx : PAD + rows.stop - shift_idx, :]
        result = term if result is None else result + term
    return result


def extend_three(idx, operands, lead_ref, halo_rows, exts):
    lead = lead_ref[:, group(idx)]
    for place, ext in enumerate(exts):
        extend_rows(lead[place * halo_rows : (place + 1) * halo_rows], operands[place], group(idx), ext)


def signals_work(idx, operands, results, exts):
    q_ref, k_ref, v_ref, grad_ref, lead_ref, taps_ref = operands
    taps = taps_ref[:, group(idx)]
    extend_three(idx, operands, lead_ref, taps.shape[0] - 1, exts)
    for rows in row_blocks(q_ref.shape[0]):
        q_short, k_short, v_short = (short_conv(ext, taps, rows) for ext in exts)
        results[0][idx, 0, rows, :] = (k_short * v_short).astype(bf16)
        results[0][idx, 1, rows, :] = (grad_ref[rows, group(idx)].astype(f32) * q_short).astype(bf16)


def short_work(idx, operands, results, exts):
    q_ref, k_ref, v_ref, lead_ref, taps_ref = operands
    taps = taps_ref[:, group(idx)]
    extend_three(idx, operands, lead_ref, taps.shape[0] - 1, exts)
    for rows in row_blocks(q_ref.shape[0]):
        for place, ext in enumerate(exts):
            results[0][place, rows, group(idx)] = short_conv(ext, taps, rows)


def fold(value):
    return jnp.sum(value.reshape(-1, 8, LANES), axis=0)


def finish_work(idx, operands, results, exts):
    q_ref, k_ref, v_ref, grad_ref, short_ref, lead_ref, taps_ref, skip_ref, long_ref, squares_ref = operands
    mixed_ref, grad_q_ref, grad_k_ref, grad_v_ref, front_ref, back_ref, sums_ref = results
    lanes = group(idx)
    taps = taps_ref[:, lanes]
    skip = skip_ref[:, lanes]
    lead = lead_ref[:, lanes]
    taps_count = taps.shape[0]
    halo_rows = taps_count - 1
    rows_here = q_ref.shape[0]
    sums = [jnp.zeros((8, LANES), f32) for _ in range(taps_count + 1)]
    for ext in exts:
        ext[rows_here:, :] = jnp.zeros((PAD, LANES), f32)
    for rows in row_blocks(rows_here):
        q_short, k_short, v_short = (short_ref[place, rows, lanes] for place in range(3))
        product = (k_short * v_short).astype(bf16).astype(f32)
        filtered = long_ref[idx, 0, rows, :].astype(f32) + skip * product
        mixed_ref[rows, lanes] = (q_short * filtered).astype(bf16)
        upstream = grad_ref[rows, lanes].astype(f32)
        back_mix = upstream * q_short
        back_prod = long_ref[idx, 1, rows, :].astype(f32) + skip * back_mix
        sums[taps_count] = sums[taps_count] + fold(back_mix * product)
        exts[0][rows, :] = upstream * filtered
        exts[1][rows, :] = back_prod * v_short
        exts[2][rows, :] = back_prod * k_short
    for place, (ext, in_ref, out_ref) in enumerate(
        zip(exts, (q_ref, k_ref, v_ref), (grad_q_ref, grad_k_ref, grad_v_ref))
    ):
        for rows in row_blocks(rows_here):
            signal = in_ref[rows, lanes].astype(f32)
            grad = None
            for shift_idx in range(taps_count):
                ahead = ext[rows.start + shift_idx : rows.stop + shift_idx, :]
                term = taps[shift_idx : shift_idx + 1] * ahead
                grad = term if grad is None else grad + term
                sums[shift_idx] = sums[shift_idx] + fold(ahead * signal)
            out_ref[rows, lanes] = grad.astype(bf16)
        back_ref[place * halo_rows : (place + 1) * halo_rows, lanes] = grad[ROWS - halo_rows :]
        front_ref[place * halo_rows : (place + 1) * halo_rows, lanes] = ext[0:halo_rows, :]
    extra = slice(sums_ref.shape[1] - LANES, sums_ref.shape[1])
    sums_ref[:, extra] = jnp.zeros((taps_count + 1, LANES), f32)
    sums_ref[0:1, extra] = squares_ref[...]
    for shift_idx in range(taps_count + 1):
        total = jnp.sum(sums[shift_idx], axis=0, keepdims=True)
        for place in range(3 if shift_idx < taps_count else 0):
            for row in range(shift_idx):
                at = place * halo_rows + halo_rows - shift_idx + row
                total = total + lead[at : at + 1] * exts[place][row : row + 1, :]
        sums_ref[shift_idx : shift_idx + 1, lanes] = total


def lead_kernel(q_ref, k_ref, v_ref, lead_ref):
    halo_rows = lead_ref.shape[0] // 3
    for place, ref in enumerate((q_ref, k_ref, v_ref)):
        rows = ref[...].astype(f32)
        lead_ref[place * halo_rows : (place + 1) * halo_rows, :] = rows[rows.shape[0] - halo_rows :]


def edges_kernel(back_ref, tail_ref, taps_ref, q_ref, k_ref, v_ref, q_out, k_out, v_out, work_ref):
    taps_count = taps_ref.shape[0]
    halo_rows = taps_count - 1
    block_rows = q_ref.shape[0]
    for place, (ref, out_ref) in enumerate(((q_ref, q_out), (k_ref, k_out), (v_ref, v_out))):
        work_ref[...] = ref[...].astype(f32)
        first = place * halo_rows
        for row in range(halo_rows):
            total = back_ref[first + row : first + row + 1, :]
            for shift_idx in range(halo_rows - row, taps_count):
                source = first + row + shift_idx - halo_rows
                total = total + taps_ref[shift_idx : shift_idx + 1, :] * tail_ref[source : source + 1, :]
            at = block_rows - halo_rows + row
            work_ref[at : at + 1, :] = total
        out_ref[...] = work_ref[...].astype(bf16)


def norm_kernel(*refs):
    values, totals_ref, square_ref = refs[:-2], refs[-2], refs[-1]
    channels = totals_ref.shape[1] - LANES
    totals = values[0][...]
    if len(values) == 4:
        totals = (totals + values[1][...]) + (values[2][...] + values[3][...])
    totals_ref[...] = totals
    square = jnp.sum(totals[:, :channels] * totals[:, :channels]) + jnp.sum(totals[0:1, channels:])
    square_ref[...] = jnp.full(square_ref.shape, square)


def scale_kernel(limit, totals_ref, norm_ref, lag_hbm, taps_out, skip_out, kernel_hbm, lag_ref, kernel_ref, sems):
    taps_count, channels = taps_out.shape
    groups = lag_ref.shape[0]
    per_step = max(groups // 4, 1)
    steps = groups // per_step
    arrivals = []
    returns = []
    for step in range(steps):
        here = pl.ds(step * per_step, per_step)
        lanes = pl.ds(step * per_step * LANES, per_step * LANES)
        arrivals.append(pltpu.make_async_copy(lag_hbm.at[here], lag_ref.at[here], sems.at[0, step]))
        returns.append(pltpu.make_async_copy(kernel_ref.at[:, lanes], kernel_hbm.at[:, lanes], sems.at[1, step]))
        arrivals[step].start()
    factor = limit / jnp.maximum(jnp.sqrt(norm_ref[...]), limit)
    for step in range(steps):
        arrivals[step].wait()
        for idx in range(step * per_step, (step + 1) * per_step):
            kernel_ref[:, idx * LANES : (idx + 1) * LANES] = lag_ref[idx].astype(f32) * factor
        returns[step].start()
    for idx in range(groups):
        lanes = slice(idx * LANES, (idx + 1) * LANES)
        taps_out[:, lanes] = totals_ref[0:taps_count, lanes] * factor
        skip_out[:, lanes] = totals_ref[taps_count : taps_count + 1, lanes] * factor
    for step in range(steps):
        returns[step].wait()


def exchange(pieces_first):
    return lax.all_to_all(pieces_first, "ctx", split_axis=0, concat_axis=0, tiled=True)


def to_pieces(groups, pieces):
    count, kinds, rows, lanes = groups.shape
    if count == pieces:
        return groups
    share = count * lanes // pieces
    split = groups.reshape(count, kinds, rows, lanes // share, share)
    return split.transpose(0, 3, 1, 2, 4).reshape(pieces, kinds, rows, share)


def to_groups(parts):
    pieces, kinds, rows, share = parts.shape
    if share == LANES:
        return parts
    joined = parts.reshape(pieces * share // LANES, LANES // share, kinds, rows, share)
    return joined.transpose(0, 2, 3, 1, 4).reshape(-1, kinds, rows, LANES)


def partners(value, axis, steps):
    size = lax.axis_size(axis)
    return [value] + [lax.ppermute(value, axis, [(i, i ^ step) for i in range(size)]) for step in steps]


def rounds_of(size):
    rounds = []
    step = 1
    while step < size:
        rounds.append((step, 2 * step, 3 * step) if size // step >= 4 else (step,))
        step *= 4 if size // step >= 4 else 2
    return rounds


def add_up(values):
    if len(values) == 2:
        return values[0] + values[1]
    return (values[0] + values[1]) + (values[2] + values[3])


def body(q_in, k_in, v_in, grad_out, short_filter, kernel, skip):
    pieces = lax.axis_size("ctx")
    sides = lax.axis_size("ch")
    rows_here, channels = q_in.shape
    seq_len = pieces * rows_here
    taps_count = short_filter.shape[0]
    halo_rows = taps_count - 1
    groups = channels // LANES
    share = channels // pieces
    per_step = min(groups, 4)
    steps = groups // per_step
    lanes2 = cut_lanes(per_step * LANES, 2)
    lanes3 = cut_lanes(per_step * LANES, 3)
    transforms = (Transforms if share == LANES else PlainTransforms)(pieces, rows_here)
    stream = functools.partial(stream_call, steps=steps, per_step=per_step)

    flat = jax.ShapeDtypeStruct((rows_here, channels), bf16)
    halo = jax.ShapeDtypeStruct((3 * halo_rows, channels), f32)
    one_sent = jax.ShapeDtypeStruct((groups, 1, rows_here, LANES), bf16)
    two_sent = jax.ShapeDtypeStruct((groups, 2, rows_here, LANES), bf16)
    exts = [pltpu.VMEM((rows_here + PAD, LANES), f32)] * 3
    last_block = 16
    last_spec = pl.BlockSpec((last_block, channels), lambda i: (rows_here // last_block - 1, 0))

    def whole(array):
        return pl.BlockSpec(array.shape, lambda i: (0,) * len(array.shape))

    lead = call(
        lead_kernel, halo, [], q_in, k_in, v_in,
        grid=(1,), in_specs=[last_spec] * 3, out_specs=whole(halo),
    )
    lead = lax.ppermute(lead, "ctx", [(i, i + 1) for i in range(pieces - 1)])

    (packed,) = stream(
        pack_work,
        operands=[(kernel, lanes2, None)],
        results=[(one_sent, cut_groups(per_step), None)],
    )
    filter_here = exchange(to_pieces(packed, pieces))
    (signals,) = stream(
        signals_work,
        operands=[(x, lanes2, None) for x in (q_in, k_in, v_in, grad_out, lead, short_filter)],
        results=[(two_sent, cut_groups(per_step), None)],
        scratch=exts,
    )
    signals_here = exchange(to_pieces(signals, pieces))
    (short,) = stream(
        short_work,
        operands=[(x, lanes2, None) for x in (q_in, k_in, v_in, lead, short_filter)],
        results=[(jax.ShapeDtypeStruct((3, rows_here, channels), f32), lanes3, None)],
        scratch=exts,
    )
    filter_spec = transforms.filter(filter_here)
    long_here, lag_spec = transforms.products(signals_here, filter_spec)
    long = to_groups(exchange(long_here))
    lag_here, lag_squares = transforms.lag(lag_spec)

    mixed, grad_q, grad_k, grad_v, front, back, sums = stream(
        finish_work,
        operands=[(x, lanes2, None) for x in (q_in, k_in, v_in, grad_out)]
        + [(short, lanes3, None)]
        + [(x, lanes2, None) for x in (lead, short_filter, skip.reshape(1, channels))]
        + [(long, cut_groups(per_step), None), (lag_squares, (cut_none, cut_none), None)],
        results=[(flat, lanes2, None)] * 4,
        scratch=exts,
        kept=[halo, halo, jax.ShapeDtypeStruct((taps_count + 1, channels + LANES), f32)],
    )
    lag_here, sums = lax.optimization_barrier((lag_here, sums))
    lag = to_groups(exchange(lag_here[:, None]))[:, 0]

    totals = sums
    rounds = rounds_of(pieces)
    for steps_of in rounds[:-1]:
        totals = add_up(partners(totals, "ctx", steps_of))
    last = partners(totals, "ctx", rounds[-1])
    if len(last) == 2:
        last = [last[0] + last[1]]

    tail = lax.ppermute(front, "ctx", [(i, i - 1) for i in range(1, pieces)])
    grad_q, grad_k, grad_v = call(
        edges_kernel, (flat, flat, flat), [pltpu.VMEM((last_block, channels), f32)],
        back, tail, short_filter, grad_q, grad_k, grad_v,
        vmem_bytes=SMALL_VMEM_BYTES,
        grid=(1,),
        in_specs=[whole(back), whole(tail), whole(short_filter)] + [last_spec] * 3,
        out_specs=(last_spec,) * 3,
        input_output_aliases={3: 0, 4: 1, 5: 2},
    )
    grad_q, grad_k, grad_v, *last = lax.optimization_barrier((grad_q, grad_k, grad_v, *last))

    totals, norm_sq = call(
        norm_kernel,
        (jax.ShapeDtypeStruct(totals.shape, f32), jax.ShapeDtypeStruct((1, LANES), f32)),
        [], *last,
        vmem_bytes=SMALL_VMEM_BYTES,
        in_specs=[IN_VMEM] * len(last), out_specs=(IN_VMEM, IN_VMEM),
    )
    for steps_of in rounds_of(sides):
        norm_sq = add_up(partners(norm_sq, "ch", steps_of))

    limit = math.sqrt(float(seq_len * channels * sides))
    grad_short, grad_skip, grad_kernel = call(
        functools.partial(scale_kernel, limit),
        (
            jax.ShapeDtypeStruct((taps_count, channels), f32),
            jax.ShapeDtypeStruct((1, channels), f32),
            jax.ShapeDtypeStruct((rows_here, channels), f32),
        ),
        [pltpu.VMEM(lag.shape, bf16), pltpu.VMEM((rows_here, channels), f32), pltpu.SemaphoreType.DMA((2, 4))],
        totals, norm_sq, lag,
        vmem_bytes=SMALL_VMEM_BYTES,
        in_specs=[IN_VMEM, IN_VMEM, ANYWHERE],
        out_specs=(IN_VMEM, IN_VMEM, ANYWHERE),
    )
    return mixed, grad_q, grad_k, grad_v, grad_short, grad_skip.reshape(channels), grad_kernel


def solution(mesh):
    in_specs = (
        P("ctx", "ch"),
        P("ctx", "ch"),
        P("ctx", "ch"),
        P("ctx", "ch"),
        P(None, "ch"),
        P("ctx", "ch"),
        P("ch"),
    )
    out_specs = (
        P("ctx", "ch"),
        P("ctx", "ch"),
        P("ctx", "ch"),
        P("ctx", "ch"),
        P(None, "ch"),
        P("ch"),
        P("ctx", "ch"),
    )
    return jax.shard_map(body, mesh=mesh, in_specs=in_specs, out_specs=out_specs, check_vma=False)
```

```python
import functools
import math

import jax
import jax.numpy as jnp
import ml_dtypes
import numpy as np
from jax import lax
from jax.experimental import pallas as pl
from jax.experimental.pallas import tpu as pltpu
from jax.sharding import PartitionSpec as P

LANES = 128
SPAN = 256
BOTH = 2 * SPAN
CHUNK = 16
CHUNKS = SPAN // CHUNK
PAD = 8
ROWS = 32
PASSES = 2
VMEM_BYTES = 60 * 1024 * 1024
SMALL_VMEM_BYTES = 8 * 1024 * 1024

f32 = jnp.float32
bf16 = jnp.bfloat16

IN_VMEM = pl.BlockSpec(memory_space=pltpu.VMEM)
IN_SMEM = pl.BlockSpec(memory_space=pltpu.SMEM)
ANYWHERE = pl.BlockSpec(memory_space=pl.ANY)


def call(kernel, outs, scratch, *args, vmem_bytes=VMEM_BYTES, **options):
    return pl.pallas_call(
        kernel,
        out_shape=outs,
        scratch_shapes=scratch,
        compiler_params=pltpu.CompilerParams(vmem_limit_bytes=vmem_bytes),
        **options,
    )(*args)


def spread_copies(held_ref, outside, me, sems):
    if len(outside) == 1:
        return [pltpu.make_async_copy(held_ref, outside[0], sems.at[0])]
    return [pltpu.make_async_copy(held_ref.at[me ^ idx], ref, sems.at[idx]) for idx, ref in enumerate(outside)]


def collect_copies(outside, held_ref, me, sems):
    if len(outside) == 1:
        return [pltpu.make_async_copy(outside[0], held_ref, sems.at[0])]
    return [pltpu.make_async_copy(ref, held_ref.at[me ^ idx], sems.at[idx]) for idx, ref in enumerate(outside)]


def start_all(copies):
    for copy in copies:
        copy.start()


def wait_all(copies):
    for copy in copies:
        copy.wait()


def leaf_phases(count):
    return [(4 * leaf + 1) / (4 * count) for leaf in range(count)]


def root_times(re, im, num, den, sign):
    if num == 0:
        return re, im
    if 4 * num == den:
        return (im, -re) if sign < 0 else (-im, re)
    cosine = math.cos(2.0 * math.pi * num / den)
    sine = sign * math.sin(2.0 * math.pi * num / den)
    if 8 * num == den:
        return ((re + im) * cosine, (im - re) * cosine) if sign < 0 else ((re - im) * cosine, (re + im) * cosine)
    if 8 * num == 3 * den:
        return ((re - im) * cosine, (re + im) * cosine) if sign < 0 else ((re + im) * cosine, (im - re) * cosine)
    return re * cosine - im * sine, im * cosine + re * sine


def short_fft(values, sign):
    count = len(values)
    if count == 1:
        return values
    even = short_fft(values[0::2], sign)
    odd = short_fft(values[1::2], sign)
    first = []
    second = []
    for num in range(count // 2):
        re, im = root_times(*odd[num], num, count, sign)
        first.append((even[num][0] + re, even[num][1] + im))
        second.append((even[num][0] - re, even[num][1] - im))
    return first + second


def to_leaves(parts):
    count = len(parts)
    turned = []
    for idx, part in enumerate(parts):
        angle = 2.0 * math.pi * idx / (4 * count)
        turned.append((part * math.cos(angle), part * (-math.sin(angle))) if idx else (part, jnp.zeros_like(part)))
    return short_fft(turned, -1)


def from_leaves(leaves, scale):
    count = len(leaves)
    parts = []
    for idx, (re, im) in enumerate(short_fft(leaves, 1)):
        angle = 2.0 * math.pi * idx / (4 * count)
        if idx == 0:
            parts.append(re * scale)
        else:
            parts.append(re * (math.cos(angle) * scale) - im * (math.sin(angle) * scale))
    return parts


def dft_matrix():
    idx = np.arange(SPAN)
    angle = (idx[:, None] * idx[None, :] % SPAN) * (2.0 * np.pi / SPAN)
    cosine, sine = np.cos(angle), np.sin(angle)
    return np.block([[cosine, sine], [-sine, cosine]])


def twist_angles(outer, inner):
    return np.asarray(leaf_phases(outer))[:, None] * np.asarray(inner)[None, :] * (2.0 * np.pi / SPAN)


def matrix_blocks():
    matrix = dft_matrix()
    high = matrix.astype(ml_dtypes.bfloat16)
    low = (matrix - high.astype(np.float64)).astype(ml_dtypes.bfloat16)
    return np.concatenate([high, low, high][:PASSES], axis=1)


def leaf_place(leaf):
    return leaf // 2, slice((leaf % 2) * LANES, (leaf % 2 + 1) * LANES)


def split_store(ref, leaf, below, here, value):
    pair, lanes = leaf_place(leaf)
    high = value.astype(bf16)
    for block in range(PASSES):
        part = high
        if PASSES == 3 and block == 2:
            part = (value - high.astype(f32)).astype(bf16)
        ref[pair, shifted_rows(here, block * BOTH + below), lanes] = part


def run_all(stages, rows_here, matmul=None, carry=0):
    tiles = matmul[2].shape[0] if matmul else 4
    ratio = SPAN // rows_here
    in_part = tiles // ratio
    per_tile = CHUNKS // tiles
    for part in range(ratio):

        def step(tile, carry, part=part):
            if matmul:
                matrix_ref, split_ref, result_ref = matmul
                place = part * in_part + tile
                result_ref[place] = jnp.dot(matrix_ref[...], split_ref[place], preferred_element_type=f32)
            for chunk in range(per_tile):
                for stage in stages:
                    carry = stage(part, chunk_row(tile * per_tile + chunk), carry)
            return carry

        carry = lax.fori_loop(0, in_part, step, carry)
    return carry


def chunk_row(idx):
    return pl.multiple_of(idx * CHUNK, CHUNK)


def in_span(part, row, rows_here):
    return pl.ds(pl.multiple_of(part * rows_here + row, CHUNK), CHUNK)


def twist_stage(coarse_ref, fine_ref, twist_ref, rows_here):
    outer = twist_ref.shape[1]

    def stage(part, row, carry):
        here = in_span(part, row, rows_here)
        idx = part * (rows_here // CHUNK) + row // CHUNK
        for leaf in range(outer):
            far_cosine = coarse_ref[idx, leaf]
            far_sine = coarse_ref[idx, outer + leaf]
            cosine = fine_ref[0, leaf]
            sine = fine_ref[1, leaf]
            twist_ref[0, leaf, here, :] = far_cosine * cosine - far_sine * sine
            twist_ref[1, leaf, here, :] = far_sine * cosine + far_cosine * sine
        return carry

    return stage


def leaves_stage(signals_ref, kind, twist_ref, split_ref):
    outer = twist_ref.shape[1]
    rows_here = signals_ref.shape[2]
    ratio = SPAN // rows_here

    def stage(part, row, carry):
        here = in_span(part, row, rows_here)
        parts = [
            signals_ref[place * ratio + part, kind, pl.ds(row, CHUNK), :].astype(f32) for place in range(outer)
        ]
        for leaf, (re, im) in enumerate(to_leaves(parts)):
            cosine = twist_ref[0, leaf, here, :]
            sine = twist_ref[1, leaf, here, :]
            split_store(split_ref, leaf, 0, here, re * cosine + im * sine)
            split_store(split_ref, leaf, SPAN, here, im * cosine - re * sine)
        return carry

    return stage


def shifted_rows(here, by):
    return pl.ds(here.start + by, here.size)


def combine_stage(left_ref, right_ref, split_ref, rows_here, conjugate):
    def stage(part, row, carry):
        here = in_span(part, row, rows_here)
        below = shifted_rows(here, SPAN)
        for leaf in range(2 * left_ref.shape[0]):
            pair, lanes = leaf_place(leaf)
            left_re = left_ref[pair, here, lanes]
            left_im = left_ref[pair, below, lanes]
            right_re = right_ref[pair, here, lanes]
            right_im = right_ref[pair, below, lanes]
            if conjugate:
                re = left_re * right_re + left_im * right_im
                minus_im = left_im * right_re - left_re * right_im
            else:
                re = left_re * right_re - left_im * right_im
                minus_im = -(left_re * right_im + left_im * right_re)
            split_store(split_ref, leaf, 0, here, re)
            split_store(split_ref, leaf, SPAN, here, minus_im)
        return carry

    return stage


def signal_stage(time_ref, twist_ref, rows_here, write):
    outer = twist_ref.shape[1]
    ratio = SPAN // rows_here
    scale = 1.0 / (SPAN * outer)

    def stage(part, row, carry):
        here = in_span(part, row, rows_here)
        below = shifted_rows(here, SPAN)
        leaves = []
        for leaf in range(outer):
            pair, lanes = leaf_place(leaf)
            cosine = twist_ref[0, leaf, here, :]
            sine = twist_ref[1, leaf, here, :]
            re = time_ref[pair, here, lanes]
            minus_im = time_ref[pair, below, lanes]
            leaves.append((re * cosine + minus_im * sine, re * sine - minus_im * cosine))
        for place, value in enumerate(from_leaves(leaves, scale)):
            carry = write(place * ratio + part, pl.ds(row, CHUNK), value, carry)
        return carry

    return stage


def products_kernel(
    count, me_ref, coarse_ref, fine_ref, matrix_hbm, *refs
):
    signals_hbm = refs[:count]
    results_hbm = refs[count : 2 * count]
    (
        lag_hbm, twist_ref, matrix_ref, signals_ref, results_ref, one_split, two_split, lag_split,
        filter_ref, product_ref, cotan_ref, time_ref, arrival_sems, return_sems, sems,
    ) = refs[2 * count :]
    me = me_ref[0]
    rows_here = signals_ref.shape[2]
    arrivals = collect_copies(signals_hbm, signals_ref, me, arrival_sems)
    returns = spread_copies(results_ref, results_hbm, me, return_sems)
    matrix_copy = pltpu.make_async_copy(matrix_hbm, matrix_ref, sems.at[0])
    lag_copy = pltpu.make_async_copy(lag_split, lag_hbm, sems.at[1])

    def leaves(kind, split_ref):
        return leaves_stage(signals_ref, kind, twist_ref, split_ref)

    def combine(left_ref, right_ref, split_ref, conjugate):
        return combine_stage(left_ref, right_ref, split_ref, rows_here, conjugate)

    def result(kind, from_ref):
        def write(piece, rows, value, carry):
            results_ref[piece, kind, rows, :] = value.astype(bf16)
            return carry

        return signal_stage(from_ref, twist_ref, rows_here, write)

    start_all(arrivals)
    matrix_copy.start()
    run_all([twist_stage(coarse_ref, fine_ref, twist_ref, rows_here)], rows_here)
    wait_all(arrivals)
    run_all([leaves(2, one_split)], rows_here)
    matrix_copy.wait()
    run_all([leaves(0, two_split)], rows_here, (matrix_ref, one_split, filter_ref))
    run_all([leaves(1, one_split)], rows_here, (matrix_ref, two_split, product_ref))
    run_all([combine(filter_ref, product_ref, two_split, False)], rows_here, (matrix_ref, one_split, cotan_ref))
    run_all([combine(filter_ref, cotan_ref, one_split, True)], rows_here, (matrix_ref, two_split, time_ref))
    run_all(
        [combine(product_ref, cotan_ref, lag_split, True), result(0, time_ref)],
        rows_here, (matrix_ref, one_split, filter_ref),
    )
    lag_copy.start()
    run_all([result(1, filter_ref)], rows_here)
    start_all(returns)
    lag_copy.wait()
    wait_all(returns)


def lag_kernel(
    count, me_ref, split_hbm, coarse_ref, fine_ref, matrix_hbm, *refs
):
    lag_hbm = refs[:count]
    square_ref, lag_ref, twist_ref, matrix_ref, split_ref, time_ref, return_sems, sems = refs[count:]
    rows_here = lag_ref.shape[1]
    copies = [
        pltpu.make_async_copy(matrix_hbm, matrix_ref, sems.at[0]),
        pltpu.make_async_copy(split_hbm, split_ref, sems.at[1]),
    ]
    start_all(copies)
    run_all([twist_stage(coarse_ref, fine_ref, twist_ref, rows_here)], rows_here)
    wait_all(copies)
    run_all([], rows_here, (matrix_ref, split_ref, time_ref))

    def write(piece, rows, value, carry):
        lag_ref[piece, rows, :] = value.astype(bf16)
        return carry + value * value

    square = run_all(
        [signal_stage(time_ref, twist_ref, rows_here, write)], rows_here, None, jnp.zeros((CHUNK, LANES), f32)
    )
    returns = spread_copies(lag_ref, lag_hbm, me_ref[0], return_sems)
    start_all(returns)
    square_ref[...] = jnp.sum(square, axis=0, keepdims=True)
    wait_all(returns)


class Transforms:
    def __init__(self, pieces, rows_here, me):
        outer = pieces * rows_here // SPAN
        pairs = outer // 2
        self.me = me
        self.pieces = pieces
        coarse = twist_angles(outer, CHUNK * np.arange(CHUNKS)).T
        fine = twist_angles(outer, np.arange(CHUNK))[..., None] * np.ones(LANES)
        self.tables = [
            jnp.asarray(np.concatenate([np.cos(coarse), np.sin(coarse)], axis=1).astype(np.float32)),
            jnp.asarray(np.stack([np.cos(fine), np.sin(fine)]).astype(np.float32)),
            jnp.asarray(matrix_blocks()),
        ]
        self.split = jax.ShapeDtypeStruct((pairs, PASSES * BOTH, 2 * LANES), bf16)
        self.signal = jax.ShapeDtypeStruct((rows_here, LANES), bf16)
        self.result = jax.ShapeDtypeStruct((2, rows_here, LANES), bf16)
        self.square = jax.ShapeDtypeStruct((1, LANES), f32)
        self.work = pltpu.VMEM((pairs, BOTH, 2 * LANES), f32)
        self.split_work = pltpu.VMEM(self.split.shape, bf16)
        self.twist_work = pltpu.VMEM((2, outer, SPAN, LANES), f32)
        self.matrix_work = pltpu.VMEM(self.tables[2].shape, bf16)

    def products(self, signals):
        *results, lag_split = call(
            functools.partial(products_kernel, self.pieces), (self.result,) * self.pieces + (self.split,),
            [self.twist_work, self.matrix_work]
            + [pltpu.VMEM((self.pieces, kinds) + self.signal.shape, bf16) for kinds in (3, 2)]
            + [self.split_work] * 3
            + [self.work] * 4
            + [pltpu.SemaphoreType.DMA((count,)) for count in (self.pieces, self.pieces, 2)],
            self.me, *self.tables, *signals,
            in_specs=[IN_SMEM, IN_SMEM, IN_VMEM, ANYWHERE] + [ANYWHERE] * self.pieces,
            out_specs=(ANYWHERE,) * (self.pieces + 1),
        )
        return results, lag_split

    def lag(self, lag_split):
        *results, squares = call(
            functools.partial(lag_kernel, self.pieces), (self.signal,) * self.pieces + (self.square,),
            [pltpu.VMEM((self.pieces,) + self.signal.shape, bf16)]
            + [self.twist_work, self.matrix_work, self.split_work, self.work]
            + [pltpu.SemaphoreType.DMA((count,)) for count in (self.pieces, 2)],
            self.me, lag_split, *self.tables,
            in_specs=[IN_SMEM, ANYWHERE, IN_SMEM, IN_VMEM, ANYWHERE],
            out_specs=(ANYWHERE,) * self.pieces + (IN_VMEM,),
        )
        return results, squares


class PlainTransforms:
    def __init__(self, pieces, rows_here, me):
        self.seq_len = pieces * rows_here
        self.pieces = pieces
        self.outer = self.seq_len // SPAN
        idx = np.arange(SPAN)
        angle = (idx[:, None] * idx[None, :] % SPAN) * (2.0 * np.pi / SPAN)
        self.cosine = jnp.asarray(np.cos(angle), f32)
        self.sine = jnp.asarray(np.sin(angle), f32)
        twist = twist_angles(self.outer, idx)
        self.twist = jnp.asarray(np.stack([np.cos(twist), np.sin(twist)]), f32)[..., None]

    def dot(self, matrix, signal):
        return jnp.einsum("fs,tsc->tfc", matrix, signal, precision=lax.Precision.HIGHEST)

    def spectrum(self, signal):
        parts = signal.astype(f32).reshape(self.outer, SPAN, -1)
        leaves = to_leaves([parts[part] for part in range(self.outer)])
        re = jnp.stack([leaf[0] for leaf in leaves])
        im = jnp.stack([leaf[1] for leaf in leaves])
        twist_re = re * self.twist[0] + im * self.twist[1]
        twist_im = im * self.twist[0] - re * self.twist[1]
        return (
            self.dot(self.cosine, twist_re) + self.dot(self.sine, twist_im),
            self.dot(self.cosine, twist_im) - self.dot(self.sine, twist_re),
        )

    def back(self, re, im):
        time_re = self.dot(self.cosine, re) - self.dot(self.sine, im)
        time_im = self.dot(self.cosine, im) + self.dot(self.sine, re)
        leaf_re = time_re * self.twist[0] - time_im * self.twist[1]
        leaf_im = time_im * self.twist[0] + time_re * self.twist[1]
        parts = from_leaves([(leaf_re[leaf], leaf_im[leaf]) for leaf in range(self.outer)], 1.0 / self.seq_len)
        return jnp.stack(parts).reshape(self.pieces, self.seq_len // self.pieces, -1)

    def products(self, signals):
        product, cotan, taps = (self.spectrum(signals[0][:, kind]) for kind in range(3))
        conv = self.back(taps[0] * product[0] - taps[1] * product[1], taps[0] * product[1] + taps[1] * product[0])
        corr = self.back(taps[0] * cotan[0] + taps[1] * cotan[1], taps[0] * cotan[1] - taps[1] * cotan[0])
        lag = (
            product[0] * cotan[0] + product[1] * cotan[1],
            product[0] * cotan[1] - product[1] * cotan[0],
        )
        return [jnp.stack([conv, corr], axis=1).astype(bf16)], lag

    def lag(self, lag_spec):
        lag = self.back(*lag_spec)
        squares = jnp.sum(lag * lag, axis=(0, 1))
        return [lag.astype(bf16)], jnp.zeros((1, LANES), f32).at[0, : squares.shape[0]].set(squares)


def group(idx):
    return pl.ds(pl.multiple_of(idx * LANES, LANES), LANES)


def streamed(work, steps, per_step, cuts, counts, me_ref, *refs):
    refs = list(refs)

    def take(count):
        taken = refs[:count]
        del refs[:count]
        return taken

    ins, gathered, outs, spread, kept = (take(count) for count in counts)
    in_held = take(len(ins))
    gathered_held = take(min(len(gathered), 1))
    out_held = take(len(outs))
    spread_held = take(min(len(spread), 1))
    partner_sems, sems = refs[-2:]
    me = me_ref[0]
    moved = len(ins) + len(outs)

    def copy(place, step):
        outside = (ins + outs)[place].at[cuts[place](step)]
        inside = (in_held + out_held)[place].at[cuts[place](step)]
        ends = (outside, inside) if place < len(ins) else (inside, outside)
        return pltpu.make_async_copy(*ends, sems.at[place, step])

    def arrivals(step):
        return [copy(place, step) for place in range(len(ins)) if cuts[place](step) is not None]

    from_partners = collect_copies(gathered, gathered_held[0], me, partner_sems.at[0]) if gathered else []
    to_partners = spread_copies(spread_held[0], spread, me, partner_sems.at[1]) if spread else []
    start_all(from_partners)
    for step in range(steps):
        start_all(arrivals(step))
    wait_all(from_partners)
    for step in range(steps):
        wait_all(arrivals(step))

        def one(idx, carry):
            work(idx, in_held + gathered_held, out_held + spread_held + kept, refs[:-2])
            return carry

        lax.fori_loop(step * per_step, (step + 1) * per_step, one, 0)
        start_all([copy(place, step) for place in range(len(ins), moved)])
    start_all(to_partners)
    for step in range(steps):
        wait_all([copy(place, step) for place in range(len(ins), moved)])
    wait_all(to_partners)


def stream_call(
    work, steps, per_step, me, operands=(), gathered=(), results=(), spread=(), kept=(), held=None, scratch=()
):
    ins = [operand[0] for operand in operands]
    outs = [result[0] for result in results]
    cuts = [entry[1] for entry in list(operands) + list(results)]
    counts = [len(part) for part in (ins, gathered, outs, spread, kept)]

    def room(arrays):
        return [pltpu.VMEM(array.shape, array.dtype) for array in arrays]

    partner_room = [pltpu.VMEM(held, bf16)] if held else []
    most = max(len(gathered), len(spread), 1)
    return call(
        functools.partial(streamed, work, steps, per_step, cuts, counts),
        tuple(outs) + tuple(spread) + tuple(kept),
        room(ins)
        + (partner_room if gathered else [])
        + room(outs)
        + (partner_room if spread else [])
        + list(scratch)
        + [pltpu.SemaphoreType.DMA((2, most)), pltpu.SemaphoreType.DMA((max(len(cuts), 1), steps))],
        me, *ins, *gathered,
        in_specs=[IN_SMEM] + [ANYWHERE] * (len(ins) + len(gathered)),
        out_specs=(ANYWHERE,) * (len(outs) + len(spread)) + (IN_VMEM,) * len(kept),
    )


def cut_lanes(width, rank):
    def place(step):
        return (slice(None),) * (rank - 1) + (pl.ds(step * width, width),)

    return place


def cut_none(step):
    return None if step else (slice(None),)


def row_blocks(rows_here):
    return [slice(start, start + ROWS) for start in range(0, rows_here, ROWS)]


def extend_rows(lead, in_ref, lanes, ext_ref):
    ext_ref[PAD - lead.shape[0] : PAD, :] = lead
    ext_ref[PAD:, :] = in_ref[:, lanes].astype(f32)


def short_conv(ext_ref, taps, rows):
    result = None
    for shift_idx in range(taps.shape[0]):
        term = taps[shift_idx : shift_idx + 1] * ext_ref[PAD + rows.start - shift_idx : PAD + rows.stop - shift_idx, :]
        result = term if result is None else result + term
    return result


def extend_three(idx, operands, lead_ref, halo_rows, exts):
    lead = lead_ref[:, group(idx)]
    for place, ext in enumerate(exts):
        extend_rows(lead[place * halo_rows : (place + 1) * halo_rows], operands[place], group(idx), ext)


def signals_work(idx, operands, results, exts):
    q_ref, k_ref, v_ref, grad_ref, kernel_ref, lead_ref, taps_ref = operands
    taps = taps_ref[:, group(idx)]
    extend_three(idx, operands, lead_ref, taps.shape[0] - 1, exts)
    for rows in row_blocks(q_ref.shape[0]):
        q_short, k_short, v_short = (short_conv(ext, taps, rows) for ext in exts)
        results[0][idx, 0, rows, :] = (k_short * v_short).astype(bf16)
        results[0][idx, 1, rows, :] = (grad_ref[rows, group(idx)].astype(f32) * q_short).astype(bf16)
        results[0][idx, 2, rows, :] = kernel_ref[rows, group(idx)].astype(bf16)


def short_work(idx, operands, results, exts):
    q_ref, k_ref, v_ref, lead_ref, taps_ref = operands
    taps = taps_ref[:, group(idx)]
    extend_three(idx, operands, lead_ref, taps.shape[0] - 1, exts)
    for rows in row_blocks(q_ref.shape[0]):
        for place, ext in enumerate(exts):
            results[0][place, rows, group(idx)] = short_conv(ext, taps, rows)


def fold(value):
    return jnp.sum(value.reshape(-1, 8, LANES), axis=0)


def finish_work(idx, operands, results, exts):
    q_ref, k_ref, v_ref, grad_ref, short_ref, lead_ref, taps_ref, skip_ref, squares_ref, long_ref = operands
    mixed_ref, grad_q_ref, grad_k_ref, grad_v_ref, front_ref, back_ref, sums_ref = results
    lanes = group(idx)
    taps = taps_ref[:, lanes]
    skip = skip_ref[:, lanes]
    lead = lead_ref[:, lanes]
    taps_count = taps.shape[0]
    halo_rows = taps_count - 1
    rows_here = q_ref.shape[0]
    sums = [jnp.zeros((8, LANES), f32) for _ in range(taps_count + 1)]
    for ext in exts:
        ext[rows_here:, :] = jnp.zeros((PAD, LANES), f32)
    for rows in row_blocks(rows_here):
        q_short, k_short, v_short = (short_ref[place, rows, lanes] for place in range(3))
        product = (k_short * v_short).astype(bf16).astype(f32)
        filtered = long_ref[idx, 0, rows, :].astype(f32) + skip * product
        mixed_ref[rows, lanes] = (q_short * filtered).astype(bf16)
        upstream = grad_ref[rows, lanes].astype(f32)
        back_mix = upstream * q_short
        back_prod = long_ref[idx, 1, rows, :].astype(f32) + skip * back_mix
        sums[taps_count] = sums[taps_count] + fold(back_mix * product)
        exts[0][rows, :] = upstream * filtered
        exts[1][rows, :] = back_prod * v_short
        exts[2][rows, :] = back_prod * k_short
    for place, (ext, in_ref, out_ref) in enumerate(
        zip(exts, (q_ref, k_ref, v_ref), (grad_q_ref, grad_k_ref, grad_v_ref))
    ):
        for rows in row_blocks(rows_here):
            signal = in_ref[rows, lanes].astype(f32)
            grad = None
            for shift_idx in range(taps_count):
                ahead = ext[rows.start + shift_idx : rows.stop + shift_idx, :]
                term = taps[shift_idx : shift_idx + 1] * ahead
                grad = term if grad is None else grad + term
                sums[shift_idx] = sums[shift_idx] + fold(ahead * signal)
            out_ref[rows, lanes] = grad.astype(bf16)
        back_ref[place * halo_rows : (place + 1) * halo_rows, lanes] = grad[ROWS - halo_rows :]
        front_ref[place * halo_rows : (place + 1) * halo_rows, lanes] = ext[0:halo_rows, :]
    extra = slice(sums_ref.shape[1] - LANES, sums_ref.shape[1])
    sums_ref[:, extra] = jnp.zeros((taps_count + 1, LANES), f32)
    sums_ref[0:1, extra] = squares_ref[...]
    for shift_idx in range(taps_count + 1):
        total = jnp.sum(sums[shift_idx], axis=0, keepdims=True)
        for place in range(3 if shift_idx < taps_count else 0):
            for row in range(shift_idx):
                at = place * halo_rows + halo_rows - shift_idx + row
                total = total + lead[at : at + 1] * exts[place][row : row + 1, :]
        sums_ref[shift_idx : shift_idx + 1, lanes] = total


def lead_kernel(q_ref, k_ref, v_ref, lead_ref):
    halo_rows = lead_ref.shape[0] // 3
    for place, ref in enumerate((q_ref, k_ref, v_ref)):
        rows = ref[...].astype(f32)
        lead_ref[place * halo_rows : (place + 1) * halo_rows, :] = rows[rows.shape[0] - halo_rows :]


def edges_kernel(back_ref, tail_ref, taps_ref, q_ref, k_ref, v_ref, q_out, k_out, v_out, work_ref):
    taps_count = taps_ref.shape[0]
    halo_rows = taps_count - 1
    block_rows = q_ref.shape[0]
    for place, (ref, out_ref) in enumerate(((q_ref, q_out), (k_ref, k_out), (v_ref, v_out))):
        work_ref[...] = ref[...].astype(f32)
        first = place * halo_rows
        for row in range(halo_rows):
            total = back_ref[first + row : first + row + 1, :]
            for shift_idx in range(halo_rows - row, taps_count):
                source = first + row + shift_idx - halo_rows
                total = total + taps_ref[shift_idx : shift_idx + 1, :] * tail_ref[source : source + 1, :]
            at = block_rows - halo_rows + row
            work_ref[at : at + 1, :] = total
        out_ref[...] = work_ref[...].astype(bf16)


def norm_kernel(*refs):
    values, totals_ref, square_ref = refs[:-2], refs[-2], refs[-1]
    channels = totals_ref.shape[1] - LANES
    totals = values[0][...]
    if len(values) == 4:
        totals = (totals + values[1][...]) + (values[2][...] + values[3][...])
    totals_ref[...] = totals
    square = jnp.sum(totals[:, :channels] * totals[:, :channels]) + jnp.sum(totals[0:1, channels:])
    square_ref[...] = jnp.full(square_ref.shape, square)


def scale_kernel(limit, count, me_ref, totals_ref, norm_ref, *refs):
    lag_hbm = refs[:count]
    taps_out, skip_out, kernel_hbm, lag_ref, kernel_ref, arrival_sems, return_sems = refs[count:]
    taps_count, channels = taps_out.shape
    groups = lag_ref.shape[0]
    arrivals = collect_copies(lag_hbm, lag_ref, me_ref[0], arrival_sems)
    start_all(arrivals)
    factor = limit / jnp.maximum(jnp.sqrt(norm_ref[...]), limit)
    for idx in range(groups):
        lanes = slice(idx * LANES, (idx + 1) * LANES)
        taps_out[:, lanes] = totals_ref[0:taps_count, lanes] * factor
        skip_out[:, lanes] = totals_ref[taps_count : taps_count + 1, lanes] * factor
    wait_all(arrivals)
    per_step = max(groups // 4, 1)
    returns = []
    for step in range(groups // per_step):
        for idx in range(step * per_step, (step + 1) * per_step):
            kernel_ref[:, idx * LANES : (idx + 1) * LANES] = lag_ref[idx].astype(f32) * factor
        lanes = pl.ds(step * per_step * LANES, per_step * LANES)
        returns.append(pltpu.make_async_copy(kernel_ref.at[:, lanes], kernel_hbm.at[:, lanes], return_sems.at[step]))
        returns[step].start()
    wait_all(returns)


def exchange(pieces_first):
    return lax.all_to_all(pieces_first, "ctx", split_axis=0, concat_axis=0, tiled=True)


def to_pieces(groups, pieces):
    count, kinds, rows, lanes = groups.shape
    if count == pieces:
        return groups
    share = count * lanes // pieces
    split = groups.reshape(count, kinds, rows, lanes // share, share)
    return split.transpose(0, 3, 1, 2, 4).reshape(pieces, kinds, rows, share)


def to_groups(parts):
    pieces, kinds, rows, share = parts.shape
    if share == LANES:
        return parts
    joined = parts.reshape(pieces * share // LANES, LANES // share, kinds, rows, share)
    return joined.transpose(0, 2, 3, 1, 4).reshape(-1, kinds, rows, LANES)


def send(arrays, to_all, from_all):
    size = lax.axis_size("ctx")
    if len(arrays) == 1:
        return [from_all(exchange(to_all(arrays[0])))]
    received = {0: arrays[0]}
    for idx in reversed(range(1, size)):
        received[idx] = lax.ppermute(arrays[idx], "ctx", [(i, i ^ idx) for i in range(size)])
    return [received[idx] for idx in range(size)]


def partners(value, axis, steps):
    size = lax.axis_size(axis)
    return [value] + [lax.ppermute(value, axis, [(i, i ^ step) for i in range(size)]) for step in steps]


def rounds_of(size):
    rounds = []
    step = 1
    while step < size:
        rounds.append((step, 2 * step, 3 * step) if size // step >= 4 else (step,))
        step *= 4 if size // step >= 4 else 2
    return rounds


def add_up(values):
    if len(values) == 2:
        return values[0] + values[1]
    return (values[0] + values[1]) + (values[2] + values[3])


def body(q_in, k_in, v_in, grad_out, short_filter, kernel, skip):
    pieces = lax.axis_size("ctx")
    sides = lax.axis_size("ch")
    rows_here, channels = q_in.shape
    seq_len = pieces * rows_here
    taps_count = short_filter.shape[0]
    halo_rows = taps_count - 1
    groups = channels // LANES
    share = channels // pieces
    per_step = min(groups, 4)
    steps = groups // per_step
    lanes2 = cut_lanes(per_step * LANES, 2)
    lanes3 = cut_lanes(per_step * LANES, 3)
    me = lax.axis_index("ctx").reshape(1)
    direct = share == LANES
    transforms = (Transforms if direct else PlainTransforms)(pieces, rows_here, me)
    stream = functools.partial(stream_call, steps=steps, per_step=per_step, me=me)

    flat = jax.ShapeDtypeStruct((rows_here, channels), bf16)
    halo = jax.ShapeDtypeStruct((3 * halo_rows, channels), f32)
    sent_dims = (groups, 3, rows_here, LANES)
    sent = jax.ShapeDtypeStruct(sent_dims[1:] if direct else sent_dims, bf16)
    exts = [pltpu.VMEM((rows_here + PAD, LANES), f32)] * 3
    last_block = 16
    last_spec = pl.BlockSpec((last_block, channels), lambda i: (rows_here // last_block - 1, 0))

    def whole(array):
        return pl.BlockSpec(array.shape, lambda i: (0,) * len(array.shape))

    lead = call(
        lead_kernel, halo, [], q_in, k_in, v_in,
        grid=(1,), in_specs=[last_spec] * 3, out_specs=whole(halo),
    )
    lead = lax.ppermute(lead, "ctx", [(i, i + 1) for i in range(pieces - 1)])

    signals = stream(
        signals_work,
        operands=[(x, lanes2) for x in (q_in, k_in, v_in, grad_out, kernel, lead, short_filter)],
        spread=(sent,) * (pieces if direct else 1),
        held=sent_dims,
        scratch=exts,
    )
    signals_here = send(signals, lambda x: to_pieces(x, pieces), lambda x: x)
    (short,) = stream(
        short_work,
        operands=[(x, lanes2) for x in (q_in, k_in, v_in, lead, short_filter)],
        results=[(jax.ShapeDtypeStruct((3, rows_here, channels), f32), lanes3)],
        scratch=exts,
    )
    long_here, lag_spec = transforms.products(signals_here)
    long = send(long_here, lambda x: x, to_groups)
    lag_here, lag_squares = transforms.lag(lag_spec)
    lag = send(lag_here, lambda x: x[:, None], lambda x: to_groups(x)[:, 0])

    mixed, grad_q, grad_k, grad_v, front, back, sums = stream(
        finish_work,
        operands=[(x, lanes2) for x in (q_in, k_in, v_in, grad_out)]
        + [(short, lanes3)]
        + [(x, lanes2) for x in (lead, short_filter, skip.reshape(1, channels))]
        + [(lag_squares, cut_none)],
        gathered=long,
        held=(groups, 2, rows_here, LANES),
        results=[(flat, lanes2)] * 4,
        scratch=exts,
        kept=[halo, halo, jax.ShapeDtypeStruct((taps_count + 1, channels + LANES), f32)],
    )

    totals = sums
    rounds = rounds_of(pieces)
    for steps_of in rounds[:-1]:
        totals = add_up(partners(totals, "ctx", steps_of))
    last = partners(totals, "ctx", rounds[-1])
    if len(last) == 2:
        last = [last[0] + last[1]]

    tail = lax.ppermute(front, "ctx", [(i, i - 1) for i in range(1, pieces)])
    grad_q, grad_k, grad_v = call(
        edges_kernel, (flat, flat, flat), [pltpu.VMEM((last_block, channels), f32)],
        back, tail, short_filter, grad_q, grad_k, grad_v,
        vmem_bytes=SMALL_VMEM_BYTES,
        grid=(1,),
        in_specs=[whole(back), whole(tail), whole(short_filter)] + [last_spec] * 3,
        out_specs=(last_spec,) * 3,
        input_output_aliases={3: 0, 4: 1, 5: 2},
    )
    grad_q, grad_k, grad_v, *last = lax.optimization_barrier((grad_q, grad_k, grad_v, *last))

    totals, norm_sq = call(
        norm_kernel,
        (jax.ShapeDtypeStruct(totals.shape, f32), jax.ShapeDtypeStruct((1, LANES), f32)),
        [], *last,
        vmem_bytes=SMALL_VMEM_BYTES,
        in_specs=[IN_VMEM] * len(last), out_specs=(IN_VMEM, IN_VMEM),
    )
    for steps_of in rounds_of(sides):
        norm_sq = add_up(partners(norm_sq, "ch", steps_of))

    limit = math.sqrt(float(seq_len * channels * sides))
    grad_short, grad_skip, grad_kernel = call(
        functools.partial(scale_kernel, limit, len(lag)),
        (
            jax.ShapeDtypeStruct((taps_count, channels), f32),
            jax.ShapeDtypeStruct((1, channels), f32),
            jax.ShapeDtypeStruct((rows_here, channels), f32),
        ),
        [
            pltpu.VMEM((groups, rows_here, LANES), bf16), pltpu.VMEM((rows_here, channels), f32),
            pltpu.SemaphoreType.DMA((len(lag),)), pltpu.SemaphoreType.DMA((4,)),
        ],
        me, totals, norm_sq, *lag,
        vmem_bytes=SMALL_VMEM_BYTES,
        in_specs=[IN_SMEM, IN_VMEM, IN_VMEM] + [ANYWHERE] * len(lag),
        out_specs=(IN_VMEM, IN_VMEM, ANYWHERE),
    )
    return mixed, grad_q, grad_k, grad_v, grad_short, grad_skip.reshape(channels), grad_kernel


def solution(mesh):
    in_specs = (
        P("ctx", "ch"),
        P("ctx", "ch"),
        P("ctx", "ch"),
        P("ctx", "ch"),
        P(None, "ch"),
        P("ctx", "ch"),
        P("ch"),
    )
    out_specs = (
        P("ctx", "ch"),
        P("ctx", "ch"),
        P("ctx", "ch"),
        P("ctx", "ch"),
        P(None, "ch"),
        P("ch"),
        P("ctx", "ch"),
    )
    return jax.shard_map(body, mesh=mesh, in_specs=in_specs, out_specs=out_specs, check_vma=False)
```

```python
import functools
import math

import jax
import jax.numpy as jnp
import ml_dtypes
import numpy as np
from jax import lax
from jax.experimental import pallas as pl
from jax.experimental.pallas import tpu as pltpu
from jax.sharding import PartitionSpec as P

LANES = 128
SPAN = 256
BOTH = 2 * SPAN
CHUNK = 16
CHUNKS = SPAN // CHUNK
PAD = 8
ROWS = 32
PASSES = 1
TILE_ROWS = 16
VMEM_BYTES = 60 * 1024 * 1024
SMALL_VMEM_BYTES = 8 * 1024 * 1024

f32 = jnp.float32
bf16 = jnp.bfloat16

IN_VMEM = pl.BlockSpec(memory_space=pltpu.VMEM)
IN_SMEM = pl.BlockSpec(memory_space=pltpu.SMEM)
ANYWHERE = pl.BlockSpec(memory_space=pl.ANY)


def call(kernel, outs, scratch, *args, vmem_bytes=VMEM_BYTES, **options):
    return pl.pallas_call(
        kernel,
        out_shape=outs,
        scratch_shapes=scratch,
        compiler_params=pltpu.CompilerParams(vmem_limit_bytes=vmem_bytes),
        **options,
    )(*args)


def leaf_phases(count):
    return [(4 * leaf + 1) / (4 * count) for leaf in range(count)]


def root_times(re, im, num, den, sign):
    if num == 0:
        return re, im
    if 4 * num == den:
        return (im, -re) if sign < 0 else (-im, re)
    cosine = math.cos(2.0 * math.pi * num / den)
    sine = sign * math.sin(2.0 * math.pi * num / den)
    if 8 * num == den:
        return ((re + im) * cosine, (im - re) * cosine) if sign < 0 else ((re - im) * cosine, (re + im) * cosine)
    if 8 * num == 3 * den:
        return ((re - im) * cosine, (re + im) * cosine) if sign < 0 else ((re + im) * cosine, (im - re) * cosine)
    return re * cosine - im * sine, im * cosine + re * sine


def short_fft(values, sign):
    count = len(values)
    if count == 1:
        return values
    even = short_fft(values[0::2], sign)
    odd = short_fft(values[1::2], sign)
    first = []
    second = []
    for num in range(count // 2):
        re, im = root_times(*odd[num], num, count, sign)
        first.append((even[num][0] + re, even[num][1] + im))
        second.append((even[num][0] - re, even[num][1] - im))
    return first + second


def to_leaves(parts):
    count = len(parts)
    turned = []
    for idx, part in enumerate(parts):
        angle = 2.0 * math.pi * idx / (4 * count)
        turned.append((part * math.cos(angle), part * (-math.sin(angle))) if idx else (part, jnp.zeros_like(part)))
    return short_fft(turned, -1)


def from_leaves(leaves, scale):
    count = len(leaves)
    parts = []
    for idx, (re, im) in enumerate(short_fft(leaves, 1)):
        angle = 2.0 * math.pi * idx / (4 * count)
        if idx == 0:
            parts.append(re * scale)
        else:
            parts.append(re * (math.cos(angle) * scale) - im * (math.sin(angle) * scale))
    return parts


def dft_matrix():
    idx = np.arange(SPAN)
    angle = (idx[:, None] * idx[None, :] % SPAN) * (2.0 * np.pi / SPAN)
    cosine, sine = np.cos(angle), np.sin(angle)
    return np.block([[cosine, sine], [-sine, cosine]])


def twist_angles(outer, inner):
    return np.asarray(leaf_phases(outer))[:, None] * np.asarray(inner)[None, :] * (2.0 * np.pi / SPAN)


def matrix_blocks():
    matrix = dft_matrix()
    high = matrix.astype(ml_dtypes.bfloat16)
    low = (matrix - high.astype(np.float64)).astype(ml_dtypes.bfloat16)
    return np.concatenate([high, low, high][:PASSES], axis=1)


def leaf_place(leaf):
    return leaf // 2, slice((leaf % 2) * LANES, (leaf % 2 + 1) * LANES)


def split_store(ref, leaf, below, here, value):
    pair, lanes = leaf_place(leaf)
    high = value.astype(bf16)
    for block in range(PASSES):
        part = high
        if PASSES == 3 and block == 2:
            part = (value - high.astype(f32)).astype(bf16)
        ref[pair, shifted_rows(here, block * BOTH + below), lanes] = part


def run_all(stages, rows_here, matmul=None, carry=0):
    tiles = matmul[2].shape[0] if matmul else 4
    ratio = SPAN // rows_here
    in_part = tiles // ratio
    per_tile = CHUNKS // tiles
    for part in range(ratio):

        def step(tile, carry, part=part):
            if matmul:
                matrix_ref, split_ref, result_ref = matmul
                place = part * in_part + tile
                result_ref[place] = jnp.dot(matrix_ref[...], split_ref[place], preferred_element_type=f32)
            for chunk in range(per_tile):
                for stage in stages:
                    carry = stage(part, chunk_row(tile * per_tile + chunk), carry)
            return carry

        carry = lax.fori_loop(0, in_part, step, carry)
    return carry


def chunk_row(idx):
    return pl.multiple_of(idx * CHUNK, CHUNK)


def in_span(part, row, rows_here):
    return pl.ds(pl.multiple_of(part * rows_here + row, CHUNK), CHUNK)


def twist_stage(coarse_ref, fine_ref, twist_ref, rows_here):
    outer = twist_ref.shape[1]

    def stage(part, row, carry):
        here = in_span(part, row, rows_here)
        idx = part * (rows_here // CHUNK) + row // CHUNK
        for leaf in range(outer):
            far_cosine = coarse_ref[idx, leaf]
            far_sine = coarse_ref[idx, outer + leaf]
            cosine = fine_ref[0, leaf]
            sine = fine_ref[1, leaf]
            twist_ref[0, leaf, here, :] = far_cosine * cosine - far_sine * sine
            twist_ref[1, leaf, here, :] = far_sine * cosine + far_cosine * sine
        return carry

    return stage


def leaves_stage(signals_ref, first_row, rows_here, twist_ref, split_ref):
    outer = twist_ref.shape[1]
    ratio = SPAN // rows_here

    def stage(part, row, carry):
        here = in_span(part, row, rows_here)
        rows = pl.ds(pl.multiple_of(first_row + row, CHUNK), CHUNK)
        parts = [signals_ref[place * ratio + part, rows, :].astype(f32) for place in range(outer)]
        for leaf, (re, im) in enumerate(to_leaves(parts)):
            cosine = twist_ref[0, leaf, here, :]
            sine = twist_ref[1, leaf, here, :]
            split_store(split_ref, leaf, 0, here, re * cosine + im * sine)
            split_store(split_ref, leaf, SPAN, here, im * cosine - re * sine)
        return carry

    return stage


def shifted_rows(here, by):
    return pl.ds(here.start + by, here.size)


def combine_stage(left_ref, right_ref, split_ref, rows_here, conjugate):
    def stage(part, row, carry):
        here = in_span(part, row, rows_here)
        below = shifted_rows(here, SPAN)
        for leaf in range(2 * left_ref.shape[0]):
            pair, lanes = leaf_place(leaf)
            left_re = left_ref[pair, here, lanes]
            left_im = left_ref[pair, below, lanes]
            right_re = right_ref[pair, here, lanes]
            right_im = right_ref[pair, below, lanes]
            if conjugate:
                re = left_re * right_re + left_im * right_im
                minus_im = left_im * right_re - left_re * right_im
            else:
                re = left_re * right_re - left_im * right_im
                minus_im = -(left_re * right_im + left_im * right_re)
            split_store(split_ref, leaf, 0, here, re)
            split_store(split_ref, leaf, SPAN, here, minus_im)
        return carry

    return stage


def signal_stage(time_ref, twist_ref, rows_here, write):
    outer = twist_ref.shape[1]
    ratio = SPAN // rows_here
    scale = 1.0 / (SPAN * outer)

    def stage(part, row, carry):
        here = in_span(part, row, rows_here)
        below = shifted_rows(here, SPAN)
        leaves = []
        for leaf in range(outer):
            pair, lanes = leaf_place(leaf)
            cosine = twist_ref[0, leaf, here, :]
            sine = twist_ref[1, leaf, here, :]
            re = time_ref[pair, here, lanes]
            minus_im = time_ref[pair, below, lanes]
            leaves.append((re * cosine + minus_im * sine, re * sine - minus_im * cosine))
        for place, value in enumerate(from_leaves(leaves, scale)):
            carry = write(place * ratio + part, pl.ds(row, CHUNK), value, carry)
        return carry

    return stage


def first_rows(lead, first, taps):
    count = len(lead)
    rows = lead + first
    return [
        functools.reduce(lambda x, y: x + y, [taps[shift] * rows[count + row - shift] for shift in range(count + 1)])
        for row in range(count)
    ]


def first_signals(ahead, own, taps):
    count = len(taps) - 1

    def kind(rows, idx):
        return rows[idx * count : (idx + 1) * count]

    q_short, k_short, v_short = (first_rows(kind(ahead, idx), kind(own, 3 + idx), taps) for idx in range(3))
    product = [k_row * v_row for k_row, v_row in zip(k_short, v_short)]
    cotan = [grad_row * q_row for grad_row, q_row in zip(kind(own, 6), q_short)]
    return product, cotan


def patch_first_rows(signals_ref, taps_ref, rows_here):
    pieces, all_rows = signals_ref.shape[:2]
    taps = [taps_ref[shift : shift + 1, :] for shift in range(taps_ref.shape[0])]
    used = 7 * (len(taps) - 1)

    def extra(piece):
        rows = signals_ref[piece, 3 * rows_here : all_rows, :].astype(f32)
        return [rows[idx : idx + 1] for idx in range(used)]

    row_idx = lax.broadcasted_iota(jnp.int32, (TILE_ROWS, LANES), 0)
    ahead = extra(0)
    for piece in range(1, pieces):
        own = extra(piece)
        for kind, rows in enumerate(first_signals(ahead, own, taps)):
            place = slice(kind * rows_here, kind * rows_here + TILE_ROWS)
            tile = signals_ref[piece, place, :].astype(f32)
            for row, value in enumerate(rows):
                tile = jnp.where(row_idx == row, value, tile)
            signals_ref[piece, place, :] = tile.astype(bf16)
        ahead = own


def products_kernel(
    rows_here, signals_hbm, taps_ref, coarse_ref, fine_ref, matrix_hbm, results_hbm, lag_hbm,
    twist_ref, matrix_ref, signals_ref, results_ref, one_split, two_split, lag_split,
    filter_ref, product_ref, cotan_ref, time_ref, sems,
):
    filter_rows = pl.ds(2 * rows_here, rows_here)
    extra_rows = pl.ds(3 * rows_here, signals_ref.shape[1] - 3 * rows_here)
    signal_rows = pl.ds(0, 2 * rows_here)
    arrivals = [
        pltpu.make_async_copy(signals_hbm.at[:, rows], signals_ref.at[:, rows], sems.at[idx])
        for idx, rows in enumerate((filter_rows, extra_rows, signal_rows))
    ]
    matrix_copy = pltpu.make_async_copy(matrix_hbm, matrix_ref, sems.at[3])
    lag_copy = pltpu.make_async_copy(lag_split, lag_hbm, sems.at[4])
    returns = [
        pltpu.make_async_copy(results_ref.at[:, kind], results_hbm.at[:, kind], sems.at[5 + kind]) for kind in range(2)
    ]

    def leaves(kind, split_ref):
        return leaves_stage(signals_ref, kind * rows_here, rows_here, twist_ref, split_ref)

    def combine(left_ref, right_ref, split_ref, conjugate):
        return combine_stage(left_ref, right_ref, split_ref, rows_here, conjugate)

    def result(kind, from_ref):
        def write(piece, rows, value, carry):
            results_ref[piece, kind, rows, :] = value.astype(bf16)
            return carry

        return signal_stage(from_ref, twist_ref, rows_here, write)

    for copy in arrivals + [matrix_copy]:
        copy.start()
    run_all([twist_stage(coarse_ref, fine_ref, twist_ref, rows_here)], rows_here)
    arrivals[0].wait()
    run_all([leaves(2, one_split)], rows_here)
    arrivals[1].wait()
    arrivals[2].wait()
    patch_first_rows(signals_ref, taps_ref, rows_here)
    matrix_copy.wait()
    run_all([leaves(0, two_split)], rows_here, (matrix_ref, one_split, filter_ref))
    run_all([leaves(1, one_split)], rows_here, (matrix_ref, two_split, product_ref))
    run_all([combine(filter_ref, product_ref, two_split, False)], rows_here, (matrix_ref, one_split, cotan_ref))
    run_all([combine(filter_ref, cotan_ref, one_split, True)], rows_here, (matrix_ref, two_split, time_ref))
    run_all(
        [combine(product_ref, cotan_ref, lag_split, True), result(0, time_ref)],
        rows_here, (matrix_ref, one_split, filter_ref),
    )
    lag_copy.start()
    returns[0].start()
    run_all([result(1, filter_ref)], rows_here)
    returns[1].start()
    lag_copy.wait()
    returns[0].wait()
    returns[1].wait()


def lag_kernel(
    split_hbm, coarse_ref, fine_ref, matrix_hbm, lag_ref, square_ref, twist_ref, matrix_ref, split_ref, time_ref, sems
):
    rows_here = lag_ref.shape[1]
    copies = [
        pltpu.make_async_copy(matrix_hbm, matrix_ref, sems.at[0]),
        pltpu.make_async_copy(split_hbm, split_ref, sems.at[1]),
    ]
    for copy in copies:
        copy.start()
    run_all([twist_stage(coarse_ref, fine_ref, twist_ref, rows_here)], rows_here)
    for copy in copies:
        copy.wait()
    run_all([], rows_here, (matrix_ref, split_ref, time_ref))

    def write(piece, rows, value, carry):
        lag_ref[piece, rows, :] = value.astype(bf16)
        return carry + value * value

    square = run_all(
        [signal_stage(time_ref, twist_ref, rows_here, write)], rows_here, None, jnp.zeros((CHUNK, LANES), f32)
    )
    square_ref[...] = jnp.sum(square, axis=0, keepdims=True)


class Transforms:
    def __init__(self, pieces, rows_here):
        outer = pieces * rows_here // SPAN
        pairs = outer // 2
        coarse = twist_angles(outer, CHUNK * np.arange(CHUNKS)).T
        fine = twist_angles(outer, np.arange(CHUNK))[..., None] * np.ones(LANES)
        self.tables = [
            jnp.asarray(np.concatenate([np.cos(coarse), np.sin(coarse)], axis=1).astype(np.float32)),
            jnp.asarray(np.stack([np.cos(fine), np.sin(fine)]).astype(np.float32)),
            jnp.asarray(matrix_blocks()),
        ]
        self.split = jax.ShapeDtypeStruct((pairs, PASSES * BOTH, 2 * LANES), bf16)
        self.signal = jax.ShapeDtypeStruct((pieces, rows_here, LANES), bf16)
        self.result = jax.ShapeDtypeStruct((pieces, 2, rows_here, LANES), bf16)
        self.square = jax.ShapeDtypeStruct((1, LANES), f32)
        self.result_work = pltpu.VMEM(self.result.shape, bf16)
        self.work = pltpu.VMEM((pairs, BOTH, 2 * LANES), f32)
        self.split_work = pltpu.VMEM(self.split.shape, bf16)
        self.twist_work = pltpu.VMEM((2, outer, SPAN, LANES), f32)
        self.matrix_work = pltpu.VMEM(self.tables[2].shape, bf16)

    def products(self, signals, taps):
        return call(
            functools.partial(products_kernel, self.signal.shape[1]), (self.result, self.split),
            [self.twist_work, self.matrix_work, pltpu.VMEM(signals.shape, bf16), self.result_work]
            + [self.split_work] * 3
            + [self.work] * 4
            + [pltpu.SemaphoreType.DMA((7,))],
            signals, taps, *self.tables,
            in_specs=[ANYWHERE, IN_VMEM, IN_SMEM, IN_VMEM, ANYWHERE],
            out_specs=(ANYWHERE, ANYWHERE),
        )

    def lag(self, lag_split):
        return call(
            lag_kernel, (self.signal, self.square),
            [self.twist_work, self.matrix_work, self.split_work, self.work, pltpu.SemaphoreType.DMA((2,))],
            lag_split, *self.tables,
            in_specs=[ANYWHERE, IN_SMEM, IN_VMEM, ANYWHERE],
            out_specs=(IN_VMEM, IN_VMEM),
        )


class PlainTransforms:
    def __init__(self, pieces, rows_here):
        self.seq_len = pieces * rows_here
        self.pieces = pieces
        self.outer = self.seq_len // SPAN
        idx = np.arange(SPAN)
        angle = (idx[:, None] * idx[None, :] % SPAN) * (2.0 * np.pi / SPAN)
        self.cosine = jnp.asarray(np.cos(angle), f32)
        self.sine = jnp.asarray(np.sin(angle), f32)
        twist = twist_angles(self.outer, idx)
        self.twist = jnp.asarray(np.stack([np.cos(twist), np.sin(twist)]), f32)[..., None]

    def dot(self, matrix, signal):
        return jnp.einsum("fs,tsc->tfc", matrix, signal, precision=lax.Precision.HIGHEST)

    def spectrum(self, signal):
        parts = signal.astype(f32).reshape(self.outer, SPAN, -1)
        leaves = to_leaves([parts[part] for part in range(self.outer)])
        re = jnp.stack([leaf[0] for leaf in leaves])
        im = jnp.stack([leaf[1] for leaf in leaves])
        twist_re = re * self.twist[0] + im * self.twist[1]
        twist_im = im * self.twist[0] - re * self.twist[1]
        return (
            self.dot(self.cosine, twist_re) + self.dot(self.sine, twist_im),
            self.dot(self.cosine, twist_im) - self.dot(self.sine, twist_re),
        )

    def back(self, re, im):
        time_re = self.dot(self.cosine, re) - self.dot(self.sine, im)
        time_im = self.dot(self.cosine, im) + self.dot(self.sine, re)
        leaf_re = time_re * self.twist[0] - time_im * self.twist[1]
        leaf_im = time_im * self.twist[0] + time_re * self.twist[1]
        parts = from_leaves([(leaf_re[leaf], leaf_im[leaf]) for leaf in range(self.outer)], 1.0 / self.seq_len)
        return jnp.stack(parts).reshape(self.pieces, self.seq_len // self.pieces, -1)

    def products(self, signals, short_taps):
        rows_here = self.seq_len // self.pieces
        parts = [signals[:, kind * rows_here : (kind + 1) * rows_here] for kind in range(3)]
        extra = signals[:, 3 * rows_here :].astype(f32)
        rows = [extra[:, idx : idx + 1] for idx in range(extra.shape[1])]
        ahead = [jnp.concatenate([jnp.zeros_like(row[:1]), row[:-1]], axis=0) for row in rows]
        short_rows = [short_taps[shift][None, None, :] for shift in range(short_taps.shape[0])]
        for kind, first in enumerate(first_signals(ahead, rows, short_rows)):
            first = jnp.concatenate(first, axis=1)
            parts[kind] = jnp.concatenate([first.astype(bf16), parts[kind][:, first.shape[1] :]], axis=1)
        product, cotan, taps = (self.spectrum(part) for part in parts)
        conv = self.back(taps[0] * product[0] - taps[1] * product[1], taps[0] * product[1] + taps[1] * product[0])
        corr = self.back(taps[0] * cotan[0] + taps[1] * cotan[1], taps[0] * cotan[1] - taps[1] * cotan[0])
        lag = (
            product[0] * cotan[0] + product[1] * cotan[1],
            product[0] * cotan[1] - product[1] * cotan[0],
        )
        return jnp.stack([conv, corr], axis=1).astype(bf16), lag

    def lag(self, lag_spec):
        lag = self.back(*lag_spec)
        squares = jnp.sum(lag * lag, axis=(0, 1))
        return lag.astype(bf16), jnp.zeros((1, LANES), f32).at[0, : squares.shape[0]].set(squares)


def group(idx):
    return pl.ds(pl.multiple_of(idx * LANES, LANES), LANES)


def streamed(work, steps, per_step, places, in_count, out_count, kept, *refs):
    moved = in_count + out_count
    hbm = refs[:moved]
    kept_refs = refs[moved : moved + kept]
    held = refs[moved + kept : 2 * moved + kept]
    scratch = refs[2 * moved + kept : -1]
    sems = refs[-1]

    def copy(place, step):
        outside = hbm[place].at[places[place][0](step)]
        inside = held[place].at[places[place][1](step)]
        ends = (outside, inside) if place < in_count else (inside, outside)
        return pltpu.make_async_copy(*ends, sems.at[place, step])

    def arrivals(step):
        return [copy(place, step) for place in range(in_count) if places[place][0](step) is not None]

    for step in range(steps):
        for arrival in arrivals(step):
            arrival.start()
    for step in range(steps):
        for arrival in arrivals(step):
            arrival.wait()

        def one(idx, carry):
            work(idx, held[:in_count], held[in_count:] + kept_refs, scratch)
            return carry

        lax.fori_loop(step * per_step, (step + 1) * per_step, one, 0)
        for place in range(in_count, moved):
            copy(place, step).start()
    for step in range(steps):
        for place in range(in_count, moved):
            copy(place, step).wait()


def stream_call(work, steps, per_step, operands, results, scratch=(), aliases=(), kept=()):
    arrays = [operand[0] for operand in operands]
    shapes = [jax.ShapeDtypeStruct(array.shape, array.dtype) for array in arrays] + [result[0] for result in results]
    cuts = [entry[1] for entry in operands] + [entry[1] for entry in results]
    held = [pltpu.VMEM(entry[2] or shape.shape, shape.dtype) for entry, shape in zip(operands + results, shapes)]
    extra = list(aliases)
    kernel = functools.partial(streamed, work, steps, per_step, cuts, len(arrays), len(results), len(kept))

    def with_aliases(*refs):
        kernel(*refs[: len(arrays)], *refs[len(arrays) + len(extra) :])

    return call(
        with_aliases,
        tuple(result[0] for result in results) + tuple(kept),
        held + list(scratch) + [pltpu.SemaphoreType.DMA((len(shapes), steps))],
        *arrays, *extra,
        in_specs=[ANYWHERE] * (len(arrays) + len(extra)),
        out_specs=(ANYWHERE,) * len(results) + (IN_VMEM,) * len(kept),
        input_output_aliases={len(arrays) + idx: idx for idx in range(len(extra))},
    )


def cut_lanes(width, rank):
    def place(step):
        return (slice(None),) * (rank - 1) + (pl.ds(step * width, width),)

    return place, place


def cut_groups(per_step):
    def place(step):
        return (pl.ds(step * per_step, per_step),)

    return place, place


def cut_none(step):
    return None if step else (slice(None),)


def row_blocks(rows_here):
    return [slice(start, start + ROWS) for start in range(0, rows_here, ROWS)]


def extend_rows(lead, in_ref, lanes, ext_ref):
    ext_ref[PAD - lead.shape[0] : PAD, :] = lead
    ext_ref[PAD:, :] = in_ref[:, lanes].astype(f32)


def short_conv(ext_ref, taps, rows):
    result = None
    for shift_idx in range(taps.shape[0]):
        term = taps[shift_idx : shift_idx + 1] * ext_ref[PAD + rows.start - shift_idx : PAD + rows.stop - shift_idx, :]
        result = term if result is None else result + term
    return result


def extend_three(idx, operands, lead_ref, halo_rows, exts):
    lead = lead_ref[:, group(idx)]
    for place, ext in enumerate(exts):
        extend_rows(lead[place * halo_rows : (place + 1) * halo_rows], operands[place], group(idx), ext)


def signals_work(idx, operands, results, exts):
    q_ref, k_ref, v_ref, grad_ref, kernel_ref, taps_ref = operands
    lanes = group(idx)
    taps = taps_ref[:, lanes]
    halo_rows = taps.shape[0] - 1
    rows_here = q_ref.shape[0]
    for ext, in_ref in zip(exts, operands):
        extend_rows(jnp.zeros((halo_rows, LANES), f32), in_ref, lanes, ext)
    for rows in row_blocks(rows_here):
        q_short, k_short, v_short = (short_conv(ext, taps, rows) for ext in exts)
        below = [slice(kind * rows_here + rows.start, kind * rows_here + rows.stop) for kind in range(3)]
        results[0][idx, below[0], :] = (k_short * v_short).astype(bf16)
        results[0][idx, below[1], :] = (grad_ref[rows, lanes].astype(f32) * q_short).astype(bf16)
        results[0][idx, below[2], :] = kernel_ref[rows, lanes].astype(bf16)
    top = grad_ref[0:TILE_ROWS, lanes].astype(f32)[:halo_rows]
    extra = [ext[ext.shape[0] - halo_rows :, :] for ext in exts] + [ext[PAD : PAD + halo_rows, :] for ext in exts]
    extra_count = results[0].shape[1] - 3 * rows_here
    blank = jnp.zeros((extra_count - 7 * halo_rows, LANES), f32)
    results[0][idx, 3 * rows_here :, :] = jnp.concatenate(extra + [top, blank], axis=0).astype(bf16)


def short_work(idx, operands, results, exts):
    q_ref, k_ref, v_ref, lead_ref, taps_ref = operands
    taps = taps_ref[:, group(idx)]
    extend_three(idx, operands, lead_ref, taps.shape[0] - 1, exts)
    for rows in row_blocks(q_ref.shape[0]):
        for place, ext in enumerate(exts):
            results[0][place, rows, group(idx)] = short_conv(ext, taps, rows)


def fold(value):
    return jnp.sum(value.reshape(-1, 8, LANES), axis=0)


def finish_work(idx, operands, results, exts):
    q_ref, k_ref, v_ref, grad_ref, short_ref, lead_ref, taps_ref, skip_ref, long_ref, squares_ref = operands
    mixed_ref, grad_q_ref, grad_k_ref, grad_v_ref, front_ref, back_ref, sums_ref = results
    lanes = group(idx)
    taps = taps_ref[:, lanes]
    skip = skip_ref[:, lanes]
    lead = lead_ref[:, lanes]
    taps_count = taps.shape[0]
    halo_rows = taps_count - 1
    rows_here = q_ref.shape[0]
    sums = [jnp.zeros((8, LANES), f32) for _ in range(taps_count + 1)]
    for ext in exts:
        ext[rows_here:, :] = jnp.zeros((PAD, LANES), f32)
    for rows in row_blocks(rows_here):
        q_short, k_short, v_short = (short_ref[place, rows, lanes] for place in range(3))
        product = (k_short * v_short).astype(bf16).astype(f32)
        filtered = long_ref[idx, 0, rows, :].astype(f32) + skip * product
        mixed_ref[rows, lanes] = (q_short * filtered).astype(bf16)
        upstream = grad_ref[rows, lanes].astype(f32)
        back_mix = upstream * q_short
        back_prod = long_ref[idx, 1, rows, :].astype(f32) + skip * back_mix
        sums[taps_count] = sums[taps_count] + fold(back_mix * product)
        exts[0][rows, :] = upstream * filtered
        exts[1][rows, :] = back_prod * v_short
        exts[2][rows, :] = back_prod * k_short
    for place, (ext, in_ref, out_ref) in enumerate(
        zip(exts, (q_ref, k_ref, v_ref), (grad_q_ref, grad_k_ref, grad_v_ref))
    ):
        for rows in row_blocks(rows_here):
            signal = in_ref[rows, lanes].astype(f32)
            grad = None
            for shift_idx in range(taps_count):
                ahead = ext[rows.start + shift_idx : rows.stop + shift_idx, :]
                term = taps[shift_idx : shift_idx + 1] * ahead
                grad = term if grad is None else grad + term
                sums[shift_idx] = sums[shift_idx] + fold(ahead * signal)
            out_ref[rows, lanes] = grad.astype(bf16)
        back_ref[place * halo_rows : (place + 1) * halo_rows, lanes] = grad[ROWS - halo_rows :]
        front_ref[place * halo_rows : (place + 1) * halo_rows, lanes] = ext[0:halo_rows, :]
    extra = slice(sums_ref.shape[1] - LANES, sums_ref.shape[1])
    sums_ref[:, extra] = jnp.zeros((taps_count + 1, LANES), f32)
    sums_ref[0:1, extra] = squares_ref[...]
    for shift_idx in range(taps_count + 1):
        total = jnp.sum(sums[shift_idx], axis=0, keepdims=True)
        for place in range(3 if shift_idx < taps_count else 0):
            for row in range(shift_idx):
                at = place * halo_rows + halo_rows - shift_idx + row
                total = total + lead[at : at + 1] * exts[place][row : row + 1, :]
        sums_ref[shift_idx : shift_idx + 1, lanes] = total


def lead_kernel(q_ref, k_ref, v_ref, after_ref, lead_ref):
    halo_rows = lead_ref.shape[0] // 3
    for place, ref in enumerate((q_ref, k_ref, v_ref)):
        rows = ref[...].astype(f32)
        lead_ref[place * halo_rows : (place + 1) * halo_rows, :] = rows[rows.shape[0] - halo_rows :]


def edges_kernel(back_ref, tail_ref, taps_ref, q_ref, k_ref, v_ref, q_out, k_out, v_out, work_ref):
    taps_count = taps_ref.shape[0]
    halo_rows = taps_count - 1
    block_rows = q_ref.shape[0]
    for place, (ref, out_ref) in enumerate(((q_ref, q_out), (k_ref, k_out), (v_ref, v_out))):
        work_ref[...] = ref[...].astype(f32)
        first = place * halo_rows
        for row in range(halo_rows):
            total = back_ref[first + row : first + row + 1, :]
            for shift_idx in range(halo_rows - row, taps_count):
                source = first + row + shift_idx - halo_rows
                total = total + taps_ref[shift_idx : shift_idx + 1, :] * tail_ref[source : source + 1, :]
            at = block_rows - halo_rows + row
            work_ref[at : at + 1, :] = total
        out_ref[...] = work_ref[...].astype(bf16)


def norm_kernel(*refs):
    values, totals_ref, square_ref = refs[:-2], refs[-2], refs[-1]
    channels = totals_ref.shape[1] - LANES
    totals = values[0][...]
    if len(values) == 4:
        totals = (totals + values[1][...]) + (values[2][...] + values[3][...])
    totals_ref[...] = totals
    square = jnp.sum(totals[:, :channels] * totals[:, :channels]) + jnp.sum(totals[0:1, channels:])
    square_ref[...] = jnp.full(square_ref.shape, square)


def scale_kernel(limit, totals_ref, norm_ref, lag_ref, taps_out, skip_out, kernel_out):
    taps_count, channels = taps_out.shape
    factor = limit / jnp.maximum(jnp.sqrt(norm_ref[...]), limit)
    for idx in range(channels // LANES):
        lanes = slice(idx * LANES, (idx + 1) * LANES)
        taps_out[:, lanes] = totals_ref[0:taps_count, lanes] * factor
        skip_out[:, lanes] = totals_ref[taps_count : taps_count + 1, lanes] * factor
        kernel_out[:, lanes] = lag_ref[idx].astype(f32) * factor


def exchange(pieces_first):
    return lax.all_to_all(pieces_first, "ctx", split_axis=0, concat_axis=0, tiled=True)


def to_pieces(groups, pieces):
    count, rows, lanes = groups.shape
    if count == pieces:
        return groups
    share = count * lanes // pieces
    split = groups.reshape(count, rows, lanes // share, share)
    return split.transpose(0, 2, 1, 3).reshape(pieces, rows, share)


def to_groups(parts):
    pieces, kinds, rows, share = parts.shape
    if share == LANES:
        return parts
    joined = parts.reshape(pieces * share // LANES, LANES // share, kinds, rows, share)
    return joined.transpose(0, 2, 3, 1, 4).reshape(-1, kinds, rows, LANES)


def partners(value, axis, steps):
    size = lax.axis_size(axis)
    return [value] + [lax.ppermute(value, axis, [(i, i ^ step) for i in range(size)]) for step in steps]


def rounds_of(size):
    rounds = []
    step = 1
    while step < size:
        rounds.append((step, 2 * step, 3 * step) if size // step >= 4 else (step,))
        step *= 4 if size // step >= 4 else 2
    return rounds


def add_up(values):
    if len(values) == 2:
        return values[0] + values[1]
    return (values[0] + values[1]) + (values[2] + values[3])


def body(q_in, k_in, v_in, grad_out, short_filter, kernel, skip):
    pieces = lax.axis_size("ctx")
    sides = lax.axis_size("ch")
    rows_here, channels = q_in.shape
    seq_len = pieces * rows_here
    taps_count = short_filter.shape[0]
    halo_rows = taps_count - 1
    groups = channels // LANES
    share = channels // pieces
    per_step = min(groups, 4)
    steps = groups // per_step
    lanes2 = cut_lanes(per_step * LANES, 2)
    lanes3 = cut_lanes(per_step * LANES, 3)
    transforms = (Transforms if share == LANES else PlainTransforms)(pieces, rows_here)
    stream = functools.partial(stream_call, steps=steps, per_step=per_step)

    flat = jax.ShapeDtypeStruct((rows_here, channels), bf16)
    halo = jax.ShapeDtypeStruct((3 * halo_rows, channels), f32)
    extra_rows = -(-7 * halo_rows // TILE_ROWS) * TILE_ROWS
    sent = jax.ShapeDtypeStruct((groups, 3 * rows_here + extra_rows, LANES), bf16)
    exts = [pltpu.VMEM((rows_here + PAD, LANES), f32)] * 3
    last_block = 16
    last_spec = pl.BlockSpec((last_block, channels), lambda i: (rows_here // last_block - 1, 0))

    def whole(array):
        return pl.BlockSpec(array.shape, lambda i: (0,) * len(array.shape))

    (signals,) = stream(
        signals_work,
        operands=[(x, lanes2, None) for x in (q_in, k_in, v_in, grad_out, kernel, short_filter)],
        results=[(sent, cut_groups(per_step), None)],
        scratch=exts,
    )
    signals_here = exchange(to_pieces(signals, pieces))
    taps_here = lax.dynamic_slice_in_dim(short_filter, lax.axis_index("ctx") * share, share, axis=1)
    long_here, lag_spec = transforms.products(signals_here, taps_here)
    long = to_groups(exchange(long_here))
    lag_here, lag_squares = transforms.lag(lag_spec)
    lag = to_groups(exchange(lag_here[:, None]))[:, 0]

    lead = call(
        lead_kernel, halo, [], q_in, k_in, v_in, long_here,
        grid=(1,), in_specs=[last_spec] * 3 + [ANYWHERE], out_specs=whole(halo),
    )
    lead = lax.ppermute(lead, "ctx", [(i, i + 1) for i in range(pieces - 1)])
    (short,) = stream(
        short_work,
        operands=[(x, lanes2, None) for x in (q_in, k_in, v_in, lead, short_filter)],
        results=[(jax.ShapeDtypeStruct((3, rows_here, channels), f32), lanes3, None)],
        scratch=exts,
    )

    mixed, grad_q, grad_k, grad_v, front, back, sums = stream(
        finish_work,
        operands=[(x, lanes2, None) for x in (q_in, k_in, v_in, grad_out)]
        + [(short, lanes3, None)]
        + [(x, lanes2, None) for x in (lead, short_filter, skip.reshape(1, channels))]
        + [(long, cut_groups(per_step), None), (lag_squares, (cut_none, cut_none), None)],
        results=[(flat, lanes2, None)] * 4,
        scratch=exts,
        kept=[halo, halo, jax.ShapeDtypeStruct((taps_count + 1, channels + LANES), f32)],
    )
    lag = to_groups(exchange(lag_here[:, None]))[:, 0]

    totals = sums
    rounds = rounds_of(pieces)
    for steps_of in rounds[:-1]:
        totals = add_up(partners(totals, "ctx", steps_of))
    last = partners(totals, "ctx", rounds[-1])
    if len(last) == 2:
        last = [last[0] + last[1]]

    tail = lax.ppermute(front, "ctx", [(i, i - 1) for i in range(1, pieces)])
    grad_q, grad_k, grad_v = call(
        edges_kernel, (flat, flat, flat), [pltpu.VMEM((last_block, channels), f32)],
        back, tail, short_filter, grad_q, grad_k, grad_v,
        vmem_bytes=SMALL_VMEM_BYTES,
        grid=(1,),
        in_specs=[whole(back), whole(tail), whole(short_filter)] + [last_spec] * 3,
        out_specs=(last_spec,) * 3,
        input_output_aliases={3: 0, 4: 1, 5: 2},
    )
    grad_q, grad_k, grad_v, *last = lax.optimization_barrier((grad_q, grad_k, grad_v, *last))

    totals, norm_sq = call(
        norm_kernel,
        (jax.ShapeDtypeStruct(totals.shape, f32), jax.ShapeDtypeStruct((1, LANES), f32)),
        [], *last,
        vmem_bytes=SMALL_VMEM_BYTES,
        in_specs=[IN_VMEM] * len(last), out_specs=(IN_VMEM, IN_VMEM),
    )
    for steps_of in rounds_of(sides):
        norm_sq = add_up(partners(norm_sq, "ch", steps_of))

    limit = math.sqrt(float(seq_len * channels * sides))
    grad_short, grad_skip, grad_kernel = call(
        functools.partial(scale_kernel, limit),
        (
            jax.ShapeDtypeStruct((taps_count, channels), f32),
            jax.ShapeDtypeStruct((1, channels), f32),
            jax.ShapeDtypeStruct((rows_here, channels), f32),
        ),
        [],
        totals, norm_sq, lag,
        vmem_bytes=SMALL_VMEM_BYTES,
        in_specs=[IN_VMEM] * 3,
        out_specs=(IN_VMEM,) * 3,
    )
    return mixed, grad_q, grad_k, grad_v, grad_short, grad_skip.reshape(channels), grad_kernel


def solution(mesh):
    in_specs = (
        P("ctx", "ch"),
        P("ctx", "ch"),
        P("ctx", "ch"),
        P("ctx", "ch"),
        P(None, "ch"),
        P("ctx", "ch"),
        P("ch"),
    )
    out_specs = (
        P("ctx", "ch"),
        P("ctx", "ch"),
        P("ctx", "ch"),
        P("ctx", "ch"),
        P(None, "ch"),
        P("ch"),
        P("ctx", "ch"),
    )
    return jax.shard_map(body, mesh=mesh, in_specs=in_specs, out_specs=out_specs, check_vma=False)
```

```python
import functools
import math

import jax
import jax.numpy as jnp
import ml_dtypes
import numpy as np
from jax import lax
from jax.experimental import pallas as pl
from jax.experimental.pallas import tpu as pltpu
from jax.sharding import PartitionSpec as P

LANES = 128
SPAN = 256
BOTH = 2 * SPAN
CHUNK = 16
CHUNKS = SPAN // CHUNK
PAD = 8
ROWS = 32
PASSES = 1
TILE_ROWS = 16
VMEM_BYTES = 60 * 1024 * 1024
SMALL_VMEM_BYTES = 8 * 1024 * 1024

f32 = jnp.float32
bf16 = jnp.bfloat16

IN_VMEM = pl.BlockSpec(memory_space=pltpu.VMEM)
IN_SMEM = pl.BlockSpec(memory_space=pltpu.SMEM)
ANYWHERE = pl.BlockSpec(memory_space=pl.ANY)


def call(kernel, outs, scratch, *args, vmem_bytes=VMEM_BYTES, **options):
    return pl.pallas_call(
        kernel,
        out_shape=outs,
        scratch_shapes=scratch,
        compiler_params=pltpu.CompilerParams(vmem_limit_bytes=vmem_bytes),
        **options,
    )(*args)


def leaf_phases(count):
    return [(4 * leaf + 1) / (4 * count) for leaf in range(count)]


def root_times(re, im, num, den, sign):
    if num == 0:
        return re, im
    if 4 * num == den:
        return (im, -re) if sign < 0 else (-im, re)
    cosine = math.cos(2.0 * math.pi * num / den)
    sine = sign * math.sin(2.0 * math.pi * num / den)
    if 8 * num == den:
        return ((re + im) * cosine, (im - re) * cosine) if sign < 0 else ((re - im) * cosine, (re + im) * cosine)
    if 8 * num == 3 * den:
        return ((re - im) * cosine, (re + im) * cosine) if sign < 0 else ((re + im) * cosine, (im - re) * cosine)
    return re * cosine - im * sine, im * cosine + re * sine


def short_fft(values, sign):
    count = len(values)
    if count == 1:
        return values
    even = short_fft(values[0::2], sign)
    odd = short_fft(values[1::2], sign)
    first = []
    second = []
    for num in range(count // 2):
        re, im = root_times(*odd[num], num, count, sign)
        first.append((even[num][0] + re, even[num][1] + im))
        second.append((even[num][0] - re, even[num][1] - im))
    return first + second


def to_leaves(parts):
    count = len(parts)
    turned = []
    for idx, part in enumerate(parts):
        angle = 2.0 * math.pi * idx / (4 * count)
        turned.append((part * math.cos(angle), part * (-math.sin(angle))) if idx else (part, jnp.zeros_like(part)))
    return short_fft(turned, -1)


def from_leaves(leaves, scale):
    count = len(leaves)
    parts = []
    for idx, (re, im) in enumerate(short_fft(leaves, 1)):
        angle = 2.0 * math.pi * idx / (4 * count)
        if idx == 0:
            parts.append(re * scale)
        else:
            parts.append(re * (math.cos(angle) * scale) - im * (math.sin(angle) * scale))
    return parts


def dft_matrix():
    idx = np.arange(SPAN)
    angle = (idx[:, None] * idx[None, :] % SPAN) * (2.0 * np.pi / SPAN)
    cosine, sine = np.cos(angle), np.sin(angle)
    return np.block([[cosine, sine], [-sine, cosine]])


def twist_angles(outer, inner):
    return np.asarray(leaf_phases(outer))[:, None] * np.asarray(inner)[None, :] * (2.0 * np.pi / SPAN)


def matrix_blocks():
    matrix = dft_matrix()
    high = matrix.astype(ml_dtypes.bfloat16)
    low = (matrix - high.astype(np.float64)).astype(ml_dtypes.bfloat16)
    return np.concatenate([high, low, high][:PASSES], axis=1)


def leaf_place(leaf):
    return leaf // 2, slice((leaf % 2) * LANES, (leaf % 2 + 1) * LANES)


def split_store(ref, leaf, below, here, value):
    pair, lanes = leaf_place(leaf)
    high = value.astype(bf16)
    for block in range(PASSES):
        part = high
        if PASSES == 3 and block == 2:
            part = (value - high.astype(f32)).astype(bf16)
        ref[pair, shifted_rows(here, block * BOTH + below), lanes] = part


def run_all(stages, rows_here, matmul=None, carry=0):
    tiles = matmul[2].shape[0] if matmul else 4
    ratio = SPAN // rows_here
    in_part = tiles // ratio
    per_tile = CHUNKS // tiles
    for part in range(ratio):

        def step(tile, carry, part=part):
            if matmul:
                matrix_ref, split_ref, result_ref = matmul
                place = part * in_part + tile
                result_ref[place] = jnp.dot(matrix_ref[...], split_ref[place], preferred_element_type=f32)
            for chunk in range(per_tile):
                for stage in stages:
                    carry = stage(part, chunk_row(tile * per_tile + chunk), carry)
            return carry

        carry = lax.fori_loop(0, in_part, step, carry)
    return carry


def chunk_row(idx):
    return pl.multiple_of(idx * CHUNK, CHUNK)


def in_span(part, row, rows_here):
    return pl.ds(pl.multiple_of(part * rows_here + row, CHUNK), CHUNK)


def twist_stage(coarse_ref, fine_ref, twist_ref, rows_here):
    outer = twist_ref.shape[1]

    def stage(part, row, carry):
        here = in_span(part, row, rows_here)
        idx = part * (rows_here // CHUNK) + row // CHUNK
        for leaf in range(outer):
            far_cosine = coarse_ref[idx, leaf]
            far_sine = coarse_ref[idx, outer + leaf]
            cosine = fine_ref[0, leaf]
            sine = fine_ref[1, leaf]
            twist_ref[0, leaf, here, :] = far_cosine * cosine - far_sine * sine
            twist_ref[1, leaf, here, :] = far_sine * cosine + far_cosine * sine
        return carry

    return stage


def leaves_stage(signals_ref, first_row, heads_ref, rows_here, twist_ref, split_ref):
    outer = twist_ref.shape[1]
    ratio = SPAN // rows_here

    def stage(part, row, carry):
        here = in_span(part, row, rows_here)
        rows = pl.ds(pl.multiple_of(first_row + row, CHUNK), CHUNK)
        parts = [signals_ref[place * ratio + part, rows, :] for place in range(outer)]
        if heads_ref is not None:
            parts = [
                jnp.where(row == 0, heads_ref[place * ratio + part], value) for place, value in enumerate(parts)
            ]
        parts = [value.astype(f32) for value in parts]
        for leaf, (re, im) in enumerate(to_leaves(parts)):
            cosine = twist_ref[0, leaf, here, :]
            sine = twist_ref[1, leaf, here, :]
            split_store(split_ref, leaf, 0, here, re * cosine + im * sine)
            split_store(split_ref, leaf, SPAN, here, im * cosine - re * sine)
        return carry

    return stage


def shifted_rows(here, by):
    return pl.ds(here.start + by, here.size)


def combine_stage(left_ref, right_ref, split_ref, rows_here, conjugate):
    def stage(part, row, carry):
        here = in_span(part, row, rows_here)
        below = shifted_rows(here, SPAN)
        for leaf in range(2 * left_ref.shape[0]):
            pair, lanes = leaf_place(leaf)
            left_re = left_ref[pair, here, lanes]
            left_im = left_ref[pair, below, lanes]
            right_re = right_ref[pair, here, lanes]
            right_im = right_ref[pair, below, lanes]
            if conjugate:
                re = left_re * right_re + left_im * right_im
                minus_im = left_im * right_re - left_re * right_im
            else:
                re = left_re * right_re - left_im * right_im
                minus_im = -(left_re * right_im + left_im * right_re)
            split_store(split_ref, leaf, 0, here, re)
            split_store(split_ref, leaf, SPAN, here, minus_im)
        return carry

    return stage


def signal_stage(time_ref, twist_ref, rows_here, write):
    outer = twist_ref.shape[1]
    ratio = SPAN // rows_here
    scale = 1.0 / (SPAN * outer)

    def stage(part, row, carry):
        here = in_span(part, row, rows_here)
        below = shifted_rows(here, SPAN)
        leaves = []
        for leaf in range(outer):
            pair, lanes = leaf_place(leaf)
            cosine = twist_ref[0, leaf, here, :]
            sine = twist_ref[1, leaf, here, :]
            re = time_ref[pair, here, lanes]
            minus_im = time_ref[pair, below, lanes]
            leaves.append((re * cosine + minus_im * sine, re * sine - minus_im * cosine))
        for place, value in enumerate(from_leaves(leaves, scale)):
            carry = write(place * ratio + part, pl.ds(row, CHUNK), value, carry)
        return carry

    return stage


def first_rows(lead, first, taps):
    count = len(lead)
    rows = lead + first
    return [
        functools.reduce(lambda x, y: x + y, [taps[shift] * rows[count + row - shift] for shift in range(count + 1)])
        for row in range(count)
    ]


def first_signals(ahead, own, taps):
    count = len(taps) - 1

    def kind(rows, idx):
        return rows[idx * count : (idx + 1) * count]

    q_short, k_short, v_short = (first_rows(kind(ahead, idx), kind(own, 3 + idx), taps) for idx in range(3))
    product = [k_row * v_row for k_row, v_row in zip(k_short, v_short)]
    cotan = [grad_row * q_row for grad_row, q_row in zip(kind(own, 6), q_short)]
    return product, cotan


def patch_first_rows(signals_ref, heads_ref, taps_ref, rows_here):
    pieces, all_rows = signals_ref.shape[:2]
    taps = [taps_ref[shift : shift + 1, :] for shift in range(taps_ref.shape[0])]
    used = 7 * (len(taps) - 1)

    def extra(piece):
        rows = signals_ref[piece, 3 * rows_here : all_rows, :].astype(f32)
        return [rows[idx : idx + 1] for idx in range(used)]

    row_idx = lax.broadcasted_iota(jnp.int32, (TILE_ROWS, LANES), 0)
    ahead = [jnp.zeros((1, LANES), f32)] * used
    for piece in range(pieces):
        own = extra(piece)
        for kind, rows in enumerate(first_signals(ahead, own, taps)):
            place = slice(kind * rows_here, kind * rows_here + TILE_ROWS)
            tile = signals_ref[piece, place, :].astype(f32)
            for row, value in enumerate(rows):
                tile = jnp.where(row_idx == row, value, tile)
            heads_ref[kind, piece] = tile.astype(bf16)
        ahead = own


def products_kernel(
    rows_here, signals_ref, taps_ref, coarse_ref, fine_ref, matrix_hbm, after_ref, results_hbm, lag_hbm,
    twist_ref, matrix_ref, heads_ref, results_ref, one_split, two_split, lag_split,
    filter_ref, product_ref, cotan_ref, time_ref, sems,
):
    matrix_copy = pltpu.make_async_copy(matrix_hbm, matrix_ref, sems.at[3])
    lag_copy = pltpu.make_async_copy(lag_split, lag_hbm, sems.at[4])
    returns = [
        pltpu.make_async_copy(results_ref.at[:, kind], results_hbm.at[:, kind], sems.at[5 + kind]) for kind in range(2)
    ]

    def leaves(kind, split_ref):
        heads = heads_ref.at[kind] if kind < 2 else None
        return leaves_stage(signals_ref, kind * rows_here, heads, rows_here, twist_ref, split_ref)

    def combine(left_ref, right_ref, split_ref, conjugate):
        return combine_stage(left_ref, right_ref, split_ref, rows_here, conjugate)

    def result(kind, from_ref):
        def write(piece, rows, value, carry):
            results_ref[piece, kind, rows, :] = value.astype(bf16)
            return carry

        return signal_stage(from_ref, twist_ref, rows_here, write)

    matrix_copy.start()
    run_all([twist_stage(coarse_ref, fine_ref, twist_ref, rows_here)], rows_here)
    run_all([leaves(2, one_split)], rows_here)
    patch_first_rows(signals_ref, heads_ref, taps_ref, rows_here)
    matrix_copy.wait()
    run_all([leaves(0, two_split)], rows_here, (matrix_ref, one_split, filter_ref))
    run_all([leaves(1, one_split)], rows_here, (matrix_ref, two_split, product_ref))
    run_all([combine(filter_ref, product_ref, two_split, False)], rows_here, (matrix_ref, one_split, cotan_ref))
    run_all([combine(filter_ref, cotan_ref, one_split, True)], rows_here, (matrix_ref, two_split, time_ref))
    run_all(
        [combine(product_ref, cotan_ref, lag_split, True), result(0, time_ref)],
        rows_here, (matrix_ref, one_split, filter_ref),
    )
    lag_copy.start()
    returns[0].start()
    run_all([result(1, filter_ref)], rows_here)
    returns[1].start()
    lag_copy.wait()
    returns[0].wait()
    returns[1].wait()


def lag_kernel(
    split_hbm, coarse_ref, fine_ref, matrix_hbm, lag_ref, square_ref, twist_ref, matrix_ref, split_ref, time_ref, sems
):
    rows_here = lag_ref.shape[1]
    copies = [
        pltpu.make_async_copy(matrix_hbm, matrix_ref, sems.at[0]),
        pltpu.make_async_copy(split_hbm, split_ref, sems.at[1]),
    ]
    for copy in copies:
        copy.start()
    run_all([twist_stage(coarse_ref, fine_ref, twist_ref, rows_here)], rows_here)
    for copy in copies:
        copy.wait()
    run_all([], rows_here, (matrix_ref, split_ref, time_ref))

    def write(piece, rows, value, carry):
        lag_ref[piece, rows, :] = value.astype(bf16)
        return carry + value * value

    square = run_all(
        [signal_stage(time_ref, twist_ref, rows_here, write)], rows_here, None, jnp.zeros((CHUNK, LANES), f32)
    )
    square_ref[...] = jnp.sum(square, axis=0, keepdims=True)


class Transforms:
    def __init__(self, pieces, rows_here):
        outer = pieces * rows_here // SPAN
        pairs = outer // 2
        coarse = twist_angles(outer, CHUNK * np.arange(CHUNKS)).T
        fine = twist_angles(outer, np.arange(CHUNK))[..., None] * np.ones(LANES)
        self.tables = [
            jnp.asarray(np.concatenate([np.cos(coarse), np.sin(coarse)], axis=1).astype(np.float32)),
            jnp.asarray(np.stack([np.cos(fine), np.sin(fine)]).astype(np.float32)),
            jnp.asarray(matrix_blocks()),
        ]
        self.split = jax.ShapeDtypeStruct((pairs, PASSES * BOTH, 2 * LANES), bf16)
        self.signal = jax.ShapeDtypeStruct((pieces, rows_here, LANES), bf16)
        self.result = jax.ShapeDtypeStruct((pieces, 2, rows_here, LANES), bf16)
        self.square = jax.ShapeDtypeStruct((1, LANES), f32)
        self.result_work = pltpu.VMEM(self.result.shape, bf16)
        self.work = pltpu.VMEM((pairs, BOTH, 2 * LANES), f32)
        self.split_work = pltpu.VMEM(self.split.shape, bf16)
        self.twist_work = pltpu.VMEM((2, outer, SPAN, LANES), f32)
        self.matrix_work = pltpu.VMEM(self.tables[2].shape, bf16)

    def products(self, signals, taps, after):
        return call(
            functools.partial(products_kernel, self.signal.shape[1]), (self.result, self.split),
            [self.twist_work, self.matrix_work]
            + [pltpu.VMEM((2, signals.shape[0], TILE_ROWS, LANES), bf16), self.result_work]
            + [self.split_work] * 3
            + [self.work] * 4
            + [pltpu.SemaphoreType.DMA((7,))],
            signals, taps, *self.tables, after,
            in_specs=[IN_VMEM, IN_VMEM, IN_SMEM, IN_VMEM, ANYWHERE, ANYWHERE],
            out_specs=(ANYWHERE, ANYWHERE),
        )

    def lag(self, lag_split):
        return call(
            lag_kernel, (self.signal, self.square),
            [self.twist_work, self.matrix_work, self.split_work, self.work, pltpu.SemaphoreType.DMA((2,))],
            lag_split, *self.tables,
            in_specs=[ANYWHERE, IN_SMEM, IN_VMEM, ANYWHERE],
            out_specs=(IN_VMEM, IN_VMEM),
        )


class PlainTransforms:
    def __init__(self, pieces, rows_here):
        self.seq_len = pieces * rows_here
        self.pieces = pieces
        self.outer = self.seq_len // SPAN
        idx = np.arange(SPAN)
        angle = (idx[:, None] * idx[None, :] % SPAN) * (2.0 * np.pi / SPAN)
        self.cosine = jnp.asarray(np.cos(angle), f32)
        self.sine = jnp.asarray(np.sin(angle), f32)
        twist = twist_angles(self.outer, idx)
        self.twist = jnp.asarray(np.stack([np.cos(twist), np.sin(twist)]), f32)[..., None]

    def dot(self, matrix, signal):
        return jnp.einsum("fs,tsc->tfc", matrix, signal, precision=lax.Precision.HIGHEST)

    def spectrum(self, signal):
        parts = signal.astype(f32).reshape(self.outer, SPAN, -1)
        leaves = to_leaves([parts[part] for part in range(self.outer)])
        re = jnp.stack([leaf[0] for leaf in leaves])
        im = jnp.stack([leaf[1] for leaf in leaves])
        twist_re = re * self.twist[0] + im * self.twist[1]
        twist_im = im * self.twist[0] - re * self.twist[1]
        return (
            self.dot(self.cosine, twist_re) + self.dot(self.sine, twist_im),
            self.dot(self.cosine, twist_im) - self.dot(self.sine, twist_re),
        )

    def back(self, re, im):
        time_re = self.dot(self.cosine, re) - self.dot(self.sine, im)
        time_im = self.dot(self.cosine, im) + self.dot(self.sine, re)
        leaf_re = time_re * self.twist[0] - time_im * self.twist[1]
        leaf_im = time_im * self.twist[0] + time_re * self.twist[1]
        parts = from_leaves([(leaf_re[leaf], leaf_im[leaf]) for leaf in range(self.outer)], 1.0 / self.seq_len)
        return jnp.stack(parts).reshape(self.pieces, self.seq_len // self.pieces, -1)

    def products(self, signals, short_taps, after):
        rows_here = self.seq_len // self.pieces
        parts = [signals[:, kind * rows_here : (kind + 1) * rows_here] for kind in range(3)]
        extra = signals[:, 3 * rows_here :].astype(f32)
        rows = [extra[:, idx : idx + 1] for idx in range(extra.shape[1])]
        ahead = [jnp.concatenate([jnp.zeros_like(row[:1]), row[:-1]], axis=0) for row in rows]
        short_rows = [short_taps[shift][None, None, :] for shift in range(short_taps.shape[0])]
        for kind, first in enumerate(first_signals(ahead, rows, short_rows)):
            first = jnp.concatenate(first, axis=1)
            parts[kind] = jnp.concatenate([first.astype(bf16), parts[kind][:, first.shape[1] :]], axis=1)
        product, cotan, taps = (self.spectrum(part) for part in parts)
        conv = self.back(taps[0] * product[0] - taps[1] * product[1], taps[0] * product[1] + taps[1] * product[0])
        corr = self.back(taps[0] * cotan[0] + taps[1] * cotan[1], taps[0] * cotan[1] - taps[1] * cotan[0])
        lag = (
            product[0] * cotan[0] + product[1] * cotan[1],
            product[0] * cotan[1] - product[1] * cotan[0],
        )
        return jnp.stack([conv, corr], axis=1).astype(bf16), lag

    def lag(self, lag_spec):
        lag = self.back(*lag_spec)
        squares = jnp.sum(lag * lag, axis=(0, 1))
        return lag.astype(bf16), jnp.zeros((1, LANES), f32).at[0, : squares.shape[0]].set(squares)


def group(idx):
    return pl.ds(pl.multiple_of(idx * LANES, LANES), LANES)


def streamed(work, steps, per_step, places, in_count, out_count, kept, *refs):
    moved = in_count + out_count
    hbm = refs[:moved]
    kept_refs = refs[moved : moved + kept]
    held = refs[moved + kept : 2 * moved + kept]
    scratch = refs[2 * moved + kept : -1]
    sems = refs[-1]

    def copy(place, step):
        outside = hbm[place].at[places[place][0](step)]
        inside = held[place].at[places[place][1](step)]
        ends = (outside, inside) if place < in_count else (inside, outside)
        return pltpu.make_async_copy(*ends, sems.at[place, step])

    def arrivals(step):
        return [copy(place, step) for place in range(in_count) if places[place][0](step) is not None]

    for step in range(steps):
        for arrival in arrivals(step):
            arrival.start()
    for step in range(steps):
        for arrival in arrivals(step):
            arrival.wait()

        def one(idx, carry):
            work(idx, held[:in_count], held[in_count:] + kept_refs, scratch)
            return carry

        lax.fori_loop(step * per_step, (step + 1) * per_step, one, 0)
        for place in range(in_count, moved):
            copy(place, step).start()
    for step in range(steps):
        for place in range(in_count, moved):
            copy(place, step).wait()


def stream_call(work, steps, per_step, operands, results, scratch=(), aliases=(), kept=()):
    arrays = [operand[0] for operand in operands]
    shapes = [jax.ShapeDtypeStruct(array.shape, array.dtype) for array in arrays] + [result[0] for result in results]
    cuts = [entry[1] for entry in operands] + [entry[1] for entry in results]
    held = [pltpu.VMEM(entry[2] or shape.shape, shape.dtype) for entry, shape in zip(operands + results, shapes)]
    extra = list(aliases)
    kernel = functools.partial(streamed, work, steps, per_step, cuts, len(arrays), len(results), len(kept))

    def with_aliases(*refs):
        kernel(*refs[: len(arrays)], *refs[len(arrays) + len(extra) :])

    return call(
        with_aliases,
        tuple(result[0] for result in results) + tuple(kept),
        held + list(scratch) + [pltpu.SemaphoreType.DMA((len(shapes), steps))],
        *arrays, *extra,
        in_specs=[ANYWHERE] * (len(arrays) + len(extra)),
        out_specs=(ANYWHERE,) * len(results) + (IN_VMEM,) * len(kept),
        input_output_aliases={len(arrays) + idx: idx for idx in range(len(extra))},
    )


def cut_lanes(width, rank):
    def place(step):
        return (slice(None),) * (rank - 1) + (pl.ds(step * width, width),)

    return place, place


def cut_groups(per_step):
    def place(step):
        return (pl.ds(step * per_step, per_step),)

    return place, place


def cut_none(step):
    return None if step else (slice(None),)


def row_blocks(rows_here):
    return [slice(start, start + ROWS) for start in range(0, rows_here, ROWS)]


def extend_rows(lead, in_ref, lanes, ext_ref):
    ext_ref[PAD - lead.shape[0] : PAD, :] = lead
    ext_ref[PAD:, :] = in_ref[:, lanes].astype(f32)


def short_conv(ext_ref, taps, rows):
    result = None
    for shift_idx in range(taps.shape[0]):
        term = taps[shift_idx : shift_idx + 1] * ext_ref[PAD + rows.start - shift_idx : PAD + rows.stop - shift_idx, :]
        result = term if result is None else result + term
    return result


def extend_three(idx, operands, lead_ref, halo_rows, exts):
    lead = lead_ref[:, group(idx)]
    for place, ext in enumerate(exts):
        extend_rows(lead[place * halo_rows : (place + 1) * halo_rows], operands[place], group(idx), ext)


def signals_work(idx, operands, results, exts):
    q_ref, k_ref, v_ref, grad_ref, kernel_ref, taps_ref = operands
    lanes = group(idx)
    taps = taps_ref[:, lanes]
    halo_rows = taps.shape[0] - 1
    rows_here = q_ref.shape[0]
    for ext, in_ref in zip(exts, operands):
        extend_rows(jnp.zeros((halo_rows, LANES), f32), in_ref, lanes, ext)
    for rows in row_blocks(rows_here):
        q_short, k_short, v_short = (short_conv(ext, taps, rows) for ext in exts)
        below = [slice(kind * rows_here + rows.start, kind * rows_here + rows.stop) for kind in range(3)]
        results[0][idx, below[0], :] = (k_short * v_short).astype(bf16)
        results[0][idx, below[1], :] = (grad_ref[rows, lanes].astype(f32) * q_short).astype(bf16)
        results[0][idx, below[2], :] = kernel_ref[rows, lanes].astype(bf16)
    top = grad_ref[0:TILE_ROWS, lanes].astype(f32)[:halo_rows]
    extra = [ext[ext.shape[0] - halo_rows :, :] for ext in exts] + [ext[PAD : PAD + halo_rows, :] for ext in exts]
    extra_count = results[0].shape[1] - 3 * rows_here
    blank = jnp.zeros((extra_count - 7 * halo_rows, LANES), f32)
    results[0][idx, 3 * rows_here :, :] = jnp.concatenate(extra + [top, blank], axis=0).astype(bf16)


def short_work(idx, operands, results, exts):
    q_ref, k_ref, v_ref, lead_ref, taps_ref = operands
    taps = taps_ref[:, group(idx)]
    extend_three(idx, operands, lead_ref, taps.shape[0] - 1, exts)
    for rows in row_blocks(q_ref.shape[0]):
        for place, ext in enumerate(exts):
            results[0][place, rows, group(idx)] = short_conv(ext, taps, rows)


def fold(value):
    return jnp.sum(value.reshape(-1, 8, LANES), axis=0)


def finish_work(idx, operands, results, exts):
    q_ref, k_ref, v_ref, grad_ref, short_ref, lead_ref, taps_ref, skip_ref, long_ref, squares_ref = operands
    mixed_ref, grad_q_ref, grad_k_ref, grad_v_ref, front_ref, back_ref, sums_ref = results
    lanes = group(idx)
    taps = taps_ref[:, lanes]
    skip = skip_ref[:, lanes]
    lead = lead_ref[:, lanes]
    taps_count = taps.shape[0]
    halo_rows = taps_count - 1
    rows_here = q_ref.shape[0]
    sums = [jnp.zeros((8, LANES), f32) for _ in range(taps_count + 1)]
    for ext in exts:
        ext[rows_here:, :] = jnp.zeros((PAD, LANES), f32)
    for rows in row_blocks(rows_here):
        q_short, k_short, v_short = (short_ref[place, rows, lanes] for place in range(3))
        product = (k_short * v_short).astype(bf16).astype(f32)
        filtered = long_ref[idx, 0, rows, :].astype(f32) + skip * product
        mixed_ref[rows, lanes] = (q_short * filtered).astype(bf16)
        upstream = grad_ref[rows, lanes].astype(f32)
        back_mix = upstream * q_short
        back_prod = long_ref[idx, 1, rows, :].astype(f32) + skip * back_mix
        sums[taps_count] = sums[taps_count] + fold(back_mix * product)
        exts[0][rows, :] = upstream * filtered
        exts[1][rows, :] = back_prod * v_short
        exts[2][rows, :] = back_prod * k_short
    for place, (ext, in_ref, out_ref) in enumerate(
        zip(exts, (q_ref, k_ref, v_ref), (grad_q_ref, grad_k_ref, grad_v_ref))
    ):
        for rows in row_blocks(rows_here):
            signal = in_ref[rows, lanes].astype(f32)
            grad = None
            for shift_idx in range(taps_count):
                ahead = ext[rows.start + shift_idx : rows.stop + shift_idx, :]
                term = taps[shift_idx : shift_idx + 1] * ahead
                grad = term if grad is None else grad + term
                sums[shift_idx] = sums[shift_idx] + fold(ahead * signal)
            out_ref[rows, lanes] = grad.astype(bf16)
        back_ref[place * halo_rows : (place + 1) * halo_rows, lanes] = grad[ROWS - halo_rows :]
        front_ref[place * halo_rows : (place + 1) * halo_rows, lanes] = ext[0:halo_rows, :]
    extra = slice(sums_ref.shape[1] - LANES, sums_ref.shape[1])
    sums_ref[:, extra] = jnp.zeros((taps_count + 1, LANES), f32)
    sums_ref[0:1, extra] = squares_ref[...]
    for shift_idx in range(taps_count + 1):
        total = jnp.sum(sums[shift_idx], axis=0, keepdims=True)
        for place in range(3 if shift_idx < taps_count else 0):
            for row in range(shift_idx):
                at = place * halo_rows + halo_rows - shift_idx + row
                total = total + lead[at : at + 1] * exts[place][row : row + 1, :]
        sums_ref[shift_idx : shift_idx + 1, lanes] = total


def lead_kernel(q_ref, k_ref, v_ref, after_ref, lead_ref):
    halo_rows = lead_ref.shape[0] // 3
    for place, ref in enumerate((q_ref, k_ref, v_ref)):
        rows = ref[...].astype(f32)
        lead_ref[place * halo_rows : (place + 1) * halo_rows, :] = rows[rows.shape[0] - halo_rows :]


def edges_kernel(back_ref, tail_ref, taps_ref, q_ref, k_ref, v_ref, q_out, k_out, v_out, work_ref):
    taps_count = taps_ref.shape[0]
    halo_rows = taps_count - 1
    block_rows = q_ref.shape[0]
    for place, (ref, out_ref) in enumerate(((q_ref, q_out), (k_ref, k_out), (v_ref, v_out))):
        work_ref[...] = ref[...].astype(f32)
        first = place * halo_rows
        for row in range(halo_rows):
            total = back_ref[first + row : first + row + 1, :]
            for shift_idx in range(halo_rows - row, taps_count):
                source = first + row + shift_idx - halo_rows
                total = total + taps_ref[shift_idx : shift_idx + 1, :] * tail_ref[source : source + 1, :]
            at = block_rows - halo_rows + row
            work_ref[at : at + 1, :] = total
        out_ref[...] = work_ref[...].astype(bf16)


def norm_kernel(*refs):
    values, totals_ref, square_ref = refs[:-2], refs[-2], refs[-1]
    channels = totals_ref.shape[1] - LANES
    totals = values[0][...]
    if len(values) == 4:
        totals = (totals + values[1][...]) + (values[2][...] + values[3][...])
    totals_ref[...] = totals
    square = jnp.sum(totals[:, :channels] * totals[:, :channels]) + jnp.sum(totals[0:1, channels:])
    square_ref[...] = jnp.full(square_ref.shape, square)


def scale_kernel(limit, totals_ref, norm_ref, lag_ref, taps_out, skip_out, kernel_out):
    taps_count, channels = taps_out.shape
    factor = limit / jnp.maximum(jnp.sqrt(norm_ref[...]), limit)
    for idx in range(channels // LANES):
        lanes = slice(idx * LANES, (idx + 1) * LANES)
        taps_out[:, lanes] = totals_ref[0:taps_count, lanes] * factor
        skip_out[:, lanes] = totals_ref[taps_count : taps_count + 1, lanes] * factor
        kernel_out[:, lanes] = lag_ref[idx].astype(f32) * factor


def exchange(pieces_first):
    return lax.all_to_all(pieces_first, "ctx", split_axis=0, concat_axis=0, tiled=True)


def to_pieces(groups, pieces):
    count, rows, lanes = groups.shape
    if count == pieces:
        return groups
    share = count * lanes // pieces
    split = groups.reshape(count, rows, lanes // share, share)
    return split.transpose(0, 2, 1, 3).reshape(pieces, rows, share)


def to_groups(parts):
    pieces, kinds, rows, share = parts.shape
    if share == LANES:
        return parts
    joined = parts.reshape(pieces * share // LANES, LANES // share, kinds, rows, share)
    return joined.transpose(0, 2, 3, 1, 4).reshape(-1, kinds, rows, LANES)


def partners(value, axis, steps):
    size = lax.axis_size(axis)
    return [value] + [lax.ppermute(value, axis, [(i, i ^ step) for i in range(size)]) for step in steps]


def rounds_of(size):
    rounds = []
    step = 1
    while step < size:
        rounds.append((step, 2 * step, 3 * step) if size // step >= 4 else (step,))
        step *= 4 if size // step >= 4 else 2
    return rounds


def add_up(values):
    if len(values) == 2:
        return values[0] + values[1]
    return (values[0] + values[1]) + (values[2] + values[3])


def body(q_in, k_in, v_in, grad_out, short_filter, kernel, skip):
    pieces = lax.axis_size("ctx")
    sides = lax.axis_size("ch")
    rows_here, channels = q_in.shape
    seq_len = pieces * rows_here
    taps_count = short_filter.shape[0]
    halo_rows = taps_count - 1
    groups = channels // LANES
    share = channels // pieces
    per_step = min(groups, 4)
    steps = groups // per_step
    lanes2 = cut_lanes(per_step * LANES, 2)
    lanes3 = cut_lanes(per_step * LANES, 3)
    transforms = (Transforms if share == LANES else PlainTransforms)(pieces, rows_here)
    stream = functools.partial(stream_call, steps=steps, per_step=per_step)

    flat = jax.ShapeDtypeStruct((rows_here, channels), bf16)
    halo = jax.ShapeDtypeStruct((3 * halo_rows, channels), f32)
    extra_rows = -(-7 * halo_rows // TILE_ROWS) * TILE_ROWS
    sent = jax.ShapeDtypeStruct((groups, 3 * rows_here + extra_rows, LANES), bf16)
    exts = [pltpu.VMEM((rows_here + PAD, LANES), f32)] * 3
    last_block = 16
    last_spec = pl.BlockSpec((last_block, channels), lambda i: (rows_here // last_block - 1, 0))

    def whole(array):
        return pl.BlockSpec(array.shape, lambda i: (0,) * len(array.shape))

    (signals,) = stream(
        signals_work,
        operands=[(x, lanes2, None) for x in (q_in, k_in, v_in, grad_out, kernel, short_filter)],
        results=[(sent, cut_groups(per_step), None)],
        scratch=exts,
    )
    signals_here = exchange(to_pieces(signals, pieces))
    taps_here = lax.dynamic_slice_in_dim(short_filter, lax.axis_index("ctx") * share, share, axis=1)
    lead = call(
        lead_kernel, halo, [], q_in, k_in, v_in, signals,
        grid=(1,), in_specs=[last_spec] * 3 + [ANYWHERE], out_specs=whole(halo),
    )
    lead = lax.ppermute(lead, "ctx", [(i, i + 1) for i in range(pieces - 1)])
    (short,) = stream(
        short_work,
        operands=[(x, lanes2, None) for x in (q_in, k_in, v_in, lead, short_filter)],
        results=[(jax.ShapeDtypeStruct((3, rows_here, channels), f32), lanes3, None)],
        scratch=exts,
    )

    long_here, lag_spec = transforms.products(signals_here, taps_here, short)
    long = to_groups(exchange(long_here))
    lag_here, lag_squares = transforms.lag(lag_spec)
    lag = to_groups(exchange(lag_here[:, None]))[:, 0]

    mixed, grad_q, grad_k, grad_v, front, back, sums = stream(
        finish_work,
        operands=[(x, lanes2, None) for x in (q_in, k_in, v_in, grad_out)]
        + [(short, lanes3, None)]
        + [(x, lanes2, None) for x in (lead, short_filter, skip.reshape(1, channels))]
        + [(long, cut_groups(per_step), None), (lag_squares, (cut_none, cut_none), None)],
        results=[(flat, lanes2, None)] * 4,
        scratch=exts,
        kept=[halo, halo, jax.ShapeDtypeStruct((taps_count + 1, channels + LANES), f32)],
    )
    lag = to_groups(exchange(lag_here[:, None]))[:, 0]

    totals = sums
    rounds = rounds_of(pieces)
    for steps_of in rounds[:-1]:
        totals = add_up(partners(totals, "ctx", steps_of))
    totals, front = lax.optimization_barrier((totals, front))
    last = partners(totals, "ctx", rounds[-1])
    if len(last) == 2:
        last = [last[0] + last[1]]

    tail = lax.ppermute(front, "ctx", [(i, i - 1) for i in range(1, pieces)])
    grad_q, grad_k, grad_v = call(
        edges_kernel, (flat, flat, flat), [pltpu.VMEM((last_block, channels), f32)],
        back, tail, short_filter, grad_q, grad_k, grad_v,
        vmem_bytes=SMALL_VMEM_BYTES,
        grid=(1,),
        in_specs=[whole(back), whole(tail), whole(short_filter)] + [last_spec] * 3,
        out_specs=(last_spec,) * 3,
        input_output_aliases={3: 0, 4: 1, 5: 2},
    )
    grad_q, grad_k, grad_v, *last = lax.optimization_barrier((grad_q, grad_k, grad_v, *last))

    totals, norm_sq = call(
        norm_kernel,
        (jax.ShapeDtypeStruct(totals.shape, f32), jax.ShapeDtypeStruct((1, LANES), f32)),
        [], *last,
        vmem_bytes=SMALL_VMEM_BYTES,
        in_specs=[IN_VMEM] * len(last), out_specs=(IN_VMEM, IN_VMEM),
    )
    for steps_of in rounds_of(sides):
        norm_sq = add_up(partners(norm_sq, "ch", steps_of))

    limit = math.sqrt(float(seq_len * channels * sides))
    grad_short, grad_skip, grad_kernel = call(
        functools.partial(scale_kernel, limit),
        (
            jax.ShapeDtypeStruct((taps_count, channels), f32),
            jax.ShapeDtypeStruct((1, channels), f32),
            jax.ShapeDtypeStruct((rows_here, channels), f32),
        ),
        [],
        totals, norm_sq, lag,
        vmem_bytes=SMALL_VMEM_BYTES,
        in_specs=[IN_VMEM] * 3,
        out_specs=(IN_VMEM,) * 3,
    )
    return mixed, grad_q, grad_k, grad_v, grad_short, grad_skip.reshape(channels), grad_kernel


def solution(mesh):
    in_specs = (
        P("ctx", "ch"),
        P("ctx", "ch"),
        P("ctx", "ch"),
        P("ctx", "ch"),
        P(None, "ch"),
        P("ctx", "ch"),
        P("ch"),
    )
    out_specs = (
        P("ctx", "ch"),
        P("ctx", "ch"),
        P("ctx", "ch"),
        P("ctx", "ch"),
        P(None, "ch"),
        P("ch"),
        P("ctx", "ch"),
    )
    return jax.shard_map(body, mesh=mesh, in_specs=in_specs, out_specs=out_specs, check_vma=False)
```

```python
import functools
import math

import jax
import jax.numpy as jnp
import ml_dtypes
import numpy as np
from jax import lax
from jax.experimental import pallas as pl
from jax.experimental.pallas import tpu as pltpu
from jax.sharding import PartitionSpec as P

LANES = 128
SPAN = 256
BOTH = 2 * SPAN
CHUNK = 16
CHUNKS = SPAN // CHUNK
PAD = 8
ROWS = 32
PASSES = 1
TILE_ROWS = 16
VMEM_BYTES = 60 * 1024 * 1024
SMALL_VMEM_BYTES = 8 * 1024 * 1024

f32 = jnp.float32
bf16 = jnp.bfloat16

IN_VMEM = pl.BlockSpec(memory_space=pltpu.VMEM)
IN_SMEM = pl.BlockSpec(memory_space=pltpu.SMEM)
ANYWHERE = pl.BlockSpec(memory_space=pl.ANY)


def call(kernel, outs, scratch, *args, vmem_bytes=VMEM_BYTES, **options):
    return pl.pallas_call(
        kernel,
        out_shape=outs,
        scratch_shapes=scratch,
        compiler_params=pltpu.CompilerParams(vmem_limit_bytes=vmem_bytes),
        **options,
    )(*args)


def leaf_phases(count):
    return [(4 * leaf + 1) / (4 * count) for leaf in range(count)]


def root_times(re, im, num, den, sign):
    if num == 0:
        return re, im
    if 4 * num == den:
        return (im, -re) if sign < 0 else (-im, re)
    cosine = math.cos(2.0 * math.pi * num / den)
    sine = sign * math.sin(2.0 * math.pi * num / den)
    if 8 * num == den:
        return ((re + im) * cosine, (im - re) * cosine) if sign < 0 else ((re - im) * cosine, (re + im) * cosine)
    if 8 * num == 3 * den:
        return ((re - im) * cosine, (re + im) * cosine) if sign < 0 else ((re + im) * cosine, (im - re) * cosine)
    return re * cosine - im * sine, im * cosine + re * sine


def short_fft(values, sign):
    count = len(values)
    if count == 1:
        return values
    even = short_fft(values[0::2], sign)
    odd = short_fft(values[1::2], sign)
    first = []
    second = []
    for num in range(count // 2):
        re, im = root_times(*odd[num], num, count, sign)
        first.append((even[num][0] + re, even[num][1] + im))
        second.append((even[num][0] - re, even[num][1] - im))
    return first + second


def to_leaves(parts):
    count = len(parts)
    turned = []
    for idx, part in enumerate(parts):
        angle = 2.0 * math.pi * idx / (4 * count)
        turned.append((part * math.cos(angle), part * (-math.sin(angle))) if idx else (part, jnp.zeros_like(part)))
    return short_fft(turned, -1)


def from_leaves(leaves, scale):
    count = len(leaves)
    parts = []
    for idx, (re, im) in enumerate(short_fft(leaves, 1)):
        angle = 2.0 * math.pi * idx / (4 * count)
        if idx == 0:
            parts.append(re * scale)
        else:
            parts.append(re * (math.cos(angle) * scale) - im * (math.sin(angle) * scale))
    return parts


def dft_matrix():
    idx = np.arange(SPAN)
    angle = (idx[:, None] * idx[None, :] % SPAN) * (2.0 * np.pi / SPAN)
    cosine, sine = np.cos(angle), np.sin(angle)
    return np.block([[cosine, sine], [-sine, cosine]])


def twist_angles(outer, inner):
    return np.asarray(leaf_phases(outer))[:, None] * np.asarray(inner)[None, :] * (2.0 * np.pi / SPAN)


def matrix_blocks():
    matrix = dft_matrix()
    high = matrix.astype(ml_dtypes.bfloat16)
    low = (matrix - high.astype(np.float64)).astype(ml_dtypes.bfloat16)
    return np.concatenate([high, low, high][:PASSES], axis=1)


def leaf_place(leaf):
    return leaf // 2, slice((leaf % 2) * LANES, (leaf % 2 + 1) * LANES)


def split_store(ref, leaf, below, here, value):
    pair, lanes = leaf_place(leaf)
    high = value.astype(bf16)
    for block in range(PASSES):
        part = high
        if PASSES == 3 and block == 2:
            part = (value - high.astype(f32)).astype(bf16)
        ref[pair, shifted_rows(here, block * BOTH + below), lanes] = part


def run_all(stages, rows_here, matmul=None, carry=0):
    tiles = matmul[2].shape[0] if matmul else 4
    ratio = SPAN // rows_here
    in_part = tiles // ratio
    per_tile = CHUNKS // tiles
    for part in range(ratio):

        def step(tile, carry, part=part):
            if matmul:
                matrix_ref, split_ref, result_ref = matmul
                place = part * in_part + tile
                result_ref[place] = jnp.dot(matrix_ref[...], split_ref[place], preferred_element_type=f32)
            for chunk in range(per_tile):
                for stage in stages:
                    carry = stage(part, chunk_row(tile * per_tile + chunk), carry)
            return carry

        carry = lax.fori_loop(0, in_part, step, carry)
    return carry


def chunk_row(idx):
    return pl.multiple_of(idx * CHUNK, CHUNK)


def in_span(part, row, rows_here):
    return pl.ds(pl.multiple_of(part * rows_here + row, CHUNK), CHUNK)


def twist_stage(coarse_ref, fine_ref, twist_ref, rows_here):
    outer = twist_ref.shape[1]

    def stage(part, row, carry):
        here = in_span(part, row, rows_here)
        idx = part * (rows_here // CHUNK) + row // CHUNK
        for leaf in range(outer):
            far_cosine = coarse_ref[idx, leaf]
            far_sine = coarse_ref[idx, outer + leaf]
            cosine = fine_ref[0, leaf]
            sine = fine_ref[1, leaf]
            twist_ref[0, leaf, here, :] = far_cosine * cosine - far_sine * sine
            twist_ref[1, leaf, here, :] = far_sine * cosine + far_cosine * sine
        return carry

    return stage


def leaves_stage(signals_ref, first_row, heads_ref, rows_here, twist_ref, split_ref):
    outer = twist_ref.shape[1]
    ratio = SPAN // rows_here

    def stage(part, row, carry):
        here = in_span(part, row, rows_here)
        rows = pl.ds(pl.multiple_of(first_row + row, CHUNK), CHUNK)
        parts = [signals_ref[place * ratio + part, rows, :] for place in range(outer)]
        if heads_ref is not None:
            parts = [
                jnp.where(row == 0, heads_ref[place * ratio + part], value) for place, value in enumerate(parts)
            ]
        parts = [value.astype(f32) for value in parts]
        for leaf, (re, im) in enumerate(to_leaves(parts)):
            cosine = twist_ref[0, leaf, here, :]
            sine = twist_ref[1, leaf, here, :]
            split_store(split_ref, leaf, 0, here, re * cosine + im * sine)
            split_store(split_ref, leaf, SPAN, here, im * cosine - re * sine)
        return carry

    return stage


def shifted_rows(here, by):
    return pl.ds(here.start + by, here.size)


def combine_stage(left_ref, right_ref, split_ref, rows_here, conjugate):
    def stage(part, row, carry):
        here = in_span(part, row, rows_here)
        below = shifted_rows(here, SPAN)
        for leaf in range(2 * left_ref.shape[0]):
            pair, lanes = leaf_place(leaf)
            left_re = left_ref[pair, here, lanes]
            left_im = left_ref[pair, below, lanes]
            right_re = right_ref[pair, here, lanes]
            right_im = right_ref[pair, below, lanes]
            if conjugate:
                re = left_re * right_re + left_im * right_im
                minus_im = left_im * right_re - left_re * right_im
            else:
                re = left_re * right_re - left_im * right_im
                minus_im = -(left_re * right_im + left_im * right_re)
            split_store(split_ref, leaf, 0, here, re)
            split_store(split_ref, leaf, SPAN, here, minus_im)
        return carry

    return stage


def signal_stage(time_ref, twist_ref, rows_here, write):
    outer = twist_ref.shape[1]
    ratio = SPAN // rows_here
    scale = 1.0 / (SPAN * outer)

    def stage(part, row, carry):
        here = in_span(part, row, rows_here)
        below = shifted_rows(here, SPAN)
        leaves = []
        for leaf in range(outer):
            pair, lanes = leaf_place(leaf)
            cosine = twist_ref[0, leaf, here, :]
            sine = twist_ref[1, leaf, here, :]
            re = time_ref[pair, here, lanes]
            minus_im = time_ref[pair, below, lanes]
            leaves.append((re * cosine + minus_im * sine, re * sine - minus_im * cosine))
        for place, value in enumerate(from_leaves(leaves, scale)):
            carry = write(place * ratio + part, pl.ds(row, CHUNK), value, carry)
        return carry

    return stage


def first_rows(lead, first, taps):
    count = len(lead)
    rows = lead + first
    return [
        functools.reduce(lambda x, y: x + y, [taps[shift] * rows[count + row - shift] for shift in range(count + 1)])
        for row in range(count)
    ]


def first_signals(ahead, own, taps):
    count = len(taps) - 1

    def kind(rows, idx):
        return rows[idx * count : (idx + 1) * count]

    shorts = [first_rows(kind(ahead, idx), kind(own, 3 + idx), taps) for idx in range(3)]
    product = [(k_row * v_row).astype(bf16) for k_row, v_row in zip(shorts[1], shorts[2])]
    back_mix = [grad_row * q_row for grad_row, q_row in zip(kind(own, 6), shorts[0])]
    return shorts, product, back_mix


def first_backs(ahead, own, taps, skip, conv, corr):
    count = len(taps) - 1
    shorts, product, back_mix = first_signals(ahead, own, taps)
    back_q = []
    back_k = []
    back_v = []
    for row in range(count):
        filtered = conv[row] + skip * product[row].astype(f32)
        back_prod = corr[row] + skip * back_mix[row]
        back_q.append(own[6 * count + row] * filtered)
        back_k.append(back_prod * shorts[2][row])
        back_v.append(back_prod * shorts[1][row])
    return back_q + back_k + back_v


def extra_of(signals_ref, piece, rows_here, used):
    rows = signals_ref[piece, 3 * rows_here :, :].astype(f32)
    return [rows[idx : idx + 1] for idx in range(used)]


def tap_rows(taps_ref):
    return [taps_ref[shift : shift + 1, :] for shift in range(taps_ref.shape[0])]


def patch_first_rows(signals_ref, heads_ref, taps_ref, rows_here):
    pieces = signals_ref.shape[0]
    taps = tap_rows(taps_ref)[:-1]
    used = 7 * (len(taps) - 1)
    row_idx = lax.broadcasted_iota(jnp.int32, (TILE_ROWS, LANES), 0)
    ahead = [jnp.zeros((1, LANES), f32)] * used
    for piece in range(pieces):
        own = extra_of(signals_ref, piece, rows_here, used)
        for kind, rows in enumerate(first_signals(ahead, own, taps)[1:]):
            tile = signals_ref[piece, kind * rows_here : kind * rows_here + TILE_ROWS, :].astype(f32)
            for row, value in enumerate(rows):
                tile = jnp.where(row_idx == row, value.astype(f32), tile)
            heads_ref[kind, piece] = tile.astype(bf16)
        ahead = own


def write_edges(signals_ref, results_ref, taps_ref, rows_here):
    pieces = signals_ref.shape[0]
    *taps, skip = tap_rows(taps_ref)
    count = len(taps) - 1
    nothing = jnp.zeros((1, LANES), f32)
    extras = [extra_of(signals_ref, piece, rows_here, 7 * count) for piece in range(pieces)]
    for piece in range(pieces):
        rows = extras[piece - 1][: 3 * count] if piece else [nothing] * (3 * count)
        if piece + 1 < pieces:
            conv, corr = (
                results_ref[piece + 1, kind * rows_here : kind * rows_here + TILE_ROWS, :].astype(f32)
                for kind in range(2)
            )
            rows = rows + first_backs(
                extras[piece], extras[piece + 1], taps, skip,
                [conv[row : row + 1] for row in range(count)], [corr[row : row + 1] for row in range(count)],
            )
        spare = results_ref.shape[1] - 2 * rows_here - len(rows)
        rows.append(jnp.zeros((spare, LANES), f32))
        results_ref[piece, 2 * rows_here :, :] = jnp.concatenate(rows, axis=0).astype(bf16)


def products_kernel(
    rows_here, signals_ref, taps_ref, coarse_ref, fine_ref, matrix_hbm, after_ref, results_hbm, lag_hbm,
    twist_ref, matrix_ref, heads_ref, results_ref, one_split, two_split, lag_split,
    filter_ref, product_ref, cotan_ref, time_ref, sems,
):
    matrix_copy = pltpu.make_async_copy(matrix_hbm, matrix_ref, sems.at[3])
    lag_copy = pltpu.make_async_copy(lag_split, lag_hbm, sems.at[4])
    returns = [
        pltpu.make_async_copy(results_ref.at[:, rows], results_hbm.at[:, rows], sems.at[5 + idx])
        for idx, rows in enumerate(
            (pl.ds(0, rows_here), pl.ds(rows_here, results_ref.shape[1] - rows_here))
        )
    ]

    def leaves(kind, split_ref):
        heads = heads_ref.at[kind] if kind < 2 else None
        return leaves_stage(signals_ref, kind * rows_here, heads, rows_here, twist_ref, split_ref)

    def combine(left_ref, right_ref, split_ref, conjugate):
        return combine_stage(left_ref, right_ref, split_ref, rows_here, conjugate)

    def result(kind, from_ref):
        def write(piece, rows, value, carry):
            place = pl.ds(pl.multiple_of(kind * rows_here + rows.start, CHUNK), CHUNK)
            results_ref[piece, place, :] = value.astype(bf16)
            return carry

        return signal_stage(from_ref, twist_ref, rows_here, write)

    matrix_copy.start()
    run_all([twist_stage(coarse_ref, fine_ref, twist_ref, rows_here)], rows_here)
    run_all([leaves(2, one_split)], rows_here)
    patch_first_rows(signals_ref, heads_ref, taps_ref, rows_here)
    matrix_copy.wait()
    run_all([leaves(0, two_split)], rows_here, (matrix_ref, one_split, filter_ref))
    run_all([leaves(1, one_split)], rows_here, (matrix_ref, two_split, product_ref))
    run_all([combine(filter_ref, product_ref, two_split, False)], rows_here, (matrix_ref, one_split, cotan_ref))
    run_all([combine(filter_ref, cotan_ref, one_split, True)], rows_here, (matrix_ref, two_split, time_ref))
    run_all(
        [combine(product_ref, cotan_ref, lag_split, True), result(0, time_ref)],
        rows_here, (matrix_ref, one_split, filter_ref),
    )
    lag_copy.start()
    returns[0].start()
    run_all([result(1, filter_ref)], rows_here)
    write_edges(signals_ref, results_ref, taps_ref, rows_here)
    returns[1].start()
    lag_copy.wait()
    returns[0].wait()
    returns[1].wait()


def lag_kernel(
    split_hbm, coarse_ref, fine_ref, matrix_hbm, lag_ref, square_ref, twist_ref, matrix_ref, split_ref, time_ref, sems
):
    rows_here = lag_ref.shape[1]
    copies = [
        pltpu.make_async_copy(matrix_hbm, matrix_ref, sems.at[0]),
        pltpu.make_async_copy(split_hbm, split_ref, sems.at[1]),
    ]
    for copy in copies:
        copy.start()
    run_all([twist_stage(coarse_ref, fine_ref, twist_ref, rows_here)], rows_here)
    for copy in copies:
        copy.wait()
    run_all([], rows_here, (matrix_ref, split_ref, time_ref))

    def write(piece, rows, value, carry):
        lag_ref[piece, rows, :] = value.astype(bf16)
        return carry + value * value

    square = run_all(
        [signal_stage(time_ref, twist_ref, rows_here, write)], rows_here, None, jnp.zeros((CHUNK, LANES), f32)
    )
    square_ref[...] = jnp.sum(square, axis=0, keepdims=True)


class Transforms:
    def __init__(self, pieces, rows_here):
        outer = pieces * rows_here // SPAN
        pairs = outer // 2
        coarse = twist_angles(outer, CHUNK * np.arange(CHUNKS)).T
        fine = twist_angles(outer, np.arange(CHUNK))[..., None] * np.ones(LANES)
        self.tables = [
            jnp.asarray(np.concatenate([np.cos(coarse), np.sin(coarse)], axis=1).astype(np.float32)),
            jnp.asarray(np.stack([np.cos(fine), np.sin(fine)]).astype(np.float32)),
            jnp.asarray(matrix_blocks()),
        ]
        self.split = jax.ShapeDtypeStruct((pairs, PASSES * BOTH, 2 * LANES), bf16)
        self.signal = jax.ShapeDtypeStruct((pieces, rows_here, LANES), bf16)
        self.result = jax.ShapeDtypeStruct((pieces, 2 * rows_here + TILE_ROWS, LANES), bf16)
        self.square = jax.ShapeDtypeStruct((1, LANES), f32)
        self.result_work = pltpu.VMEM(self.result.shape, bf16)
        self.work = pltpu.VMEM((pairs, BOTH, 2 * LANES), f32)
        self.split_work = pltpu.VMEM(self.split.shape, bf16)
        self.twist_work = pltpu.VMEM((2, outer, SPAN, LANES), f32)
        self.matrix_work = pltpu.VMEM(self.tables[2].shape, bf16)

    def products(self, signals, taps, after):
        return call(
            functools.partial(products_kernel, self.signal.shape[1]), (self.result, self.split),
            [self.twist_work, self.matrix_work]
            + [pltpu.VMEM((2, signals.shape[0], TILE_ROWS, LANES), bf16), self.result_work]
            + [self.split_work] * 3
            + [self.work] * 4
            + [pltpu.SemaphoreType.DMA((7,))],
            signals, taps, *self.tables, after,
            in_specs=[IN_VMEM, IN_VMEM, IN_SMEM, IN_VMEM, ANYWHERE, ANYWHERE],
            out_specs=(ANYWHERE, ANYWHERE),
        )

    def lag(self, lag_split):
        return call(
            lag_kernel, (self.signal, self.square),
            [self.twist_work, self.matrix_work, self.split_work, self.work, pltpu.SemaphoreType.DMA((2,))],
            lag_split, *self.tables,
            in_specs=[ANYWHERE, IN_SMEM, IN_VMEM, ANYWHERE],
            out_specs=(IN_VMEM, IN_VMEM),
        )


class PlainTransforms:
    def __init__(self, pieces, rows_here):
        self.seq_len = pieces * rows_here
        self.pieces = pieces
        self.outer = self.seq_len // SPAN
        idx = np.arange(SPAN)
        angle = (idx[:, None] * idx[None, :] % SPAN) * (2.0 * np.pi / SPAN)
        self.cosine = jnp.asarray(np.cos(angle), f32)
        self.sine = jnp.asarray(np.sin(angle), f32)
        twist = twist_angles(self.outer, idx)
        self.twist = jnp.asarray(np.stack([np.cos(twist), np.sin(twist)]), f32)[..., None]

    def dot(self, matrix, signal):
        return jnp.einsum("fs,tsc->tfc", matrix, signal, precision=lax.Precision.HIGHEST)

    def spectrum(self, signal):
        parts = signal.astype(f32).reshape(self.outer, SPAN, -1)
        leaves = to_leaves([parts[part] for part in range(self.outer)])
        re = jnp.stack([leaf[0] for leaf in leaves])
        im = jnp.stack([leaf[1] for leaf in leaves])
        twist_re = re * self.twist[0] + im * self.twist[1]
        twist_im = im * self.twist[0] - re * self.twist[1]
        return (
            self.dot(self.cosine, twist_re) + self.dot(self.sine, twist_im),
            self.dot(self.cosine, twist_im) - self.dot(self.sine, twist_re),
        )

    def back(self, re, im):
        time_re = self.dot(self.cosine, re) - self.dot(self.sine, im)
        time_im = self.dot(self.cosine, im) + self.dot(self.sine, re)
        leaf_re = time_re * self.twist[0] - time_im * self.twist[1]
        leaf_im = time_im * self.twist[0] + time_re * self.twist[1]
        parts = from_leaves([(leaf_re[leaf], leaf_im[leaf]) for leaf in range(self.outer)], 1.0 / self.seq_len)
        return jnp.stack(parts).reshape(self.pieces, self.seq_len // self.pieces, -1)

    def products(self, signals, taps_and_skip, after):
        rows_here = self.seq_len // self.pieces
        parts = [signals[:, kind * rows_here : (kind + 1) * rows_here] for kind in range(3)]
        extra = signals[:, 3 * rows_here :].astype(f32)
        rows = [extra[:, idx : idx + 1] for idx in range(extra.shape[1])]
        ahead = [jnp.concatenate([jnp.zeros_like(row[:1]), row[:-1]], axis=0) for row in rows]
        *taps, skip = [taps_and_skip[row][None, None, :] for row in range(taps_and_skip.shape[0])]
        count = len(taps) - 1
        for kind, first in enumerate(first_signals(ahead, rows, taps)[1:]):
            first = jnp.concatenate(first, axis=1)
            parts[kind] = jnp.concatenate([first.astype(bf16), parts[kind][:, first.shape[1] :]], axis=1)
        product, cotan, taps_spec = (self.spectrum(part) for part in parts)
        conv = self.back(
            taps_spec[0] * product[0] - taps_spec[1] * product[1], taps_spec[0] * product[1] + taps_spec[1] * product[0]
        ).astype(bf16)
        corr = self.back(
            taps_spec[0] * cotan[0] + taps_spec[1] * cotan[1], taps_spec[0] * cotan[1] - taps_spec[1] * cotan[0]
        ).astype(bf16)
        lag = (
            product[0] * cotan[0] + product[1] * cotan[1],
            product[0] * cotan[1] - product[1] * cotan[0],
        )
        backs = first_backs(
            ahead, rows, taps, skip,
            [conv[:, row : row + 1].astype(f32) for row in range(count)],
            [corr[:, row : row + 1].astype(f32) for row in range(count)],
        )
        behind = [jnp.concatenate([row[1:], jnp.zeros_like(row[:1])], axis=0) for row in backs]
        edge = jnp.concatenate(ahead[: 3 * count] + behind, axis=1).astype(bf16)
        edge = jnp.pad(edge, ((0, 0), (0, TILE_ROWS - edge.shape[1]), (0, 0)))
        return jnp.concatenate([conv, corr, edge], axis=1), lag

    def lag(self, lag_spec):
        lag = self.back(*lag_spec)
        squares = jnp.sum(lag * lag, axis=(0, 1))
        return lag.astype(bf16), jnp.zeros((1, LANES), f32).at[0, : squares.shape[0]].set(squares)


def group(idx):
    return pl.ds(pl.multiple_of(idx * LANES, LANES), LANES)


def streamed(work, steps, per_step, places, in_count, out_count, kept, *refs):
    moved = in_count + out_count
    hbm = refs[:moved]
    kept_refs = refs[moved : moved + kept]
    held = refs[moved + kept : 2 * moved + kept]
    scratch = refs[2 * moved + kept : -1]
    sems = refs[-1]

    def copy(place, step):
        outside = hbm[place].at[places[place](step)]
        inside = held[place].at[places[place](step)]
        ends = (outside, inside) if place < in_count else (inside, outside)
        return pltpu.make_async_copy(*ends, sems.at[place, step])

    def arrivals(step):
        return [copy(place, step) for place in range(in_count) if places[place](step) is not None]

    for step in range(steps):
        for arrival in arrivals(step):
            arrival.start()
    for step in range(steps):
        for arrival in arrivals(step):
            arrival.wait()

        def one(idx, carry):
            work(idx, held[:in_count], held[in_count:] + kept_refs, scratch)
            return carry

        lax.fori_loop(step * per_step, (step + 1) * per_step, one, 0)
        for place in range(in_count, moved):
            copy(place, step).start()
    for step in range(steps):
        for place in range(in_count, moved):
            copy(place, step).wait()


def stream_call(work, steps, per_step, operands, results, scratch=(), after=(), kept=()):
    arrays = [operand[0] for operand in operands]
    shapes = [jax.ShapeDtypeStruct(array.shape, array.dtype) for array in arrays] + [result[0] for result in results]
    cuts = [entry[1] for entry in list(operands) + list(results)]
    held = [pltpu.VMEM(shape.shape, shape.dtype) for shape in shapes]
    extra = list(after)
    kernel = functools.partial(streamed, work, steps, per_step, cuts, len(arrays), len(results), len(kept))

    def without_extra(*refs):
        kernel(*refs[: len(arrays)], *refs[len(arrays) + len(extra) :])

    return call(
        without_extra,
        tuple(result[0] for result in results) + tuple(kept),
        held + list(scratch) + [pltpu.SemaphoreType.DMA((len(shapes), steps))],
        *arrays, *extra,
        in_specs=[ANYWHERE] * (len(arrays) + len(extra)),
        out_specs=(ANYWHERE,) * len(results) + (IN_VMEM,) * len(kept),
    )


def cut_lanes(width, rank):
    def place(step):
        return (slice(None),) * (rank - 1) + (pl.ds(step * width, width),)

    return place


def cut_groups(per_step):
    def place(step):
        return (pl.ds(step * per_step, per_step),)

    return place


def cut_none(step):
    return None if step else (slice(None),)


def row_blocks(rows_here):
    return [slice(start, start + ROWS) for start in range(0, rows_here, ROWS)]


def extend_rows(lead, in_ref, lanes, ext_ref):
    ext_ref[PAD - lead.shape[0] : PAD, :] = lead
    ext_ref[PAD:, :] = in_ref[:, lanes].astype(f32)


def short_conv(ext_ref, taps, rows):
    result = None
    for shift_idx in range(taps.shape[0]):
        term = taps[shift_idx : shift_idx + 1] * ext_ref[PAD + rows.start - shift_idx : PAD + rows.stop - shift_idx, :]
        result = term if result is None else result + term
    return result


def signals_work(idx, operands, results, exts):
    q_ref, k_ref, v_ref, grad_ref, kernel_ref, taps_ref = operands
    lanes = group(idx)
    taps = taps_ref[:, lanes]
    halo_rows = taps.shape[0] - 1
    rows_here = q_ref.shape[0]
    for ext, in_ref in zip(exts, operands):
        extend_rows(jnp.zeros((halo_rows, LANES), f32), in_ref, lanes, ext)
    for rows in row_blocks(rows_here):
        q_short, k_short, v_short = (short_conv(ext, taps, rows) for ext in exts)
        below = [slice(kind * rows_here + rows.start, kind * rows_here + rows.stop) for kind in range(3)]
        results[0][idx, below[0], :] = (k_short * v_short).astype(bf16)
        results[0][idx, below[1], :] = (grad_ref[rows, lanes].astype(f32) * q_short).astype(bf16)
        results[0][idx, below[2], :] = kernel_ref[rows, lanes].astype(bf16)
    top = grad_ref[0:TILE_ROWS, lanes].astype(f32)[:halo_rows]
    extra = [ext[ext.shape[0] - halo_rows :, :] for ext in exts] + [ext[PAD : PAD + halo_rows, :] for ext in exts]
    extra_count = results[0].shape[1] - 3 * rows_here
    blank = jnp.zeros((extra_count - 7 * halo_rows, LANES), f32)
    results[0][idx, 3 * rows_here :, :] = jnp.concatenate(extra + [top, blank], axis=0).astype(bf16)


def short_work(idx, operands, results, exts):
    lanes = group(idx)
    taps = operands[3][:, lanes]
    for ext, in_ref in zip(exts, operands):
        extend_rows(jnp.zeros((taps.shape[0] - 1, LANES), f32), in_ref, lanes, ext)
    for rows in row_blocks(operands[0].shape[0]):
        for place, ext in enumerate(exts):
            results[0][place, rows, lanes] = short_conv(ext, taps, rows)


def fold(value):
    return jnp.sum(value.reshape(-1, 8, LANES), axis=0)


def finish_work(idx, operands, results, exts):
    q_ref, k_ref, v_ref, grad_ref, short_ref, taps_ref, skip_ref, long_ref, squares_ref = operands
    mixed_ref, grad_q_ref, grad_k_ref, grad_v_ref, sums_ref = results
    lanes = group(idx)
    taps = taps_ref[:, lanes]
    skip = skip_ref[:, lanes]
    taps_count = taps.shape[0]
    halo_rows = taps_count - 1
    rows_here = q_ref.shape[0]
    sums = [jnp.zeros((8, LANES), f32) for _ in range(taps_count + 1)]
    edge = long_ref[idx, 2 * rows_here :, :].astype(f32)
    for place, ext in enumerate(exts):
        at = (3 + place) * halo_rows
        ext[rows_here : rows_here + halo_rows, :] = edge[at : at + halo_rows]
    row_idx = lax.broadcasted_iota(jnp.int32, (ROWS, LANES), 0)

    def short(place, rows):
        value = short_ref[place, rows, lanes]
        if rows.start == 0:
            for shift_idx in range(1, taps_count):
                terms = jnp.zeros((ROWS, LANES), f32)
                for row in range(shift_idx):
                    at = place * halo_rows + halo_rows + row - shift_idx
                    term = taps[shift_idx : shift_idx + 1] * edge[at : at + 1]
                    terms = jnp.where(row_idx == row, term, terms)
                value = value + terms
        return value

    for rows in row_blocks(rows_here):
        q_short, k_short, v_short = (short(place, rows) for place in range(3))
        product = (k_short * v_short).astype(bf16).astype(f32)
        filtered = long_ref[idx, rows, :].astype(f32) + skip * product
        mixed_ref[rows, lanes] = (q_short * filtered).astype(bf16)
        upstream = grad_ref[rows, lanes].astype(f32)
        back_mix = upstream * q_short
        below = slice(rows_here + rows.start, rows_here + rows.stop)
        back_prod = long_ref[idx, below, :].astype(f32) + skip * back_mix
        sums[taps_count] = sums[taps_count] + fold(back_mix * product)
        exts[0][rows, :] = upstream * filtered
        exts[1][rows, :] = back_prod * v_short
        exts[2][rows, :] = back_prod * k_short
    for ext, in_ref, out_ref in zip(exts, (q_ref, k_ref, v_ref), (grad_q_ref, grad_k_ref, grad_v_ref)):
        for rows in row_blocks(rows_here):
            signal = in_ref[rows, lanes].astype(f32)
            grad = None
            for shift_idx in range(taps_count):
                ahead = ext[rows.start + shift_idx : rows.stop + shift_idx, :]
                term = taps[shift_idx : shift_idx + 1] * ahead
                grad = term if grad is None else grad + term
                sums[shift_idx] = sums[shift_idx] + fold(ahead * signal)
            out_ref[rows, lanes] = grad.astype(bf16)
    extra = slice(sums_ref.shape[1] - LANES, sums_ref.shape[1])
    sums_ref[:, extra] = jnp.zeros((taps_count + 1, LANES), f32)
    sums_ref[0:1, extra] = squares_ref[...]
    for shift_idx in range(taps_count + 1):
        sums_ref[shift_idx : shift_idx + 1, lanes] = jnp.sum(sums[shift_idx], axis=0, keepdims=True)


def norm_kernel(*refs):
    values, totals_ref, square_ref = refs[:-2], refs[-2], refs[-1]
    channels = totals_ref.shape[1] - LANES
    totals = values[0][...]
    if len(values) == 4:
        totals = (totals + values[1][...]) + (values[2][...] + values[3][...])
    totals_ref[...] = totals
    square = jnp.sum(totals[:, :channels] * totals[:, :channels]) + jnp.sum(totals[0:1, channels:])
    square_ref[...] = jnp.full(square_ref.shape, square)


def scale_kernel(limit, totals_ref, norm_ref, lag_ref, taps_out, skip_out, kernel_out):
    taps_count, channels = taps_out.shape
    factor = limit / jnp.maximum(jnp.sqrt(norm_ref[...]), limit)
    for idx in range(channels // LANES):
        lanes = slice(idx * LANES, (idx + 1) * LANES)
        taps_out[:, lanes] = totals_ref[0:taps_count, lanes] * factor
        skip_out[:, lanes] = totals_ref[taps_count : taps_count + 1, lanes] * factor
        kernel_out[:, lanes] = lag_ref[idx].astype(f32) * factor


def exchange(pieces_first):
    return lax.all_to_all(pieces_first, "ctx", split_axis=0, concat_axis=0, tiled=True)


def to_pieces(groups, pieces):
    count, rows, lanes = groups.shape
    if count == pieces:
        return groups
    share = count * lanes // pieces
    split = groups.reshape(count, rows, lanes // share, share)
    return split.transpose(0, 2, 1, 3).reshape(pieces, rows, share)


def to_groups(parts):
    pieces, rows, share = parts.shape
    if share == LANES:
        return parts
    joined = parts.reshape(pieces * share // LANES, LANES // share, rows, share)
    return joined.transpose(0, 2, 1, 3).reshape(-1, rows, LANES)


def partners(value, axis, steps):
    size = lax.axis_size(axis)
    return [value] + [lax.ppermute(value, axis, [(i, i ^ step) for i in range(size)]) for step in steps]


def rounds_of(size):
    rounds = []
    step = 1
    while step < size:
        rounds.append((step, 2 * step, 3 * step) if size // step >= 4 else (step,))
        step *= 4 if size // step >= 4 else 2
    return rounds


def add_up(values):
    if len(values) == 2:
        return values[0] + values[1]
    return (values[0] + values[1]) + (values[2] + values[3])


def body(q_in, k_in, v_in, grad_out, short_filter, kernel, skip):
    pieces = lax.axis_size("ctx")
    sides = lax.axis_size("ch")
    rows_here, channels = q_in.shape
    seq_len = pieces * rows_here
    taps_count = short_filter.shape[0]
    halo_rows = taps_count - 1
    groups = channels // LANES
    share = channels // pieces
    per_step = min(groups, 4)
    steps = groups // per_step
    lanes2 = cut_lanes(per_step * LANES, 2)
    lanes3 = cut_lanes(per_step * LANES, 3)
    skip_row = skip.reshape(1, channels)
    transforms = (Transforms if share == LANES else PlainTransforms)(pieces, rows_here)
    stream = functools.partial(stream_call, steps=steps, per_step=per_step)

    flat = jax.ShapeDtypeStruct((rows_here, channels), bf16)
    extra_rows = -(-7 * halo_rows // TILE_ROWS) * TILE_ROWS
    sent = jax.ShapeDtypeStruct((groups, 3 * rows_here + extra_rows, LANES), bf16)
    exts = [pltpu.VMEM((rows_here + PAD, LANES), f32)] * 3

    (signals,) = stream(
        signals_work,
        operands=[(x, lanes2) for x in (q_in, k_in, v_in, grad_out, kernel, short_filter)],
        results=[(sent, cut_groups(per_step))],
        scratch=exts,
    )
    signals_here = exchange(to_pieces(signals, pieces))
    (short,) = stream(
        short_work,
        operands=[(x, lanes2) for x in (q_in, k_in, v_in, short_filter)],
        results=[(jax.ShapeDtypeStruct((3, rows_here, channels), f32), lanes3)],
        scratch=exts,
        after=[signals],
    )
    taps_and_skip = jnp.concatenate([short_filter, skip_row], axis=0)
    taps_here = lax.dynamic_slice_in_dim(taps_and_skip, lax.axis_index("ctx") * share, share, axis=1)
    long_here, lag_spec = transforms.products(signals_here, taps_here, short)
    long = to_groups(exchange(long_here))
    lag_here, lag_squares = transforms.lag(lag_spec)
    lag = to_groups(exchange(lag_here))

    mixed, grad_q, grad_k, grad_v, sums = stream(
        finish_work,
        operands=[(x, lanes2) for x in (q_in, k_in, v_in, grad_out)]
        + [(short, lanes3), (short_filter, lanes2), (skip_row, lanes2)]
        + [(long, cut_groups(per_step)), (lag_squares, cut_none)],
        results=[(flat, lanes2)] * 4,
        scratch=exts,
        kept=[jax.ShapeDtypeStruct((taps_count + 1, channels + LANES), f32)],
    )

    totals = sums
    rounds = rounds_of(pieces)
    for steps_of in rounds[:-1]:
        totals = add_up(partners(totals, "ctx", steps_of))
    last = partners(totals, "ctx", rounds[-1])
    if len(last) == 2:
        last = [last[0] + last[1]]

    totals, norm_sq = call(
        norm_kernel,
        (jax.ShapeDtypeStruct(totals.shape, f32), jax.ShapeDtypeStruct((1, LANES), f32)),
        [], *last,
        vmem_bytes=SMALL_VMEM_BYTES,
        in_specs=[IN_VMEM] * len(last), out_specs=(IN_VMEM, IN_VMEM),
    )
    for steps_of in rounds_of(sides):
        norm_sq = add_up(partners(norm_sq, "ch", steps_of))

    limit = math.sqrt(float(seq_len * channels * sides))
    grad_short, grad_skip, grad_kernel = call(
        functools.partial(scale_kernel, limit),
        (
            jax.ShapeDtypeStruct((taps_count, channels), f32),
            jax.ShapeDtypeStruct((1, channels), f32),
            jax.ShapeDtypeStruct((rows_here, channels), f32),
        ),
        [],
        totals, norm_sq, lag,
        vmem_bytes=SMALL_VMEM_BYTES,
        in_specs=[IN_VMEM] * 3,
        out_specs=(IN_VMEM,) * 3,
    )
    return mixed, grad_q, grad_k, grad_v, grad_short, grad_skip.reshape(channels), grad_kernel


def solution(mesh):
    in_specs = (
        P("ctx", "ch"),
        P("ctx", "ch"),
        P("ctx", "ch"),
        P("ctx", "ch"),
        P(None, "ch"),
        P("ctx", "ch"),
        P("ch"),
    )
    out_specs = (
        P("ctx", "ch"),
        P("ctx", "ch"),
        P("ctx", "ch"),
        P("ctx", "ch"),
        P(None, "ch"),
        P("ch"),
        P("ctx", "ch"),
    )
    return jax.shard_map(body, mesh=mesh, in_specs=in_specs, out_specs=out_specs, check_vma=False)
```

```python
import functools
import math

import jax
import jax.numpy as jnp
import ml_dtypes
import numpy as np
from jax import lax
from jax.experimental import pallas as pl
from jax.experimental.pallas import tpu as pltpu
from jax.sharding import PartitionSpec as P

LANES = 128
SPAN = 256
BOTH = 2 * SPAN
CHUNK = 16
CHUNKS = SPAN // CHUNK
PAD = 8
ROWS = 32
PASSES = 1
TILE_ROWS = 16
VMEM_BYTES = 60 * 1024 * 1024
SMALL_VMEM_BYTES = 8 * 1024 * 1024

f32 = jnp.float32
bf16 = jnp.bfloat16

IN_VMEM = pl.BlockSpec(memory_space=pltpu.VMEM)
IN_SMEM = pl.BlockSpec(memory_space=pltpu.SMEM)
ANYWHERE = pl.BlockSpec(memory_space=pl.ANY)


def call(kernel, outs, scratch, *args, vmem_bytes=VMEM_BYTES, **options):
    return pl.pallas_call(
        kernel,
        out_shape=outs,
        scratch_shapes=scratch,
        compiler_params=pltpu.CompilerParams(vmem_limit_bytes=vmem_bytes),
        **options,
    )(*args)


def leaf_phases(count):
    return [(4 * leaf + 1) / (4 * count) for leaf in range(count)]


def root_times(re, im, num, den, sign):
    if num == 0:
        return re, im
    if 4 * num == den:
        return (im, -re) if sign < 0 else (-im, re)
    cosine = math.cos(2.0 * math.pi * num / den)
    sine = sign * math.sin(2.0 * math.pi * num / den)
    if 8 * num == den:
        return ((re + im) * cosine, (im - re) * cosine) if sign < 0 else ((re - im) * cosine, (re + im) * cosine)
    if 8 * num == 3 * den:
        return ((re - im) * cosine, (re + im) * cosine) if sign < 0 else ((re + im) * cosine, (im - re) * cosine)
    return re * cosine - im * sine, im * cosine + re * sine


def short_fft(values, sign):
    count = len(values)
    if count == 1:
        return values
    even = short_fft(values[0::2], sign)
    odd = short_fft(values[1::2], sign)
    first = []
    second = []
    for num in range(count // 2):
        re, im = root_times(*odd[num], num, count, sign)
        first.append((even[num][0] + re, even[num][1] + im))
        second.append((even[num][0] - re, even[num][1] - im))
    return first + second


def to_leaves(parts):
    count = len(parts)
    turned = []
    for idx, part in enumerate(parts):
        angle = 2.0 * math.pi * idx / (4 * count)
        turned.append((part * math.cos(angle), part * (-math.sin(angle))) if idx else (part, jnp.zeros_like(part)))
    return short_fft(turned, -1)


def from_leaves(leaves, scale):
    count = len(leaves)
    parts = []
    for idx, (re, im) in enumerate(short_fft(leaves, 1)):
        angle = 2.0 * math.pi * idx / (4 * count)
        if idx == 0:
            parts.append(re * scale)
        else:
            parts.append(re * (math.cos(angle) * scale) - im * (math.sin(angle) * scale))
    return parts


def dft_matrix():
    idx = np.arange(SPAN)
    angle = (idx[:, None] * idx[None, :] % SPAN) * (2.0 * np.pi / SPAN)
    cosine, sine = np.cos(angle), np.sin(angle)
    return np.block([[cosine, sine], [-sine, cosine]])


def twist_angles(outer, inner):
    return np.asarray(leaf_phases(outer))[:, None] * np.asarray(inner)[None, :] * (2.0 * np.pi / SPAN)


def matrix_blocks():
    matrix = dft_matrix()
    high = matrix.astype(ml_dtypes.bfloat16)
    low = (matrix - high.astype(np.float64)).astype(ml_dtypes.bfloat16)
    return np.concatenate([high, low, high][:PASSES], axis=1)


def leaf_place(leaf):
    return leaf // 2, slice((leaf % 2) * LANES, (leaf % 2 + 1) * LANES)


def split_store(ref, leaf, below, here, value):
    pair, lanes = leaf_place(leaf)
    high = value.astype(bf16)
    for block in range(PASSES):
        part = high
        if PASSES == 3 and block == 2:
            part = (value - high.astype(f32)).astype(bf16)
        ref[pair, shifted_rows(here, block * BOTH + below), lanes] = part


def run_all(stages, rows_here, matmul=None, carry=0):
    tiles = matmul[2].shape[0] if matmul else 4
    per_tile = CHUNKS // tiles
    in_part = rows_here // CHUNK
    for tile in range(tiles):
        if matmul:
            matrix_ref, split_ref, result_ref = matmul
            result_ref[tile] = jnp.dot(matrix_ref[...], split_ref[tile], preferred_element_type=f32)
        for chunk in range(tile * per_tile, (tile + 1) * per_tile):
            for stage in stages:
                carry = stage(chunk // in_part, chunk % in_part * CHUNK, carry)
    return carry


def in_span(part, row, rows_here):
    return pl.ds(part * rows_here + row, CHUNK)


def twist_stage(coarse_ref, fine_ref, twist_ref, rows_here):
    outer = twist_ref.shape[1]

    def stage(part, row, carry):
        here = in_span(part, row, rows_here)
        idx = part * (rows_here // CHUNK) + row // CHUNK
        for leaf in range(outer):
            far_cosine = coarse_ref[idx, leaf]
            far_sine = coarse_ref[idx, outer + leaf]
            cosine = fine_ref[0, leaf]
            sine = fine_ref[1, leaf]
            twist_ref[0, leaf, here, :] = far_cosine * cosine - far_sine * sine
            twist_ref[1, leaf, here, :] = far_sine * cosine + far_cosine * sine
        return carry

    return stage


def leaves_stage(signals_ref, first_row, heads_ref, rows_here, twist_ref, split_ref):
    outer = twist_ref.shape[1]
    ratio = SPAN // rows_here

    def stage(part, row, carry):
        here = in_span(part, row, rows_here)
        rows = pl.ds(first_row + row, CHUNK)
        parts = [signals_ref[place * ratio + part, rows, :] for place in range(outer)]
        if heads_ref is not None and row == 0:
            parts = [heads_ref[place * ratio + part] for place in range(outer)]
        parts = [value.astype(f32) for value in parts]
        for leaf, (re, im) in enumerate(to_leaves(parts)):
            cosine = twist_ref[0, leaf, here, :]
            sine = twist_ref[1, leaf, here, :]
            split_store(split_ref, leaf, 0, here, re * cosine + im * sine)
            split_store(split_ref, leaf, SPAN, here, im * cosine - re * sine)
        return carry

    return stage


def shifted_rows(here, by):
    return pl.ds(here.start + by, here.size)


def combine_stage(left_ref, right_ref, split_ref, rows_here, conjugate):
    def stage(part, row, carry):
        here = in_span(part, row, rows_here)
        below = shifted_rows(here, SPAN)
        for leaf in range(2 * left_ref.shape[0]):
            pair, lanes = leaf_place(leaf)
            left_re = left_ref[pair, here, lanes]
            left_im = left_ref[pair, below, lanes]
            right_re = right_ref[pair, here, lanes]
            right_im = right_ref[pair, below, lanes]
            if conjugate:
                re = left_re * right_re + left_im * right_im
                minus_im = left_im * right_re - left_re * right_im
            else:
                re = left_re * right_re - left_im * right_im
                minus_im = -(left_re * right_im + left_im * right_re)
            split_store(split_ref, leaf, 0, here, re)
            split_store(split_ref, leaf, SPAN, here, minus_im)
        return carry

    return stage


def signal_stage(time_ref, twist_ref, rows_here, write):
    outer = twist_ref.shape[1]
    ratio = SPAN // rows_here
    scale = 1.0 / (SPAN * outer)

    def stage(part, row, carry):
        here = in_span(part, row, rows_here)
        below = shifted_rows(here, SPAN)
        leaves = []
        for leaf in range(outer):
            pair, lanes = leaf_place(leaf)
            cosine = twist_ref[0, leaf, here, :]
            sine = twist_ref[1, leaf, here, :]
            re = time_ref[pair, here, lanes]
            minus_im = time_ref[pair, below, lanes]
            leaves.append((re * cosine + minus_im * sine, re * sine - minus_im * cosine))
        for place, value in enumerate(from_leaves(leaves, scale)):
            carry = write(place * ratio + part, pl.ds(row, CHUNK), value, carry)
        return carry

    return stage


def first_rows(lead, first, taps):
    count = len(lead)
    rows = lead + first
    return [
        functools.reduce(lambda x, y: x + y, [taps[shift] * rows[count + row - shift] for shift in range(count + 1)])
        for row in range(count)
    ]


def first_signals(ahead, own, taps):
    count = len(taps) - 1

    def kind(rows, idx):
        return rows[idx * count : (idx + 1) * count]

    shorts = [first_rows(kind(ahead, idx), kind(own, 3 + idx), taps) for idx in range(3)]
    product = [(k_row * v_row).astype(bf16) for k_row, v_row in zip(shorts[1], shorts[2])]
    back_mix = [grad_row * q_row for grad_row, q_row in zip(kind(own, 6), shorts[0])]
    return shorts, product, back_mix


def first_backs(ahead, own, taps, skip, conv, corr):
    count = len(taps) - 1
    shorts, product, back_mix = first_signals(ahead, own, taps)
    back_q = []
    back_k = []
    back_v = []
    for row in range(count):
        filtered = conv[row] + skip * product[row].astype(f32)
        back_prod = corr[row] + skip * back_mix[row]
        back_q.append(own[6 * count + row] * filtered)
        back_k.append(back_prod * shorts[2][row])
        back_v.append(back_prod * shorts[1][row])
    return back_q + back_k + back_v


def extra_of(signals_ref, piece, rows_here, used):
    rows = signals_ref[piece, 3 * rows_here :, :].astype(f32)
    return [rows[idx : idx + 1] for idx in range(used)]


def tap_rows(taps_ref):
    return [taps_ref[shift : shift + 1, :] for shift in range(taps_ref.shape[0])]


def patch_first_rows(signals_ref, heads_ref, taps_ref, rows_here):
    pieces = signals_ref.shape[0]
    taps = tap_rows(taps_ref)[:-1]
    used = 7 * (len(taps) - 1)
    row_idx = lax.broadcasted_iota(jnp.int32, (TILE_ROWS, LANES), 0)
    ahead = [jnp.zeros((1, LANES), f32)] * used
    for piece in range(pieces):
        own = extra_of(signals_ref, piece, rows_here, used)
        for kind, rows in enumerate(first_signals(ahead, own, taps)[1:]):
            tile = signals_ref[piece, kind * rows_here : kind * rows_here + TILE_ROWS, :].astype(f32)
            for row, value in enumerate(rows):
                tile = jnp.where(row_idx == row, value.astype(f32), tile)
            heads_ref[kind, piece] = tile.astype(bf16)
        ahead = own


def write_edges(signals_ref, results_ref, taps_ref, rows_here):
    pieces = signals_ref.shape[0]
    *taps, skip = tap_rows(taps_ref)
    count = len(taps) - 1
    nothing = jnp.zeros((1, LANES), f32)
    extras = [extra_of(signals_ref, piece, rows_here, 7 * count) for piece in range(pieces)]
    for piece in range(pieces):
        rows = extras[piece - 1][: 3 * count] if piece else [nothing] * (3 * count)
        if piece + 1 < pieces:
            conv, corr = (
                results_ref[piece + 1, kind * rows_here : kind * rows_here + TILE_ROWS, :].astype(f32)
                for kind in range(2)
            )
            rows = rows + first_backs(
                extras[piece], extras[piece + 1], taps, skip,
                [conv[row : row + 1] for row in range(count)], [corr[row : row + 1] for row in range(count)],
            )
        spare = results_ref.shape[1] - 2 * rows_here - len(rows)
        rows.append(jnp.zeros((spare, LANES), f32))
        results_ref[piece, 2 * rows_here :, :] = jnp.concatenate(rows, axis=0).astype(bf16)


def products_kernel(
    rows_here, signals_hbm, taps_ref, coarse_ref, fine_ref, matrix_hbm, after_ref, results_hbm, lag_hbm, same_hbm,
    signals_ref, twist_ref, matrix_ref, heads_ref, results_ref, one_split, two_split, lag_split,
    filter_ref, product_ref, cotan_ref, time_ref, sems,
):
    filter_rows = pl.ds(2 * rows_here, rows_here)
    extra_rows = pl.ds(3 * rows_here, signals_ref.shape[1] - 3 * rows_here)
    signal_rows = pl.ds(0, 2 * rows_here)
    arrivals = [
        pltpu.make_async_copy(signals_hbm.at[:, rows], signals_ref.at[:, rows], sems.at[idx])
        for idx, rows in enumerate((filter_rows, extra_rows, signal_rows))
    ]
    matrix_copy = pltpu.make_async_copy(matrix_hbm, matrix_ref, sems.at[3])
    lag_copy = pltpu.make_async_copy(lag_split, lag_hbm, sems.at[4])
    returns = [
        pltpu.make_async_copy(results_ref.at[:, rows], results_hbm.at[:, rows], sems.at[5 + idx])
        for idx, rows in enumerate(
            (pl.ds(0, rows_here), pl.ds(rows_here, results_ref.shape[1] - rows_here))
        )
    ]

    def leaves(kind, split_ref):
        heads = heads_ref.at[kind] if kind < 2 else None
        return leaves_stage(signals_ref, kind * rows_here, heads, rows_here, twist_ref, split_ref)

    def combine(left_ref, right_ref, split_ref, conjugate):
        return combine_stage(left_ref, right_ref, split_ref, rows_here, conjugate)

    def result(kind, from_ref):
        def write(piece, rows, value, carry):
            place = pl.ds(kind * rows_here + rows.start, CHUNK)
            results_ref[piece, place, :] = value.astype(bf16)
            return carry

        return signal_stage(from_ref, twist_ref, rows_here, write)

    for copy in arrivals + [matrix_copy]:
        copy.start()
    run_all([twist_stage(coarse_ref, fine_ref, twist_ref, rows_here)], rows_here)
    arrivals[0].wait()
    run_all([leaves(2, one_split)], rows_here)
    arrivals[1].wait()
    arrivals[2].wait()
    patch_first_rows(signals_ref, heads_ref, taps_ref, rows_here)
    matrix_copy.wait()
    run_all([leaves(0, two_split)], rows_here, (matrix_ref, one_split, filter_ref))
    run_all([leaves(1, one_split)], rows_here, (matrix_ref, two_split, product_ref))
    run_all([combine(filter_ref, product_ref, two_split, False)], rows_here, (matrix_ref, one_split, cotan_ref))
    run_all([combine(filter_ref, cotan_ref, one_split, True)], rows_here, (matrix_ref, two_split, time_ref))
    run_all(
        [combine(product_ref, cotan_ref, lag_split, True), result(0, time_ref)],
        rows_here, (matrix_ref, one_split, filter_ref),
    )
    lag_copy.start()
    returns[0].start()
    run_all([result(1, filter_ref)], rows_here)
    write_edges(signals_ref, results_ref, taps_ref, rows_here)
    returns[1].start()
    lag_copy.wait()
    returns[0].wait()
    returns[1].wait()


def lag_kernel(
    split_hbm, coarse_ref, fine_ref, matrix_hbm, lag_ref, square_ref, twist_ref, matrix_ref, split_ref, time_ref, sems
):
    rows_here = lag_ref.shape[1]
    copies = [
        pltpu.make_async_copy(matrix_hbm, matrix_ref, sems.at[0]),
        pltpu.make_async_copy(split_hbm, split_ref, sems.at[1]),
    ]
    for copy in copies:
        copy.start()
    run_all([twist_stage(coarse_ref, fine_ref, twist_ref, rows_here)], rows_here)
    for copy in copies:
        copy.wait()
    run_all([], rows_here, (matrix_ref, split_ref, time_ref))

    def write(piece, rows, value, carry):
        lag_ref[piece, rows, :] = value.astype(bf16)
        return carry + value * value

    square = run_all(
        [signal_stage(time_ref, twist_ref, rows_here, write)], rows_here, None, jnp.zeros((CHUNK, LANES), f32)
    )
    square_ref[...] = jnp.sum(square, axis=0, keepdims=True)


class Transforms:
    def __init__(self, pieces, rows_here):
        outer = pieces * rows_here // SPAN
        pairs = outer // 2
        coarse = twist_angles(outer, CHUNK * np.arange(CHUNKS)).T
        fine = twist_angles(outer, np.arange(CHUNK))[..., None] * np.ones(LANES)
        self.tables = [
            jnp.asarray(np.concatenate([np.cos(coarse), np.sin(coarse)], axis=1).astype(np.float32)),
            jnp.asarray(np.stack([np.cos(fine), np.sin(fine)]).astype(np.float32)),
            jnp.asarray(matrix_blocks()),
        ]
        self.split = jax.ShapeDtypeStruct((pairs, PASSES * BOTH, 2 * LANES), bf16)
        self.signal = jax.ShapeDtypeStruct((pieces, rows_here, LANES), bf16)
        self.result = jax.ShapeDtypeStruct((pieces, 2 * rows_here + TILE_ROWS, LANES), bf16)
        self.square = jax.ShapeDtypeStruct((1, LANES), f32)
        self.result_work = pltpu.VMEM(self.result.shape, bf16)
        self.work = pltpu.VMEM((pairs, BOTH, 2 * LANES), f32)
        self.split_work = pltpu.VMEM(self.split.shape, bf16)
        self.twist_work = pltpu.VMEM((2, outer, SPAN, LANES), f32)
        self.matrix_work = pltpu.VMEM(self.tables[2].shape, bf16)

    def products(self, signals, taps, after):
        results, lag_split, _ = call(
            functools.partial(products_kernel, self.signal.shape[1]),
            (self.result, self.split, jax.ShapeDtypeStruct(signals.shape, bf16)),
            [pltpu.VMEM(signals.shape, bf16), self.twist_work, self.matrix_work]
            + [pltpu.VMEM((2, signals.shape[0], TILE_ROWS, LANES), bf16), self.result_work]
            + [self.split_work] * 3
            + [self.work] * 4
            + [pltpu.SemaphoreType.DMA((7,))],
            signals, taps, *self.tables, after,
            in_specs=[ANYWHERE, IN_VMEM, IN_SMEM, IN_VMEM, ANYWHERE, ANYWHERE],
            out_specs=(ANYWHERE, ANYWHERE, ANYWHERE),
            input_output_aliases={0: 2},
        )
        return results, lag_split

    def lag(self, lag_split):
        return call(
            lag_kernel, (self.signal, self.square),
            [self.twist_work, self.matrix_work, self.split_work, self.work, pltpu.SemaphoreType.DMA((2,))],
            lag_split, *self.tables,
            in_specs=[ANYWHERE, IN_SMEM, IN_VMEM, ANYWHERE],
            out_specs=(IN_VMEM, IN_VMEM),
        )


class PlainTransforms:
    def __init__(self, pieces, rows_here):
        self.seq_len = pieces * rows_here
        self.pieces = pieces
        self.outer = self.seq_len // SPAN
        idx = np.arange(SPAN)
        angle = (idx[:, None] * idx[None, :] % SPAN) * (2.0 * np.pi / SPAN)
        self.cosine = jnp.asarray(np.cos(angle), f32)
        self.sine = jnp.asarray(np.sin(angle), f32)
        twist = twist_angles(self.outer, idx)
        self.twist = jnp.asarray(np.stack([np.cos(twist), np.sin(twist)]), f32)[..., None]

    def dot(self, matrix, signal):
        return jnp.einsum("fs,tsc->tfc", matrix, signal, precision=lax.Precision.HIGHEST)

    def spectrum(self, signal):
        parts = signal.astype(f32).reshape(self.outer, SPAN, -1)
        leaves = to_leaves([parts[part] for part in range(self.outer)])
        re = jnp.stack([leaf[0] for leaf in leaves])
        im = jnp.stack([leaf[1] for leaf in leaves])
        twist_re = re * self.twist[0] + im * self.twist[1]
        twist_im = im * self.twist[0] - re * self.twist[1]
        return (
            self.dot(self.cosine, twist_re) + self.dot(self.sine, twist_im),
            self.dot(self.cosine, twist_im) - self.dot(self.sine, twist_re),
        )

    def back(self, re, im):
        time_re = self.dot(self.cosine, re) - self.dot(self.sine, im)
        time_im = self.dot(self.cosine, im) + self.dot(self.sine, re)
        leaf_re = time_re * self.twist[0] - time_im * self.twist[1]
        leaf_im = time_im * self.twist[0] + time_re * self.twist[1]
        parts = from_leaves([(leaf_re[leaf], leaf_im[leaf]) for leaf in range(self.outer)], 1.0 / self.seq_len)
        return jnp.stack(parts).reshape(self.pieces, self.seq_len // self.pieces, -1)

    def products(self, signals, taps_and_skip, after):
        rows_here = self.seq_len // self.pieces
        parts = [signals[:, kind * rows_here : (kind + 1) * rows_here] for kind in range(3)]
        extra = signals[:, 3 * rows_here :].astype(f32)
        rows = [extra[:, idx : idx + 1] for idx in range(extra.shape[1])]
        ahead = [jnp.concatenate([jnp.zeros_like(row[:1]), row[:-1]], axis=0) for row in rows]
        *taps, skip = [taps_and_skip[row][None, None, :] for row in range(taps_and_skip.shape[0])]
        count = len(taps) - 1
        for kind, first in enumerate(first_signals(ahead, rows, taps)[1:]):
            first = jnp.concatenate(first, axis=1)
            parts[kind] = jnp.concatenate([first.astype(bf16), parts[kind][:, first.shape[1] :]], axis=1)
        product, cotan, taps_spec = (self.spectrum(part) for part in parts)
        conv = self.back(
            taps_spec[0] * product[0] - taps_spec[1] * product[1], taps_spec[0] * product[1] + taps_spec[1] * product[0]
        ).astype(bf16)
        corr = self.back(
            taps_spec[0] * cotan[0] + taps_spec[1] * cotan[1], taps_spec[0] * cotan[1] - taps_spec[1] * cotan[0]
        ).astype(bf16)
        lag = (
            product[0] * cotan[0] + product[1] * cotan[1],
            product[0] * cotan[1] - product[1] * cotan[0],
        )
        backs = first_backs(
            ahead, rows, taps, skip,
            [conv[:, row : row + 1].astype(f32) for row in range(count)],
            [corr[:, row : row + 1].astype(f32) for row in range(count)],
        )
        behind = [jnp.concatenate([row[1:], jnp.zeros_like(row[:1])], axis=0) for row in backs]
        edge = jnp.concatenate(ahead[: 3 * count] + behind, axis=1).astype(bf16)
        edge = jnp.pad(edge, ((0, 0), (0, TILE_ROWS - edge.shape[1]), (0, 0)))
        return jnp.concatenate([conv, corr, edge], axis=1), lag

    def lag(self, lag_spec):
        lag = self.back(*lag_spec)
        squares = jnp.sum(lag * lag, axis=(0, 1))
        return lag.astype(bf16), jnp.zeros((1, LANES), f32).at[0, : squares.shape[0]].set(squares)


def group(idx):
    return pl.ds(pl.multiple_of(idx * LANES, LANES), LANES)


def streamed(work, steps, per_step, places, in_count, out_count, kept, *refs):
    moved = in_count + out_count
    hbm = refs[:moved]
    kept_refs = refs[moved : moved + kept]
    held = refs[moved + kept : 2 * moved + kept]
    scratch = refs[2 * moved + kept : -1]
    sems = refs[-1]

    def copy(place, step):
        outside = hbm[place].at[places[place](step)]
        inside = held[place].at[places[place](step)]
        ends = (outside, inside) if place < in_count else (inside, outside)
        return pltpu.make_async_copy(*ends, sems.at[place, step])

    def arrivals(step):
        return [copy(place, step) for place in range(in_count) if places[place](step) is not None]

    for step in range(steps):
        for arrival in arrivals(step):
            arrival.start()
    for step in range(steps):
        for arrival in arrivals(step):
            arrival.wait()

        def one(idx, carry):
            work(idx, held[:in_count], held[in_count:] + kept_refs, scratch)
            return carry

        lax.fori_loop(step * per_step, (step + 1) * per_step, one, 0)
        for place in range(in_count, moved):
            copy(place, step).start()
    for step in range(steps):
        for place in range(in_count, moved):
            copy(place, step).wait()


def stream_call(work, steps, per_step, operands, results, scratch=(), after=(), kept=()):
    arrays = [operand[0] for operand in operands]
    shapes = [jax.ShapeDtypeStruct(array.shape, array.dtype) for array in arrays] + [result[0] for result in results]
    cuts = [entry[1] for entry in list(operands) + list(results)]
    held = [pltpu.VMEM(shape.shape, shape.dtype) for shape in shapes]
    extra = list(after)
    kernel = functools.partial(streamed, work, steps, per_step, cuts, len(arrays), len(results), len(kept))

    def without_extra(*refs):
        kernel(*refs[: len(arrays)], *refs[len(arrays) + len(extra) :])

    return call(
        without_extra,
        tuple(result[0] for result in results) + tuple(kept),
        held + list(scratch) + [pltpu.SemaphoreType.DMA((len(shapes), steps))],
        *arrays, *extra,
        in_specs=[ANYWHERE] * (len(arrays) + len(extra)),
        out_specs=(ANYWHERE,) * len(results) + (IN_VMEM,) * len(kept),
    )


def cut_lanes(width, rank):
    def place(step):
        return (slice(None),) * (rank - 1) + (pl.ds(step * width, width),)

    return place


def cut_groups(per_step):
    def place(step):
        return (pl.ds(step * per_step, per_step),)

    return place


def cut_none(step):
    return None if step else (slice(None),)


def row_blocks(rows_here):
    return [slice(start, start + ROWS) for start in range(0, rows_here, ROWS)]


def extend_rows(lead, in_ref, lanes, ext_ref):
    ext_ref[PAD - lead.shape[0] : PAD, :] = lead
    ext_ref[PAD:, :] = in_ref[:, lanes].astype(f32)


def short_conv(ext_ref, taps, rows):
    result = None
    for shift_idx in range(taps.shape[0]):
        term = taps[shift_idx : shift_idx + 1] * ext_ref[PAD + rows.start - shift_idx : PAD + rows.stop - shift_idx, :]
        result = term if result is None else result + term
    return result


def signals_work(idx, operands, results, exts):
    q_ref, k_ref, v_ref, grad_ref, kernel_ref, taps_ref = operands
    lanes = group(idx)
    taps = taps_ref[:, lanes]
    halo_rows = taps.shape[0] - 1
    rows_here = q_ref.shape[0]
    for ext, in_ref in zip(exts, operands):
        extend_rows(jnp.zeros((halo_rows, LANES), f32), in_ref, lanes, ext)
    for rows in row_blocks(rows_here):
        q_short, k_short, v_short = (short_conv(ext, taps, rows) for ext in exts)
        below = [slice(kind * rows_here + rows.start, kind * rows_here + rows.stop) for kind in range(3)]
        results[0][idx, below[0], :] = (k_short * v_short).astype(bf16)
        results[0][idx, below[1], :] = (grad_ref[rows, lanes].astype(f32) * q_short).astype(bf16)
        results[0][idx, below[2], :] = kernel_ref[rows, lanes].astype(bf16)
    top = grad_ref[0:TILE_ROWS, lanes].astype(f32)[:halo_rows]
    extra = [ext[ext.shape[0] - halo_rows :, :] for ext in exts] + [ext[PAD : PAD + halo_rows, :] for ext in exts]
    extra_count = results[0].shape[1] - 3 * rows_here
    blank = jnp.zeros((extra_count - 7 * halo_rows, LANES), f32)
    results[0][idx, 3 * rows_here :, :] = jnp.concatenate(extra + [top, blank], axis=0).astype(bf16)


def short_work(idx, operands, results, exts):
    lanes = group(idx)
    taps = operands[3][:, lanes]
    for ext, in_ref in zip(exts, operands):
        extend_rows(jnp.zeros((taps.shape[0] - 1, LANES), f32), in_ref, lanes, ext)
    for rows in row_blocks(operands[0].shape[0]):
        for place, ext in enumerate(exts):
            results[0][place, rows, lanes] = short_conv(ext, taps, rows)


def fold(value):
    return jnp.sum(value.reshape(-1, 8, LANES), axis=0)


def finish_work(idx, operands, results, exts):
    q_ref, k_ref, v_ref, grad_ref, short_ref, taps_ref, skip_ref, long_ref, squares_ref = operands
    mixed_ref, grad_q_ref, grad_k_ref, grad_v_ref, sums_ref = results
    lanes = group(idx)
    taps = taps_ref[:, lanes]
    skip = skip_ref[:, lanes]
    taps_count = taps.shape[0]
    halo_rows = taps_count - 1
    rows_here = q_ref.shape[0]
    sums = [jnp.zeros((8, LANES), f32) for _ in range(taps_count + 1)]
    edge = long_ref[idx, 2 * rows_here :, :].astype(f32)
    for place, ext in enumerate(exts):
        at = (3 + place) * halo_rows
        ext[rows_here : rows_here + halo_rows, :] = edge[at : at + halo_rows]
    row_idx = lax.broadcasted_iota(jnp.int32, (ROWS, LANES), 0)

    def short(place, rows):
        value = short_ref[place, rows, lanes]
        if rows.start == 0:
            for shift_idx in range(1, taps_count):
                terms = jnp.zeros((ROWS, LANES), f32)
                for row in range(shift_idx):
                    at = place * halo_rows + halo_rows + row - shift_idx
                    term = taps[shift_idx : shift_idx + 1] * edge[at : at + 1]
                    terms = jnp.where(row_idx == row, term, terms)
                value = value + terms
        return value

    for rows in row_blocks(rows_here):
        q_short, k_short, v_short = (short(place, rows) for place in range(3))
        product = (k_short * v_short).astype(bf16).astype(f32)
        filtered = long_ref[idx, rows, :].astype(f32) + skip * product
        mixed_ref[rows, lanes] = (q_short * filtered).astype(bf16)
        upstream = grad_ref[rows, lanes].astype(f32)
        back_mix = upstream * q_short
        below = slice(rows_here + rows.start, rows_here + rows.stop)
        back_prod = long_ref[idx, below, :].astype(f32) + skip * back_mix
        sums[taps_count] = sums[taps_count] + fold(back_mix * product)
        exts[0][rows, :] = upstream * filtered
        exts[1][rows, :] = back_prod * v_short
        exts[2][rows, :] = back_prod * k_short
    for ext, in_ref, out_ref in zip(exts, (q_ref, k_ref, v_ref), (grad_q_ref, grad_k_ref, grad_v_ref)):
        for rows in row_blocks(rows_here):
            signal = in_ref[rows, lanes].astype(f32)
            grad = None
            for shift_idx in range(taps_count):
                ahead = ext[rows.start + shift_idx : rows.stop + shift_idx, :]
                term = taps[shift_idx : shift_idx + 1] * ahead
                grad = term if grad is None else grad + term
                sums[shift_idx] = sums[shift_idx] + fold(ahead * signal)
            out_ref[rows, lanes] = grad.astype(bf16)
    extra = slice(sums_ref.shape[1] - LANES, sums_ref.shape[1])
    sums_ref[:, extra] = jnp.zeros((taps_count + 1, LANES), f32)
    sums_ref[0:1, extra] = squares_ref[...]
    for shift_idx in range(taps_count + 1):
        sums_ref[shift_idx : shift_idx + 1, lanes] = jnp.sum(sums[shift_idx], axis=0, keepdims=True)


def norm_kernel(*refs):
    values, totals_ref, square_ref = refs[:-2], refs[-2], refs[-1]
    channels = totals_ref.shape[1] - LANES
    totals = values[0][...]
    if len(values) == 4:
        totals = (totals + values[1][...]) + (values[2][...] + values[3][...])
    totals_ref[...] = totals
    square = jnp.sum(totals[:, :channels] * totals[:, :channels]) + jnp.sum(totals[0:1, channels:])
    square_ref[...] = jnp.full(square_ref.shape, square)


def add_kernel(*refs):
    refs[-1][...] = add_up([ref[...] for ref in refs[:-1]])


def scale_kernel(limit, totals_ref, norm_ref, lag_ref, taps_out, skip_out, kernel_out):
    taps_count, channels = taps_out.shape
    factor = limit / jnp.maximum(jnp.sqrt(norm_ref[...]), limit)
    for idx in range(channels // LANES):
        lanes = slice(idx * LANES, (idx + 1) * LANES)
        taps_out[:, lanes] = totals_ref[0:taps_count, lanes] * factor
        skip_out[:, lanes] = totals_ref[taps_count : taps_count + 1, lanes] * factor
        kernel_out[:, lanes] = lag_ref[idx].astype(f32) * factor


def exchange(pieces_first):
    return lax.all_to_all(pieces_first, "ctx", split_axis=0, concat_axis=0, tiled=True)


def to_pieces(groups, pieces):
    count, rows, lanes = groups.shape
    if count == pieces:
        return groups
    share = count * lanes // pieces
    split = groups.reshape(count, rows, lanes // share, share)
    return split.transpose(0, 2, 1, 3).reshape(pieces, rows, share)


def to_groups(parts):
    pieces, rows, share = parts.shape
    if share == LANES:
        return parts
    joined = parts.reshape(pieces * share // LANES, LANES // share, rows, share)
    return joined.transpose(0, 2, 1, 3).reshape(-1, rows, LANES)


def partners(value, axis, steps):
    size = lax.axis_size(axis)
    return [value] + [lax.ppermute(value, axis, [(i, i ^ step) for i in range(size)]) for step in steps]


def rounds_of(size):
    rounds = []
    step = 1
    while step < size:
        rounds.append((step, 2 * step, 3 * step) if size // step >= 4 else (step,))
        step *= 4 if size // step >= 4 else 2
    return rounds


def add_up(values):
    if len(values) == 2:
        return values[0] + values[1]
    return (values[0] + values[1]) + (values[2] + values[3])


def body(q_in, k_in, v_in, grad_out, short_filter, kernel, skip):
    pieces = lax.axis_size("ctx")
    sides = lax.axis_size("ch")
    rows_here, channels = q_in.shape
    seq_len = pieces * rows_here
    taps_count = short_filter.shape[0]
    halo_rows = taps_count - 1
    groups = channels // LANES
    share = channels // pieces
    per_step = min(groups, 4)
    steps = groups // per_step
    lanes2 = cut_lanes(per_step * LANES, 2)
    lanes3 = cut_lanes(per_step * LANES, 3)
    skip_row = skip.reshape(1, channels)
    transforms = (Transforms if share == LANES else PlainTransforms)(pieces, rows_here)
    stream = functools.partial(stream_call, steps=steps, per_step=per_step)

    flat = jax.ShapeDtypeStruct((rows_here, channels), bf16)
    extra_rows = -(-7 * halo_rows // TILE_ROWS) * TILE_ROWS
    sent = jax.ShapeDtypeStruct((groups, 3 * rows_here + extra_rows, LANES), bf16)
    exts = [pltpu.VMEM((rows_here + PAD, LANES), f32)] * 3

    (signals,) = stream(
        signals_work,
        operands=[(x, lanes2) for x in (q_in, k_in, v_in, grad_out, kernel, short_filter)],
        results=[(sent, cut_groups(per_step))],
        scratch=exts,
    )
    signals_here = exchange(to_pieces(signals, pieces))
    (short,) = stream(
        short_work,
        operands=[(x, lanes2) for x in (q_in, k_in, v_in, short_filter)],
        results=[(jax.ShapeDtypeStruct((3, rows_here, channels), f32), lanes3)],
        scratch=exts,
        after=[signals],
    )
    taps_and_skip = jnp.concatenate([short_filter, skip_row], axis=0)
    taps_here = lax.dynamic_slice_in_dim(taps_and_skip, lax.axis_index("ctx") * share, share, axis=1)
    long_here, lag_spec = transforms.products(signals_here, taps_here, short)
    long = to_groups(exchange(long_here))
    lag_here, lag_squares = transforms.lag(lag_spec)
    lag = to_groups(exchange(lag_here))

    mixed, grad_q, grad_k, grad_v, sums = stream(
        finish_work,
        operands=[(x, lanes2) for x in (q_in, k_in, v_in, grad_out)]
        + [(short, lanes3), (short_filter, lanes2), (skip_row, lanes2)]
        + [(long, cut_groups(per_step)), (lag_squares, cut_none)],
        results=[(flat, lanes2)] * 4,
        scratch=exts,
        kept=[jax.ShapeDtypeStruct((taps_count + 1, channels + LANES), f32)],
    )

    totals = sums
    rounds = rounds_of(pieces)
    for steps_of in rounds[:-1]:
        values = partners(totals, "ctx", steps_of)
        totals = call(
            add_kernel, jax.ShapeDtypeStruct(totals.shape, f32), [], *values,
            vmem_bytes=SMALL_VMEM_BYTES, in_specs=[IN_VMEM] * len(values), out_specs=IN_VMEM,
        )
    last = partners(totals, "ctx", rounds[-1])
    if len(last) == 2:
        last = [last[0] + last[1]]

    totals, norm_sq = call(
        norm_kernel,
        (jax.ShapeDtypeStruct(totals.shape, f32), jax.ShapeDtypeStruct((1, LANES), f32)),
        [], *last,
        vmem_bytes=SMALL_VMEM_BYTES,
        in_specs=[IN_VMEM] * len(last), out_specs=(IN_VMEM, IN_VMEM),
    )
    for steps_of in rounds_of(sides):
        norm_sq = add_up(partners(norm_sq, "ch", steps_of))

    limit = math.sqrt(float(seq_len * channels * sides))
    grad_short, grad_skip, grad_kernel = call(
        functools.partial(scale_kernel, limit),
        (
            jax.ShapeDtypeStruct((taps_count, channels), f32),
            jax.ShapeDtypeStruct((1, channels), f32),
            jax.ShapeDtypeStruct((rows_here, channels), f32),
        ),
        [],
        totals, norm_sq, lag,
        vmem_bytes=SMALL_VMEM_BYTES,
        in_specs=[IN_VMEM] * 3,
        out_specs=(IN_VMEM,) * 3,
    )
    return mixed, grad_q, grad_k, grad_v, grad_short, grad_skip.reshape(channels), grad_kernel


def solution(mesh):
    in_specs = (
        P("ctx", "ch"),
        P("ctx", "ch"),
        P("ctx", "ch"),
        P("ctx", "ch"),
        P(None, "ch"),
        P("ctx", "ch"),
        P("ch"),
    )
    out_specs = (
        P("ctx", "ch"),
        P("ctx", "ch"),
        P("ctx", "ch"),
        P("ctx", "ch"),
        P(None, "ch"),
        P("ch"),
        P("ctx", "ch"),
    )
    return jax.shard_map(body, mesh=mesh, in_specs=in_specs, out_specs=out_specs, check_vma=False)
```

```python
import functools
import math

import jax
import jax.numpy as jnp
import ml_dtypes
import numpy as np
from jax import lax
from jax.experimental import pallas as pl
from jax.experimental.pallas import tpu as pltpu
from jax.sharding import PartitionSpec as P

LANES = 128
SPAN = 256
BOTH = 2 * SPAN
CHUNK = 16
CHUNKS = SPAN // CHUNK
PAD = 8
ROWS = 32
PASSES = 1
TILE_ROWS = 16
VMEM_BYTES = 24 * 1024 * 1024
MOST_VMEM_BYTES = 60 * 1024 * 1024
SMALL_VMEM_BYTES = 8 * 1024 * 1024

f32 = jnp.float32
bf16 = jnp.bfloat16

IN_VMEM = pl.BlockSpec(memory_space=pltpu.VMEM)
IN_SMEM = pl.BlockSpec(memory_space=pltpu.SMEM)
ANYWHERE = pl.BlockSpec(memory_space=pl.ANY)


def call(kernel, outs, scratch, *args, vmem_bytes=VMEM_BYTES, **options):
    return pl.pallas_call(
        kernel,
        out_shape=outs,
        scratch_shapes=scratch,
        compiler_params=pltpu.CompilerParams(vmem_limit_bytes=vmem_bytes),
        **options,
    )(*args)


def leaf_phases(count):
    return [(4 * leaf + 1) / (4 * count) for leaf in range(count)]


def root_times(re, im, num, den, sign):
    if num == 0:
        return re, im
    if 4 * num == den:
        return (im, -re) if sign < 0 else (-im, re)
    cosine = math.cos(2.0 * math.pi * num / den)
    sine = sign * math.sin(2.0 * math.pi * num / den)
    if 8 * num == den:
        return ((re + im) * cosine, (im - re) * cosine) if sign < 0 else ((re - im) * cosine, (re + im) * cosine)
    if 8 * num == 3 * den:
        return ((re - im) * cosine, (re + im) * cosine) if sign < 0 else ((re + im) * cosine, (im - re) * cosine)
    return re * cosine - im * sine, im * cosine + re * sine


def short_fft(values, sign):
    count = len(values)
    if count == 1:
        return values
    even = short_fft(values[0::2], sign)
    odd = short_fft(values[1::2], sign)
    first = []
    second = []
    for num in range(count // 2):
        re, im = root_times(*odd[num], num, count, sign)
        first.append((even[num][0] + re, even[num][1] + im))
        second.append((even[num][0] - re, even[num][1] - im))
    return first + second


def to_leaves(parts):
    count = len(parts)
    turned = []
    for idx, part in enumerate(parts):
        angle = 2.0 * math.pi * idx / (4 * count)
        turned.append((part * math.cos(angle), part * (-math.sin(angle))) if idx else (part, jnp.zeros_like(part)))
    return short_fft(turned, -1)


def from_leaves(leaves, scale):
    count = len(leaves)
    parts = []
    for idx, (re, im) in enumerate(short_fft(leaves, 1)):
        angle = 2.0 * math.pi * idx / (4 * count)
        if idx == 0:
            parts.append(re * scale)
        else:
            parts.append(re * (math.cos(angle) * scale) - im * (math.sin(angle) * scale))
    return parts


def dft_matrix():
    idx = np.arange(SPAN)
    angle = (idx[:, None] * idx[None, :] % SPAN) * (2.0 * np.pi / SPAN)
    cosine, sine = np.cos(angle), np.sin(angle)
    return np.block([[cosine, sine], [-sine, cosine]])


def twist_angles(outer, inner):
    return np.asarray(leaf_phases(outer))[:, None] * np.asarray(inner)[None, :] * (2.0 * np.pi / SPAN)


def matrix_blocks():
    matrix = dft_matrix()
    high = matrix.astype(ml_dtypes.bfloat16)
    low = (matrix - high.astype(np.float64)).astype(ml_dtypes.bfloat16)
    return np.concatenate([high, low, high][:PASSES], axis=1)


def leaf_place(leaf):
    return leaf // 2, slice((leaf % 2) * LANES, (leaf % 2 + 1) * LANES)


def split_store(ref, leaf, below, here, value):
    pair, lanes = leaf_place(leaf)
    high = value.astype(bf16)
    for block in range(PASSES):
        part = high
        if PASSES == 3 and block == 2:
            part = (value - high.astype(f32)).astype(bf16)
        ref[pair, shifted_rows(here, block * BOTH + below), lanes] = part


def run_all(stages, rows_here, matmul=None, carry=0):
    tiles = matmul[2].shape[0] if matmul else 4
    per_tile = CHUNKS // tiles
    in_part = rows_here // CHUNK
    for tile in range(tiles):
        if matmul:
            matrix_ref, split_ref, result_ref = matmul
            result_ref[tile] = jnp.dot(matrix_ref[...], split_ref[tile], preferred_element_type=f32)
        for chunk in range(tile * per_tile, (tile + 1) * per_tile):
            for stage in stages:
                carry = stage(chunk // in_part, chunk % in_part * CHUNK, carry)
    return carry


def in_span(part, row, rows_here):
    return pl.ds(part * rows_here + row, CHUNK)


def twist_stage(coarse_ref, fine_ref, twist_ref, rows_here):
    outer = twist_ref.shape[1]

    def stage(part, row, carry):
        here = in_span(part, row, rows_here)
        idx = part * (rows_here // CHUNK) + row // CHUNK
        for leaf in range(outer):
            far_cosine = coarse_ref[idx, leaf]
            far_sine = coarse_ref[idx, outer + leaf]
            cosine = fine_ref[0, leaf]
            sine = fine_ref[1, leaf]
            twist_ref[0, leaf, here, :] = far_cosine * cosine - far_sine * sine
            twist_ref[1, leaf, here, :] = far_sine * cosine + far_cosine * sine
        return carry

    return stage


def leaves_stage(signals_ref, first_row, heads_ref, rows_here, twist_ref, split_ref):
    outer = twist_ref.shape[1]
    ratio = SPAN // rows_here

    def stage(part, row, carry):
        here = in_span(part, row, rows_here)
        rows = pl.ds(first_row + row, CHUNK)
        parts = [signals_ref[place * ratio + part, rows, :] for place in range(outer)]
        if heads_ref is not None and row == 0:
            parts = [heads_ref[place * ratio + part] for place in range(outer)]
        parts = [value.astype(f32) for value in parts]
        for leaf, (re, im) in enumerate(to_leaves(parts)):
            cosine = twist_ref[0, leaf, here, :]
            sine = twist_ref[1, leaf, here, :]
            split_store(split_ref, leaf, 0, here, re * cosine + im * sine)
            split_store(split_ref, leaf, SPAN, here, im * cosine - re * sine)
        return carry

    return stage


def shifted_rows(here, by):
    return pl.ds(here.start + by, here.size)


def combine_stage(left_ref, right_ref, split_ref, rows_here, conjugate):
    def stage(part, row, carry):
        here = in_span(part, row, rows_here)
        below = shifted_rows(here, SPAN)
        for leaf in range(2 * left_ref.shape[0]):
            pair, lanes = leaf_place(leaf)
            left_re = left_ref[pair, here, lanes]
            left_im = left_ref[pair, below, lanes]
            right_re = right_ref[pair, here, lanes]
            right_im = right_ref[pair, below, lanes]
            if conjugate:
                re = left_re * right_re + left_im * right_im
                minus_im = left_im * right_re - left_re * right_im
            else:
                re = left_re * right_re - left_im * right_im
                minus_im = -(left_re * right_im + left_im * right_re)
            split_store(split_ref, leaf, 0, here, re)
            split_store(split_ref, leaf, SPAN, here, minus_im)
        return carry

    return stage


def signal_stage(time_ref, twist_ref, rows_here, write):
    outer = twist_ref.shape[1]
    ratio = SPAN // rows_here
    scale = 1.0 / (SPAN * outer)

    def stage(part, row, carry):
        here = in_span(part, row, rows_here)
        below = shifted_rows(here, SPAN)
        leaves = []
        for leaf in range(outer):
            pair, lanes = leaf_place(leaf)
            cosine = twist_ref[0, leaf, here, :]
            sine = twist_ref[1, leaf, here, :]
            re = time_ref[pair, here, lanes]
            minus_im = time_ref[pair, below, lanes]
            leaves.append((re * cosine + minus_im * sine, re * sine - minus_im * cosine))
        for place, value in enumerate(from_leaves(leaves, scale)):
            carry = write(place * ratio + part, pl.ds(row, CHUNK), value, carry)
        return carry

    return stage


def first_rows(lead, first, taps):
    count = len(lead)
    rows = lead + first
    return [
        functools.reduce(lambda x, y: x + y, [taps[shift] * rows[count + row - shift] for shift in range(count + 1)])
        for row in range(count)
    ]


def first_signals(ahead, own, taps):
    count = len(taps) - 1

    def kind(rows, idx):
        return rows[idx * count : (idx + 1) * count]

    shorts = [first_rows(kind(ahead, idx), kind(own, 3 + idx), taps) for idx in range(3)]
    product = [(k_row * v_row).astype(bf16) for k_row, v_row in zip(shorts[1], shorts[2])]
    back_mix = [grad_row * q_row for grad_row, q_row in zip(kind(own, 6), shorts[0])]
    return shorts, product, back_mix


def first_backs(ahead, own, taps, skip, conv, corr):
    count = len(taps) - 1
    shorts, product, back_mix = first_signals(ahead, own, taps)
    back_q = []
    back_k = []
    back_v = []
    for row in range(count):
        filtered = conv[row] + skip * product[row].astype(f32)
        back_prod = corr[row] + skip * back_mix[row]
        back_q.append(own[6 * count + row] * filtered)
        back_k.append(back_prod * shorts[2][row])
        back_v.append(back_prod * shorts[1][row])
    return back_q + back_k + back_v


def extra_of(signals_ref, piece, rows_here, used):
    rows = signals_ref[piece, 3 * rows_here :, :].astype(f32)
    return [rows[idx : idx + 1] for idx in range(used)]


def tap_rows(taps_ref):
    return [taps_ref[shift : shift + 1, :] for shift in range(taps_ref.shape[0])]


def patch_first_rows(signals_ref, heads_ref, taps_ref, rows_here):
    pieces = signals_ref.shape[0]
    taps = tap_rows(taps_ref)[:-1]
    used = 7 * (len(taps) - 1)
    row_idx = lax.broadcasted_iota(jnp.int32, (TILE_ROWS, LANES), 0)
    ahead = [jnp.zeros((1, LANES), f32)] * used
    for piece in range(pieces):
        own = extra_of(signals_ref, piece, rows_here, used)
        for kind, rows in enumerate(first_signals(ahead, own, taps)[1:]):
            tile = signals_ref[piece, kind * rows_here : kind * rows_here + TILE_ROWS, :].astype(f32)
            for row, value in enumerate(rows):
                tile = jnp.where(row_idx == row, value.astype(f32), tile)
            heads_ref[kind, piece] = tile.astype(bf16)
        ahead = own


def write_edges(signals_ref, results_ref, taps_ref, rows_here):
    pieces = signals_ref.shape[0]
    *taps, skip = tap_rows(taps_ref)
    count = len(taps) - 1
    nothing = jnp.zeros((1, LANES), f32)
    extras = [extra_of(signals_ref, piece, rows_here, 7 * count) for piece in range(pieces)]
    for piece in range(pieces):
        rows = extras[piece - 1][: 3 * count] if piece else [nothing] * (3 * count)
        if piece + 1 < pieces:
            conv, corr = (
                results_ref[piece + 1, kind * rows_here : kind * rows_here + TILE_ROWS, :].astype(f32)
                for kind in range(2)
            )
            rows = rows + first_backs(
                extras[piece], extras[piece + 1], taps, skip,
                [conv[row : row + 1] for row in range(count)], [corr[row : row + 1] for row in range(count)],
            )
        spare = results_ref.shape[1] - 2 * rows_here - len(rows)
        rows.append(jnp.zeros((spare, LANES), f32))
        results_ref[piece, 2 * rows_here :, :] = jnp.concatenate(rows, axis=0).astype(bf16)


def products_kernel(
    rows_here, signals_ref, taps_ref, coarse_ref, fine_ref, matrix_hbm, after_ref, results_hbm, lag_hbm,
    twist_ref, matrix_ref, heads_ref, results_ref, one_split, two_split, lag_split,
    filter_ref, product_ref, cotan_ref, time_ref, sems,
):
    matrix_copy = pltpu.make_async_copy(matrix_hbm, matrix_ref, sems.at[3])
    lag_copy = pltpu.make_async_copy(lag_split, lag_hbm, sems.at[4])
    returns = [
        pltpu.make_async_copy(results_ref.at[:, rows], results_hbm.at[:, rows], sems.at[5 + idx])
        for idx, rows in enumerate(
            (pl.ds(0, rows_here), pl.ds(rows_here, results_ref.shape[1] - rows_here))
        )
    ]

    def leaves(kind, split_ref):
        heads = heads_ref.at[kind] if kind < 2 else None
        return leaves_stage(signals_ref, kind * rows_here, heads, rows_here, twist_ref, split_ref)

    def combine(left_ref, right_ref, split_ref, conjugate):
        return combine_stage(left_ref, right_ref, split_ref, rows_here, conjugate)

    def result(kind, from_ref):
        def write(piece, rows, value, carry):
            place = pl.ds(kind * rows_here + rows.start, CHUNK)
            results_ref[piece, place, :] = value.astype(bf16)
            return carry

        return signal_stage(from_ref, twist_ref, rows_here, write)

    matrix_copy.start()
    run_all([twist_stage(coarse_ref, fine_ref, twist_ref, rows_here)], rows_here)
    run_all([leaves(2, one_split)], rows_here)
    patch_first_rows(signals_ref, heads_ref, taps_ref, rows_here)
    matrix_copy.wait()
    run_all([leaves(0, two_split)], rows_here, (matrix_ref, one_split, filter_ref))
    run_all([leaves(1, one_split)], rows_here, (matrix_ref, two_split, product_ref))
    run_all([combine(filter_ref, product_ref, two_split, False)], rows_here, (matrix_ref, one_split, cotan_ref))
    run_all([combine(filter_ref, cotan_ref, one_split, True)], rows_here, (matrix_ref, two_split, time_ref))
    run_all(
        [combine(product_ref, cotan_ref, lag_split, True), result(0, time_ref)],
        rows_here, (matrix_ref, one_split, filter_ref),
    )
    lag_copy.start()
    returns[0].start()
    run_all([result(1, filter_ref)], rows_here)
    write_edges(signals_ref, results_ref, taps_ref, rows_here)
    returns[1].start()
    lag_copy.wait()
    returns[0].wait()
    returns[1].wait()


def lag_kernel(
    split_hbm, coarse_ref, fine_ref, matrix_hbm, lag_ref, square_ref, twist_ref, matrix_ref, split_ref, time_ref, sems
):
    rows_here = lag_ref.shape[1]
    copies = [
        pltpu.make_async_copy(matrix_hbm, matrix_ref, sems.at[0]),
        pltpu.make_async_copy(split_hbm, split_ref, sems.at[1]),
    ]
    for copy in copies:
        copy.start()
    run_all([twist_stage(coarse_ref, fine_ref, twist_ref, rows_here)], rows_here)
    for copy in copies:
        copy.wait()
    run_all([], rows_here, (matrix_ref, split_ref, time_ref))

    def write(piece, rows, value, carry):
        lag_ref[piece, rows, :] = value.astype(bf16)
        return carry + value * value

    square = run_all(
        [signal_stage(time_ref, twist_ref, rows_here, write)], rows_here, None, jnp.zeros((CHUNK, LANES), f32)
    )
    square_ref[...] = jnp.sum(square, axis=0, keepdims=True)


class Transforms:
    def __init__(self, pieces, rows_here):
        outer = pieces * rows_here // SPAN
        pairs = outer // 2
        coarse = twist_angles(outer, CHUNK * np.arange(CHUNKS)).T
        fine = twist_angles(outer, np.arange(CHUNK))[..., None] * np.ones(LANES)
        self.tables = [
            jnp.asarray(np.concatenate([np.cos(coarse), np.sin(coarse)], axis=1).astype(np.float32)),
            jnp.asarray(np.stack([np.cos(fine), np.sin(fine)]).astype(np.float32)),
            jnp.asarray(matrix_blocks()),
        ]
        self.split = jax.ShapeDtypeStruct((pairs, PASSES * BOTH, 2 * LANES), bf16)
        self.signal = jax.ShapeDtypeStruct((pieces, rows_here, LANES), bf16)
        self.result = jax.ShapeDtypeStruct((pieces, 2 * rows_here + TILE_ROWS, LANES), bf16)
        self.square = jax.ShapeDtypeStruct((1, LANES), f32)
        self.result_work = pltpu.VMEM(self.result.shape, bf16)
        self.work = pltpu.VMEM((pairs, BOTH, 2 * LANES), f32)
        self.split_work = pltpu.VMEM(self.split.shape, bf16)
        self.twist_work = pltpu.VMEM((2, outer, SPAN, LANES), f32)
        self.matrix_work = pltpu.VMEM(self.tables[2].shape, bf16)

    def products(self, signals, taps, after):
        return call(
            functools.partial(products_kernel, self.signal.shape[1]), (self.result, self.split),
            [self.twist_work, self.matrix_work]
            + [pltpu.VMEM((2, signals.shape[0], TILE_ROWS, LANES), bf16), self.result_work]
            + [self.split_work] * 3
            + [self.work] * 4
            + [pltpu.SemaphoreType.DMA((7,))],
            signals, taps, *self.tables, after,
            in_specs=[IN_VMEM, IN_VMEM, IN_SMEM, IN_VMEM, ANYWHERE, ANYWHERE],
            out_specs=(ANYWHERE, ANYWHERE),
        )

    def lag(self, lag_split):
        return call(
            lag_kernel, (self.signal, self.square),
            [self.twist_work, self.matrix_work, self.split_work, self.work, pltpu.SemaphoreType.DMA((2,))],
            lag_split, *self.tables,
            in_specs=[ANYWHERE, IN_SMEM, IN_VMEM, ANYWHERE],
            out_specs=(IN_VMEM, IN_VMEM),
        )


class PlainTransforms:
    def __init__(self, pieces, rows_here):
        self.seq_len = pieces * rows_here
        self.pieces = pieces
        self.outer = self.seq_len // SPAN
        idx = np.arange(SPAN)
        angle = (idx[:, None] * idx[None, :] % SPAN) * (2.0 * np.pi / SPAN)
        self.cosine = jnp.asarray(np.cos(angle), f32)
        self.sine = jnp.asarray(np.sin(angle), f32)
        twist = twist_angles(self.outer, idx)
        self.twist = jnp.asarray(np.stack([np.cos(twist), np.sin(twist)]), f32)[..., None]

    def dot(self, matrix, signal):
        return jnp.einsum("fs,tsc->tfc", matrix, signal, precision=lax.Precision.HIGHEST)

    def spectrum(self, signal):
        parts = signal.astype(f32).reshape(self.outer, SPAN, -1)
        leaves = to_leaves([parts[part] for part in range(self.outer)])
        re = jnp.stack([leaf[0] for leaf in leaves])
        im = jnp.stack([leaf[1] for leaf in leaves])
        twist_re = re * self.twist[0] + im * self.twist[1]
        twist_im = im * self.twist[0] - re * self.twist[1]
        return (
            self.dot(self.cosine, twist_re) + self.dot(self.sine, twist_im),
            self.dot(self.cosine, twist_im) - self.dot(self.sine, twist_re),
        )

    def back(self, re, im):
        time_re = self.dot(self.cosine, re) - self.dot(self.sine, im)
        time_im = self.dot(self.cosine, im) + self.dot(self.sine, re)
        leaf_re = time_re * self.twist[0] - time_im * self.twist[1]
        leaf_im = time_im * self.twist[0] + time_re * self.twist[1]
        parts = from_leaves([(leaf_re[leaf], leaf_im[leaf]) for leaf in range(self.outer)], 1.0 / self.seq_len)
        return jnp.stack(parts).reshape(self.pieces, self.seq_len // self.pieces, -1)

    def products(self, signals, taps_and_skip, after):
        rows_here = self.seq_len // self.pieces
        parts = [signals[:, kind * rows_here : (kind + 1) * rows_here] for kind in range(3)]
        extra = signals[:, 3 * rows_here :].astype(f32)
        rows = [extra[:, idx : idx + 1] for idx in range(extra.shape[1])]
        ahead = [jnp.concatenate([jnp.zeros_like(row[:1]), row[:-1]], axis=0) for row in rows]
        *taps, skip = [taps_and_skip[row][None, None, :] for row in range(taps_and_skip.shape[0])]
        count = len(taps) - 1
        for kind, first in enumerate(first_signals(ahead, rows, taps)[1:]):
            first = jnp.concatenate(first, axis=1)
            parts[kind] = jnp.concatenate([first.astype(bf16), parts[kind][:, first.shape[1] :]], axis=1)
        product, cotan, taps_spec = (self.spectrum(part) for part in parts)
        conv = self.back(
            taps_spec[0] * product[0] - taps_spec[1] * product[1], taps_spec[0] * product[1] + taps_spec[1] * product[0]
        ).astype(bf16)
        corr = self.back(
            taps_spec[0] * cotan[0] + taps_spec[1] * cotan[1], taps_spec[0] * cotan[1] - taps_spec[1] * cotan[0]
        ).astype(bf16)
        lag = (
            product[0] * cotan[0] + product[1] * cotan[1],
            product[0] * cotan[1] - product[1] * cotan[0],
        )
        backs = first_backs(
            ahead, rows, taps, skip,
            [conv[:, row : row + 1].astype(f32) for row in range(count)],
            [corr[:, row : row + 1].astype(f32) for row in range(count)],
        )
        behind = [jnp.concatenate([row[1:], jnp.zeros_like(row[:1])], axis=0) for row in backs]
        edge = jnp.concatenate(ahead[: 3 * count] + behind, axis=1).astype(bf16)
        edge = jnp.pad(edge, ((0, 0), (0, TILE_ROWS - edge.shape[1]), (0, 0)))
        return jnp.concatenate([conv, corr, edge], axis=1), lag

    def lag(self, lag_spec):
        lag = self.back(*lag_spec)
        squares = jnp.sum(lag * lag, axis=(0, 1))
        return lag.astype(bf16), jnp.zeros((1, LANES), f32).at[0, : squares.shape[0]].set(squares)


def group(idx):
    return pl.ds(pl.multiple_of(idx * LANES, LANES), LANES)


def streamed(work, steps, per_step, places, in_count, out_count, kept, *refs):
    moved = in_count + out_count
    hbm = refs[:moved]
    kept_refs = refs[moved : moved + kept]
    held = refs[moved + kept : 2 * moved + kept]
    scratch = refs[2 * moved + kept : -1]
    sems = refs[-1]

    def copy(place, step):
        outside = hbm[place].at[places[place](step)]
        inside = held[place].at[places[place](step)]
        ends = (outside, inside) if place < in_count else (inside, outside)
        return pltpu.make_async_copy(*ends, sems.at[place, step])

    def arrivals(step):
        return [copy(place, step) for place in range(in_count) if places[place](step) is not None]

    for step in range(steps):
        for arrival in arrivals(step):
            arrival.start()
    for step in range(steps):
        for arrival in arrivals(step):
            arrival.wait()

        def one(idx, carry):
            work(idx, held[:in_count], held[in_count:] + kept_refs, scratch)
            return carry

        lax.fori_loop(step * per_step, (step + 1) * per_step, one, 0)
        for place in range(in_count, moved):
            copy(place, step).start()
    for step in range(steps):
        for place in range(in_count, moved):
            copy(place, step).wait()


def stream_call(work, steps, per_step, operands, results, scratch=(), after=(), kept=(), vmem_bytes=VMEM_BYTES):
    arrays = [operand[0] for operand in operands]
    shapes = [jax.ShapeDtypeStruct(array.shape, array.dtype) for array in arrays] + [result[0] for result in results]
    cuts = [entry[1] for entry in list(operands) + list(results)]
    held = [pltpu.VMEM(shape.shape, shape.dtype) for shape in shapes]
    extra = list(after)
    kernel = functools.partial(streamed, work, steps, per_step, cuts, len(arrays), len(results), len(kept))

    def without_extra(*refs):
        kernel(*refs[: len(arrays)], *refs[len(arrays) + len(extra) :])

    return call(
        without_extra,
        tuple(result[0] for result in results) + tuple(kept),
        held + list(scratch) + [pltpu.SemaphoreType.DMA((len(shapes), steps))],
        *arrays, *extra,
        vmem_bytes=vmem_bytes,
        in_specs=[ANYWHERE] * (len(arrays) + len(extra)),
        out_specs=(ANYWHERE,) * len(results) + (IN_VMEM,) * len(kept),
    )


def cut_lanes(width, rank):
    def place(step):
        return (slice(None),) * (rank - 1) + (pl.ds(step * width, width),)

    return place


def cut_groups(per_step):
    def place(step):
        return (pl.ds(step * per_step, per_step),)

    return place


def cut_none(step):
    return None if step else (slice(None),)


def row_blocks(rows_here):
    return [slice(start, start + ROWS) for start in range(0, rows_here, ROWS)]


def extend_rows(lead, in_ref, lanes, ext_ref):
    ext_ref[PAD - lead.shape[0] : PAD, :] = lead
    ext_ref[PAD:, :] = in_ref[:, lanes].astype(f32)


def short_conv(ext_ref, taps, rows):
    result = None
    for shift_idx in range(taps.shape[0]):
        term = taps[shift_idx : shift_idx + 1] * ext_ref[PAD + rows.start - shift_idx : PAD + rows.stop - shift_idx, :]
        result = term if result is None else result + term
    return result


def signals_work(idx, operands, results, exts):
    q_ref, k_ref, v_ref, grad_ref, kernel_ref, taps_ref = operands
    lanes = group(idx)
    taps = taps_ref[:, lanes]
    halo_rows = taps.shape[0] - 1
    rows_here = q_ref.shape[0]
    for ext, in_ref in zip(exts, operands):
        extend_rows(jnp.zeros((halo_rows, LANES), f32), in_ref, lanes, ext)
    for rows in row_blocks(rows_here):
        q_short, k_short, v_short = (short_conv(ext, taps, rows) for ext in exts)
        below = [slice(kind * rows_here + rows.start, kind * rows_here + rows.stop) for kind in range(3)]
        results[0][idx, below[0], :] = (k_short * v_short).astype(bf16)
        results[0][idx, below[1], :] = (grad_ref[rows, lanes].astype(f32) * q_short).astype(bf16)
        results[0][idx, below[2], :] = kernel_ref[rows, lanes].astype(bf16)
    top = grad_ref[0:TILE_ROWS, lanes].astype(f32)[:halo_rows]
    extra = [ext[ext.shape[0] - halo_rows :, :] for ext in exts] + [ext[PAD : PAD + halo_rows, :] for ext in exts]
    extra_count = results[0].shape[1] - 3 * rows_here
    blank = jnp.zeros((extra_count - 7 * halo_rows, LANES), f32)
    results[0][idx, 3 * rows_here :, :] = jnp.concatenate(extra + [top, blank], axis=0).astype(bf16)


def short_work(idx, operands, results, exts):
    lanes = group(idx)
    taps = operands[3][:, lanes]
    for ext, in_ref in zip(exts, operands):
        extend_rows(jnp.zeros((taps.shape[0] - 1, LANES), f32), in_ref, lanes, ext)
    for rows in row_blocks(operands[0].shape[0]):
        for place, ext in enumerate(exts):
            results[0][place, rows, lanes] = short_conv(ext, taps, rows)


def fold(value):
    return jnp.sum(value.reshape(-1, 8, LANES), axis=0)


def finish_work(idx, operands, results, exts):
    q_ref, k_ref, v_ref, grad_ref, short_ref, taps_ref, skip_ref, long_ref, squares_ref = operands
    mixed_ref, grad_q_ref, grad_k_ref, grad_v_ref, sums_ref = results
    lanes = group(idx)
    taps = taps_ref[:, lanes]
    skip = skip_ref[:, lanes]
    taps_count = taps.shape[0]
    halo_rows = taps_count - 1
    rows_here = q_ref.shape[0]
    sums = [jnp.zeros((8, LANES), f32) for _ in range(taps_count + 1)]
    edge = long_ref[idx, 2 * rows_here :, :].astype(f32)
    for place, ext in enumerate(exts):
        at = (3 + place) * halo_rows
        ext[rows_here : rows_here + halo_rows, :] = edge[at : at + halo_rows]
    row_idx = lax.broadcasted_iota(jnp.int32, (ROWS, LANES), 0)

    def short(place, rows):
        value = short_ref[place, rows, lanes]
        if rows.start == 0:
            for shift_idx in range(1, taps_count):
                terms = jnp.zeros((ROWS, LANES), f32)
                for row in range(shift_idx):
                    at = place * halo_rows + halo_rows + row - shift_idx
                    term = taps[shift_idx : shift_idx + 1] * edge[at : at + 1]
                    terms = jnp.where(row_idx == row, term, terms)
                value = value + terms
        return value

    for rows in row_blocks(rows_here):
        q_short, k_short, v_short = (short(place, rows) for place in range(3))
        product = (k_short * v_short).astype(bf16).astype(f32)
        filtered = long_ref[idx, rows, :].astype(f32) + skip * product
        mixed_ref[rows, lanes] = (q_short * filtered).astype(bf16)
        upstream = grad_ref[rows, lanes].astype(f32)
        back_mix = upstream * q_short
        below = slice(rows_here + rows.start, rows_here + rows.stop)
        back_prod = long_ref[idx, below, :].astype(f32) + skip * back_mix
        sums[taps_count] = sums[taps_count] + fold(back_mix * product)
        exts[0][rows, :] = upstream * filtered
        exts[1][rows, :] = back_prod * v_short
        exts[2][rows, :] = back_prod * k_short
    for ext, in_ref, out_ref in zip(exts, (q_ref, k_ref, v_ref), (grad_q_ref, grad_k_ref, grad_v_ref)):
        for rows in row_blocks(rows_here):
            signal = in_ref[rows, lanes].astype(f32)
            grad = None
            for shift_idx in range(taps_count):
                ahead = ext[rows.start + shift_idx : rows.stop + shift_idx, :]
                term = taps[shift_idx : shift_idx + 1] * ahead
                grad = term if grad is None else grad + term
                sums[shift_idx] = sums[shift_idx] + fold(ahead * signal)
            out_ref[rows, lanes] = grad.astype(bf16)
    extra = slice(sums_ref.shape[1] - LANES, sums_ref.shape[1])
    sums_ref[:, extra] = jnp.zeros((taps_count + 1, LANES), f32)
    sums_ref[0:1, extra] = squares_ref[...]
    for shift_idx in range(taps_count + 1):
        sums_ref[shift_idx : shift_idx + 1, lanes] = jnp.sum(sums[shift_idx], axis=0, keepdims=True)


def norm_kernel(*refs):
    values, totals_ref, square_ref = refs[:-2], refs[-2], refs[-1]
    channels = totals_ref.shape[1] - LANES
    totals = values[0][...]
    if len(values) == 4:
        totals = (totals + values[1][...]) + (values[2][...] + values[3][...])
    totals_ref[...] = totals
    square = jnp.sum(totals[:, :channels] * totals[:, :channels]) + jnp.sum(totals[0:1, channels:])
    square_ref[...] = jnp.full(square_ref.shape, square)


def add_kernel(*refs):
    refs[-1][...] = add_up([ref[...] for ref in refs[:-1]])


def scale_kernel(limit, totals_ref, norm_ref, lag_ref, taps_out, skip_out, kernel_out):
    taps_count, channels = taps_out.shape
    factor = limit / jnp.maximum(jnp.sqrt(norm_ref[...]), limit)
    for idx in range(channels // LANES):
        lanes = slice(idx * LANES, (idx + 1) * LANES)
        taps_out[:, lanes] = totals_ref[0:taps_count, lanes] * factor
        skip_out[:, lanes] = totals_ref[taps_count : taps_count + 1, lanes] * factor
        kernel_out[:, lanes] = lag_ref[idx].astype(f32) * factor


def exchange(pieces_first):
    return lax.all_to_all(pieces_first, "ctx", split_axis=0, concat_axis=0, tiled=True)


def to_pieces(groups, pieces):
    count, rows, lanes = groups.shape
    if count == pieces:
        return groups
    share = count * lanes // pieces
    split = groups.reshape(count, rows, lanes // share, share)
    return split.transpose(0, 2, 1, 3).reshape(pieces, rows, share)


def to_groups(parts):
    pieces, rows, share = parts.shape
    if share == LANES:
        return parts
    joined = parts.reshape(pieces * share // LANES, LANES // share, rows, share)
    return joined.transpose(0, 2, 1, 3).reshape(-1, rows, LANES)


def partners(value, axis, steps):
    size = lax.axis_size(axis)
    return [value] + [lax.ppermute(value, axis, [(i, i ^ step) for i in range(size)]) for step in steps]


def rounds_of(size):
    rounds = []
    step = 1
    while step < size:
        rounds.append((step, 2 * step, 3 * step) if size // step >= 4 else (step,))
        step *= 4 if size // step >= 4 else 2
    return rounds


def add_up(values):
    if len(values) == 2:
        return values[0] + values[1]
    return (values[0] + values[1]) + (values[2] + values[3])


def body(q_in, k_in, v_in, grad_out, short_filter, kernel, skip):
    pieces = lax.axis_size("ctx")
    sides = lax.axis_size("ch")
    rows_here, channels = q_in.shape
    seq_len = pieces * rows_here
    taps_count = short_filter.shape[0]
    halo_rows = taps_count - 1
    groups = channels // LANES
    share = channels // pieces
    per_step = min(groups, 4)
    steps = groups // per_step
    lanes2 = cut_lanes(per_step * LANES, 2)
    lanes3 = cut_lanes(per_step * LANES, 3)
    skip_row = skip.reshape(1, channels)
    transforms = (Transforms if share == LANES else PlainTransforms)(pieces, rows_here)
    stream = functools.partial(stream_call, steps=steps, per_step=per_step)

    flat = jax.ShapeDtypeStruct((rows_here, channels), bf16)
    extra_rows = -(-7 * halo_rows // TILE_ROWS) * TILE_ROWS
    sent = jax.ShapeDtypeStruct((groups, 3 * rows_here + extra_rows, LANES), bf16)
    exts = [pltpu.VMEM((rows_here + PAD, LANES), f32)] * 3

    (signals,) = stream(
        signals_work,
        operands=[(x, lanes2) for x in (q_in, k_in, v_in, grad_out, kernel, short_filter)],
        results=[(sent, cut_groups(per_step))],
        scratch=exts,
        vmem_bytes=MOST_VMEM_BYTES,
    )
    signals_here = exchange(to_pieces(signals, pieces))
    (short,) = stream(
        short_work,
        operands=[(x, lanes2) for x in (q_in, k_in, v_in, short_filter)],
        results=[(jax.ShapeDtypeStruct((3, rows_here, channels), f32), lanes3)],
        scratch=exts,
        after=[signals],
    )
    taps_and_skip = jnp.concatenate([short_filter, skip_row], axis=0)
    taps_here = lax.dynamic_slice_in_dim(taps_and_skip, lax.axis_index("ctx") * share, share, axis=1)
    long_here, lag_spec = transforms.products(signals_here, taps_here, short)
    long = to_groups(exchange(long_here))
    lag_here, lag_squares = transforms.lag(lag_spec)
    lag = to_groups(exchange(lag_here))

    mixed, grad_q, grad_k, grad_v, sums = stream(
        finish_work,
        operands=[(x, lanes2) for x in (q_in, k_in, v_in, grad_out)]
        + [(short, lanes3), (short_filter, lanes2), (skip_row, lanes2)]
        + [(long, cut_groups(per_step)), (lag_squares, cut_none)],
        results=[(flat, lanes2)] * 4,
        scratch=exts,
        kept=[jax.ShapeDtypeStruct((taps_count + 1, channels + LANES), f32)],
    )

    totals = sums
    rounds = rounds_of(pieces)
    for steps_of in rounds[:-1]:
        values = partners(totals, "ctx", steps_of)
        totals = call(
            add_kernel, jax.ShapeDtypeStruct(totals.shape, f32), [], *values,
            vmem_bytes=SMALL_VMEM_BYTES, in_specs=[IN_VMEM] * len(values), out_specs=IN_VMEM,
        )
    last = partners(totals, "ctx", rounds[-1])
    if len(last) == 2:
        last = [last[0] + last[1]]

    totals, norm_sq = call(
        norm_kernel,
        (jax.ShapeDtypeStruct(totals.shape, f32), jax.ShapeDtypeStruct((1, LANES), f32)),
        [], *last,
        vmem_bytes=SMALL_VMEM_BYTES,
        in_specs=[IN_VMEM] * len(last), out_specs=(IN_VMEM, IN_VMEM),
    )
    for steps_of in rounds_of(sides):
        norm_sq = add_up(partners(norm_sq, "ch", steps_of))

    limit = math.sqrt(float(seq_len * channels * sides))
    grad_short, grad_skip, grad_kernel = call(
        functools.partial(scale_kernel, limit),
        (
            jax.ShapeDtypeStruct((taps_count, channels), f32),
            jax.ShapeDtypeStruct((1, channels), f32),
            jax.ShapeDtypeStruct((rows_here, channels), f32),
        ),
        [],
        totals, norm_sq, lag,
        vmem_bytes=SMALL_VMEM_BYTES,
        in_specs=[IN_VMEM] * 3,
        out_specs=(IN_VMEM,) * 3,
    )
    return mixed, grad_q, grad_k, grad_v, grad_short, grad_skip.reshape(channels), grad_kernel


def solution(mesh):
    in_specs = (
        P("ctx", "ch"),
        P("ctx", "ch"),
        P("ctx", "ch"),
        P("ctx", "ch"),
        P(None, "ch"),
        P("ctx", "ch"),
        P("ch"),
    )
    out_specs = (
        P("ctx", "ch"),
        P("ctx", "ch"),
        P("ctx", "ch"),
        P("ctx", "ch"),
        P(None, "ch"),
        P("ch"),
        P("ctx", "ch"),
    )
    return jax.shard_map(body, mesh=mesh, in_specs=in_specs, out_specs=out_specs, check_vma=False)
```

```python
import functools
import math

import jax
import jax.numpy as jnp
import ml_dtypes
import numpy as np
from jax import lax
from jax.experimental import pallas as pl
from jax.experimental.pallas import tpu as pltpu
from jax.sharding import PartitionSpec as P

LANES = 128
SPAN = 256
BOTH = 2 * SPAN
CHUNK = 16
CHUNKS = SPAN // CHUNK
PAD = 8
ROWS = 32
PASSES = 1
TILE_ROWS = 16
VMEM_BYTES = 60 * 1024 * 1024
MOST_VMEM_BYTES = 251 * 256 * 1024
SMALL_VMEM_BYTES = 8 * 1024 * 1024

f32 = jnp.float32
bf16 = jnp.bfloat16

IN_VMEM = pl.BlockSpec(memory_space=pltpu.VMEM)
IN_SMEM = pl.BlockSpec(memory_space=pltpu.SMEM)
ANYWHERE = pl.BlockSpec(memory_space=pl.ANY)


def call(kernel, outs, scratch, *args, vmem_bytes=VMEM_BYTES, **options):
    return pl.pallas_call(
        kernel,
        out_shape=outs,
        scratch_shapes=scratch,
        compiler_params=pltpu.CompilerParams(vmem_limit_bytes=vmem_bytes),
        **options,
    )(*args)


def leaf_phases(count):
    return [(4 * leaf + 1) / (4 * count) for leaf in range(count)]


def root_times(re, im, num, den, sign):
    if num == 0:
        return re, im
    if 4 * num == den:
        return (im, -re) if sign < 0 else (-im, re)
    cosine = math.cos(2.0 * math.pi * num / den)
    sine = sign * math.sin(2.0 * math.pi * num / den)
    if 8 * num == den:
        return ((re + im) * cosine, (im - re) * cosine) if sign < 0 else ((re - im) * cosine, (re + im) * cosine)
    if 8 * num == 3 * den:
        return ((re - im) * cosine, (re + im) * cosine) if sign < 0 else ((re + im) * cosine, (im - re) * cosine)
    return re * cosine - im * sine, im * cosine + re * sine


def short_fft(values, sign):
    count = len(values)
    if count == 1:
        return values
    even = short_fft(values[0::2], sign)
    odd = short_fft(values[1::2], sign)
    first = []
    second = []
    for num in range(count // 2):
        re, im = root_times(*odd[num], num, count, sign)
        first.append((even[num][0] + re, even[num][1] + im))
        second.append((even[num][0] - re, even[num][1] - im))
    return first + second


def to_leaves(parts):
    count = len(parts)
    turned = []
    for idx, part in enumerate(parts):
        angle = 2.0 * math.pi * idx / (4 * count)
        turned.append((part * math.cos(angle), part * (-math.sin(angle))) if idx else (part, jnp.zeros_like(part)))
    return short_fft(turned, -1)


def from_leaves(leaves, scale):
    count = len(leaves)
    parts = []
    for idx, (re, im) in enumerate(short_fft(leaves, 1)):
        angle = 2.0 * math.pi * idx / (4 * count)
        if idx == 0:
            parts.append(re * scale)
        else:
            parts.append(re * (math.cos(angle) * scale) - im * (math.sin(angle) * scale))
    return parts


def dft_matrix():
    idx = np.arange(SPAN)
    angle = (idx[:, None] * idx[None, :] % SPAN) * (2.0 * np.pi / SPAN)
    cosine, sine = np.cos(angle), np.sin(angle)
    return np.block([[cosine, sine], [-sine, cosine]])


def twist_angles(outer, inner):
    return np.asarray(leaf_phases(outer))[:, None] * np.asarray(inner)[None, :] * (2.0 * np.pi / SPAN)


def matrix_blocks():
    matrix = dft_matrix()
    high = matrix.astype(ml_dtypes.bfloat16)
    low = (matrix - high.astype(np.float64)).astype(ml_dtypes.bfloat16)
    return np.concatenate([high, low, high][:PASSES], axis=1)


def leaf_place(leaf):
    return leaf // 2, slice((leaf % 2) * LANES, (leaf % 2 + 1) * LANES)


def split_store(ref, leaf, below, here, value):
    pair, lanes = leaf_place(leaf)
    high = value.astype(bf16)
    for block in range(PASSES):
        part = high
        if PASSES == 3 and block == 2:
            part = (value - high.astype(f32)).astype(bf16)
        ref[pair, shifted_rows(here, block * BOTH + below), lanes] = part


def run_all(stages, rows_here, matmul=None, carry=0):
    tiles = matmul[2].shape[0] if matmul else 4
    per_tile = CHUNKS // tiles
    in_part = rows_here // CHUNK
    for tile in range(tiles):
        if matmul:
            matrix_ref, split_ref, result_ref = matmul
            result_ref[tile] = jnp.dot(matrix_ref[...], split_ref[tile], preferred_element_type=f32)
        for chunk in range(tile * per_tile, (tile + 1) * per_tile):
            for stage in stages:
                carry = stage(chunk // in_part, chunk % in_part * CHUNK, carry)
    return carry


def in_span(part, row, rows_here):
    return pl.ds(part * rows_here + row, CHUNK)


def twist_stage(coarse_ref, fine_ref, twist_ref, rows_here):
    outer = twist_ref.shape[1]

    def stage(part, row, carry):
        here = in_span(part, row, rows_here)
        idx = part * (rows_here // CHUNK) + row // CHUNK
        for leaf in range(outer):
            far_cosine = coarse_ref[idx, leaf]
            far_sine = coarse_ref[idx, outer + leaf]
            cosine = fine_ref[0, leaf]
            sine = fine_ref[1, leaf]
            twist_ref[0, leaf, here, :] = far_cosine * cosine - far_sine * sine
            twist_ref[1, leaf, here, :] = far_sine * cosine + far_cosine * sine
        return carry

    return stage


def leaves_stage(signals_ref, first_row, heads_ref, rows_here, twist_ref, split_ref):
    outer = twist_ref.shape[1]
    ratio = SPAN // rows_here

    def stage(part, row, carry):
        here = in_span(part, row, rows_here)
        rows = pl.ds(first_row + row, CHUNK)
        parts = [signals_ref[place * ratio + part, rows, :] for place in range(outer)]
        if heads_ref is not None and row == 0:
            parts = [heads_ref[place * ratio + part] for place in range(outer)]
        parts = [value.astype(f32) for value in parts]
        for leaf, (re, im) in enumerate(to_leaves(parts)):
            cosine = twist_ref[0, leaf, here, :]
            sine = twist_ref[1, leaf, here, :]
            split_store(split_ref, leaf, 0, here, re * cosine + im * sine)
            split_store(split_ref, leaf, SPAN, here, im * cosine - re * sine)
        return carry

    return stage


def shifted_rows(here, by):
    return pl.ds(here.start + by, here.size)


def combine_stage(left_ref, right_ref, split_ref, rows_here, conjugate):
    def stage(part, row, carry):
        here = in_span(part, row, rows_here)
        below = shifted_rows(here, SPAN)
        for leaf in range(2 * left_ref.shape[0]):
            pair, lanes = leaf_place(leaf)
            left_re = left_ref[pair, here, lanes]
            left_im = left_ref[pair, below, lanes]
            right_re = right_ref[pair, here, lanes]
            right_im = right_ref[pair, below, lanes]
            if conjugate:
                re = left_re * right_re + left_im * right_im
                minus_im = left_im * right_re - left_re * right_im
            else:
                re = left_re * right_re - left_im * right_im
                minus_im = -(left_re * right_im + left_im * right_re)
            split_store(split_ref, leaf, 0, here, re)
            split_store(split_ref, leaf, SPAN, here, minus_im)
        return carry

    return stage


def signal_stage(time_ref, twist_ref, rows_here, write):
    outer = twist_ref.shape[1]
    ratio = SPAN // rows_here
    scale = 1.0 / (SPAN * outer)

    def stage(part, row, carry):
        here = in_span(part, row, rows_here)
        below = shifted_rows(here, SPAN)
        leaves = []
        for leaf in range(outer):
            pair, lanes = leaf_place(leaf)
            cosine = twist_ref[0, leaf, here, :]
            sine = twist_ref[1, leaf, here, :]
            re = time_ref[pair, here, lanes]
            minus_im = time_ref[pair, below, lanes]
            leaves.append((re * cosine + minus_im * sine, re * sine - minus_im * cosine))
        for place, value in enumerate(from_leaves(leaves, scale)):
            carry = write(place * ratio + part, pl.ds(row, CHUNK), value, carry)
        return carry

    return stage


def first_rows(lead, first, taps):
    count = len(lead)
    rows = lead + first
    return [
        functools.reduce(lambda x, y: x + y, [taps[shift] * rows[count + row - shift] for shift in range(count + 1)])
        for row in range(count)
    ]


def first_signals(ahead, own, taps):
    count = len(taps) - 1

    def kind(rows, idx):
        return rows[idx * count : (idx + 1) * count]

    shorts = [first_rows(kind(ahead, idx), kind(own, 3 + idx), taps) for idx in range(3)]
    product = [(k_row * v_row).astype(bf16) for k_row, v_row in zip(shorts[1], shorts[2])]
    back_mix = [grad_row * q_row for grad_row, q_row in zip(kind(own, 6), shorts[0])]
    return shorts, product, back_mix


def first_backs(ahead, own, taps, skip, conv, corr):
    count = len(taps) - 1
    shorts, product, back_mix = first_signals(ahead, own, taps)
    back_q = []
    back_k = []
    back_v = []
    for row in range(count):
        filtered = conv[row] + skip * product[row].astype(f32)
        back_prod = corr[row] + skip * back_mix[row]
        back_q.append(own[6 * count + row] * filtered)
        back_k.append(back_prod * shorts[2][row])
        back_v.append(back_prod * shorts[1][row])
    return back_q + back_k + back_v


def extra_of(signals_ref, piece, rows_here, used):
    rows = signals_ref[piece, 3 * rows_here :, :].astype(f32)
    return [rows[idx : idx + 1] for idx in range(used)]


def tap_rows(taps_ref):
    return [taps_ref[shift : shift + 1, :] for shift in range(taps_ref.shape[0])]


def patch_first_rows(signals_ref, heads_ref, taps_ref, rows_here):
    pieces = signals_ref.shape[0]
    taps = tap_rows(taps_ref)[:-1]
    used = 7 * (len(taps) - 1)
    row_idx = lax.broadcasted_iota(jnp.int32, (TILE_ROWS, LANES), 0)
    ahead = [jnp.zeros((1, LANES), f32)] * used
    for piece in range(pieces):
        own = extra_of(signals_ref, piece, rows_here, used)
        for kind, rows in enumerate(first_signals(ahead, own, taps)[1:]):
            tile = signals_ref[piece, kind * rows_here : kind * rows_here + TILE_ROWS, :].astype(f32)
            for row, value in enumerate(rows):
                tile = jnp.where(row_idx == row, value.astype(f32), tile)
            heads_ref[kind, piece] = tile.astype(bf16)
        ahead = own


def write_edges(signals_ref, results_ref, taps_ref, rows_here):
    pieces = signals_ref.shape[0]
    *taps, skip = tap_rows(taps_ref)
    count = len(taps) - 1
    nothing = jnp.zeros((1, LANES), f32)
    extras = [extra_of(signals_ref, piece, rows_here, 7 * count) for piece in range(pieces)]
    for piece in range(pieces):
        rows = extras[piece - 1][: 3 * count] if piece else [nothing] * (3 * count)
        if piece + 1 < pieces:
            conv, corr = (
                results_ref[piece + 1, kind * rows_here : kind * rows_here + TILE_ROWS, :].astype(f32)
                for kind in range(2)
            )
            rows = rows + first_backs(
                extras[piece], extras[piece + 1], taps, skip,
                [conv[row : row + 1] for row in range(count)], [corr[row : row + 1] for row in range(count)],
            )
        spare = results_ref.shape[1] - 2 * rows_here - len(rows)
        rows.append(jnp.zeros((spare, LANES), f32))
        results_ref[piece, 2 * rows_here :, :] = jnp.concatenate(rows, axis=0).astype(bf16)


def products_kernel(
    rows_here, signals_hbm, taps_ref, coarse_ref, fine_ref, matrix_hbm, after_ref, results_hbm, lag_hbm,
    signals_ref, twist_ref, matrix_ref, heads_ref, results_ref, one_split, two_split, lag_split,
    filter_ref, product_ref, cotan_ref, time_ref, sems,
):
    filter_rows = pl.ds(2 * rows_here, rows_here)
    extra_rows = pl.ds(3 * rows_here, signals_ref.shape[1] - 3 * rows_here)
    signal_rows = pl.ds(0, 2 * rows_here)
    arrivals = [
        pltpu.make_async_copy(signals_hbm.at[:, rows], signals_ref.at[:, rows], sems.at[idx])
        for idx, rows in enumerate((filter_rows, extra_rows, signal_rows))
    ]
    matrix_copy = pltpu.make_async_copy(matrix_hbm, matrix_ref, sems.at[3])
    lag_copy = pltpu.make_async_copy(lag_split, lag_hbm, sems.at[4])
    returns = [
        pltpu.make_async_copy(results_ref.at[:, rows], results_hbm.at[:, rows], sems.at[5 + idx])
        for idx, rows in enumerate(
            (pl.ds(0, rows_here), pl.ds(rows_here, results_ref.shape[1] - rows_here))
        )
    ]

    def leaves(kind, split_ref):
        heads = heads_ref.at[kind] if kind < 2 else None
        return leaves_stage(signals_ref, kind * rows_here, heads, rows_here, twist_ref, split_ref)

    def combine(left_ref, right_ref, split_ref, conjugate):
        return combine_stage(left_ref, right_ref, split_ref, rows_here, conjugate)

    def result(kind, from_ref):
        def write(piece, rows, value, carry):
            place = pl.ds(kind * rows_here + rows.start, CHUNK)
            results_ref[piece, place, :] = value.astype(bf16)
            return carry

        return signal_stage(from_ref, twist_ref, rows_here, write)

    for copy in arrivals + [matrix_copy]:
        copy.start()
    run_all([twist_stage(coarse_ref, fine_ref, twist_ref, rows_here)], rows_here)
    arrivals[0].wait()
    run_all([leaves(2, one_split)], rows_here)
    arrivals[1].wait()
    arrivals[2].wait()
    patch_first_rows(signals_ref, heads_ref, taps_ref, rows_here)
    matrix_copy.wait()
    run_all([leaves(0, two_split)], rows_here, (matrix_ref, one_split, filter_ref))
    run_all([leaves(1, one_split)], rows_here, (matrix_ref, two_split, product_ref))
    run_all([combine(filter_ref, product_ref, two_split, False)], rows_here, (matrix_ref, one_split, cotan_ref))
    run_all([combine(filter_ref, cotan_ref, one_split, True)], rows_here, (matrix_ref, two_split, time_ref))
    run_all(
        [combine(product_ref, cotan_ref, lag_split, True), result(0, time_ref)],
        rows_here, (matrix_ref, one_split, filter_ref),
    )
    lag_copy.start()
    returns[0].start()
    run_all([result(1, filter_ref)], rows_here)
    write_edges(signals_ref, results_ref, taps_ref, rows_here)
    returns[1].start()
    lag_copy.wait()
    returns[0].wait()
    returns[1].wait()


def lag_kernel(
    split_hbm, coarse_ref, fine_ref, matrix_hbm, lag_ref, square_ref, twist_ref, matrix_ref, split_ref, time_ref, sems
):
    rows_here = lag_ref.shape[1]
    copies = [
        pltpu.make_async_copy(matrix_hbm, matrix_ref, sems.at[0]),
        pltpu.make_async_copy(split_hbm, split_ref, sems.at[1]),
    ]
    for copy in copies:
        copy.start()
    run_all([twist_stage(coarse_ref, fine_ref, twist_ref, rows_here)], rows_here)
    for copy in copies:
        copy.wait()
    run_all([], rows_here, (matrix_ref, split_ref, time_ref))

    def write(piece, rows, value, carry):
        lag_ref[piece, rows, :] = value.astype(bf16)
        return carry + value * value

    square = run_all(
        [signal_stage(time_ref, twist_ref, rows_here, write)], rows_here, None, jnp.zeros((CHUNK, LANES), f32)
    )
    square_ref[...] = jnp.sum(square, axis=0, keepdims=True)


class Transforms:
    def __init__(self, pieces, rows_here):
        outer = pieces * rows_here // SPAN
        pairs = outer // 2
        coarse = twist_angles(outer, CHUNK * np.arange(CHUNKS)).T
        fine = twist_angles(outer, np.arange(CHUNK))[..., None] * np.ones(LANES)
        self.tables = [
            jnp.asarray(np.concatenate([np.cos(coarse), np.sin(coarse)], axis=1).astype(np.float32)),
            jnp.asarray(np.stack([np.cos(fine), np.sin(fine)]).astype(np.float32)),
            jnp.asarray(matrix_blocks()),
        ]
        self.split = jax.ShapeDtypeStruct((pairs, PASSES * BOTH, 2 * LANES), bf16)
        self.signal = jax.ShapeDtypeStruct((pieces, rows_here, LANES), bf16)
        self.result = jax.ShapeDtypeStruct((pieces, 2 * rows_here + TILE_ROWS, LANES), bf16)
        self.square = jax.ShapeDtypeStruct((1, LANES), f32)
        self.result_work = pltpu.VMEM(self.result.shape, bf16)
        self.work = pltpu.VMEM((pairs, BOTH, 2 * LANES), f32)
        self.split_work = pltpu.VMEM(self.split.shape, bf16)
        self.twist_work = pltpu.VMEM((2, outer, SPAN, LANES), f32)
        self.matrix_work = pltpu.VMEM(self.tables[2].shape, bf16)

    def products(self, signals, taps, after):
        return call(
            functools.partial(products_kernel, self.signal.shape[1]), (self.result, self.split),
            [pltpu.VMEM(signals.shape, bf16), self.twist_work, self.matrix_work]
            + [pltpu.VMEM((2, signals.shape[0], TILE_ROWS, LANES), bf16), self.result_work]
            + [self.split_work] * 3
            + [self.work] * 4
            + [pltpu.SemaphoreType.DMA((7,))],
            signals, taps, *self.tables, after,
            vmem_bytes=MOST_VMEM_BYTES,
            in_specs=[ANYWHERE, IN_VMEM, IN_SMEM, IN_VMEM, ANYWHERE, ANYWHERE],
            out_specs=(ANYWHERE, ANYWHERE),
        )

    def lag(self, lag_split):
        return call(
            lag_kernel, (self.signal, self.square),
            [self.twist_work, self.matrix_work, self.split_work, self.work, pltpu.SemaphoreType.DMA((2,))],
            lag_split, *self.tables,
            in_specs=[ANYWHERE, IN_SMEM, IN_VMEM, ANYWHERE],
            out_specs=(IN_VMEM, IN_VMEM),
        )


class PlainTransforms:
    def __init__(self, pieces, rows_here):
        self.seq_len = pieces * rows_here
        self.pieces = pieces
        self.outer = self.seq_len // SPAN
        idx = np.arange(SPAN)
        angle = (idx[:, None] * idx[None, :] % SPAN) * (2.0 * np.pi / SPAN)
        self.cosine = jnp.asarray(np.cos(angle), f32)
        self.sine = jnp.asarray(np.sin(angle), f32)
        twist = twist_angles(self.outer, idx)
        self.twist = jnp.asarray(np.stack([np.cos(twist), np.sin(twist)]), f32)[..., None]

    def dot(self, matrix, signal):
        return jnp.einsum("fs,tsc->tfc", matrix, signal, precision=lax.Precision.HIGHEST)

    def spectrum(self, signal):
        parts = signal.astype(f32).reshape(self.outer, SPAN, -1)
        leaves = to_leaves([parts[part] for part in range(self.outer)])
        re = jnp.stack([leaf[0] for leaf in leaves])
        im = jnp.stack([leaf[1] for leaf in leaves])
        twist_re = re * self.twist[0] + im * self.twist[1]
        twist_im = im * self.twist[0] - re * self.twist[1]
        return (
            self.dot(self.cosine, twist_re) + self.dot(self.sine, twist_im),
            self.dot(self.cosine, twist_im) - self.dot(self.sine, twist_re),
        )

    def back(self, re, im):
        time_re = self.dot(self.cosine, re) - self.dot(self.sine, im)
        time_im = self.dot(self.cosine, im) + self.dot(self.sine, re)
        leaf_re = time_re * self.twist[0] - time_im * self.twist[1]
        leaf_im = time_im * self.twist[0] + time_re * self.twist[1]
        parts = from_leaves([(leaf_re[leaf], leaf_im[leaf]) for leaf in range(self.outer)], 1.0 / self.seq_len)
        return jnp.stack(parts).reshape(self.pieces, self.seq_len // self.pieces, -1)

    def products(self, signals, taps_and_skip, after):
        rows_here = self.seq_len // self.pieces
        parts = [signals[:, kind * rows_here : (kind + 1) * rows_here] for kind in range(3)]
        extra = signals[:, 3 * rows_here :].astype(f32)
        rows = [extra[:, idx : idx + 1] for idx in range(extra.shape[1])]
        ahead = [jnp.concatenate([jnp.zeros_like(row[:1]), row[:-1]], axis=0) for row in rows]
        *taps, skip = [taps_and_skip[row][None, None, :] for row in range(taps_and_skip.shape[0])]
        count = len(taps) - 1
        for kind, first in enumerate(first_signals(ahead, rows, taps)[1:]):
            first = jnp.concatenate(first, axis=1)
            parts[kind] = jnp.concatenate([first.astype(bf16), parts[kind][:, first.shape[1] :]], axis=1)
        product, cotan, taps_spec = (self.spectrum(part) for part in parts)
        conv = self.back(
            taps_spec[0] * product[0] - taps_spec[1] * product[1], taps_spec[0] * product[1] + taps_spec[1] * product[0]
        ).astype(bf16)
        corr = self.back(
            taps_spec[0] * cotan[0] + taps_spec[1] * cotan[1], taps_spec[0] * cotan[1] - taps_spec[1] * cotan[0]
        ).astype(bf16)
        lag = (
            product[0] * cotan[0] + product[1] * cotan[1],
            product[0] * cotan[1] - product[1] * cotan[0],
        )
        backs = first_backs(
            ahead, rows, taps, skip,
            [conv[:, row : row + 1].astype(f32) for row in range(count)],
            [corr[:, row : row + 1].astype(f32) for row in range(count)],
        )
        behind = [jnp.concatenate([row[1:], jnp.zeros_like(row[:1])], axis=0) for row in backs]
        edge = jnp.concatenate(ahead[: 3 * count] + behind, axis=1).astype(bf16)
        edge = jnp.pad(edge, ((0, 0), (0, TILE_ROWS - edge.shape[1]), (0, 0)))
        return jnp.concatenate([conv, corr, edge], axis=1), lag

    def lag(self, lag_spec):
        lag = self.back(*lag_spec)
        squares = jnp.sum(lag * lag, axis=(0, 1))
        return lag.astype(bf16), jnp.zeros((1, LANES), f32).at[0, : squares.shape[0]].set(squares)


def group(idx):
    return slice(idx * LANES, (idx + 1) * LANES)


def streamed(work, steps, per_step, places, in_count, out_count, kept, *refs):
    moved = in_count + out_count
    hbm = refs[:moved]
    kept_refs = refs[moved : moved + kept]
    held = refs[moved + kept : 2 * moved + kept]
    scratch = refs[2 * moved + kept : -1]
    sems = refs[-1]

    def copy(place, step):
        outside = hbm[place].at[places[place](step)]
        inside = held[place].at[places[place](step)]
        ends = (outside, inside) if place < in_count else (inside, outside)
        return pltpu.make_async_copy(*ends, sems.at[place, step])

    def arrivals(step):
        return [copy(place, step) for place in range(in_count) if places[place](step) is not None]

    for step in range(steps):
        for arrival in arrivals(step):
            arrival.start()
    for step in range(steps):
        for arrival in arrivals(step):
            arrival.wait()
        for idx in range(step * per_step, (step + 1) * per_step):
            exts = scratch[idx % 2 :: 2]
            work(idx, held[:in_count], held[in_count:] + kept_refs, exts)
        for place in range(in_count, moved):
            copy(place, step).start()
    for step in range(steps):
        for place in range(in_count, moved):
            copy(place, step).wait()


def stream_call(work, steps, per_step, operands, results, scratch=(), after=(), kept=(), vmem_bytes=VMEM_BYTES):
    arrays = [operand[0] for operand in operands]
    shapes = [jax.ShapeDtypeStruct(array.shape, array.dtype) for array in arrays] + [result[0] for result in results]
    cuts = [entry[1] for entry in list(operands) + list(results)]
    held = [pltpu.VMEM(shape.shape, shape.dtype) for shape in shapes]
    extra = list(after)
    kernel = functools.partial(streamed, work, steps, per_step, cuts, len(arrays), len(results), len(kept))

    def without_extra(*refs):
        kernel(*refs[: len(arrays)], *refs[len(arrays) + len(extra) :])

    return call(
        without_extra,
        tuple(result[0] for result in results) + tuple(kept),
        held + list(scratch) + [pltpu.SemaphoreType.DMA((len(shapes), steps))],
        *arrays, *extra,
        vmem_bytes=vmem_bytes,
        in_specs=[ANYWHERE] * (len(arrays) + len(extra)),
        out_specs=(ANYWHERE,) * len(results) + (IN_VMEM,) * len(kept),
    )


def cut_lanes(width, rank):
    def place(step):
        return (slice(None),) * (rank - 1) + (pl.ds(step * width, width),)

    return place


def cut_groups(per_step):
    def place(step):
        return (pl.ds(step * per_step, per_step),)

    return place


def cut_none(step):
    return None if step else (slice(None),)


def row_blocks(rows_here):
    return [slice(start, start + ROWS) for start in range(0, rows_here, ROWS)]


def extend_rows(lead, in_ref, lanes, ext_ref):
    ext_ref[PAD - lead.shape[0] : PAD, :] = lead
    ext_ref[PAD:, :] = in_ref[:, lanes].astype(f32)


def short_conv(ext_ref, taps, rows):
    result = None
    for shift_idx in range(taps.shape[0]):
        term = taps[shift_idx : shift_idx + 1] * ext_ref[PAD + rows.start - shift_idx : PAD + rows.stop - shift_idx, :]
        result = term if result is None else result + term
    return result


def signals_work(idx, operands, results, exts):
    q_ref, k_ref, v_ref, grad_ref, kernel_ref, taps_ref = operands
    lanes = group(idx)
    taps = taps_ref[:, lanes]
    halo_rows = taps.shape[0] - 1
    rows_here = q_ref.shape[0]
    for ext, in_ref in zip(exts, operands):
        extend_rows(jnp.zeros((halo_rows, LANES), f32), in_ref, lanes, ext)
    for rows in row_blocks(rows_here):
        q_short, k_short, v_short = (short_conv(ext, taps, rows) for ext in exts)
        below = [slice(kind * rows_here + rows.start, kind * rows_here + rows.stop) for kind in range(3)]
        results[0][idx, below[0], :] = (k_short * v_short).astype(bf16)
        results[0][idx, below[1], :] = (grad_ref[rows, lanes].astype(f32) * q_short).astype(bf16)
        results[0][idx, below[2], :] = kernel_ref[rows, lanes].astype(bf16)
    top = grad_ref[0:TILE_ROWS, lanes].astype(f32)[:halo_rows]
    extra = [ext[ext.shape[0] - halo_rows :, :] for ext in exts] + [ext[PAD : PAD + halo_rows, :] for ext in exts]
    extra_count = results[0].shape[1] - 3 * rows_here
    blank = jnp.zeros((extra_count - 7 * halo_rows, LANES), f32)
    results[0][idx, 3 * rows_here :, :] = jnp.concatenate(extra + [top, blank], axis=0).astype(bf16)


def short_work(idx, operands, results, exts):
    lanes = group(idx)
    taps = operands[3][:, lanes]
    for ext, in_ref in zip(exts, operands):
        extend_rows(jnp.zeros((taps.shape[0] - 1, LANES), f32), in_ref, lanes, ext)
    for rows in row_blocks(operands[0].shape[0]):
        for place, ext in enumerate(exts):
            results[0][place, rows, lanes] = short_conv(ext, taps, rows)


def fold(value):
    return jnp.sum(value.reshape(-1, 8, LANES), axis=0)


def finish_work(idx, operands, results, exts):
    q_ref, k_ref, v_ref, grad_ref, short_ref, taps_ref, skip_ref, long_ref, squares_ref = operands
    mixed_ref, grad_q_ref, grad_k_ref, grad_v_ref, sums_ref = results
    lanes = group(idx)
    taps = taps_ref[:, lanes]
    skip = skip_ref[:, lanes]
    taps_count = taps.shape[0]
    halo_rows = taps_count - 1
    rows_here = q_ref.shape[0]
    sums = [jnp.zeros((8, LANES), f32) for _ in range(taps_count + 1)]
    edge = long_ref[idx, 2 * rows_here :, :].astype(f32)
    for place, ext in enumerate(exts):
        at = (3 + place) * halo_rows
        ext[rows_here : rows_here + halo_rows, :] = edge[at : at + halo_rows]
    row_idx = lax.broadcasted_iota(jnp.int32, (ROWS, LANES), 0)

    def short(place, rows):
        value = short_ref[place, rows, lanes]
        if rows.start == 0:
            for shift_idx in range(1, taps_count):
                terms = jnp.zeros((ROWS, LANES), f32)
                for row in range(shift_idx):
                    at = place * halo_rows + halo_rows + row - shift_idx
                    term = taps[shift_idx : shift_idx + 1] * edge[at : at + 1]
                    terms = jnp.where(row_idx == row, term, terms)
                value = value + terms
        return value

    for rows in row_blocks(rows_here):
        q_short, k_short, v_short = (short(place, rows) for place in range(3))
        product = (k_short * v_short).astype(bf16).astype(f32)
        filtered = long_ref[idx, rows, :].astype(f32) + skip * product
        mixed_ref[rows, lanes] = (q_short * filtered).astype(bf16)
        upstream = grad_ref[rows, lanes].astype(f32)
        back_mix = upstream * q_short
        below = slice(rows_here + rows.start, rows_here + rows.stop)
        back_prod = long_ref[idx, below, :].astype(f32) + skip * back_mix
        sums[taps_count] = sums[taps_count] + fold(back_mix * product)
        exts[0][rows, :] = upstream * filtered
        exts[1][rows, :] = back_prod * v_short
        exts[2][rows, :] = back_prod * k_short
    for ext, in_ref, out_ref in zip(exts, (q_ref, k_ref, v_ref), (grad_q_ref, grad_k_ref, grad_v_ref)):
        for rows in row_blocks(rows_here):
            signal = in_ref[rows, lanes].astype(f32)
            grad = None
            for shift_idx in range(taps_count):
                ahead = ext[rows.start + shift_idx : rows.stop + shift_idx, :]
                term = taps[shift_idx : shift_idx + 1] * ahead
                grad = term if grad is None else grad + term
                sums[shift_idx] = sums[shift_idx] + fold(ahead * signal)
            out_ref[rows, lanes] = grad.astype(bf16)
    if idx == 0:
        extra = slice(sums_ref.shape[1] - LANES, sums_ref.shape[1])
        sums_ref[:, extra] = jnp.zeros((taps_count + 1, LANES), f32)
        sums_ref[0:1, extra] = squares_ref[...]
    for shift_idx in range(taps_count + 1):
        sums_ref[shift_idx : shift_idx + 1, lanes] = jnp.sum(sums[shift_idx], axis=0, keepdims=True)


def norm_kernel(*refs):
    values, totals_ref, square_ref = refs[:-2], refs[-2], refs[-1]
    channels = totals_ref.shape[1] - LANES
    totals = values[0][...]
    if len(values) == 4:
        totals = (totals + values[1][...]) + (values[2][...] + values[3][...])
    totals_ref[...] = totals
    square = jnp.sum(totals[:, :channels] * totals[:, :channels]) + jnp.sum(totals[0:1, channels:])
    square_ref[...] = jnp.full(square_ref.shape, square)


def add_kernel(own_hbm, *refs):
    *others, total_ref, own_ref, sem = refs
    own_copy = pltpu.make_async_copy(own_hbm, own_ref, sem)
    own_copy.start()
    own_copy.wait()
    total_ref[...] = add_up([own_ref[...]] + [ref[...] for ref in others])


def scale_kernel(limit, totals_ref, norm_ref, lag_ref, taps_out, skip_out, kernel_out):
    taps_count, channels = taps_out.shape
    factor = limit / jnp.maximum(jnp.sqrt(norm_ref[...]), limit)
    for idx in range(channels // LANES):
        lanes = slice(idx * LANES, (idx + 1) * LANES)
        taps_out[:, lanes] = totals_ref[0:taps_count, lanes] * factor
        skip_out[:, lanes] = totals_ref[taps_count : taps_count + 1, lanes] * factor
        kernel_out[:, lanes] = lag_ref[idx].astype(f32) * factor


def exchange(pieces_first):
    return lax.all_to_all(pieces_first, "ctx", split_axis=0, concat_axis=0, tiled=True)


def to_pieces(groups, pieces):
    count, rows, lanes = groups.shape
    if count == pieces:
        return groups
    share = count * lanes // pieces
    split = groups.reshape(count, rows, lanes // share, share)
    return split.transpose(0, 2, 1, 3).reshape(pieces, rows, share)


def to_groups(parts):
    pieces, rows, share = parts.shape
    if share == LANES:
        return parts
    joined = parts.reshape(pieces * share // LANES, LANES // share, rows, share)
    return joined.transpose(0, 2, 1, 3).reshape(-1, rows, LANES)


def partners(value, axis, steps):
    size = lax.axis_size(axis)
    return [value] + [lax.ppermute(value, axis, [(i, i ^ step) for i in range(size)]) for step in steps]


def rounds_of(size):
    rounds = []
    step = 1
    while step < size:
        rounds.append((step, 2 * step, 3 * step) if size // step >= 4 else (step,))
        step *= 4 if size // step >= 4 else 2
    return rounds


def add_up(values):
    if len(values) == 2:
        return values[0] + values[1]
    return (values[0] + values[1]) + (values[2] + values[3])


def body(q_in, k_in, v_in, grad_out, short_filter, kernel, skip):
    pieces = lax.axis_size("ctx")
    sides = lax.axis_size("ch")
    rows_here, channels = q_in.shape
    seq_len = pieces * rows_here
    taps_count = short_filter.shape[0]
    halo_rows = taps_count - 1
    groups = channels // LANES
    share = channels // pieces
    per_step = min(groups, 4)
    steps = groups // per_step
    lanes2 = cut_lanes(per_step * LANES, 2)
    lanes3 = cut_lanes(per_step * LANES, 3)
    skip_row = skip.reshape(1, channels)
    transforms = (Transforms if share == LANES else PlainTransforms)(pieces, rows_here)
    stream = functools.partial(stream_call, steps=steps, per_step=per_step)

    flat = jax.ShapeDtypeStruct((rows_here, channels), bf16)
    extra_rows = -(-7 * halo_rows // TILE_ROWS) * TILE_ROWS
    sent = jax.ShapeDtypeStruct((groups, 3 * rows_here + extra_rows, LANES), bf16)
    exts = [pltpu.VMEM((rows_here + PAD, LANES), f32)] * 6

    (signals,) = stream(
        signals_work,
        operands=[(x, lanes2) for x in (q_in, k_in, v_in, grad_out, kernel, short_filter)],
        results=[(sent, cut_groups(per_step))],
        scratch=exts,
        vmem_bytes=MOST_VMEM_BYTES,
    )
    signals_here = exchange(to_pieces(signals, pieces))
    (short,) = stream(
        short_work,
        operands=[(x, lanes2) for x in (q_in, k_in, v_in, short_filter)],
        results=[(jax.ShapeDtypeStruct((3, rows_here, channels), f32), lanes3)],
        scratch=exts,
        after=[signals],
    )
    taps_and_skip = jnp.concatenate([short_filter, skip_row], axis=0)
    taps_here = lax.dynamic_slice_in_dim(taps_and_skip, lax.axis_index("ctx") * share, share, axis=1)
    long_here, lag_spec = transforms.products(signals_here, taps_here, short)
    long = to_groups(exchange(long_here))
    lag_here, lag_squares = transforms.lag(lag_spec)
    lag = to_groups(exchange(lag_here))

    mixed, grad_q, grad_k, grad_v, sums = stream(
        finish_work,
        operands=[(x, lanes2) for x in (q_in, k_in, v_in, grad_out)]
        + [(short, lanes3), (short_filter, lanes2), (skip_row, lanes2)]
        + [(long, cut_groups(per_step)), (lag_squares, cut_none)],
        results=[(flat, lanes2)] * 4,
        scratch=exts,
        kept=[jax.ShapeDtypeStruct((taps_count + 1, channels + LANES), f32)],
    )

    totals = sums
    rounds = rounds_of(pieces)
    for steps_of in rounds[:-1]:
        values = partners(totals, "ctx", steps_of)
        totals = call(
            add_kernel, jax.ShapeDtypeStruct(totals.shape, f32),
            [pltpu.VMEM(totals.shape, f32), pltpu.SemaphoreType.DMA], *values,
            vmem_bytes=SMALL_VMEM_BYTES,
            in_specs=[ANYWHERE] + [IN_VMEM] * (len(values) - 1), out_specs=IN_VMEM,
        )
    last = partners(totals, "ctx", rounds[-1])
    if len(last) == 2:
        last = [last[0] + last[1]]

    totals, norm_sq = call(
        norm_kernel,
        (jax.ShapeDtypeStruct(totals.shape, f32), jax.ShapeDtypeStruct((1, LANES), f32)),
        [], *last,
        vmem_bytes=SMALL_VMEM_BYTES,
        in_specs=[IN_VMEM] * len(last), out_specs=(IN_VMEM, IN_VMEM),
    )
    for steps_of in rounds_of(sides):
        norm_sq = add_up(partners(norm_sq, "ch", steps_of))

    limit = math.sqrt(float(seq_len * channels * sides))
    grad_short, grad_skip, grad_kernel = call(
        functools.partial(scale_kernel, limit),
        (
            jax.ShapeDtypeStruct((taps_count, channels), f32),
            jax.ShapeDtypeStruct((1, channels), f32),
            jax.ShapeDtypeStruct((rows_here, channels), f32),
        ),
        [],
        totals, norm_sq, lag,
        vmem_bytes=SMALL_VMEM_BYTES,
        in_specs=[IN_VMEM] * 3,
        out_specs=(IN_VMEM,) * 3,
    )
    return mixed, grad_q, grad_k, grad_v, grad_short, grad_skip.reshape(channels), grad_kernel


def solution(mesh):
    in_specs = (
        P("ctx", "ch"),
        P("ctx", "ch"),
        P("ctx", "ch"),
        P("ctx", "ch"),
        P(None, "ch"),
        P("ctx", "ch"),
        P("ch"),
    )
    out_specs = (
        P("ctx", "ch"),
        P("ctx", "ch"),
        P("ctx", "ch"),
        P("ctx", "ch"),
        P(None, "ch"),
        P("ch"),
        P("ctx", "ch"),
    )
    return jax.shard_map(body, mesh=mesh, in_specs=in_specs, out_specs=out_specs, check_vma=False)
```

```python
import functools
import math

import jax
import jax.numpy as jnp
import ml_dtypes
import numpy as np
from jax import lax
from jax.experimental import pallas as pl
from jax.experimental.pallas import tpu as pltpu
from jax.sharding import PartitionSpec as P

LANES = 128
SPAN = 256
BOTH = 2 * SPAN
CHUNK = 16
CHUNKS = SPAN // CHUNK
PAD = 8
ROWS = 32
PASSES = 1
TILE_ROWS = 16
VMEM_BYTES = 60 * 1024 * 1024
MOST_VMEM_BYTES = 251 * 256 * 1024
SMALL_VMEM_BYTES = 8 * 1024 * 1024

f32 = jnp.float32
bf16 = jnp.bfloat16

IN_VMEM = pl.BlockSpec(memory_space=pltpu.VMEM)
IN_SMEM = pl.BlockSpec(memory_space=pltpu.SMEM)
ANYWHERE = pl.BlockSpec(memory_space=pl.ANY)


def call(kernel, outs, scratch, *args, vmem_bytes=VMEM_BYTES, **options):
    return pl.pallas_call(
        kernel,
        out_shape=outs,
        scratch_shapes=scratch,
        compiler_params=pltpu.CompilerParams(vmem_limit_bytes=vmem_bytes),
        **options,
    )(*args)


def leaf_phases(count):
    return [(4 * leaf + 1) / (4 * count) for leaf in range(count)]


def root_times(re, im, num, den, sign):
    if num == 0:
        return re, im
    if 4 * num == den:
        return (im, -re) if sign < 0 else (-im, re)
    cosine = math.cos(2.0 * math.pi * num / den)
    sine = sign * math.sin(2.0 * math.pi * num / den)
    if 8 * num == den:
        return ((re + im) * cosine, (im - re) * cosine) if sign < 0 else ((re - im) * cosine, (re + im) * cosine)
    if 8 * num == 3 * den:
        return ((re - im) * cosine, (re + im) * cosine) if sign < 0 else ((re + im) * cosine, (im - re) * cosine)
    return re * cosine - im * sine, im * cosine + re * sine


def short_fft(values, sign):
    count = len(values)
    if count == 1:
        return values
    even = short_fft(values[0::2], sign)
    odd = short_fft(values[1::2], sign)
    first = []
    second = []
    for num in range(count // 2):
        re, im = root_times(*odd[num], num, count, sign)
        first.append((even[num][0] + re, even[num][1] + im))
        second.append((even[num][0] - re, even[num][1] - im))
    return first + second


def to_leaves(parts):
    count = len(parts)
    turned = []
    for idx, part in enumerate(parts):
        angle = 2.0 * math.pi * idx / (4 * count)
        turned.append((part * math.cos(angle), part * (-math.sin(angle))) if idx else (part, jnp.zeros_like(part)))
    return short_fft(turned, -1)


def from_leaves(leaves, scale):
    count = len(leaves)
    parts = []
    for idx, (re, im) in enumerate(short_fft(leaves, 1)):
        angle = 2.0 * math.pi * idx / (4 * count)
        if idx == 0:
            parts.append(re * scale)
        else:
            parts.append(re * (math.cos(angle) * scale) - im * (math.sin(angle) * scale))
    return parts


def dft_matrix():
    idx = np.arange(SPAN)
    angle = (idx[:, None] * idx[None, :] % SPAN) * (2.0 * np.pi / SPAN)
    cosine, sine = np.cos(angle), np.sin(angle)
    return np.block([[cosine, sine], [-sine, cosine]])


def twist_angles(outer, inner):
    return np.asarray(leaf_phases(outer))[:, None] * np.asarray(inner)[None, :] * (2.0 * np.pi / SPAN)


def matrix_blocks():
    matrix = dft_matrix()
    high = matrix.astype(ml_dtypes.bfloat16)
    low = (matrix - high.astype(np.float64)).astype(ml_dtypes.bfloat16)
    return np.concatenate([high, low, high][:PASSES], axis=1)


def leaf_place(leaf):
    return leaf // 2, slice((leaf % 2) * LANES, (leaf % 2 + 1) * LANES)


def split_store(ref, leaf, below, here, value):
    pair, lanes = leaf_place(leaf)
    high = value.astype(bf16)
    for block in range(PASSES):
        part = high
        if PASSES == 3 and block == 2:
            part = (value - high.astype(f32)).astype(bf16)
        ref[pair, shifted_rows(here, block * BOTH + below), lanes] = part


def run_all(stages, rows_here, matmul=None, carry=0):
    tiles = matmul[2].shape[0] if matmul else 4
    per_tile = CHUNKS // tiles
    in_part = rows_here // CHUNK
    for tile in range(tiles):
        if matmul:
            matrix_ref, split_ref, result_ref = matmul
            result_ref[tile] = jnp.dot(matrix_ref[...], split_ref[tile], preferred_element_type=f32)
        for chunk in range(tile * per_tile, (tile + 1) * per_tile):
            for stage in stages:
                carry = stage(chunk // in_part, chunk % in_part * CHUNK, carry)
    return carry


def in_span(part, row, rows_here):
    return pl.ds(part * rows_here + row, CHUNK)


def twist_stage(coarse_ref, fine_ref, twist_ref, rows_here):
    outer = twist_ref.shape[1]

    def stage(part, row, carry):
        here = in_span(part, row, rows_here)
        idx = part * (rows_here // CHUNK) + row // CHUNK
        for leaf in range(outer):
            far_cosine = coarse_ref[idx, leaf]
            far_sine = coarse_ref[idx, outer + leaf]
            cosine = fine_ref[0, leaf]
            sine = fine_ref[1, leaf]
            twist_ref[0, leaf, here, :] = far_cosine * cosine - far_sine * sine
            twist_ref[1, leaf, here, :] = far_sine * cosine + far_cosine * sine
        return carry

    return stage


def leaves_stage(signals_ref, first_row, heads_ref, rows_here, twist_ref, split_ref):
    outer = twist_ref.shape[1]
    ratio = SPAN // rows_here

    def stage(part, row, carry):
        here = in_span(part, row, rows_here)
        rows = pl.ds(first_row + row, CHUNK)
        parts = [signals_ref[place * ratio + part, rows, :] for place in range(outer)]
        if heads_ref is not None and row == 0:
            parts = [heads_ref[place * ratio + part] for place in range(outer)]
        parts = [value.astype(f32) for value in parts]
        for leaf, (re, im) in enumerate(to_leaves(parts)):
            cosine = twist_ref[0, leaf, here, :]
            sine = twist_ref[1, leaf, here, :]
            split_store(split_ref, leaf, 0, here, re * cosine + im * sine)
            split_store(split_ref, leaf, SPAN, here, im * cosine - re * sine)
        return carry

    return stage


def shifted_rows(here, by):
    return pl.ds(here.start + by, here.size)


def combine_stage(left_ref, right_ref, split_ref, rows_here, conjugate):
    def stage(part, row, carry):
        here = in_span(part, row, rows_here)
        below = shifted_rows(here, SPAN)
        for leaf in range(2 * left_ref.shape[0]):
            pair, lanes = leaf_place(leaf)
            left_re = left_ref[pair, here, lanes]
            left_im = left_ref[pair, below, lanes]
            right_re = right_ref[pair, here, lanes]
            right_im = right_ref[pair, below, lanes]
            if conjugate:
                re = left_re * right_re + left_im * right_im
                minus_im = left_im * right_re - left_re * right_im
            else:
                re = left_re * right_re - left_im * right_im
                minus_im = -(left_re * right_im + left_im * right_re)
            split_store(split_ref, leaf, 0, here, re)
            split_store(split_ref, leaf, SPAN, here, minus_im)
        return carry

    return stage


def signal_stage(time_ref, twist_ref, rows_here, write):
    outer = twist_ref.shape[1]
    ratio = SPAN // rows_here
    scale = 1.0 / (SPAN * outer)

    def stage(part, row, carry):
        here = in_span(part, row, rows_here)
        below = shifted_rows(here, SPAN)
        leaves = []
        for leaf in range(outer):
            pair, lanes = leaf_place(leaf)
            cosine = twist_ref[0, leaf, here, :]
            sine = twist_ref[1, leaf, here, :]
            re = time_ref[pair, here, lanes]
            minus_im = time_ref[pair, below, lanes]
            leaves.append((re * cosine + minus_im * sine, re * sine - minus_im * cosine))
        for place, value in enumerate(from_leaves(leaves, scale)):
            carry = write(place * ratio + part, pl.ds(row, CHUNK), value, carry)
        return carry

    return stage


def first_rows(lead, first, taps):
    count = len(lead)
    rows = lead + first
    return [
        functools.reduce(lambda x, y: x + y, [taps[shift] * rows[count + row - shift] for shift in range(count + 1)])
        for row in range(count)
    ]


def first_signals(ahead, own, taps):
    count = len(taps) - 1

    def kind(rows, idx):
        return rows[idx * count : (idx + 1) * count]

    shorts = [first_rows(kind(ahead, idx), kind(own, 3 + idx), taps) for idx in range(3)]
    product = [(k_row * v_row).astype(bf16) for k_row, v_row in zip(shorts[1], shorts[2])]
    back_mix = [grad_row * q_row for grad_row, q_row in zip(kind(own, 6), shorts[0])]
    return shorts, product, back_mix


def first_backs(ahead, own, taps, skip, conv, corr):
    count = len(taps) - 1
    shorts, product, back_mix = first_signals(ahead, own, taps)
    back_q = []
    back_k = []
    back_v = []
    for row in range(count):
        filtered = conv[row] + skip * product[row].astype(f32)
        back_prod = corr[row] + skip * back_mix[row]
        back_q.append(own[6 * count + row] * filtered)
        back_k.append(back_prod * shorts[2][row])
        back_v.append(back_prod * shorts[1][row])
    return back_q + back_k + back_v


def extra_of(signals_ref, piece, rows_here, used):
    rows = signals_ref[piece, 3 * rows_here :, :].astype(f32)
    return [rows[idx : idx + 1] for idx in range(used)]


def tap_rows(taps_ref):
    return [taps_ref[shift : shift + 1, :] for shift in range(taps_ref.shape[0])]


def patch_first_rows(signals_ref, heads_ref, taps_ref, rows_here):
    pieces = signals_ref.shape[0]
    taps = tap_rows(taps_ref)[:-1]
    used = 7 * (len(taps) - 1)
    row_idx = lax.broadcasted_iota(jnp.int32, (TILE_ROWS, LANES), 0)
    ahead = [jnp.zeros((1, LANES), f32)] * used
    for piece in range(pieces):
        own = extra_of(signals_ref, piece, rows_here, used)
        for kind, rows in enumerate(first_signals(ahead, own, taps)[1:]):
            tile = signals_ref[piece, kind * rows_here : kind * rows_here + TILE_ROWS, :].astype(f32)
            for row, value in enumerate(rows):
                tile = jnp.where(row_idx == row, value.astype(f32), tile)
            heads_ref[kind, piece] = tile.astype(bf16)
        ahead = own


def write_edges(signals_ref, results_ref, taps_ref, rows_here):
    pieces = signals_ref.shape[0]
    *taps, skip = tap_rows(taps_ref)
    count = len(taps) - 1
    nothing = jnp.zeros((1, LANES), f32)
    extras = [extra_of(signals_ref, piece, rows_here, 7 * count) for piece in range(pieces)]
    for piece in range(pieces):
        rows = extras[piece - 1][: 3 * count] if piece else [nothing] * (3 * count)
        if piece + 1 < pieces:
            conv, corr = (
                results_ref[piece + 1, kind * rows_here : kind * rows_here + TILE_ROWS, :].astype(f32)
                for kind in range(2)
            )
            rows = rows + first_backs(
                extras[piece], extras[piece + 1], taps, skip,
                [conv[row : row + 1] for row in range(count)], [corr[row : row + 1] for row in range(count)],
            )
        spare = results_ref.shape[1] - 2 * rows_here - len(rows)
        rows.append(jnp.zeros((spare, LANES), f32))
        results_ref[piece, 2 * rows_here :, :] = jnp.concatenate(rows, axis=0).astype(bf16)


def products_kernel(
    rows_here, signals_hbm, taps_ref, coarse_ref, fine_ref, matrix_hbm, after_ref, results_hbm, lag_hbm,
    signals_ref, twist_ref, matrix_ref, heads_ref, results_ref, one_split, two_split, lag_split,
    filter_ref, product_ref, cotan_ref, time_ref, sems,
):
    filter_rows = pl.ds(2 * rows_here, rows_here)
    extra_rows = pl.ds(3 * rows_here, signals_ref.shape[1] - 3 * rows_here)
    signal_rows = pl.ds(0, 2 * rows_here)
    arrivals = [
        pltpu.make_async_copy(signals_hbm.at[:, rows], signals_ref.at[:, rows], sems.at[idx])
        for idx, rows in enumerate((filter_rows, extra_rows, signal_rows))
    ]
    matrix_copy = pltpu.make_async_copy(matrix_hbm, matrix_ref, sems.at[3])
    lag_copy = pltpu.make_async_copy(lag_split, lag_hbm, sems.at[4])
    returns = [
        pltpu.make_async_copy(results_ref.at[:, rows], results_hbm.at[:, rows], sems.at[5 + idx])
        for idx, rows in enumerate(
            (pl.ds(0, rows_here), pl.ds(rows_here, results_ref.shape[1] - rows_here))
        )
    ]

    def leaves(kind, split_ref):
        heads = heads_ref.at[kind] if kind < 2 else None
        return leaves_stage(signals_ref, kind * rows_here, heads, rows_here, twist_ref, split_ref)

    def combine(left_ref, right_ref, split_ref, conjugate):
        return combine_stage(left_ref, right_ref, split_ref, rows_here, conjugate)

    def result(kind, from_ref):
        def write(piece, rows, value, carry):
            place = pl.ds(kind * rows_here + rows.start, CHUNK)
            results_ref[piece, place, :] = value.astype(bf16)
            return carry

        return signal_stage(from_ref, twist_ref, rows_here, write)

    arrivals[0].start()
    run_all([twist_stage(coarse_ref, fine_ref, twist_ref, rows_here)], rows_here)
    arrivals[0].wait()
    for copy in (matrix_copy, arrivals[1], arrivals[2]):
        copy.start()
    run_all([leaves(2, one_split)], rows_here)
    arrivals[1].wait()
    arrivals[2].wait()
    patch_first_rows(signals_ref, heads_ref, taps_ref, rows_here)
    matrix_copy.wait()
    run_all([leaves(0, two_split)], rows_here, (matrix_ref, one_split, filter_ref))
    run_all([leaves(1, one_split)], rows_here, (matrix_ref, two_split, product_ref))
    run_all([combine(filter_ref, product_ref, two_split, False)], rows_here, (matrix_ref, one_split, cotan_ref))
    run_all([combine(filter_ref, cotan_ref, one_split, True)], rows_here, (matrix_ref, two_split, time_ref))
    run_all(
        [combine(product_ref, cotan_ref, lag_split, True), result(0, time_ref)],
        rows_here, (matrix_ref, one_split, filter_ref),
    )
    lag_copy.start()
    returns[0].start()
    run_all([result(1, filter_ref)], rows_here)
    write_edges(signals_ref, results_ref, taps_ref, rows_here)
    returns[1].start()
    lag_copy.wait()
    returns[0].wait()
    returns[1].wait()


def lag_kernel(
    split_hbm, coarse_ref, fine_ref, matrix_hbm, lag_ref, square_ref, twist_ref, matrix_ref, split_ref, time_ref, sems
):
    rows_here = lag_ref.shape[1]
    copies = [
        pltpu.make_async_copy(matrix_hbm, matrix_ref, sems.at[0]),
        pltpu.make_async_copy(split_hbm, split_ref, sems.at[1]),
    ]
    for copy in copies:
        copy.start()
    run_all([twist_stage(coarse_ref, fine_ref, twist_ref, rows_here)], rows_here)
    for copy in copies:
        copy.wait()
    run_all([], rows_here, (matrix_ref, split_ref, time_ref))

    def write(piece, rows, value, carry):
        lag_ref[piece, rows, :] = value.astype(bf16)
        return carry + value * value

    square = run_all(
        [signal_stage(time_ref, twist_ref, rows_here, write)], rows_here, None, jnp.zeros((CHUNK, LANES), f32)
    )
    square_ref[...] = jnp.sum(square, axis=0, keepdims=True)


class Transforms:
    def __init__(self, pieces, rows_here):
        outer = pieces * rows_here // SPAN
        pairs = outer // 2
        coarse = twist_angles(outer, CHUNK * np.arange(CHUNKS)).T
        fine = twist_angles(outer, np.arange(CHUNK))[..., None] * np.ones(LANES)
        self.tables = [
            jnp.asarray(np.concatenate([np.cos(coarse), np.sin(coarse)], axis=1).astype(np.float32)),
            jnp.asarray(np.stack([np.cos(fine), np.sin(fine)]).astype(np.float32)),
            jnp.asarray(matrix_blocks()),
        ]
        self.split = jax.ShapeDtypeStruct((pairs, PASSES * BOTH, 2 * LANES), bf16)
        self.signal = jax.ShapeDtypeStruct((pieces, rows_here, LANES), bf16)
        self.result = jax.ShapeDtypeStruct((pieces, 2 * rows_here + TILE_ROWS, LANES), bf16)
        self.square = jax.ShapeDtypeStruct((1, LANES), f32)
        self.result_work = pltpu.VMEM(self.result.shape, bf16)
        self.work = pltpu.VMEM((pairs, BOTH, 2 * LANES), f32)
        self.split_work = pltpu.VMEM(self.split.shape, bf16)
        self.twist_work = pltpu.VMEM((2, outer, SPAN, LANES), f32)
        self.matrix_work = pltpu.VMEM(self.tables[2].shape, bf16)

    def products(self, signals, taps, after):
        return call(
            functools.partial(products_kernel, self.signal.shape[1]), (self.result, self.split),
            [pltpu.VMEM(signals.shape, bf16), self.twist_work, self.matrix_work]
            + [pltpu.VMEM((2, signals.shape[0], TILE_ROWS, LANES), bf16), self.result_work]
            + [self.split_work] * 3
            + [self.work] * 4
            + [pltpu.SemaphoreType.DMA((7,))],
            signals, taps, *self.tables, after,
            vmem_bytes=MOST_VMEM_BYTES,
            in_specs=[ANYWHERE, IN_VMEM, IN_SMEM, IN_VMEM, ANYWHERE, ANYWHERE],
            out_specs=(ANYWHERE, ANYWHERE),
        )

    def lag(self, lag_split):
        return call(
            lag_kernel, (self.signal, self.square),
            [self.twist_work, self.matrix_work, self.split_work, self.work, pltpu.SemaphoreType.DMA((2,))],
            lag_split, *self.tables,
            in_specs=[ANYWHERE, IN_SMEM, IN_VMEM, ANYWHERE],
            out_specs=(IN_VMEM, IN_VMEM),
        )


class PlainTransforms:
    def __init__(self, pieces, rows_here):
        self.seq_len = pieces * rows_here
        self.pieces = pieces
        self.outer = self.seq_len // SPAN
        idx = np.arange(SPAN)
        angle = (idx[:, None] * idx[None, :] % SPAN) * (2.0 * np.pi / SPAN)
        self.cosine = jnp.asarray(np.cos(angle), f32)
        self.sine = jnp.asarray(np.sin(angle), f32)
        twist = twist_angles(self.outer, idx)
        self.twist = jnp.asarray(np.stack([np.cos(twist), np.sin(twist)]), f32)[..., None]

    def dot(self, matrix, signal):
        return jnp.einsum("fs,tsc->tfc", matrix, signal, precision=lax.Precision.HIGHEST)

    def spectrum(self, signal):
        parts = signal.astype(f32).reshape(self.outer, SPAN, -1)
        leaves = to_leaves([parts[part] for part in range(self.outer)])
        re = jnp.stack([leaf[0] for leaf in leaves])
        im = jnp.stack([leaf[1] for leaf in leaves])
        twist_re = re * self.twist[0] + im * self.twist[1]
        twist_im = im * self.twist[0] - re * self.twist[1]
        return (
            self.dot(self.cosine, twist_re) + self.dot(self.sine, twist_im),
            self.dot(self.cosine, twist_im) - self.dot(self.sine, twist_re),
        )

    def back(self, re, im):
        time_re = self.dot(self.cosine, re) - self.dot(self.sine, im)
        time_im = self.dot(self.cosine, im) + self.dot(self.sine, re)
        leaf_re = time_re * self.twist[0] - time_im * self.twist[1]
        leaf_im = time_im * self.twist[0] + time_re * self.twist[1]
        parts = from_leaves([(leaf_re[leaf], leaf_im[leaf]) for leaf in range(self.outer)], 1.0 / self.seq_len)
        return jnp.stack(parts).reshape(self.pieces, self.seq_len // self.pieces, -1)

    def products(self, signals, taps_and_skip, after):
        rows_here = self.seq_len // self.pieces
        parts = [signals[:, kind * rows_here : (kind + 1) * rows_here] for kind in range(3)]
        extra = signals[:, 3 * rows_here :].astype(f32)
        rows = [extra[:, idx : idx + 1] for idx in range(extra.shape[1])]
        ahead = [jnp.concatenate([jnp.zeros_like(row[:1]), row[:-1]], axis=0) for row in rows]
        *taps, skip = [taps_and_skip[row][None, None, :] for row in range(taps_and_skip.shape[0])]
        count = len(taps) - 1
        for kind, first in enumerate(first_signals(ahead, rows, taps)[1:]):
            first = jnp.concatenate(first, axis=1)
            parts[kind] = jnp.concatenate([first.astype(bf16), parts[kind][:, first.shape[1] :]], axis=1)
        product, cotan, taps_spec = (self.spectrum(part) for part in parts)
        conv = self.back(
            taps_spec[0] * product[0] - taps_spec[1] * product[1], taps_spec[0] * product[1] + taps_spec[1] * product[0]
        ).astype(bf16)
        corr = self.back(
            taps_spec[0] * cotan[0] + taps_spec[1] * cotan[1], taps_spec[0] * cotan[1] - taps_spec[1] * cotan[0]
        ).astype(bf16)
        lag = (
            product[0] * cotan[0] + product[1] * cotan[1],
            product[0] * cotan[1] - product[1] * cotan[0],
        )
        backs = first_backs(
            ahead, rows, taps, skip,
            [conv[:, row : row + 1].astype(f32) for row in range(count)],
            [corr[:, row : row + 1].astype(f32) for row in range(count)],
        )
        behind = [jnp.concatenate([row[1:], jnp.zeros_like(row[:1])], axis=0) for row in backs]
        edge = jnp.concatenate(ahead[: 3 * count] + behind, axis=1).astype(bf16)
        edge = jnp.pad(edge, ((0, 0), (0, TILE_ROWS - edge.shape[1]), (0, 0)))
        return jnp.concatenate([conv, corr, edge], axis=1), lag

    def lag(self, lag_spec):
        lag = self.back(*lag_spec)
        squares = jnp.sum(lag * lag, axis=(0, 1))
        return lag.astype(bf16), jnp.zeros((1, LANES), f32).at[0, : squares.shape[0]].set(squares)


def group(idx):
    return slice(idx * LANES, (idx + 1) * LANES)


def streamed(work, steps, per_step, places, in_count, out_count, kept, *refs):
    moved = in_count + out_count
    hbm = refs[:moved]
    kept_refs = refs[moved : moved + kept]
    held = refs[moved + kept : 2 * moved + kept]
    scratch = refs[2 * moved + kept : -1]
    sems = refs[-1]

    def copy(place, step):
        outside = hbm[place].at[places[place](step)]
        inside = held[place].at[places[place](step)]
        ends = (outside, inside) if place < in_count else (inside, outside)
        return pltpu.make_async_copy(*ends, sems.at[place, step])

    def arrivals(step):
        return [copy(place, step) for place in range(in_count) if places[place](step) is not None]

    for step in range(steps):
        for arrival in arrivals(step):
            arrival.start()
    for step in range(steps):
        for arrival in arrivals(step):
            arrival.wait()
        for idx in range(step * per_step, (step + 1) * per_step):
            exts = scratch[idx % 2 :: 2]
            work(idx, held[:in_count], held[in_count:] + kept_refs, exts)
        for place in range(in_count, moved):
            copy(place, step).start()
    for step in range(steps):
        for place in range(in_count, moved):
            copy(place, step).wait()


def stream_call(work, steps, per_step, operands, results, scratch=(), after=(), kept=(), vmem_bytes=VMEM_BYTES):
    arrays = [operand[0] for operand in operands]
    shapes = [jax.ShapeDtypeStruct(array.shape, array.dtype) for array in arrays] + [result[0] for result in results]
    cuts = [entry[1] for entry in list(operands) + list(results)]
    held = [pltpu.VMEM(shape.shape, shape.dtype) for shape in shapes]
    extra = list(after)
    kernel = functools.partial(streamed, work, steps, per_step, cuts, len(arrays), len(results), len(kept))

    def without_extra(*refs):
        kernel(*refs[: len(arrays)], *refs[len(arrays) + len(extra) :])

    return call(
        without_extra,
        tuple(result[0] for result in results) + tuple(kept),
        held + list(scratch) + [pltpu.SemaphoreType.DMA((len(shapes), steps))],
        *arrays, *extra,
        vmem_bytes=vmem_bytes,
        in_specs=[ANYWHERE] * (len(arrays) + len(extra)),
        out_specs=(ANYWHERE,) * len(results) + (IN_VMEM,) * len(kept),
    )


def cut_lanes(width, rank):
    def place(step):
        return (slice(None),) * (rank - 1) + (pl.ds(step * width, width),)

    return place


def cut_groups(per_step):
    def place(step):
        return (pl.ds(step * per_step, per_step),)

    return place


def cut_none(step):
    return None if step else (slice(None),)


def row_blocks(rows_here):
    return [slice(start, start + ROWS) for start in range(0, rows_here, ROWS)]


def extend_rows(lead, in_ref, lanes, ext_ref):
    ext_ref[PAD - lead.shape[0] : PAD, :] = lead
    ext_ref[PAD:, :] = in_ref[:, lanes].astype(f32)


def short_conv(ext_ref, taps, rows):
    result = None
    for shift_idx in range(taps.shape[0]):
        term = taps[shift_idx : shift_idx + 1] * ext_ref[PAD + rows.start - shift_idx : PAD + rows.stop - shift_idx, :]
        result = term if result is None else result + term
    return result


def signals_work(idx, operands, results, exts):
    q_ref, k_ref, v_ref, grad_ref, kernel_ref, taps_ref = operands
    lanes = group(idx)
    taps = taps_ref[:, lanes]
    halo_rows = taps.shape[0] - 1
    rows_here = q_ref.shape[0]
    for ext, in_ref in zip(exts, operands):
        extend_rows(jnp.zeros((halo_rows, LANES), f32), in_ref, lanes, ext)
    for rows in row_blocks(rows_here):
        q_short, k_short, v_short = (short_conv(ext, taps, rows) for ext in exts)
        below = [slice(kind * rows_here + rows.start, kind * rows_here + rows.stop) for kind in range(3)]
        results[0][idx, below[0], :] = (k_short * v_short).astype(bf16)
        results[0][idx, below[1], :] = (grad_ref[rows, lanes].astype(f32) * q_short).astype(bf16)
        results[0][idx, below[2], :] = kernel_ref[rows, lanes].astype(bf16)
    top = grad_ref[0:TILE_ROWS, lanes].astype(f32)[:halo_rows]
    extra = [ext[ext.shape[0] - halo_rows :, :] for ext in exts] + [ext[PAD : PAD + halo_rows, :] for ext in exts]
    extra_count = results[0].shape[1] - 3 * rows_here
    blank = jnp.zeros((extra_count - 7 * halo_rows, LANES), f32)
    results[0][idx, 3 * rows_here :, :] = jnp.concatenate(extra + [top, blank], axis=0).astype(bf16)


def short_work(idx, operands, results, exts):
    lanes = group(idx)
    taps = operands[3][:, lanes]
    for ext, in_ref in zip(exts, operands):
        extend_rows(jnp.zeros((taps.shape[0] - 1, LANES), f32), in_ref, lanes, ext)
    for rows in row_blocks(operands[0].shape[0]):
        for place, ext in enumerate(exts):
            results[0][place, rows, lanes] = short_conv(ext, taps, rows)


def fold(value):
    return jnp.sum(value.reshape(-1, 8, LANES), axis=0)


def finish_work(idx, operands, results, exts):
    q_ref, k_ref, v_ref, grad_ref, short_ref, taps_ref, skip_ref, long_ref, squares_ref = operands
    mixed_ref, grad_q_ref, grad_k_ref, grad_v_ref, sums_ref = results
    lanes = group(idx)
    taps = taps_ref[:, lanes]
    skip = skip_ref[:, lanes]
    taps_count = taps.shape[0]
    halo_rows = taps_count - 1
    rows_here = q_ref.shape[0]
    sums = [jnp.zeros((8, LANES), f32) for _ in range(taps_count + 1)]
    edge = long_ref[idx, 2 * rows_here :, :].astype(f32)
    for place, ext in enumerate(exts):
        at = (3 + place) * halo_rows
        ext[rows_here : rows_here + halo_rows, :] = edge[at : at + halo_rows]
    row_idx = lax.broadcasted_iota(jnp.int32, (ROWS, LANES), 0)

    def short(place, rows):
        value = short_ref[place, rows, lanes]
        if rows.start == 0:
            for shift_idx in range(1, taps_count):
                terms = jnp.zeros((ROWS, LANES), f32)
                for row in range(shift_idx):
                    at = place * halo_rows + halo_rows + row - shift_idx
                    term = taps[shift_idx : shift_idx + 1] * edge[at : at + 1]
                    terms = jnp.where(row_idx == row, term, terms)
                value = value + terms
        return value

    for rows in row_blocks(rows_here):
        q_short, k_short, v_short = (short(place, rows) for place in range(3))
        product = (k_short * v_short).astype(bf16).astype(f32)
        filtered = long_ref[idx, rows, :].astype(f32) + skip * product
        mixed_ref[rows, lanes] = (q_short * filtered).astype(bf16)
        upstream = grad_ref[rows, lanes].astype(f32)
        back_mix = upstream * q_short
        below = slice(rows_here + rows.start, rows_here + rows.stop)
        back_prod = long_ref[idx, below, :].astype(f32) + skip * back_mix
        sums[taps_count] = sums[taps_count] + fold(back_mix * product)
        exts[0][rows, :] = upstream * filtered
        exts[1][rows, :] = back_prod * v_short
        exts[2][rows, :] = back_prod * k_short
    for ext, in_ref, out_ref in zip(exts, (q_ref, k_ref, v_ref), (grad_q_ref, grad_k_ref, grad_v_ref)):
        for rows in row_blocks(rows_here):
            signal = in_ref[rows, lanes].astype(f32)
            grad = None
            for shift_idx in range(taps_count):
                ahead = ext[rows.start + shift_idx : rows.stop + shift_idx, :]
                term = taps[shift_idx : shift_idx + 1] * ahead
                grad = term if grad is None else grad + term
                sums[shift_idx] = sums[shift_idx] + fold(ahead * signal)
            out_ref[rows, lanes] = grad.astype(bf16)
    if idx == 0:
        extra = slice(sums_ref.shape[1] - LANES, sums_ref.shape[1])
        sums_ref[:, extra] = jnp.zeros((taps_count + 1, LANES), f32)
        sums_ref[0:1, extra] = squares_ref[...]
    for shift_idx in range(taps_count + 1):
        sums_ref[shift_idx : shift_idx + 1, lanes] = jnp.sum(sums[shift_idx], axis=0, keepdims=True)


def norm_kernel(*refs):
    values, totals_ref, square_ref = refs[:-2], refs[-2], refs[-1]
    channels = totals_ref.shape[1] - LANES
    totals = values[0][...]
    if len(values) == 4:
        totals = (totals + values[1][...]) + (values[2][...] + values[3][...])
    totals_ref[...] = totals
    square = jnp.sum(totals[:, :channels] * totals[:, :channels]) + jnp.sum(totals[0:1, channels:])
    square_ref[...] = jnp.full(square_ref.shape, square)


def add_kernel(*refs):
    refs[-1][...] = add_up([ref[...] for ref in refs[:-1]])


def same_kernel(value_ref, same_ref):
    same_ref[...] = value_ref[...]


def scale_kernel(limit, totals_ref, norm_ref, lag_ref, taps_out, skip_out, kernel_out):
    taps_count, channels = taps_out.shape
    factor = limit / jnp.maximum(jnp.sqrt(norm_ref[...]), limit)
    for idx in range(channels // LANES):
        lanes = slice(idx * LANES, (idx + 1) * LANES)
        taps_out[:, lanes] = totals_ref[0:taps_count, lanes] * factor
        skip_out[:, lanes] = totals_ref[taps_count : taps_count + 1, lanes] * factor
        kernel_out[:, lanes] = lag_ref[idx].astype(f32) * factor


def exchange(pieces_first):
    return lax.all_to_all(pieces_first, "ctx", split_axis=0, concat_axis=0, tiled=True)


def to_pieces(groups, pieces):
    count, rows, lanes = groups.shape
    if count == pieces:
        return groups
    share = count * lanes // pieces
    split = groups.reshape(count, rows, lanes // share, share)
    return split.transpose(0, 2, 1, 3).reshape(pieces, rows, share)


def to_groups(parts):
    pieces, rows, share = parts.shape
    if share == LANES:
        return parts
    joined = parts.reshape(pieces * share // LANES, LANES // share, rows, share)
    return joined.transpose(0, 2, 1, 3).reshape(-1, rows, LANES)


def partners(value, axis, steps):
    size = lax.axis_size(axis)
    return [value] + [lax.ppermute(value, axis, [(i, i ^ step) for i in range(size)]) for step in steps]


def rounds_of(size):
    rounds = []
    step = 1
    while step < size:
        rounds.append((step, 2 * step, 3 * step) if size // step >= 4 else (step,))
        step *= 4 if size // step >= 4 else 2
    return rounds


def add_up(values):
    if len(values) == 2:
        return values[0] + values[1]
    return (values[0] + values[1]) + (values[2] + values[3])


def body(q_in, k_in, v_in, grad_out, short_filter, kernel, skip):
    pieces = lax.axis_size("ctx")
    sides = lax.axis_size("ch")
    rows_here, channels = q_in.shape
    seq_len = pieces * rows_here
    taps_count = short_filter.shape[0]
    halo_rows = taps_count - 1
    groups = channels // LANES
    share = channels // pieces
    per_step = min(groups, 8)
    steps = groups // per_step
    lanes2 = cut_lanes(per_step * LANES, 2)
    lanes3 = cut_lanes(per_step * LANES, 3)
    skip_row = skip.reshape(1, channels)
    transforms = (Transforms if share == LANES else PlainTransforms)(pieces, rows_here)
    stream = functools.partial(stream_call, steps=steps, per_step=per_step)

    flat = jax.ShapeDtypeStruct((rows_here, channels), bf16)
    extra_rows = -(-7 * halo_rows // TILE_ROWS) * TILE_ROWS
    sent = jax.ShapeDtypeStruct((groups, 3 * rows_here + extra_rows, LANES), bf16)
    exts = [pltpu.VMEM((rows_here + PAD, LANES), f32)] * 6

    (signals,) = stream(
        signals_work,
        operands=[(x, lanes2) for x in (q_in, k_in, v_in, grad_out, kernel, short_filter)],
        results=[(sent, cut_groups(per_step))],
        scratch=exts,
        vmem_bytes=MOST_VMEM_BYTES,
    )
    signals_here = exchange(to_pieces(signals, pieces))
    (short,) = stream(
        short_work,
        operands=[(x, lanes2) for x in (q_in, k_in, v_in, short_filter)],
        results=[(jax.ShapeDtypeStruct((3, rows_here, channels), f32), lanes3)],
        scratch=exts,
        after=[signals],
    )
    taps_and_skip = jnp.concatenate([short_filter, skip_row], axis=0)
    taps_here = lax.dynamic_slice_in_dim(taps_and_skip, lax.axis_index("ctx") * share, share, axis=1)
    long_here, lag_spec = transforms.products(signals_here, taps_here, short)
    long = to_groups(exchange(long_here))
    lag_here, lag_squares = transforms.lag(lag_spec)
    lag = to_groups(exchange(lag_here))

    mixed, grad_q, grad_k, grad_v, sums = stream(
        finish_work,
        operands=[(x, lanes2) for x in (q_in, k_in, v_in, grad_out)]
        + [(short, lanes3), (short_filter, lanes2), (skip_row, lanes2)]
        + [(long, cut_groups(per_step)), (lag_squares, cut_none)],
        results=[(flat, lanes2)] * 4,
        scratch=exts,
        kept=[jax.ShapeDtypeStruct((taps_count + 1, channels + LANES), f32)],
    )

    totals = sums
    rounds = rounds_of(pieces)
    for steps_of in rounds[:-1]:
        values = partners(totals, "ctx", steps_of)
        values[0] = call(
            same_kernel, jax.ShapeDtypeStruct(totals.shape, f32), [], totals,
            vmem_bytes=SMALL_VMEM_BYTES, in_specs=[IN_VMEM], out_specs=IN_VMEM,
        )
        totals = call(
            add_kernel, jax.ShapeDtypeStruct(totals.shape, f32), [], *values,
            vmem_bytes=SMALL_VMEM_BYTES, in_specs=[IN_VMEM] * len(values), out_specs=IN_VMEM,
        )
    last = partners(totals, "ctx", rounds[-1])
    if len(last) == 2:
        last = [last[0] + last[1]]

    totals, norm_sq = call(
        norm_kernel,
        (jax.ShapeDtypeStruct(totals.shape, f32), jax.ShapeDtypeStruct((1, LANES), f32)),
        [], *last,
        vmem_bytes=SMALL_VMEM_BYTES,
        in_specs=[IN_VMEM] * len(last), out_specs=(IN_VMEM, IN_VMEM),
    )
    for steps_of in rounds_of(sides):
        norm_sq = add_up(partners(norm_sq, "ch", steps_of))

    limit = math.sqrt(float(seq_len * channels * sides))
    grad_short, grad_skip, grad_kernel = call(
        functools.partial(scale_kernel, limit),
        (
            jax.ShapeDtypeStruct((taps_count, channels), f32),
            jax.ShapeDtypeStruct((1, channels), f32),
            jax.ShapeDtypeStruct((rows_here, channels), f32),
        ),
        [],
        totals, norm_sq, lag,
        vmem_bytes=SMALL_VMEM_BYTES,
        in_specs=[IN_VMEM] * 3,
        out_specs=(IN_VMEM,) * 3,
    )
    return mixed, grad_q, grad_k, grad_v, grad_short, grad_skip.reshape(channels), grad_kernel


def solution(mesh):
    in_specs = (
        P("ctx", "ch"),
        P("ctx", "ch"),
        P("ctx", "ch"),
        P("ctx", "ch"),
        P(None, "ch"),
        P("ctx", "ch"),
        P("ch"),
    )
    out_specs = (
        P("ctx", "ch"),
        P("ctx", "ch"),
        P("ctx", "ch"),
        P("ctx", "ch"),
        P(None, "ch"),
        P("ch"),
        P("ctx", "ch"),
    )
    return jax.shard_map(body, mesh=mesh, in_specs=in_specs, out_specs=out_specs, check_vma=False)
```

```python
import functools
import math

import jax
import jax.numpy as jnp
import ml_dtypes
import numpy as np
from jax import lax
from jax.experimental import pallas as pl
from jax.experimental.pallas import tpu as pltpu
from jax.sharding import PartitionSpec as P

LANES = 128
SPAN = 256
BOTH = 2 * SPAN
CHUNK = 16
CHUNKS = SPAN // CHUNK
PAD = 8
ROWS = 16
CUTS = 4
PASSES = 1
TILE_ROWS = 16
VMEM_BYTES = 60 * 1024 * 1024
MOST_VMEM_BYTES = 251 * 256 * 1024
SMALL_VMEM_BYTES = 8 * 1024 * 1024

f32 = jnp.float32
bf16 = jnp.bfloat16

IN_VMEM = pl.BlockSpec(memory_space=pltpu.VMEM)
IN_SMEM = pl.BlockSpec(memory_space=pltpu.SMEM)
ANYWHERE = pl.BlockSpec(memory_space=pl.ANY)


def call(kernel, outs, scratch, *args, vmem_bytes=VMEM_BYTES, **options):
    return pl.pallas_call(
        kernel,
        out_shape=outs,
        scratch_shapes=scratch,
        compiler_params=pltpu.CompilerParams(vmem_limit_bytes=vmem_bytes),
        **options,
    )(*args)


def leaf_phases(count):
    return [(4 * leaf + 1) / (4 * count) for leaf in range(count)]


def root_times(re, im, num, den, sign):
    if num == 0:
        return re, im
    if 4 * num == den:
        return (im, -re) if sign < 0 else (-im, re)
    cosine = math.cos(2.0 * math.pi * num / den)
    sine = sign * math.sin(2.0 * math.pi * num / den)
    if 8 * num == den:
        return ((re + im) * cosine, (im - re) * cosine) if sign < 0 else ((re - im) * cosine, (re + im) * cosine)
    if 8 * num == 3 * den:
        return ((re - im) * cosine, (re + im) * cosine) if sign < 0 else ((re + im) * cosine, (im - re) * cosine)
    return re * cosine - im * sine, im * cosine + re * sine


def short_fft(values, sign):
    count = len(values)
    if count == 1:
        return values
    even = short_fft(values[0::2], sign)
    odd = short_fft(values[1::2], sign)
    first = []
    second = []
    for num in range(count // 2):
        re, im = root_times(*odd[num], num, count, sign)
        first.append((even[num][0] + re, even[num][1] + im))
        second.append((even[num][0] - re, even[num][1] - im))
    return first + second


def to_leaves(parts):
    count = len(parts)
    turned = []
    for idx, part in enumerate(parts):
        angle = 2.0 * math.pi * idx / (4 * count)
        turned.append((part * math.cos(angle), part * (-math.sin(angle))) if idx else (part, jnp.zeros_like(part)))
    return short_fft(turned, -1)


def from_leaves(leaves, scale):
    count = len(leaves)
    parts = []
    for idx, (re, im) in enumerate(short_fft(leaves, 1)):
        angle = 2.0 * math.pi * idx / (4 * count)
        if idx == 0:
            parts.append(re * scale)
        else:
            parts.append(re * (math.cos(angle) * scale) - im * (math.sin(angle) * scale))
    return parts


def dft_matrix():
    idx = np.arange(SPAN)
    angle = (idx[:, None] * idx[None, :] % SPAN) * (2.0 * np.pi / SPAN)
    cosine, sine = np.cos(angle), np.sin(angle)
    return np.block([[cosine, sine], [-sine, cosine]])


def twist_angles(outer, inner):
    return np.asarray(leaf_phases(outer))[:, None] * np.asarray(inner)[None, :] * (2.0 * np.pi / SPAN)


def matrix_blocks():
    matrix = dft_matrix()
    high = matrix.astype(ml_dtypes.bfloat16)
    low = (matrix - high.astype(np.float64)).astype(ml_dtypes.bfloat16)
    return np.concatenate([high, low, high][:PASSES], axis=1)


def leaf_place(leaf):
    return leaf // 2, slice((leaf % 2) * LANES, (leaf % 2 + 1) * LANES)


def split_store(ref, leaf, below, here, value):
    pair, lanes = leaf_place(leaf)
    high = value.astype(bf16)
    for block in range(PASSES):
        part = high
        if PASSES == 3 and block == 2:
            part = (value - high.astype(f32)).astype(bf16)
        ref[pair, shifted_rows(here, block * BOTH + below), lanes] = part


def run_all(stages, rows_here, matmul=None, carry=0):
    tiles = matmul[2].shape[0] if matmul else 4
    per_tile = CHUNKS // tiles
    in_part = rows_here // CHUNK
    for tile in range(tiles):
        if matmul:
            matrix_ref, split_ref, result_ref = matmul
            result_ref[tile] = jnp.dot(matrix_ref[...], split_ref[tile], preferred_element_type=f32)
        for chunk in range(tile * per_tile, (tile + 1) * per_tile):
            for stage in stages:
                carry = stage(chunk // in_part, chunk % in_part * CHUNK, carry)
    return carry


def in_span(part, row, rows_here):
    return pl.ds(part * rows_here + row, CHUNK)


def twist_stage(coarse_ref, fine_ref, twist_ref, rows_here):
    outer = twist_ref.shape[1]

    def stage(part, row, carry):
        here = in_span(part, row, rows_here)
        idx = part * (rows_here // CHUNK) + row // CHUNK
        for leaf in range(outer):
            far_cosine = coarse_ref[idx, leaf]
            far_sine = coarse_ref[idx, outer + leaf]
            cosine = fine_ref[0, leaf]
            sine = fine_ref[1, leaf]
            twist_ref[0, leaf, here, :] = far_cosine * cosine - far_sine * sine
            twist_ref[1, leaf, here, :] = far_sine * cosine + far_cosine * sine
        return carry

    return stage


def leaves_stage(signals_ref, first_row, heads_ref, rows_here, twist_ref, split_ref):
    outer = twist_ref.shape[1]
    ratio = SPAN // rows_here

    def stage(part, row, carry):
        here = in_span(part, row, rows_here)
        rows = pl.ds(first_row + row, CHUNK)
        parts = [signals_ref[place * ratio + part, rows, :] for place in range(outer)]
        if heads_ref is not None and row == 0:
            parts = [heads_ref[place * ratio + part] for place in range(outer)]
        parts = [value.astype(f32) for value in parts]
        for leaf, (re, im) in enumerate(to_leaves(parts)):
            cosine = twist_ref[0, leaf, here, :]
            sine = twist_ref[1, leaf, here, :]
            split_store(split_ref, leaf, 0, here, re * cosine + im * sine)
            split_store(split_ref, leaf, SPAN, here, im * cosine - re * sine)
        return carry

    return stage


def shifted_rows(here, by):
    return pl.ds(here.start + by, here.size)


def combine_stage(left_ref, right_ref, split_ref, rows_here, conjugate):
    def stage(part, row, carry):
        here = in_span(part, row, rows_here)
        below = shifted_rows(here, SPAN)
        for leaf in range(2 * left_ref.shape[0]):
            pair, lanes = leaf_place(leaf)
            left_re = left_ref[pair, here, lanes]
            left_im = left_ref[pair, below, lanes]
            right_re = right_ref[pair, here, lanes]
            right_im = right_ref[pair, below, lanes]
            if conjugate:
                re = left_re * right_re + left_im * right_im
                minus_im = left_im * right_re - left_re * right_im
            else:
                re = left_re * right_re - left_im * right_im
                minus_im = -(left_re * right_im + left_im * right_re)
            split_store(split_ref, leaf, 0, here, re)
            split_store(split_ref, leaf, SPAN, here, minus_im)
        return carry

    return stage


def signal_stage(time_ref, twist_ref, rows_here, write):
    outer = twist_ref.shape[1]
    ratio = SPAN // rows_here
    scale = 1.0 / (SPAN * outer)

    def stage(part, row, carry):
        here = in_span(part, row, rows_here)
        below = shifted_rows(here, SPAN)
        leaves = []
        for leaf in range(outer):
            pair, lanes = leaf_place(leaf)
            cosine = twist_ref[0, leaf, here, :]
            sine = twist_ref[1, leaf, here, :]
            re = time_ref[pair, here, lanes]
            minus_im = time_ref[pair, below, lanes]
            leaves.append((re * cosine + minus_im * sine, re * sine - minus_im * cosine))
        for place, value in enumerate(from_leaves(leaves, scale)):
            carry = write(place * ratio + part, pl.ds(row, CHUNK), value, carry)
        return carry

    return stage


def first_rows(lead, first, taps):
    count = len(lead)
    rows = lead + first
    return [
        functools.reduce(lambda x, y: x + y, [taps[shift] * rows[count + row - shift] for shift in range(count + 1)])
        for row in range(count)
    ]


def first_signals(ahead, own, taps):
    count = len(taps) - 1

    def kind(rows, idx):
        return rows[idx * count : (idx + 1) * count]

    shorts = [first_rows(kind(ahead, idx), kind(own, 3 + idx), taps) for idx in range(3)]
    product = [(k_row * v_row).astype(bf16) for k_row, v_row in zip(shorts[1], shorts[2])]
    back_mix = [grad_row * q_row for grad_row, q_row in zip(kind(own, 6), shorts[0])]
    return shorts, product, back_mix


def first_backs(ahead, own, taps, skip, conv, corr):
    count = len(taps) - 1
    shorts, product, back_mix = first_signals(ahead, own, taps)
    back_q = []
    back_k = []
    back_v = []
    for row in range(count):
        filtered = conv[row] + skip * product[row].astype(f32)
        back_prod = corr[row] + skip * back_mix[row]
        back_q.append(own[6 * count + row] * filtered)
        back_k.append(back_prod * shorts[2][row])
        back_v.append(back_prod * shorts[1][row])
    return back_q + back_k + back_v


def extra_of(signals_ref, piece, rows_here, used):
    rows = signals_ref[piece, 3 * rows_here :, :].astype(f32)
    return [rows[idx : idx + 1] for idx in range(used)]


def tap_rows(taps_ref):
    return [taps_ref[shift : shift + 1, :] for shift in range(taps_ref.shape[0])]


def patch_first_rows(signals_ref, heads_ref, taps_ref, rows_here):
    pieces = signals_ref.shape[0]
    taps = tap_rows(taps_ref)[:-1]
    used = 7 * (len(taps) - 1)
    row_idx = lax.broadcasted_iota(jnp.int32, (TILE_ROWS, LANES), 0)
    ahead = [jnp.zeros((1, LANES), f32)] * used
    for piece in range(pieces):
        own = extra_of(signals_ref, piece, rows_here, used)
        for kind, rows in enumerate(first_signals(ahead, own, taps)[1:]):
            tile = signals_ref[piece, kind * rows_here : kind * rows_here + TILE_ROWS, :].astype(f32)
            for row, value in enumerate(rows):
                tile = jnp.where(row_idx == row, value.astype(f32), tile)
            heads_ref[kind, piece] = tile.astype(bf16)
        ahead = own


def write_edges(signals_ref, results_ref, taps_ref, rows_here):
    pieces = signals_ref.shape[0]
    *taps, skip = tap_rows(taps_ref)
    count = len(taps) - 1
    nothing = jnp.zeros((1, LANES), f32)
    extras = [extra_of(signals_ref, piece, rows_here, 7 * count) for piece in range(pieces)]
    for piece in range(pieces):
        rows = extras[piece - 1][: 3 * count] if piece else [nothing] * (3 * count)
        if piece + 1 < pieces:
            conv, corr = (
                results_ref[piece + 1, kind * rows_here : kind * rows_here + TILE_ROWS, :].astype(f32)
                for kind in range(2)
            )
            rows = rows + first_backs(
                extras[piece], extras[piece + 1], taps, skip,
                [conv[row : row + 1] for row in range(count)], [corr[row : row + 1] for row in range(count)],
            )
        spare = results_ref.shape[1] - 2 * rows_here - len(rows)
        rows.append(jnp.zeros((spare, LANES), f32))
        results_ref[piece, 2 * rows_here :, :] = jnp.concatenate(rows, axis=0).astype(bf16)


def products_kernel(
    rows_here, signals_hbm, taps_ref, coarse_ref, fine_ref, matrix_hbm, after_ref, results_hbm, lag_hbm,
    signals_ref, twist_ref, matrix_ref, heads_ref, results_ref, one_split, two_split, lag_split,
    filter_ref, product_ref, cotan_ref, time_ref, sems,
):
    all_rows = signals_ref.shape[1]
    back_rows = results_ref.shape[1]
    sem_idx = iter(range(sems.shape[0]))

    def cut_copies(source, target, rows):
        each = source.shape[0] // CUTS
        places = [(pl.ds(cut * each, each), pl.ds(*rows)) for cut in range(CUTS)]
        return [pltpu.make_async_copy(source.at[at], target.at[at], sems.at[next(sem_idx)]) for at in places]

    filter_copies = cut_copies(signals_hbm, signals_ref, (2 * rows_here, all_rows - 2 * rows_here))
    matrix_copies = [
        pltpu.make_async_copy(
            matrix_hbm.at[pl.ds(cut * BOTH // CUTS, BOTH // CUTS)],
            matrix_ref.at[pl.ds(cut * BOTH // CUTS, BOTH // CUTS)],
            sems.at[next(sem_idx)],
        )
        for cut in range(CUTS)
    ]
    signal_copies = [cut_copies(signals_hbm, signals_ref, (kind * rows_here, rows_here)) for kind in range(2)]
    lag_copies = [
        pltpu.make_async_copy(lag_split.at[pair], lag_hbm.at[pair], sems.at[next(sem_idx)])
        for pair in range(lag_split.shape[0])
    ]
    return_copies = [
        cut_copies(results_ref, results_hbm, rows)
        for rows in ((0, rows_here), (rows_here, back_rows - rows_here))
    ]

    def start_all(copies):
        for copy in copies:
            copy.start()

    def wait_all(copies):
        for copy in copies:
            copy.wait()

    def leaves(kind, split_ref):
        heads = heads_ref.at[kind] if kind < 2 else None
        return leaves_stage(signals_ref, kind * rows_here, heads, rows_here, twist_ref, split_ref)

    def combine(left_ref, right_ref, split_ref, conjugate):
        return combine_stage(left_ref, right_ref, split_ref, rows_here, conjugate)

    def result(kind, from_ref):
        def write(piece, rows, value, carry):
            place = pl.ds(kind * rows_here + rows.start, CHUNK)
            results_ref[piece, place, :] = value.astype(bf16)
            return carry

        return signal_stage(from_ref, twist_ref, rows_here, write)

    start_all(filter_copies + matrix_copies + signal_copies[0] + signal_copies[1])
    run_all([twist_stage(coarse_ref, fine_ref, twist_ref, rows_here)], rows_here)
    wait_all(filter_copies)
    run_all([leaves(2, one_split)], rows_here)
    wait_all(signal_copies[0] + signal_copies[1] + matrix_copies)
    patch_first_rows(signals_ref, heads_ref, taps_ref, rows_here)
    run_all([leaves(0, two_split)], rows_here, (matrix_ref, one_split, filter_ref))
    run_all([leaves(1, one_split)], rows_here, (matrix_ref, two_split, product_ref))
    run_all([combine(filter_ref, product_ref, two_split, False)], rows_here, (matrix_ref, one_split, cotan_ref))
    run_all([combine(filter_ref, cotan_ref, one_split, True)], rows_here, (matrix_ref, two_split, time_ref))
    run_all(
        [combine(product_ref, cotan_ref, lag_split, True), result(0, time_ref)],
        rows_here, (matrix_ref, one_split, filter_ref),
    )
    start_all(return_copies[0] + lag_copies)
    run_all([result(1, filter_ref)], rows_here)
    write_edges(signals_ref, results_ref, taps_ref, rows_here)
    start_all(return_copies[1])
    wait_all(lag_copies + return_copies[0] + return_copies[1])


def lag_kernel(
    split_hbm, coarse_ref, fine_ref, matrix_hbm, lag_ref, square_ref, twist_ref, matrix_ref, split_ref, time_ref, sems
):
    rows_here = lag_ref.shape[1]
    copies = [
        pltpu.make_async_copy(matrix_hbm, matrix_ref, sems.at[0]),
        pltpu.make_async_copy(split_hbm, split_ref, sems.at[1]),
    ]
    for copy in copies:
        copy.start()
    run_all([twist_stage(coarse_ref, fine_ref, twist_ref, rows_here)], rows_here)
    for copy in copies:
        copy.wait()
    run_all([], rows_here, (matrix_ref, split_ref, time_ref))

    def write(piece, rows, value, carry):
        lag_ref[piece, rows, :] = value.astype(bf16)
        return carry + value * value

    square = run_all(
        [signal_stage(time_ref, twist_ref, rows_here, write)], rows_here, None, jnp.zeros((CHUNK, LANES), f32)
    )
    square_ref[...] = jnp.sum(square, axis=0, keepdims=True)


class Transforms:
    def __init__(self, pieces, rows_here):
        outer = pieces * rows_here // SPAN
        pairs = outer // 2
        coarse = twist_angles(outer, CHUNK * np.arange(CHUNKS)).T
        fine = twist_angles(outer, np.arange(CHUNK))[..., None] * np.ones(LANES)
        self.tables = [
            jnp.asarray(np.concatenate([np.cos(coarse), np.sin(coarse)], axis=1).astype(np.float32)),
            jnp.asarray(np.stack([np.cos(fine), np.sin(fine)]).astype(np.float32)),
            jnp.asarray(matrix_blocks()),
        ]
        self.split = jax.ShapeDtypeStruct((pairs, PASSES * BOTH, 2 * LANES), bf16)
        self.signal = jax.ShapeDtypeStruct((pieces, rows_here, LANES), bf16)
        self.result = jax.ShapeDtypeStruct((pieces, 2 * rows_here + TILE_ROWS, LANES), bf16)
        self.square = jax.ShapeDtypeStruct((1, LANES), f32)
        self.result_work = pltpu.VMEM(self.result.shape, bf16)
        self.work = pltpu.VMEM((pairs, BOTH, 2 * LANES), f32)
        self.split_work = pltpu.VMEM(self.split.shape, bf16)
        self.twist_work = pltpu.VMEM((2, outer, SPAN, LANES), f32)
        self.matrix_work = pltpu.VMEM(self.tables[2].shape, bf16)

    def products(self, signals, taps, after):
        return call(
            functools.partial(products_kernel, self.signal.shape[1]), (self.result, self.split),
            [pltpu.VMEM(signals.shape, bf16), self.twist_work, self.matrix_work]
            + [pltpu.VMEM((2, signals.shape[0], TILE_ROWS, LANES), bf16), self.result_work]
            + [self.split_work] * 3
            + [self.work] * 4
            + [pltpu.SemaphoreType.DMA((6 * CUTS + self.split.shape[0],))],
            signals, taps, *self.tables, after,
            vmem_bytes=MOST_VMEM_BYTES,
            in_specs=[ANYWHERE, IN_VMEM, IN_SMEM, IN_VMEM, ANYWHERE, ANYWHERE],
            out_specs=(ANYWHERE, ANYWHERE),
        )

    def lag(self, lag_split):
        return call(
            lag_kernel, (self.signal, self.square),
            [self.twist_work, self.matrix_work, self.split_work, self.work, pltpu.SemaphoreType.DMA((2,))],
            lag_split, *self.tables,
            in_specs=[ANYWHERE, IN_SMEM, IN_VMEM, ANYWHERE],
            out_specs=(IN_VMEM, IN_VMEM),
        )


class PlainTransforms:
    def __init__(self, pieces, rows_here):
        self.seq_len = pieces * rows_here
        self.pieces = pieces
        self.outer = self.seq_len // SPAN
        idx = np.arange(SPAN)
        angle = (idx[:, None] * idx[None, :] % SPAN) * (2.0 * np.pi / SPAN)
        self.cosine = jnp.asarray(np.cos(angle), f32)
        self.sine = jnp.asarray(np.sin(angle), f32)
        twist = twist_angles(self.outer, idx)
        self.twist = jnp.asarray(np.stack([np.cos(twist), np.sin(twist)]), f32)[..., None]

    def dot(self, matrix, signal):
        return jnp.einsum("fs,tsc->tfc", matrix, signal, precision=lax.Precision.HIGHEST)

    def spectrum(self, signal):
        parts = signal.astype(f32).reshape(self.outer, SPAN, -1)
        leaves = to_leaves([parts[part] for part in range(self.outer)])
        re = jnp.stack([leaf[0] for leaf in leaves])
        im = jnp.stack([leaf[1] for leaf in leaves])
        twist_re = re * self.twist[0] + im * self.twist[1]
        twist_im = im * self.twist[0] - re * self.twist[1]
        return (
            self.dot(self.cosine, twist_re) + self.dot(self.sine, twist_im),
            self.dot(self.cosine, twist_im) - self.dot(self.sine, twist_re),
        )

    def back(self, re, im):
        time_re = self.dot(self.cosine, re) - self.dot(self.sine, im)
        time_im = self.dot(self.cosine, im) + self.dot(self.sine, re)
        leaf_re = time_re * self.twist[0] - time_im * self.twist[1]
        leaf_im = time_im * self.twist[0] + time_re * self.twist[1]
        parts = from_leaves([(leaf_re[leaf], leaf_im[leaf]) for leaf in range(self.outer)], 1.0 / self.seq_len)
        return jnp.stack(parts).reshape(self.pieces, self.seq_len // self.pieces, -1)

    def products(self, signals, taps_and_skip, after):
        rows_here = self.seq_len // self.pieces
        parts = [signals[:, kind * rows_here : (kind + 1) * rows_here] for kind in range(3)]
        extra = signals[:, 3 * rows_here :].astype(f32)
        rows = [extra[:, idx : idx + 1] for idx in range(extra.shape[1])]
        ahead = [jnp.concatenate([jnp.zeros_like(row[:1]), row[:-1]], axis=0) for row in rows]
        *taps, skip = [taps_and_skip[row][None, None, :] for row in range(taps_and_skip.shape[0])]
        count = len(taps) - 1
        for kind, first in enumerate(first_signals(ahead, rows, taps)[1:]):
            first = jnp.concatenate(first, axis=1)
            parts[kind] = jnp.concatenate([first.astype(bf16), parts[kind][:, first.shape[1] :]], axis=1)
        product, cotan, taps_spec = (self.spectrum(part) for part in parts)
        conv = self.back(
            taps_spec[0] * product[0] - taps_spec[1] * product[1], taps_spec[0] * product[1] + taps_spec[1] * product[0]
        ).astype(bf16)
        corr = self.back(
            taps_spec[0] * cotan[0] + taps_spec[1] * cotan[1], taps_spec[0] * cotan[1] - taps_spec[1] * cotan[0]
        ).astype(bf16)
        lag = (
            product[0] * cotan[0] + product[1] * cotan[1],
            product[0] * cotan[1] - product[1] * cotan[0],
        )
        backs = first_backs(
            ahead, rows, taps, skip,
            [conv[:, row : row + 1].astype(f32) for row in range(count)],
            [corr[:, row : row + 1].astype(f32) for row in range(count)],
        )
        behind = [jnp.concatenate([row[1:], jnp.zeros_like(row[:1])], axis=0) for row in backs]
        edge = jnp.concatenate(ahead[: 3 * count] + behind, axis=1).astype(bf16)
        edge = jnp.pad(edge, ((0, 0), (0, TILE_ROWS - edge.shape[1]), (0, 0)))
        return jnp.concatenate([conv, corr, edge], axis=1), lag

    def lag(self, lag_spec):
        lag = self.back(*lag_spec)
        squares = jnp.sum(lag * lag, axis=(0, 1))
        return lag.astype(bf16), jnp.zeros((1, LANES), f32).at[0, : squares.shape[0]].set(squares)


def group(idx):
    return slice(idx * LANES, (idx + 1) * LANES)


def streamed(work, steps, per_step, places, in_count, out_count, kept, *refs):
    moved = in_count + out_count
    hbm = refs[:moved]
    kept_refs = refs[moved : moved + kept]
    held = refs[moved + kept : 2 * moved + kept]
    scratch = refs[2 * moved + kept : -1]
    sems = refs[-1]

    def copy(place, step):
        outside = hbm[place].at[places[place](step)]
        inside = held[place].at[places[place](step)]
        ends = (outside, inside) if place < in_count else (inside, outside)
        return pltpu.make_async_copy(*ends, sems.at[place, step])

    def arrivals(step):
        return [copy(place, step) for place in range(in_count) if places[place](step) is not None]

    for step in range(steps):
        for arrival in arrivals(step):
            arrival.start()
    for step in range(steps):
        for arrival in arrivals(step):
            arrival.wait()
        for idx in range(step * per_step, (step + 1) * per_step):
            exts = scratch[idx % 2 :: 2]
            work(idx, held[:in_count], held[in_count:] + kept_refs, exts)
        for place in range(in_count, moved):
            copy(place, step).start()
    for step in range(steps):
        for place in range(in_count, moved):
            copy(place, step).wait()


def stream_call(work, steps, per_step, operands, results, scratch=(), after=(), kept=(), vmem_bytes=VMEM_BYTES):
    arrays = [operand[0] for operand in operands]
    shapes = [jax.ShapeDtypeStruct(array.shape, array.dtype) for array in arrays] + [result[0] for result in results]
    cuts = [entry[1] for entry in list(operands) + list(results)]
    held = [pltpu.VMEM(shape.shape, shape.dtype) for shape in shapes]
    extra = list(after)
    kernel = functools.partial(streamed, work, steps, per_step, cuts, len(arrays), len(results), len(kept))

    def without_extra(*refs):
        kernel(*refs[: len(arrays)], *refs[len(arrays) + len(extra) :])

    return call(
        without_extra,
        tuple(result[0] for result in results) + tuple(kept),
        held + list(scratch) + [pltpu.SemaphoreType.DMA((len(shapes), steps))],
        *arrays, *extra,
        vmem_bytes=vmem_bytes,
        in_specs=[ANYWHERE] * (len(arrays) + len(extra)),
        out_specs=(ANYWHERE,) * len(results) + (IN_VMEM,) * len(kept),
    )


def cut_lanes(width, rank):
    def place(step):
        return (slice(None),) * (rank - 1) + (pl.ds(step * width, width),)

    return place


def cut_groups(per_step):
    def place(step):
        return (pl.ds(step * per_step, per_step),)

    return place


def cut_none(step):
    return None if step else (slice(None),)


def row_blocks(rows_here):
    return [slice(start, start + ROWS) for start in range(0, rows_here, ROWS)]


def extend_rows(lead, in_ref, lanes, ext_ref):
    ext_ref[PAD - lead.shape[0] : PAD, :] = lead
    ext_ref[PAD:, :] = in_ref[:, lanes].astype(f32)


def short_conv(ext_ref, taps, rows):
    result = None
    for shift_idx in range(taps.shape[0]):
        term = taps[shift_idx : shift_idx + 1] * ext_ref[PAD + rows.start - shift_idx : PAD + rows.stop - shift_idx, :]
        result = term if result is None else result + term
    return result


def signals_work(idx, operands, results, exts):
    q_ref, k_ref, v_ref, grad_ref, kernel_ref, taps_ref = operands
    lanes = group(idx)
    taps = taps_ref[:, lanes]
    halo_rows = taps.shape[0] - 1
    rows_here = q_ref.shape[0]
    for ext, in_ref in zip(exts, operands):
        extend_rows(jnp.zeros((halo_rows, LANES), f32), in_ref, lanes, ext)
    for rows in row_blocks(rows_here):
        q_short, k_short, v_short = (short_conv(ext, taps, rows) for ext in exts)
        below = [slice(kind * rows_here + rows.start, kind * rows_here + rows.stop) for kind in range(3)]
        results[0][idx, below[0], :] = (k_short * v_short).astype(bf16)
        results[0][idx, below[1], :] = (grad_ref[rows, lanes].astype(f32) * q_short).astype(bf16)
        results[0][idx, below[2], :] = kernel_ref[rows, lanes].astype(bf16)
    top = grad_ref[0:TILE_ROWS, lanes].astype(f32)[:halo_rows]
    extra = [ext[ext.shape[0] - halo_rows :, :] for ext in exts] + [ext[PAD : PAD + halo_rows, :] for ext in exts]
    extra_count = results[0].shape[1] - 3 * rows_here
    blank = jnp.zeros((extra_count - 7 * halo_rows, LANES), f32)
    results[0][idx, 3 * rows_here :, :] = jnp.concatenate(extra + [top, blank], axis=0).astype(bf16)


def short_work(idx, operands, results, exts):
    lanes = group(idx)
    taps = operands[3][:, lanes]
    for ext, in_ref in zip(exts, operands):
        extend_rows(jnp.zeros((taps.shape[0] - 1, LANES), f32), in_ref, lanes, ext)
    for rows in row_blocks(operands[0].shape[0]):
        for place, ext in enumerate(exts):
            results[0][place, rows, lanes] = short_conv(ext, taps, rows)


def fold(value):
    return jnp.sum(value.reshape(-1, 8, LANES), axis=0)


def finish_work(idx, operands, results, exts):
    q_ref, k_ref, v_ref, grad_ref, short_ref, taps_ref, skip_ref, long_ref, squares_ref = operands
    mixed_ref, grad_q_ref, grad_k_ref, grad_v_ref, sums_ref = results
    lanes = group(idx)
    taps = taps_ref[:, lanes]
    skip = skip_ref[:, lanes]
    taps_count = taps.shape[0]
    halo_rows = taps_count - 1
    rows_here = q_ref.shape[0]
    sums = [jnp.zeros((8, LANES), f32) for _ in range(taps_count + 1)]
    edge = long_ref[idx, 2 * rows_here :, :].astype(f32)
    for place, ext in enumerate(exts):
        at = (3 + place) * halo_rows
        ext[rows_here : rows_here + halo_rows, :] = edge[at : at + halo_rows]
    row_idx = lax.broadcasted_iota(jnp.int32, (ROWS, LANES), 0)

    def short(place, rows):
        value = short_ref[place, rows, lanes]
        if rows.start == 0:
            for shift_idx in range(1, taps_count):
                terms = jnp.zeros((ROWS, LANES), f32)
                for row in range(shift_idx):
                    at = place * halo_rows + halo_rows + row - shift_idx
                    term = taps[shift_idx : shift_idx + 1] * edge[at : at + 1]
                    terms = jnp.where(row_idx == row, term, terms)
                value = value + terms
        return value

    for rows in row_blocks(rows_here):
        q_short, k_short, v_short = (short(place, rows) for place in range(3))
        product = (k_short * v_short).astype(bf16).astype(f32)
        filtered = long_ref[idx, rows, :].astype(f32) + skip * product
        mixed_ref[rows, lanes] = (q_short * filtered).astype(bf16)
        upstream = grad_ref[rows, lanes].astype(f32)
        back_mix = upstream * q_short
        below = slice(rows_here + rows.start, rows_here + rows.stop)
        back_prod = long_ref[idx, below, :].astype(f32) + skip * back_mix
        sums[taps_count] = sums[taps_count] + fold(back_mix * product)
        exts[0][rows, :] = upstream * filtered
        exts[1][rows, :] = back_prod * v_short
        exts[2][rows, :] = back_prod * k_short
    for ext, in_ref, out_ref in zip(exts, (q_ref, k_ref, v_ref), (grad_q_ref, grad_k_ref, grad_v_ref)):
        for rows in row_blocks(rows_here):
            signal = in_ref[rows, lanes].astype(f32)
            grad = None
            for shift_idx in range(taps_count):
                ahead = ext[rows.start + shift_idx : rows.stop + shift_idx, :]
                term = taps[shift_idx : shift_idx + 1] * ahead
                grad = term if grad is None else grad + term
                sums[shift_idx] = sums[shift_idx] + fold(ahead * signal)
            out_ref[rows, lanes] = grad.astype(bf16)
    if idx == 0:
        extra = slice(sums_ref.shape[1] - LANES, sums_ref.shape[1])
        sums_ref[:, extra] = jnp.zeros((taps_count + 1, LANES), f32)
        sums_ref[0:1, extra] = squares_ref[...]
    for shift_idx in range(taps_count + 1):
        sums_ref[shift_idx : shift_idx + 1, lanes] = jnp.sum(sums[shift_idx], axis=0, keepdims=True)


def norm_kernel(*refs):
    values, totals_ref, square_ref = refs[:-2], refs[-2], refs[-1]
    channels = totals_ref.shape[1] - LANES
    totals = values[0][...]
    if len(values) == 4:
        totals = (totals + values[1][...]) + (values[2][...] + values[3][...])
    totals_ref[...] = totals
    square = jnp.sum(totals[:, :channels] * totals[:, :channels]) + jnp.sum(totals[0:1, channels:])
    square_ref[...] = jnp.full(square_ref.shape, square)


def add_kernel(*refs):
    refs[-1][...] = add_up([ref[...] for ref in refs[:-1]])


def same_kernel(value_ref, same_ref):
    same_ref[...] = value_ref[...]


def scale_kernel(limit, totals_ref, norm_ref, lag_ref, taps_out, skip_out, kernel_out):
    taps_count, channels = taps_out.shape
    factor = limit / jnp.maximum(jnp.sqrt(norm_ref[...]), limit)
    for idx in range(channels // LANES):
        lanes = slice(idx * LANES, (idx + 1) * LANES)
        taps_out[:, lanes] = totals_ref[0:taps_count, lanes] * factor
        skip_out[:, lanes] = totals_ref[taps_count : taps_count + 1, lanes] * factor
        kernel_out[:, lanes] = lag_ref[idx].astype(f32) * factor


def exchange(pieces_first):
    return lax.all_to_all(pieces_first, "ctx", split_axis=0, concat_axis=0, tiled=True)


def to_pieces(groups, pieces):
    count, rows, lanes = groups.shape
    if count == pieces:
        return groups
    share = count * lanes // pieces
    split = groups.reshape(count, rows, lanes // share, share)
    return split.transpose(0, 2, 1, 3).reshape(pieces, rows, share)


def to_groups(parts):
    pieces, rows, share = parts.shape
    if share == LANES:
        return parts
    joined = parts.reshape(pieces * share // LANES, LANES // share, rows, share)
    return joined.transpose(0, 2, 1, 3).reshape(-1, rows, LANES)


def partners(value, axis, steps):
    size = lax.axis_size(axis)
    return [value] + [lax.ppermute(value, axis, [(i, i ^ step) for i in range(size)]) for step in steps]


def rounds_of(size):
    rounds = []
    step = 1
    while step < size:
        rounds.append((step, 2 * step, 3 * step) if size // step >= 4 else (step,))
        step *= 4 if size // step >= 4 else 2
    return rounds


def add_up(values):
    if len(values) == 2:
        return values[0] + values[1]
    return (values[0] + values[1]) + (values[2] + values[3])


def body(q_in, k_in, v_in, grad_out, short_filter, kernel, skip):
    pieces = lax.axis_size("ctx")
    sides = lax.axis_size("ch")
    rows_here, channels = q_in.shape
    seq_len = pieces * rows_here
    taps_count = short_filter.shape[0]
    halo_rows = taps_count - 1
    groups = channels // LANES
    share = channels // pieces
    per_step = min(groups, 2)
    steps = groups // per_step
    lanes2 = cut_lanes(per_step * LANES, 2)
    lanes3 = cut_lanes(per_step * LANES, 3)
    skip_row = skip.reshape(1, channels)
    transforms = (Transforms if share == LANES else PlainTransforms)(pieces, rows_here)
    stream = functools.partial(stream_call, steps=steps, per_step=per_step)

    flat = jax.ShapeDtypeStruct((rows_here, channels), bf16)
    extra_rows = -(-7 * halo_rows // TILE_ROWS) * TILE_ROWS
    sent = jax.ShapeDtypeStruct((groups, 3 * rows_here + extra_rows, LANES), bf16)
    exts = [pltpu.VMEM((rows_here + PAD, LANES), f32)] * 6

    (signals,) = stream(
        signals_work,
        operands=[(x, lanes2) for x in (q_in, k_in, v_in, grad_out, kernel, short_filter)],
        results=[(sent, cut_groups(per_step))],
        scratch=exts,
        vmem_bytes=MOST_VMEM_BYTES,
    )
    signals_here = exchange(to_pieces(signals, pieces))
    (short,) = stream(
        short_work,
        operands=[(x, lanes2) for x in (q_in, k_in, v_in, short_filter)],
        results=[(jax.ShapeDtypeStruct((3, rows_here, channels), f32), lanes3)],
        scratch=exts,
        after=[signals],
    )
    taps_and_skip = jnp.concatenate([short_filter, skip_row], axis=0)
    taps_here = lax.dynamic_slice_in_dim(taps_and_skip, lax.axis_index("ctx") * share, share, axis=1)
    long_here, lag_spec = transforms.products(signals_here, taps_here, short)
    long = to_groups(exchange(long_here))
    lag_here, lag_squares = transforms.lag(lag_spec)
    lag = to_groups(exchange(lag_here))

    mixed, grad_q, grad_k, grad_v, sums = stream(
        finish_work,
        operands=[(x, lanes2) for x in (q_in, k_in, v_in, grad_out)]
        + [(short, lanes3), (short_filter, lanes2), (skip_row, lanes2)]
        + [(long, cut_groups(per_step)), (lag_squares, cut_none)],
        results=[(flat, lanes2)] * 4,
        scratch=exts,
        kept=[jax.ShapeDtypeStruct((taps_count + 1, channels + LANES), f32)],
    )

    totals = sums
    rounds = rounds_of(pieces)
    for steps_of in rounds[:-1]:
        values = partners(totals, "ctx", steps_of)
        values[0] = call(
            same_kernel, jax.ShapeDtypeStruct(totals.shape, f32), [], totals,
            vmem_bytes=SMALL_VMEM_BYTES, in_specs=[IN_VMEM], out_specs=IN_VMEM,
        )
        totals = call(
            add_kernel, jax.ShapeDtypeStruct(totals.shape, f32), [], *values,
            vmem_bytes=SMALL_VMEM_BYTES, in_specs=[IN_VMEM] * len(values), out_specs=IN_VMEM,
        )
    last = partners(totals, "ctx", rounds[-1])
    if len(last) == 2:
        last = [last[0] + last[1]]

    totals, norm_sq = call(
        norm_kernel,
        (jax.ShapeDtypeStruct(totals.shape, f32), jax.ShapeDtypeStruct((1, LANES), f32)),
        [], *last,
        vmem_bytes=SMALL_VMEM_BYTES,
        in_specs=[IN_VMEM] * len(last), out_specs=(IN_VMEM, IN_VMEM),
    )
    for steps_of in rounds_of(sides):
        norm_sq = add_up(partners(norm_sq, "ch", steps_of))

    limit = math.sqrt(float(seq_len * channels * sides))
    grad_short, grad_skip, grad_kernel = call(
        functools.partial(scale_kernel, limit),
        (
            jax.ShapeDtypeStruct((taps_count, channels), f32),
            jax.ShapeDtypeStruct((1, channels), f32),
            jax.ShapeDtypeStruct((rows_here, channels), f32),
        ),
        [],
        totals, norm_sq, lag,
        vmem_bytes=SMALL_VMEM_BYTES,
        in_specs=[IN_VMEM] * 3,
        out_specs=(IN_VMEM,) * 3,
    )
    return mixed, grad_q, grad_k, grad_v, grad_short, grad_skip.reshape(channels), grad_kernel


def solution(mesh):
    in_specs = (
        P("ctx", "ch"),
        P("ctx", "ch"),
        P("ctx", "ch"),
        P("ctx", "ch"),
        P(None, "ch"),
        P("ctx", "ch"),
        P("ch"),
    )
    out_specs = (
        P("ctx", "ch"),
        P("ctx", "ch"),
        P("ctx", "ch"),
        P("ctx", "ch"),
        P(None, "ch"),
        P("ch"),
        P("ctx", "ch"),
    )
    return jax.shard_map(body, mesh=mesh, in_specs=in_specs, out_specs=out_specs, check_vma=False)
```

```python
import functools
import math

import jax
import jax.numpy as jnp
import ml_dtypes
import numpy as np
from jax import lax
from jax.experimental import pallas as pl
from jax.experimental.pallas import tpu as pltpu
from jax.sharding import PartitionSpec as P

LANES = 128
SPAN = 256
BOTH = 2 * SPAN
CHUNK = 16
CHUNKS = SPAN // CHUNK
PAD = 8
ROWS = 32
CUTS = 4
PASSES = 1
TILE_ROWS = 16
VMEM_BYTES = 60 * 1024 * 1024
MOST_VMEM_BYTES = 251 * 256 * 1024
SMALL_VMEM_BYTES = 8 * 1024 * 1024

f32 = jnp.float32
bf16 = jnp.bfloat16

IN_VMEM = pl.BlockSpec(memory_space=pltpu.VMEM)
IN_SMEM = pl.BlockSpec(memory_space=pltpu.SMEM)
ANYWHERE = pl.BlockSpec(memory_space=pl.ANY)


def call(kernel, outs, scratch, *args, vmem_bytes=VMEM_BYTES, **options):
    return pl.pallas_call(
        kernel,
        out_shape=outs,
        scratch_shapes=scratch,
        compiler_params=pltpu.CompilerParams(vmem_limit_bytes=vmem_bytes),
        **options,
    )(*args)


def leaf_phases(count):
    return [(4 * leaf + 1) / (4 * count) for leaf in range(count)]


def root_times(re, im, num, den, sign):
    if num == 0:
        return re, im
    if 4 * num == den:
        return (im, -re) if sign < 0 else (-im, re)
    cosine = math.cos(2.0 * math.pi * num / den)
    sine = sign * math.sin(2.0 * math.pi * num / den)
    if 8 * num == den:
        return ((re + im) * cosine, (im - re) * cosine) if sign < 0 else ((re - im) * cosine, (re + im) * cosine)
    if 8 * num == 3 * den:
        return ((re - im) * cosine, (re + im) * cosine) if sign < 0 else ((re + im) * cosine, (im - re) * cosine)
    return re * cosine - im * sine, im * cosine + re * sine


def short_fft(values, sign):
    count = len(values)
    if count == 1:
        return values
    even = short_fft(values[0::2], sign)
    odd = short_fft(values[1::2], sign)
    first = []
    second = []
    for num in range(count // 2):
        re, im = root_times(*odd[num], num, count, sign)
        first.append((even[num][0] + re, even[num][1] + im))
        second.append((even[num][0] - re, even[num][1] - im))
    return first + second


def to_leaves(parts):
    count = len(parts)
    turned = []
    for idx, part in enumerate(parts):
        angle = 2.0 * math.pi * idx / (4 * count)
        turned.append((part * math.cos(angle), part * (-math.sin(angle))) if idx else (part, jnp.zeros_like(part)))
    return short_fft(turned, -1)


def from_leaves(leaves, scale):
    count = len(leaves)
    parts = []
    for idx, (re, im) in enumerate(short_fft(leaves, 1)):
        angle = 2.0 * math.pi * idx / (4 * count)
        if idx == 0:
            parts.append(re * scale)
        else:
            parts.append(re * (math.cos(angle) * scale) - im * (math.sin(angle) * scale))
    return parts


def dft_matrix():
    idx = np.arange(SPAN)
    angle = (idx[:, None] * idx[None, :] % SPAN) * (2.0 * np.pi / SPAN)
    cosine, sine = np.cos(angle), np.sin(angle)
    return np.block([[cosine, sine], [-sine, cosine]])


def twist_angles(outer, inner):
    return np.asarray(leaf_phases(outer))[:, None] * np.asarray(inner)[None, :] * (2.0 * np.pi / SPAN)


def matrix_blocks():
    matrix = dft_matrix()
    high = matrix.astype(ml_dtypes.bfloat16)
    low = (matrix - high.astype(np.float64)).astype(ml_dtypes.bfloat16)
    return np.concatenate([high, low, high][:PASSES], axis=1)


def leaf_place(leaf):
    return leaf // 2, slice((leaf % 2) * LANES, (leaf % 2 + 1) * LANES)


def split_store(ref, leaf, below, here, value):
    pair, lanes = leaf_place(leaf)
    high = value.astype(bf16)
    for block in range(PASSES):
        part = high
        if PASSES == 3 and block == 2:
            part = (value - high.astype(f32)).astype(bf16)
        ref[pair, shifted_rows(here, block * BOTH + below), lanes] = part


def run_all(stages, rows_here, matmul=None, carry=0):
    tiles = matmul[2].shape[0] if matmul else 4
    per_tile = CHUNKS // tiles
    in_part = rows_here // CHUNK
    for tile in range(tiles):
        if matmul:
            matrix_ref, split_ref, result_ref = matmul
            result_ref[tile] = jnp.dot(matrix_ref[...], split_ref[tile], preferred_element_type=f32)
        for chunk in range(tile * per_tile, (tile + 1) * per_tile):
            for stage in stages:
                carry = stage(chunk // in_part, chunk % in_part * CHUNK, carry)
    return carry


def in_span(part, row, rows_here):
    return pl.ds(part * rows_here + row, CHUNK)


def twist_stage(coarse_ref, fine_ref, twist_ref, rows_here):
    outer = twist_ref.shape[1]

    def stage(part, row, carry):
        here = in_span(part, row, rows_here)
        idx = part * (rows_here // CHUNK) + row // CHUNK
        for leaf in range(outer):
            far_cosine = coarse_ref[idx, leaf]
            far_sine = coarse_ref[idx, outer + leaf]
            cosine = fine_ref[0, leaf]
            sine = fine_ref[1, leaf]
            twist_ref[0, leaf, here, :] = far_cosine * cosine - far_sine * sine
            twist_ref[1, leaf, here, :] = far_sine * cosine + far_cosine * sine
        return carry

    return stage


def leaves_stage(signals_ref, first_row, heads_ref, rows_here, twist_ref, split_ref):
    outer = twist_ref.shape[1]
    ratio = SPAN // rows_here

    def stage(part, row, carry):
        here = in_span(part, row, rows_here)
        rows = pl.ds(first_row + row, CHUNK)
        parts = [signals_ref[place * ratio + part, rows, :] for place in range(outer)]
        if heads_ref is not None and row == 0:
            parts = [heads_ref[place * ratio + part] for place in range(outer)]
        parts = [value.astype(f32) for value in parts]
        for leaf, (re, im) in enumerate(to_leaves(parts)):
            cosine = twist_ref[0, leaf, here, :]
            sine = twist_ref[1, leaf, here, :]
            split_store(split_ref, leaf, 0, here, re * cosine + im * sine)
            split_store(split_ref, leaf, SPAN, here, im * cosine - re * sine)
        return carry

    return stage


def shifted_rows(here, by):
    return pl.ds(here.start + by, here.size)


def combine_stage(left_ref, right_ref, split_ref, rows_here, conjugate):
    def stage(part, row, carry):
        here = in_span(part, row, rows_here)
        below = shifted_rows(here, SPAN)
        for leaf in range(2 * left_ref.shape[0]):
            pair, lanes = leaf_place(leaf)
            left_re = left_ref[pair, here, lanes]
            left_im = left_ref[pair, below, lanes]
            right_re = right_ref[pair, here, lanes]
            right_im = right_ref[pair, below, lanes]
            if conjugate:
                re = left_re * right_re + left_im * right_im
                minus_im = left_im * right_re - left_re * right_im
            else:
                re = left_re * right_re - left_im * right_im
                minus_im = -(left_re * right_im + left_im * right_re)
            split_store(split_ref, leaf, 0, here, re)
            split_store(split_ref, leaf, SPAN, here, minus_im)
        return carry

    return stage


def signal_stage(time_ref, twist_ref, rows_here, write):
    outer = twist_ref.shape[1]
    ratio = SPAN // rows_here
    scale = 1.0 / (SPAN * outer)

    def stage(part, row, carry):
        here = in_span(part, row, rows_here)
        below = shifted_rows(here, SPAN)
        leaves = []
        for leaf in range(outer):
            pair, lanes = leaf_place(leaf)
            cosine = twist_ref[0, leaf, here, :]
            sine = twist_ref[1, leaf, here, :]
            re = time_ref[pair, here, lanes]
            minus_im = time_ref[pair, below, lanes]
            leaves.append((re * cosine + minus_im * sine, re * sine - minus_im * cosine))
        for place, value in enumerate(from_leaves(leaves, scale)):
            carry = write(place * ratio + part, pl.ds(row, CHUNK), value, carry)
        return carry

    return stage


def first_rows(lead, first, taps):
    count = len(lead)
    rows = lead + first
    return [
        functools.reduce(lambda x, y: x + y, [taps[shift] * rows[count + row - shift] for shift in range(count + 1)])
        for row in range(count)
    ]


def first_signals(ahead, own, taps):
    count = len(taps) - 1

    def kind(rows, idx):
        return rows[idx * count : (idx + 1) * count]

    shorts = [first_rows(kind(ahead, idx), kind(own, 3 + idx), taps) for idx in range(3)]
    product = [(k_row * v_row).astype(bf16) for k_row, v_row in zip(shorts[1], shorts[2])]
    back_mix = [grad_row * q_row for grad_row, q_row in zip(kind(own, 6), shorts[0])]
    return shorts, product, back_mix


def first_backs(ahead, own, taps, skip, conv, corr):
    count = len(taps) - 1
    shorts, product, back_mix = first_signals(ahead, own, taps)
    back_q = []
    back_k = []
    back_v = []
    for row in range(count):
        filtered = conv[row] + skip * product[row].astype(f32)
        back_prod = corr[row] + skip * back_mix[row]
        back_q.append(own[6 * count + row] * filtered)
        back_k.append(back_prod * shorts[2][row])
        back_v.append(back_prod * shorts[1][row])
    return back_q + back_k + back_v


def extra_of(signals_ref, piece, rows_here, used):
    rows = signals_ref[piece, 3 * rows_here :, :].astype(f32)
    return [rows[idx : idx + 1] for idx in range(used)]


def tap_rows(taps_ref):
    return [taps_ref[shift : shift + 1, :] for shift in range(taps_ref.shape[0])]


def patch_first_rows(signals_ref, heads_ref, taps_ref, rows_here):
    pieces = signals_ref.shape[0]
    taps = tap_rows(taps_ref)[:-1]
    used = 7 * (len(taps) - 1)
    row_idx = lax.broadcasted_iota(jnp.int32, (TILE_ROWS, LANES), 0)
    ahead = [jnp.zeros((1, LANES), f32)] * used
    for piece in range(pieces):
        own = extra_of(signals_ref, piece, rows_here, used)
        for kind, rows in enumerate(first_signals(ahead, own, taps)[1:]):
            tile = signals_ref[piece, kind * rows_here : kind * rows_here + TILE_ROWS, :].astype(f32)
            for row, value in enumerate(rows):
                tile = jnp.where(row_idx == row, value.astype(f32), tile)
            heads_ref[kind, piece] = tile.astype(bf16)
        ahead = own


def write_edges(signals_ref, results_ref, taps_ref, rows_here):
    pieces = signals_ref.shape[0]
    *taps, skip = tap_rows(taps_ref)
    count = len(taps) - 1
    nothing = jnp.zeros((1, LANES), f32)
    extras = [extra_of(signals_ref, piece, rows_here, 7 * count) for piece in range(pieces)]
    for piece in range(pieces):
        rows = extras[piece - 1][: 3 * count] if piece else [nothing] * (3 * count)
        if piece + 1 < pieces:
            conv, corr = (
                results_ref[piece + 1, kind * rows_here : kind * rows_here + TILE_ROWS, :].astype(f32)
                for kind in range(2)
            )
            rows = rows + first_backs(
                extras[piece], extras[piece + 1], taps, skip,
                [conv[row : row + 1] for row in range(count)], [corr[row : row + 1] for row in range(count)],
            )
        spare = results_ref.shape[1] - 2 * rows_here - len(rows)
        rows.append(jnp.zeros((spare, LANES), f32))
        results_ref[piece, 2 * rows_here :, :] = jnp.concatenate(rows, axis=0).astype(bf16)


def products_kernel(
    rows_here, signals_hbm, taps_ref, coarse_ref, fine_ref, matrix_hbm, after_ref, results_hbm, lag_hbm,
    signals_ref, twist_ref, matrix_ref, heads_ref, results_ref, one_split, two_split, lag_split,
    filter_ref, product_ref, cotan_ref, time_ref, sems,
):
    all_rows = signals_ref.shape[1]
    back_rows = results_ref.shape[1]
    sem_idx = iter(range(sems.shape[0]))

    def cut_copies(source, target, rows):
        each = source.shape[0] // CUTS
        places = [(pl.ds(cut * each, each), pl.ds(*rows)) for cut in range(CUTS)]
        return [pltpu.make_async_copy(source.at[at], target.at[at], sems.at[next(sem_idx)]) for at in places]

    filter_copies = cut_copies(signals_hbm, signals_ref, (2 * rows_here, all_rows - 2 * rows_here))
    matrix_copies = [
        pltpu.make_async_copy(
            matrix_hbm.at[pl.ds(cut * BOTH // CUTS, BOTH // CUTS)],
            matrix_ref.at[pl.ds(cut * BOTH // CUTS, BOTH // CUTS)],
            sems.at[next(sem_idx)],
        )
        for cut in range(CUTS)
    ]
    signal_copies = [cut_copies(signals_hbm, signals_ref, (kind * rows_here, rows_here)) for kind in range(2)]
    lag_copies = [
        pltpu.make_async_copy(lag_split.at[pair], lag_hbm.at[pair], sems.at[next(sem_idx)])
        for pair in range(lag_split.shape[0])
    ]
    return_copies = [
        cut_copies(results_ref, results_hbm, rows)
        for rows in ((0, rows_here), (rows_here, back_rows - rows_here))
    ]

    def start_all(copies):
        for copy in copies:
            copy.start()

    def wait_all(copies):
        for copy in copies:
            copy.wait()

    def leaves(kind, split_ref):
        heads = heads_ref.at[kind] if kind < 2 else None
        return leaves_stage(signals_ref, kind * rows_here, heads, rows_here, twist_ref, split_ref)

    def combine(left_ref, right_ref, split_ref, conjugate):
        return combine_stage(left_ref, right_ref, split_ref, rows_here, conjugate)

    def result(kind, from_ref):
        def write(piece, rows, value, carry):
            place = pl.ds(kind * rows_here + rows.start, CHUNK)
            results_ref[piece, place, :] = value.astype(bf16)
            return carry

        return signal_stage(from_ref, twist_ref, rows_here, write)

    start_all(filter_copies + matrix_copies + signal_copies[0] + signal_copies[1])
    run_all([twist_stage(coarse_ref, fine_ref, twist_ref, rows_here)], rows_here)
    wait_all(filter_copies)
    run_all([leaves(2, one_split)], rows_here)
    wait_all(signal_copies[0] + signal_copies[1] + matrix_copies)
    patch_first_rows(signals_ref, heads_ref, taps_ref, rows_here)
    run_all([leaves(0, two_split)], rows_here, (matrix_ref, one_split, filter_ref))
    run_all([leaves(1, one_split)], rows_here, (matrix_ref, two_split, product_ref))
    run_all([combine(filter_ref, product_ref, two_split, False)], rows_here, (matrix_ref, one_split, cotan_ref))
    run_all([combine(filter_ref, cotan_ref, one_split, True)], rows_here, (matrix_ref, two_split, time_ref))
    run_all(
        [combine(product_ref, cotan_ref, lag_split, True), result(0, time_ref)],
        rows_here, (matrix_ref, one_split, filter_ref),
    )
    start_all(return_copies[0] + lag_copies)
    run_all([result(1, filter_ref)], rows_here)
    write_edges(signals_ref, results_ref, taps_ref, rows_here)
    start_all(return_copies[1])
    wait_all(lag_copies + return_copies[0] + return_copies[1])


def lag_kernel(
    split_hbm, coarse_ref, fine_ref, matrix_hbm, lag_ref, square_ref, twist_ref, matrix_ref, split_ref, time_ref, sems
):
    rows_here = lag_ref.shape[1]
    copies = [
        pltpu.make_async_copy(matrix_hbm, matrix_ref, sems.at[0]),
        pltpu.make_async_copy(split_hbm, split_ref, sems.at[1]),
    ]
    for copy in copies:
        copy.start()
    run_all([twist_stage(coarse_ref, fine_ref, twist_ref, rows_here)], rows_here)
    for copy in copies:
        copy.wait()
    run_all([], rows_here, (matrix_ref, split_ref, time_ref))

    def write(piece, rows, value, carry):
        lag_ref[piece, rows, :] = value.astype(bf16)
        return carry + value * value

    square = run_all(
        [signal_stage(time_ref, twist_ref, rows_here, write)], rows_here, None, jnp.zeros((CHUNK, LANES), f32)
    )
    square_ref[...] = jnp.sum(square, axis=0, keepdims=True)


class Transforms:
    def __init__(self, pieces, rows_here):
        outer = pieces * rows_here // SPAN
        pairs = outer // 2
        coarse = twist_angles(outer, CHUNK * np.arange(CHUNKS)).T
        fine = twist_angles(outer, np.arange(CHUNK))[..., None] * np.ones(LANES)
        self.tables = [
            jnp.asarray(np.concatenate([np.cos(coarse), np.sin(coarse)], axis=1).astype(np.float32)),
            jnp.asarray(np.stack([np.cos(fine), np.sin(fine)]).astype(np.float32)),
            jnp.asarray(matrix_blocks()),
        ]
        self.split = jax.ShapeDtypeStruct((pairs, PASSES * BOTH, 2 * LANES), bf16)
        self.signal = jax.ShapeDtypeStruct((pieces, rows_here, LANES), bf16)
        self.result = jax.ShapeDtypeStruct((pieces, 2 * rows_here + TILE_ROWS, LANES), bf16)
        self.square = jax.ShapeDtypeStruct((1, LANES), f32)
        self.result_work = pltpu.VMEM(self.result.shape, bf16)
        self.work = pltpu.VMEM((pairs, BOTH, 2 * LANES), f32)
        self.split_work = pltpu.VMEM(self.split.shape, bf16)
        self.twist_work = pltpu.VMEM((2, outer, SPAN, LANES), f32)
        self.matrix_work = pltpu.VMEM(self.tables[2].shape, bf16)

    def products(self, signals, taps, after):
        return call(
            functools.partial(products_kernel, self.signal.shape[1]), (self.result, self.split),
            [pltpu.VMEM(signals.shape, bf16), self.twist_work, self.matrix_work]
            + [pltpu.VMEM((2, signals.shape[0], TILE_ROWS, LANES), bf16), self.result_work]
            + [self.split_work] * 3
            + [self.work] * 4
            + [pltpu.SemaphoreType.DMA((6 * CUTS + self.split.shape[0],))],
            signals, taps, *self.tables, after,
            vmem_bytes=MOST_VMEM_BYTES,
            in_specs=[ANYWHERE, IN_VMEM, IN_SMEM, IN_VMEM, ANYWHERE, ANYWHERE],
            out_specs=(ANYWHERE, ANYWHERE),
        )

    def lag(self, lag_split):
        return call(
            lag_kernel, (self.signal, self.square),
            [self.twist_work, self.matrix_work, self.split_work, self.work, pltpu.SemaphoreType.DMA((2,))],
            lag_split, *self.tables,
            in_specs=[ANYWHERE, IN_SMEM, IN_VMEM, ANYWHERE],
            out_specs=(IN_VMEM, IN_VMEM),
        )


class PlainTransforms:
    def __init__(self, pieces, rows_here):
        self.seq_len = pieces * rows_here
        self.pieces = pieces
        self.outer = self.seq_len // SPAN
        idx = np.arange(SPAN)
        angle = (idx[:, None] * idx[None, :] % SPAN) * (2.0 * np.pi / SPAN)
        self.cosine = jnp.asarray(np.cos(angle), f32)
        self.sine = jnp.asarray(np.sin(angle), f32)
        twist = twist_angles(self.outer, idx)
        self.twist = jnp.asarray(np.stack([np.cos(twist), np.sin(twist)]), f32)[..., None]

    def dot(self, matrix, signal):
        return jnp.einsum("fs,tsc->tfc", matrix, signal, precision=lax.Precision.HIGHEST)

    def spectrum(self, signal):
        parts = signal.astype(f32).reshape(self.outer, SPAN, -1)
        leaves = to_leaves([parts[part] for part in range(self.outer)])
        re = jnp.stack([leaf[0] for leaf in leaves])
        im = jnp.stack([leaf[1] for leaf in leaves])
        twist_re = re * self.twist[0] + im * self.twist[1]
        twist_im = im * self.twist[0] - re * self.twist[1]
        return (
            self.dot(self.cosine, twist_re) + self.dot(self.sine, twist_im),
            self.dot(self.cosine, twist_im) - self.dot(self.sine, twist_re),
        )

    def back(self, re, im):
        time_re = self.dot(self.cosine, re) - self.dot(self.sine, im)
        time_im = self.dot(self.cosine, im) + self.dot(self.sine, re)
        leaf_re = time_re * self.twist[0] - time_im * self.twist[1]
        leaf_im = time_im * self.twist[0] + time_re * self.twist[1]
        parts = from_leaves([(leaf_re[leaf], leaf_im[leaf]) for leaf in range(self.outer)], 1.0 / self.seq_len)
        return jnp.stack(parts).reshape(self.pieces, self.seq_len // self.pieces, -1)

    def products(self, signals, taps_and_skip, after):
        rows_here = self.seq_len // self.pieces
        parts = [signals[:, kind * rows_here : (kind + 1) * rows_here] for kind in range(3)]
        extra = signals[:, 3 * rows_here :].astype(f32)
        rows = [extra[:, idx : idx + 1] for idx in range(extra.shape[1])]
        ahead = [jnp.concatenate([jnp.zeros_like(row[:1]), row[:-1]], axis=0) for row in rows]
        *taps, skip = [taps_and_skip[row][None, None, :] for row in range(taps_and_skip.shape[0])]
        count = len(taps) - 1
        for kind, first in enumerate(first_signals(ahead, rows, taps)[1:]):
            first = jnp.concatenate(first, axis=1)
            parts[kind] = jnp.concatenate([first.astype(bf16), parts[kind][:, first.shape[1] :]], axis=1)
        product, cotan, taps_spec = (self.spectrum(part) for part in parts)
        conv = self.back(
            taps_spec[0] * product[0] - taps_spec[1] * product[1], taps_spec[0] * product[1] + taps_spec[1] * product[0]
        ).astype(bf16)
        corr = self.back(
            taps_spec[0] * cotan[0] + taps_spec[1] * cotan[1], taps_spec[0] * cotan[1] - taps_spec[1] * cotan[0]
        ).astype(bf16)
        lag = (
            product[0] * cotan[0] + product[1] * cotan[1],
            product[0] * cotan[1] - product[1] * cotan[0],
        )
        backs = first_backs(
            ahead, rows, taps, skip,
            [conv[:, row : row + 1].astype(f32) for row in range(count)],
            [corr[:, row : row + 1].astype(f32) for row in range(count)],
        )
        behind = [jnp.concatenate([row[1:], jnp.zeros_like(row[:1])], axis=0) for row in backs]
        edge = jnp.concatenate(ahead[: 3 * count] + behind, axis=1).astype(bf16)
        edge = jnp.pad(edge, ((0, 0), (0, TILE_ROWS - edge.shape[1]), (0, 0)))
        return jnp.concatenate([conv, corr, edge], axis=1), lag

    def lag(self, lag_spec):
        lag = self.back(*lag_spec)
        squares = jnp.sum(lag * lag, axis=(0, 1))
        return lag.astype(bf16), jnp.zeros((1, LANES), f32).at[0, : squares.shape[0]].set(squares)


def group(idx):
    return slice(idx * LANES, (idx + 1) * LANES)


def streamed(work, steps, per_step, places, in_count, out_count, kept, *refs):
    moved = in_count + out_count
    hbm = refs[:moved]
    kept_refs = refs[moved : moved + kept]
    held = refs[moved + kept : 2 * moved + kept]
    scratch = refs[2 * moved + kept : -1]
    sems = refs[-1]

    def copy(place, step):
        outside = hbm[place].at[places[place](step)]
        inside = held[place].at[places[place](step)]
        ends = (outside, inside) if place < in_count else (inside, outside)
        return pltpu.make_async_copy(*ends, sems.at[place, step])

    def arrivals(step):
        return [copy(place, step) for place in range(in_count) if places[place](step) is not None]

    for step in range(steps):
        for arrival in arrivals(step):
            arrival.start()
    for step in range(steps):
        for arrival in arrivals(step):
            arrival.wait()
        for idx in range(step * per_step, (step + 1) * per_step):
            exts = scratch[idx % 2 :: 2]
            work(idx, held[:in_count], held[in_count:] + kept_refs, exts)
        for place in range(in_count, moved):
            copy(place, step).start()
    for step in range(steps):
        for place in range(in_count, moved):
            copy(place, step).wait()


def stream_call(work, steps, per_step, operands, results, scratch=(), after=(), kept=(), vmem_bytes=VMEM_BYTES):
    arrays = [operand[0] for operand in operands]
    shapes = [jax.ShapeDtypeStruct(array.shape, array.dtype) for array in arrays] + [result[0] for result in results]
    cuts = [entry[1] for entry in list(operands) + list(results)]
    held = [pltpu.VMEM(shape.shape, shape.dtype) for shape in shapes]
    extra = list(after)
    kernel = functools.partial(streamed, work, steps, per_step, cuts, len(arrays), len(results), len(kept))

    def without_extra(*refs):
        kernel(*refs[: len(arrays)], *refs[len(arrays) + len(extra) :])

    return call(
        without_extra,
        tuple(result[0] for result in results) + tuple(kept),
        held + list(scratch) + [pltpu.SemaphoreType.DMA((len(shapes), steps))],
        *arrays, *extra,
        vmem_bytes=vmem_bytes,
        in_specs=[ANYWHERE] * (len(arrays) + len(extra)),
        out_specs=(ANYWHERE,) * len(results) + (IN_VMEM,) * len(kept),
    )


def cut_lanes(width, rank):
    def place(step):
        return (slice(None),) * (rank - 1) + (pl.ds(step * width, width),)

    return place


def cut_groups(per_step):
    def place(step):
        return (pl.ds(step * per_step, per_step),)

    return place


def cut_none(step):
    return None if step else (slice(None),)


def row_blocks(rows_here):
    return [slice(start, start + ROWS) for start in range(0, rows_here, ROWS)]


def extend_rows(lead, in_ref, lanes, ext_ref):
    ext_ref[PAD - lead.shape[0] : PAD, :] = lead
    ext_ref[PAD:, :] = in_ref[:, lanes].astype(f32)


def short_conv(ext_ref, taps, rows):
    result = None
    for shift_idx in range(taps.shape[0]):
        term = taps[shift_idx : shift_idx + 1] * ext_ref[PAD + rows.start - shift_idx : PAD + rows.stop - shift_idx, :]
        result = term if result is None else result + term
    return result


def signals_work(idx, operands, results, exts):
    q_ref, k_ref, v_ref, grad_ref, kernel_ref, taps_ref = operands
    lanes = group(idx)
    taps = taps_ref[:, lanes]
    halo_rows = taps.shape[0] - 1
    rows_here = q_ref.shape[0]
    for ext, in_ref in zip(exts, operands):
        extend_rows(jnp.zeros((halo_rows, LANES), f32), in_ref, lanes, ext)
    for rows in row_blocks(rows_here):
        q_short, k_short, v_short = (short_conv(ext, taps, rows) for ext in exts)
        below = [slice(kind * rows_here + rows.start, kind * rows_here + rows.stop) for kind in range(3)]
        results[0][idx, below[0], :] = (k_short * v_short).astype(bf16)
        results[0][idx, below[1], :] = (grad_ref[rows, lanes].astype(f32) * q_short).astype(bf16)
        results[0][idx, below[2], :] = kernel_ref[rows, lanes].astype(bf16)
    top = grad_ref[0:TILE_ROWS, lanes].astype(f32)[:halo_rows]
    extra = [ext[ext.shape[0] - halo_rows :, :] for ext in exts] + [ext[PAD : PAD + halo_rows, :] for ext in exts]
    extra_count = results[0].shape[1] - 3 * rows_here
    blank = jnp.zeros((extra_count - 7 * halo_rows, LANES), f32)
    results[0][idx, 3 * rows_here :, :] = jnp.concatenate(extra + [top, blank], axis=0).astype(bf16)


def short_work(idx, operands, results, exts):
    lanes = group(idx)
    taps = operands[3][:, lanes]
    for ext, in_ref in zip(exts, operands):
        extend_rows(jnp.zeros((taps.shape[0] - 1, LANES), f32), in_ref, lanes, ext)
    for rows in row_blocks(operands[0].shape[0]):
        for place, ext in enumerate(exts):
            results[0][place, rows, lanes] = short_conv(ext, taps, rows)


def fold(value):
    return jnp.sum(value.reshape(-1, 8, LANES), axis=0)


def finish_work(idx, operands, results, exts):
    q_ref, k_ref, v_ref, grad_ref, short_ref, taps_ref, skip_ref, long_ref, squares_ref = operands
    mixed_ref, grad_q_ref, grad_k_ref, grad_v_ref, sums_ref = results
    lanes = group(idx)
    taps = taps_ref[:, lanes]
    skip = skip_ref[:, lanes]
    taps_count = taps.shape[0]
    halo_rows = taps_count - 1
    rows_here = q_ref.shape[0]
    sums = [jnp.zeros((8, LANES), f32) for _ in range(taps_count + 1)]
    edge = long_ref[idx, 2 * rows_here :, :].astype(f32)
    for place, ext in enumerate(exts):
        at = (3 + place) * halo_rows
        ext[rows_here : rows_here + halo_rows, :] = edge[at : at + halo_rows]
    row_idx = lax.broadcasted_iota(jnp.int32, (ROWS, LANES), 0)

    def short(place, rows):
        value = short_ref[place, rows, lanes]
        if rows.start == 0:
            for shift_idx in range(1, taps_count):
                terms = jnp.zeros((ROWS, LANES), f32)
                for row in range(shift_idx):
                    at = place * halo_rows + halo_rows + row - shift_idx
                    term = taps[shift_idx : shift_idx + 1] * edge[at : at + 1]
                    terms = jnp.where(row_idx == row, term, terms)
                value = value + terms
        return value

    for rows in row_blocks(rows_here):
        q_short, k_short, v_short = (short(place, rows) for place in range(3))
        product = (k_short * v_short).astype(bf16).astype(f32)
        filtered = long_ref[idx, rows, :].astype(f32) + skip * product
        mixed_ref[rows, lanes] = (q_short * filtered).astype(bf16)
        upstream = grad_ref[rows, lanes].astype(f32)
        back_mix = upstream * q_short
        below = slice(rows_here + rows.start, rows_here + rows.stop)
        back_prod = long_ref[idx, below, :].astype(f32) + skip * back_mix
        sums[taps_count] = sums[taps_count] + fold(back_mix * product)
        exts[0][rows, :] = upstream * filtered
        exts[1][rows, :] = back_prod * v_short
        exts[2][rows, :] = back_prod * k_short
    for ext, in_ref, out_ref in zip(exts, (q_ref, k_ref, v_ref), (grad_q_ref, grad_k_ref, grad_v_ref)):
        for rows in row_blocks(rows_here):
            signal = in_ref[rows, lanes].astype(f32)
            grad = None
            for shift_idx in range(taps_count):
                ahead = ext[rows.start + shift_idx : rows.stop + shift_idx, :]
                term = taps[shift_idx : shift_idx + 1] * ahead
                grad = term if grad is None else grad + term
                sums[shift_idx] = sums[shift_idx] + fold(ahead * signal)
            out_ref[rows, lanes] = grad.astype(bf16)
    if idx == 0:
        extra = slice(sums_ref.shape[1] - LANES, sums_ref.shape[1])
        sums_ref[:, extra] = jnp.zeros((taps_count + 1, LANES), f32)
        sums_ref[0:1, extra] = squares_ref[...]
    for shift_idx in range(taps_count + 1):
        sums_ref[shift_idx : shift_idx + 1, lanes] = jnp.sum(sums[shift_idx], axis=0, keepdims=True)


def norm_kernel(*refs):
    values, totals_ref, square_ref = refs[:-2], refs[-2], refs[-1]
    channels = totals_ref.shape[1] - LANES
    totals = add_up([value[...] for value in values])
    totals_ref[...] = totals
    square = jnp.sum(totals[:, :channels] * totals[:, :channels]) + jnp.sum(totals[0:1, channels:])
    square_ref[...] = jnp.full(square_ref.shape, square)


def add_kernel(*refs):
    refs[-1][...] = add_up([ref[...] for ref in refs[:-1]])


def same_kernel(value_ref, same_ref):
    same_ref[...] = value_ref[...]


def scale_kernel(limit, totals_ref, norm_ref, lag_ref, taps_out, skip_out, kernel_out):
    taps_count, channels = taps_out.shape
    factor = limit / jnp.maximum(jnp.sqrt(norm_ref[...]), limit)
    for idx in range(channels // LANES):
        lanes = slice(idx * LANES, (idx + 1) * LANES)
        taps_out[:, lanes] = totals_ref[0:taps_count, lanes] * factor
        skip_out[:, lanes] = totals_ref[taps_count : taps_count + 1, lanes] * factor
        kernel_out[:, lanes] = lag_ref[idx].astype(f32) * factor


def exchange(pieces_first):
    return lax.all_to_all(pieces_first, "ctx", split_axis=0, concat_axis=0, tiled=True)


def to_pieces(groups, pieces):
    count, rows, lanes = groups.shape
    if count == pieces:
        return groups
    share = count * lanes // pieces
    split = groups.reshape(count, rows, lanes // share, share)
    return split.transpose(0, 2, 1, 3).reshape(pieces, rows, share)


def to_groups(parts):
    pieces, rows, share = parts.shape
    if share == LANES:
        return parts
    joined = parts.reshape(pieces * share // LANES, LANES // share, rows, share)
    return joined.transpose(0, 2, 1, 3).reshape(-1, rows, LANES)


def partners(value, axis, steps):
    size = lax.axis_size(axis)
    return [value] + [lax.ppermute(value, axis, [(i, i ^ step) for i in range(size)]) for step in steps]


def rounds_of(size):
    return [(1 << bit,) for bit in range(size.bit_length() - 1)]


def add_up(values):
    if len(values) == 2:
        return values[0] + values[1]
    return (values[0] + values[1]) + (values[2] + values[3])


def body(q_in, k_in, v_in, grad_out, short_filter, kernel, skip):
    pieces = lax.axis_size("ctx")
    sides = lax.axis_size("ch")
    rows_here, channels = q_in.shape
    seq_len = pieces * rows_here
    taps_count = short_filter.shape[0]
    halo_rows = taps_count - 1
    groups = channels // LANES
    share = channels // pieces
    per_step = min(groups, 4)
    steps = groups // per_step
    lanes2 = cut_lanes(per_step * LANES, 2)
    lanes3 = cut_lanes(per_step * LANES, 3)
    skip_row = skip.reshape(1, channels)
    transforms = (Transforms if share == LANES else PlainTransforms)(pieces, rows_here)
    stream = functools.partial(stream_call, steps=steps, per_step=per_step)

    flat = jax.ShapeDtypeStruct((rows_here, channels), bf16)
    extra_rows = -(-7 * halo_rows // TILE_ROWS) * TILE_ROWS
    sent = jax.ShapeDtypeStruct((groups, 3 * rows_here + extra_rows, LANES), bf16)
    exts = [pltpu.VMEM((rows_here + PAD, LANES), f32)] * 6

    (signals,) = stream(
        signals_work,
        operands=[(x, lanes2) for x in (q_in, k_in, v_in, grad_out, kernel, short_filter)],
        results=[(sent, cut_groups(per_step))],
        scratch=exts,
        vmem_bytes=MOST_VMEM_BYTES,
    )
    signals_here = exchange(to_pieces(signals, pieces))
    (short,) = stream(
        short_work,
        operands=[(x, lanes2) for x in (q_in, k_in, v_in, short_filter)],
        results=[(jax.ShapeDtypeStruct((3, rows_here, channels), f32), lanes3)],
        scratch=exts,
        after=[signals],
    )
    taps_and_skip = jnp.concatenate([short_filter, skip_row], axis=0)
    taps_here = lax.dynamic_slice_in_dim(taps_and_skip, lax.axis_index("ctx") * share, share, axis=1)
    long_here, lag_spec = transforms.products(signals_here, taps_here, short)
    long = to_groups(exchange(long_here))
    lag_here, lag_squares = transforms.lag(lag_spec)
    lag = to_groups(exchange(lag_here))

    mixed, grad_q, grad_k, grad_v, sums = stream(
        finish_work,
        operands=[(x, lanes2) for x in (q_in, k_in, v_in, grad_out)]
        + [(short, lanes3), (short_filter, lanes2), (skip_row, lanes2)]
        + [(long, cut_groups(per_step)), (lag_squares, cut_none)],
        results=[(flat, lanes2)] * 4,
        scratch=exts,
        kept=[jax.ShapeDtypeStruct((taps_count + 1, channels + LANES), f32)],
    )

    totals = sums
    rounds = rounds_of(pieces)
    for idx, steps_of in enumerate(rounds[:-1]):
        values = partners(totals, "ctx", steps_of)
        if idx == 0:
            values[0] = call(
                same_kernel, jax.ShapeDtypeStruct(totals.shape, f32), [], totals,
                vmem_bytes=SMALL_VMEM_BYTES, in_specs=[IN_VMEM], out_specs=IN_VMEM,
            )
        totals = call(
            add_kernel, jax.ShapeDtypeStruct(totals.shape, f32), [], *values,
            vmem_bytes=SMALL_VMEM_BYTES, in_specs=[IN_VMEM] * len(values), out_specs=IN_VMEM,
        )
    last = partners(totals, "ctx", rounds[-1])

    totals, norm_sq = call(
        norm_kernel,
        (jax.ShapeDtypeStruct(totals.shape, f32), jax.ShapeDtypeStruct((1, LANES), f32)),
        [], *last,
        vmem_bytes=SMALL_VMEM_BYTES,
        in_specs=[IN_VMEM] * len(last), out_specs=(IN_VMEM, IN_VMEM),
    )
    for steps_of in rounds_of(sides):
        norm_sq = add_up(partners(norm_sq, "ch", steps_of))

    limit = math.sqrt(float(seq_len * channels * sides))
    grad_short, grad_skip, grad_kernel = call(
        functools.partial(scale_kernel, limit),
        (
            jax.ShapeDtypeStruct((taps_count, channels), f32),
            jax.ShapeDtypeStruct((1, channels), f32),
            jax.ShapeDtypeStruct((rows_here, channels), f32),
        ),
        [],
        totals, norm_sq, lag,
        vmem_bytes=SMALL_VMEM_BYTES,
        in_specs=[IN_VMEM] * 3,
        out_specs=(IN_VMEM,) * 3,
    )
    return mixed, grad_q, grad_k, grad_v, grad_short, grad_skip.reshape(channels), grad_kernel


def solution(mesh):
    in_specs = (
        P("ctx", "ch"),
        P("ctx", "ch"),
        P("ctx", "ch"),
        P("ctx", "ch"),
        P(None, "ch"),
        P("ctx", "ch"),
        P("ch"),
    )
    out_specs = (
        P("ctx", "ch"),
        P("ctx", "ch"),
        P("ctx", "ch"),
        P("ctx", "ch"),
        P(None, "ch"),
        P("ch"),
        P("ctx", "ch"),
    )
    return jax.shard_map(body, mesh=mesh, in_specs=in_specs, out_specs=out_specs, check_vma=False)
```

```python
import functools
import math

import jax
import jax.numpy as jnp
import ml_dtypes
import numpy as np
from jax import lax
from jax.experimental import pallas as pl
from jax.experimental.pallas import tpu as pltpu
from jax.sharding import PartitionSpec as P

LANES = 128
SPAN = 256
BOTH = 2 * SPAN
CHUNK = 16
CHUNKS = SPAN // CHUNK
PAD = 8
ROWS = 32
CUTS = 1
PASSES = 1
TILE_ROWS = 16
VMEM_BYTES = 60 * 1024 * 1024
MOST_VMEM_BYTES = 251 * 256 * 1024
SMALL_VMEM_BYTES = 8 * 1024 * 1024

f32 = jnp.float32
bf16 = jnp.bfloat16

IN_VMEM = pl.BlockSpec(memory_space=pltpu.VMEM)
IN_SMEM = pl.BlockSpec(memory_space=pltpu.SMEM)
ANYWHERE = pl.BlockSpec(memory_space=pl.ANY)


def call(kernel, outs, scratch, *args, vmem_bytes=VMEM_BYTES, **options):
    return pl.pallas_call(
        kernel,
        out_shape=outs,
        scratch_shapes=scratch,
        compiler_params=pltpu.CompilerParams(vmem_limit_bytes=vmem_bytes),
        **options,
    )(*args)


def leaf_phases(count):
    return [(4 * leaf + 1) / (4 * count) for leaf in range(count)]


def root_times(re, im, num, den, sign):
    if num == 0:
        return re, im
    if 4 * num == den:
        return (im, -re) if sign < 0 else (-im, re)
    cosine = math.cos(2.0 * math.pi * num / den)
    sine = sign * math.sin(2.0 * math.pi * num / den)
    if 8 * num == den:
        return ((re + im) * cosine, (im - re) * cosine) if sign < 0 else ((re - im) * cosine, (re + im) * cosine)
    if 8 * num == 3 * den:
        return ((re - im) * cosine, (re + im) * cosine) if sign < 0 else ((re + im) * cosine, (im - re) * cosine)
    return re * cosine - im * sine, im * cosine + re * sine


def short_fft(values, sign):
    count = len(values)
    if count == 1:
        return values
    even = short_fft(values[0::2], sign)
    odd = short_fft(values[1::2], sign)
    first = []
    second = []
    for num in range(count // 2):
        re, im = root_times(*odd[num], num, count, sign)
        first.append((even[num][0] + re, even[num][1] + im))
        second.append((even[num][0] - re, even[num][1] - im))
    return first + second


def to_leaves(parts):
    count = len(parts)
    turned = []
    for idx, part in enumerate(parts):
        angle = 2.0 * math.pi * idx / (4 * count)
        turned.append((part * math.cos(angle), part * (-math.sin(angle))) if idx else (part, jnp.zeros_like(part)))
    return short_fft(turned, -1)


def from_leaves(leaves, scale):
    count = len(leaves)
    parts = []
    for idx, (re, im) in enumerate(short_fft(leaves, 1)):
        angle = 2.0 * math.pi * idx / (4 * count)
        if idx == 0:
            parts.append(re * scale)
        else:
            parts.append(re * (math.cos(angle) * scale) - im * (math.sin(angle) * scale))
    return parts


def dft_matrix():
    idx = np.arange(SPAN)
    angle = (idx[:, None] * idx[None, :] % SPAN) * (2.0 * np.pi / SPAN)
    cosine, sine = np.cos(angle), np.sin(angle)
    return np.block([[cosine, sine], [-sine, cosine]])


def twist_angles(outer, inner):
    return np.asarray(leaf_phases(outer))[:, None] * np.asarray(inner)[None, :] * (2.0 * np.pi / SPAN)


def matrix_blocks():
    matrix = dft_matrix()
    high = matrix.astype(ml_dtypes.bfloat16)
    low = (matrix - high.astype(np.float64)).astype(ml_dtypes.bfloat16)
    return np.concatenate([high, low, high][:PASSES], axis=1)


def leaf_place(leaf):
    return leaf // 2, slice((leaf % 2) * LANES, (leaf % 2 + 1) * LANES)


def split_store(ref, leaf, below, here, value):
    pair, lanes = leaf_place(leaf)
    high = value.astype(bf16)
    for block in range(PASSES):
        part = high
        if PASSES == 3 and block == 2:
            part = (value - high.astype(f32)).astype(bf16)
        ref[pair, shifted_rows(here, block * BOTH + below), lanes] = part


def run_all(stages, rows_here, matmul=None, carry=0):
    tiles = matmul[2].shape[0] if matmul else 4
    per_tile = CHUNKS // tiles
    in_part = rows_here // CHUNK
    for tile in range(tiles):
        if matmul:
            matrix_ref, split_ref, result_ref = matmul
            result_ref[tile] = jnp.dot(matrix_ref[...], split_ref[tile], preferred_element_type=f32)
        for chunk in range(tile * per_tile, (tile + 1) * per_tile):
            for stage in stages:
                carry = stage(chunk // in_part, chunk % in_part * CHUNK, carry)
    return carry


def in_span(part, row, rows_here):
    return pl.ds(part * rows_here + row, CHUNK)


def twist_stage(coarse_ref, fine_ref, twist_ref, rows_here):
    outer = twist_ref.shape[1]

    def stage(part, row, carry):
        here = in_span(part, row, rows_here)
        idx = part * (rows_here // CHUNK) + row // CHUNK
        for leaf in range(outer):
            far_cosine = coarse_ref[idx, leaf]
            far_sine = coarse_ref[idx, outer + leaf]
            cosine = fine_ref[0, leaf]
            sine = fine_ref[1, leaf]
            twist_ref[0, leaf, here, :] = far_cosine * cosine - far_sine * sine
            twist_ref[1, leaf, here, :] = far_sine * cosine + far_cosine * sine
        return carry

    return stage


def leaves_stage(signals_ref, first_row, heads_ref, rows_here, twist_ref, split_ref):
    outer = twist_ref.shape[1]
    ratio = SPAN // rows_here

    def stage(part, row, carry):
        here = in_span(part, row, rows_here)
        rows = pl.ds(first_row + row, CHUNK)
        parts = [signals_ref[place * ratio + part, rows, :] for place in range(outer)]
        if heads_ref is not None and row == 0:
            parts = [heads_ref[place * ratio + part] for place in range(outer)]
        parts = [value.astype(f32) for value in parts]
        for leaf, (re, im) in enumerate(to_leaves(parts)):
            cosine = twist_ref[0, leaf, here, :]
            sine = twist_ref[1, leaf, here, :]
            split_store(split_ref, leaf, 0, here, re * cosine + im * sine)
            split_store(split_ref, leaf, SPAN, here, im * cosine - re * sine)
        return carry

    return stage


def shifted_rows(here, by):
    return pl.ds(here.start + by, here.size)


def combine_stage(left_ref, right_ref, split_ref, rows_here, conjugate):
    def stage(part, row, carry):
        here = in_span(part, row, rows_here)
        below = shifted_rows(here, SPAN)
        for leaf in range(2 * left_ref.shape[0]):
            pair, lanes = leaf_place(leaf)
            left_re = left_ref[pair, here, lanes]
            left_im = left_ref[pair, below, lanes]
            right_re = right_ref[pair, here, lanes]
            right_im = right_ref[pair, below, lanes]
            if conjugate:
                re = left_re * right_re + left_im * right_im
                minus_im = left_im * right_re - left_re * right_im
            else:
                re = left_re * right_re - left_im * right_im
                minus_im = -(left_re * right_im + left_im * right_re)
            split_store(split_ref, leaf, 0, here, re)
            split_store(split_ref, leaf, SPAN, here, minus_im)
        return carry

    return stage


def signal_stage(time_ref, twist_ref, rows_here, write):
    outer = twist_ref.shape[1]
    ratio = SPAN // rows_here
    scale = 1.0 / (SPAN * outer)

    def stage(part, row, carry):
        here = in_span(part, row, rows_here)
        below = shifted_rows(here, SPAN)
        leaves = []
        for leaf in range(outer):
            pair, lanes = leaf_place(leaf)
            cosine = twist_ref[0, leaf, here, :]
            sine = twist_ref[1, leaf, here, :]
            re = time_ref[pair, here, lanes]
            minus_im = time_ref[pair, below, lanes]
            leaves.append((re * cosine + minus_im * sine, re * sine - minus_im * cosine))
        for place, value in enumerate(from_leaves(leaves, scale)):
            carry = write(place * ratio + part, pl.ds(row, CHUNK), value, carry)
        return carry

    return stage


def first_rows(lead, first, taps):
    count = len(lead)
    rows = lead + first
    return [
        functools.reduce(lambda x, y: x + y, [taps[shift] * rows[count + row - shift] for shift in range(count + 1)])
        for row in range(count)
    ]


def first_signals(ahead, own, taps):
    count = len(taps) - 1

    def kind(rows, idx):
        return rows[idx * count : (idx + 1) * count]

    shorts = [first_rows(kind(ahead, idx), kind(own, 3 + idx), taps) for idx in range(3)]
    product = [(k_row * v_row).astype(bf16) for k_row, v_row in zip(shorts[1], shorts[2])]
    back_mix = [grad_row * q_row for grad_row, q_row in zip(kind(own, 6), shorts[0])]
    return shorts, product, back_mix


def first_backs(ahead, own, taps, skip, conv, corr):
    count = len(taps) - 1
    shorts, product, back_mix = first_signals(ahead, own, taps)
    back_q = []
    back_k = []
    back_v = []
    for row in range(count):
        filtered = conv[row] + skip * product[row].astype(f32)
        back_prod = corr[row] + skip * back_mix[row]
        back_q.append(own[6 * count + row] * filtered)
        back_k.append(back_prod * shorts[2][row])
        back_v.append(back_prod * shorts[1][row])
    return back_q + back_k + back_v


def extra_of(signals_ref, piece, rows_here, used):
    rows = signals_ref[piece, 3 * rows_here :, :].astype(f32)
    return [rows[idx : idx + 1] for idx in range(used)]


def tap_rows(taps_ref):
    return [taps_ref[shift : shift + 1, :] for shift in range(taps_ref.shape[0])]


def patch_first_rows(signals_ref, heads_ref, taps_ref, rows_here):
    pieces = signals_ref.shape[0]
    taps = tap_rows(taps_ref)[:-1]
    used = 7 * (len(taps) - 1)
    row_idx = lax.broadcasted_iota(jnp.int32, (TILE_ROWS, LANES), 0)
    ahead = [jnp.zeros((1, LANES), f32)] * used
    for piece in range(pieces):
        own = extra_of(signals_ref, piece, rows_here, used)
        for kind, rows in enumerate(first_signals(ahead, own, taps)[1:]):
            tile = signals_ref[piece, kind * rows_here : kind * rows_here + TILE_ROWS, :].astype(f32)
            for row, value in enumerate(rows):
                tile = jnp.where(row_idx == row, value.astype(f32), tile)
            heads_ref[kind, piece] = tile.astype(bf16)
        ahead = own


def write_edges(signals_ref, results_ref, taps_ref, rows_here):
    pieces = signals_ref.shape[0]
    *taps, skip = tap_rows(taps_ref)
    count = len(taps) - 1
    nothing = jnp.zeros((1, LANES), f32)
    extras = [extra_of(signals_ref, piece, rows_here, 7 * count) for piece in range(pieces)]
    for piece in range(pieces):
        rows = extras[piece - 1][: 3 * count] if piece else [nothing] * (3 * count)
        if piece + 1 < pieces:
            conv, corr = (
                results_ref[piece + 1, kind * rows_here : kind * rows_here + TILE_ROWS, :].astype(f32)
                for kind in range(2)
            )
            rows = rows + first_backs(
                extras[piece], extras[piece + 1], taps, skip,
                [conv[row : row + 1] for row in range(count)], [corr[row : row + 1] for row in range(count)],
            )
        spare = results_ref.shape[1] - 2 * rows_here - len(rows)
        rows.append(jnp.zeros((spare, LANES), f32))
        results_ref[piece, 2 * rows_here :, :] = jnp.concatenate(rows, axis=0).astype(bf16)


def products_kernel(
    rows_here, signals_hbm, taps_ref, coarse_ref, fine_ref, matrix_hbm, after_ref, results_hbm, lag_hbm,
    signals_ref, twist_ref, matrix_ref, heads_ref, results_ref, one_split, two_split, lag_split,
    filter_ref, product_ref, cotan_ref, time_ref, sems,
):
    all_rows = signals_ref.shape[1]
    back_rows = results_ref.shape[1]
    sem_idx = iter(range(sems.shape[0]))

    def cut_copies(source, target, rows):
        each = source.shape[0] // CUTS
        places = [(pl.ds(cut * each, each), pl.ds(*rows)) for cut in range(CUTS)]
        return [pltpu.make_async_copy(source.at[at], target.at[at], sems.at[next(sem_idx)]) for at in places]

    filter_copies = cut_copies(signals_hbm, signals_ref, (2 * rows_here, all_rows - 2 * rows_here))
    matrix_copies = [
        pltpu.make_async_copy(
            matrix_hbm.at[pl.ds(cut * BOTH // CUTS, BOTH // CUTS)],
            matrix_ref.at[pl.ds(cut * BOTH // CUTS, BOTH // CUTS)],
            sems.at[next(sem_idx)],
        )
        for cut in range(CUTS)
    ]
    signal_copies = [cut_copies(signals_hbm, signals_ref, (kind * rows_here, rows_here)) for kind in range(2)]
    lag_copies = [
        pltpu.make_async_copy(lag_split.at[pair], lag_hbm.at[pair], sems.at[next(sem_idx)])
        for pair in range(lag_split.shape[0])
    ]
    return_copies = [
        cut_copies(results_ref, results_hbm, rows)
        for rows in ((0, rows_here), (rows_here, back_rows - rows_here))
    ]

    def start_all(copies):
        for copy in copies:
            copy.start()

    def wait_all(copies):
        for copy in copies:
            copy.wait()

    def leaves(kind, split_ref):
        heads = heads_ref.at[kind] if kind < 2 else None
        return leaves_stage(signals_ref, kind * rows_here, heads, rows_here, twist_ref, split_ref)

    def combine(left_ref, right_ref, split_ref, conjugate):
        return combine_stage(left_ref, right_ref, split_ref, rows_here, conjugate)

    def result(kind, from_ref):
        def write(piece, rows, value, carry):
            place = pl.ds(kind * rows_here + rows.start, CHUNK)
            results_ref[piece, place, :] = value.astype(bf16)
            return carry

        return signal_stage(from_ref, twist_ref, rows_here, write)

    start_all(filter_copies + matrix_copies + signal_copies[0] + signal_copies[1])
    run_all([twist_stage(coarse_ref, fine_ref, twist_ref, rows_here)], rows_here)
    wait_all(filter_copies)
    run_all([leaves(2, one_split)], rows_here)
    wait_all(signal_copies[0] + signal_copies[1] + matrix_copies)
    patch_first_rows(signals_ref, heads_ref, taps_ref, rows_here)
    run_all([leaves(0, two_split)], rows_here, (matrix_ref, one_split, filter_ref))
    run_all([leaves(1, one_split)], rows_here, (matrix_ref, two_split, product_ref))
    run_all([combine(filter_ref, product_ref, two_split, False)], rows_here, (matrix_ref, one_split, cotan_ref))
    run_all([combine(filter_ref, cotan_ref, one_split, True)], rows_here, (matrix_ref, two_split, time_ref))
    run_all(
        [combine(product_ref, cotan_ref, lag_split, True), result(0, time_ref)],
        rows_here, (matrix_ref, one_split, filter_ref),
    )
    start_all(return_copies[0] + lag_copies)
    run_all([result(1, filter_ref)], rows_here)
    write_edges(signals_ref, results_ref, taps_ref, rows_here)
    start_all(return_copies[1])
    wait_all(lag_copies + return_copies[0] + return_copies[1])


def lag_kernel(
    split_hbm, coarse_ref, fine_ref, matrix_hbm, lag_ref, square_ref, twist_ref, matrix_ref, split_ref, time_ref, sems
):
    rows_here = lag_ref.shape[1]
    copies = [
        pltpu.make_async_copy(matrix_hbm, matrix_ref, sems.at[0]),
        pltpu.make_async_copy(split_hbm, split_ref, sems.at[1]),
    ]
    for copy in copies:
        copy.start()
    run_all([twist_stage(coarse_ref, fine_ref, twist_ref, rows_here)], rows_here)
    for copy in copies:
        copy.wait()
    run_all([], rows_here, (matrix_ref, split_ref, time_ref))

    def write(piece, rows, value, carry):
        lag_ref[piece, rows, :] = value.astype(bf16)
        return carry + value * value

    square = run_all(
        [signal_stage(time_ref, twist_ref, rows_here, write)], rows_here, None, jnp.zeros((CHUNK, LANES), f32)
    )
    square_ref[...] = jnp.sum(square, axis=0, keepdims=True)


class Transforms:
    def __init__(self, pieces, rows_here):
        outer = pieces * rows_here // SPAN
        pairs = outer // 2
        coarse = twist_angles(outer, CHUNK * np.arange(CHUNKS)).T
        fine = twist_angles(outer, np.arange(CHUNK))[..., None] * np.ones(LANES)
        self.tables = [
            jnp.asarray(np.concatenate([np.cos(coarse), np.sin(coarse)], axis=1).astype(np.float32)),
            jnp.asarray(np.stack([np.cos(fine), np.sin(fine)]).astype(np.float32)),
            jnp.asarray(matrix_blocks()),
        ]
        self.split = jax.ShapeDtypeStruct((pairs, PASSES * BOTH, 2 * LANES), bf16)
        self.signal = jax.ShapeDtypeStruct((pieces, rows_here, LANES), bf16)
        self.result = jax.ShapeDtypeStruct((pieces, 2 * rows_here + TILE_ROWS, LANES), bf16)
        self.square = jax.ShapeDtypeStruct((1, LANES), f32)
        self.result_work = pltpu.VMEM(self.result.shape, bf16)
        self.work = pltpu.VMEM((pairs, BOTH, 2 * LANES), f32)
        self.split_work = pltpu.VMEM(self.split.shape, bf16)
        self.twist_work = pltpu.VMEM((2, outer, SPAN, LANES), f32)
        self.matrix_work = pltpu.VMEM(self.tables[2].shape, bf16)

    def products(self, signals, taps, after):
        return call(
            functools.partial(products_kernel, self.signal.shape[1]), (self.result, self.split),
            [pltpu.VMEM(signals.shape, bf16), self.twist_work, self.matrix_work]
            + [pltpu.VMEM((2, signals.shape[0], TILE_ROWS, LANES), bf16), self.result_work]
            + [self.split_work] * 3
            + [self.work] * 4
            + [pltpu.SemaphoreType.DMA((6 * CUTS + self.split.shape[0],))],
            signals, taps, *self.tables, after,
            vmem_bytes=MOST_VMEM_BYTES,
            in_specs=[ANYWHERE, IN_VMEM, IN_SMEM, IN_VMEM, ANYWHERE, ANYWHERE],
            out_specs=(ANYWHERE, ANYWHERE),
        )

    def lag(self, lag_split):
        return call(
            lag_kernel, (self.signal, self.square),
            [self.twist_work, self.matrix_work, self.split_work, self.work, pltpu.SemaphoreType.DMA((2,))],
            lag_split, *self.tables,
            in_specs=[ANYWHERE, IN_SMEM, IN_VMEM, ANYWHERE],
            out_specs=(IN_VMEM, IN_VMEM),
        )


class PlainTransforms:
    def __init__(self, pieces, rows_here):
        self.seq_len = pieces * rows_here
        self.pieces = pieces
        self.outer = self.seq_len // SPAN
        idx = np.arange(SPAN)
        angle = (idx[:, None] * idx[None, :] % SPAN) * (2.0 * np.pi / SPAN)
        self.cosine = jnp.asarray(np.cos(angle), f32)
        self.sine = jnp.asarray(np.sin(angle), f32)
        twist = twist_angles(self.outer, idx)
        self.twist = jnp.asarray(np.stack([np.cos(twist), np.sin(twist)]), f32)[..., None]

    def dot(self, matrix, signal):
        return jnp.einsum("fs,tsc->tfc", matrix, signal, precision=lax.Precision.HIGHEST)

    def spectrum(self, signal):
        parts = signal.astype(f32).reshape(self.outer, SPAN, -1)
        leaves = to_leaves([parts[part] for part in range(self.outer)])
        re = jnp.stack([leaf[0] for leaf in leaves])
        im = jnp.stack([leaf[1] for leaf in leaves])
        twist_re = re * self.twist[0] + im * self.twist[1]
        twist_im = im * self.twist[0] - re * self.twist[1]
        return (
            self.dot(self.cosine, twist_re) + self.dot(self.sine, twist_im),
            self.dot(self.cosine, twist_im) - self.dot(self.sine, twist_re),
        )

    def back(self, re, im):
        time_re = self.dot(self.cosine, re) - self.dot(self.sine, im)
        time_im = self.dot(self.cosine, im) + self.dot(self.sine, re)
        leaf_re = time_re * self.twist[0] - time_im * self.twist[1]
        leaf_im = time_im * self.twist[0] + time_re * self.twist[1]
        parts = from_leaves([(leaf_re[leaf], leaf_im[leaf]) for leaf in range(self.outer)], 1.0 / self.seq_len)
        return jnp.stack(parts).reshape(self.pieces, self.seq_len // self.pieces, -1)

    def products(self, signals, taps_and_skip, after):
        rows_here = self.seq_len // self.pieces
        parts = [signals[:, kind * rows_here : (kind + 1) * rows_here] for kind in range(3)]
        extra = signals[:, 3 * rows_here :].astype(f32)
        rows = [extra[:, idx : idx + 1] for idx in range(extra.shape[1])]
        ahead = [jnp.concatenate([jnp.zeros_like(row[:1]), row[:-1]], axis=0) for row in rows]
        *taps, skip = [taps_and_skip[row][None, None, :] for row in range(taps_and_skip.shape[0])]
        count = len(taps) - 1
        for kind, first in enumerate(first_signals(ahead, rows, taps)[1:]):
            first = jnp.concatenate(first, axis=1)
            parts[kind] = jnp.concatenate([first.astype(bf16), parts[kind][:, first.shape[1] :]], axis=1)
        product, cotan, taps_spec = (self.spectrum(part) for part in parts)
        conv = self.back(
            taps_spec[0] * product[0] - taps_spec[1] * product[1], taps_spec[0] * product[1] + taps_spec[1] * product[0]
        ).astype(bf16)
        corr = self.back(
            taps_spec[0] * cotan[0] + taps_spec[1] * cotan[1], taps_spec[0] * cotan[1] - taps_spec[1] * cotan[0]
        ).astype(bf16)
        lag = (
            product[0] * cotan[0] + product[1] * cotan[1],
            product[0] * cotan[1] - product[1] * cotan[0],
        )
        backs = first_backs(
            ahead, rows, taps, skip,
            [conv[:, row : row + 1].astype(f32) for row in range(count)],
            [corr[:, row : row + 1].astype(f32) for row in range(count)],
        )
        behind = [jnp.concatenate([row[1:], jnp.zeros_like(row[:1])], axis=0) for row in backs]
        edge = jnp.concatenate(ahead[: 3 * count] + behind, axis=1).astype(bf16)
        edge = jnp.pad(edge, ((0, 0), (0, TILE_ROWS - edge.shape[1]), (0, 0)))
        return jnp.concatenate([conv, corr, edge], axis=1), lag

    def lag(self, lag_spec):
        lag = self.back(*lag_spec)
        squares = jnp.sum(lag * lag, axis=(0, 1))
        return lag.astype(bf16), jnp.zeros((1, LANES), f32).at[0, : squares.shape[0]].set(squares)


def group(idx):
    return slice(idx * LANES, (idx + 1) * LANES)


def streamed(work, steps, per_step, places, in_count, out_count, kept, *refs):
    moved = in_count + out_count
    hbm = refs[:moved]
    kept_refs = refs[moved : moved + kept]
    held = refs[moved + kept : 2 * moved + kept]
    scratch = refs[2 * moved + kept : -1]
    sems = refs[-1]

    def copy(place, step):
        outside = hbm[place].at[places[place](step)]
        inside = held[place].at[places[place](step)]
        ends = (outside, inside) if place < in_count else (inside, outside)
        return pltpu.make_async_copy(*ends, sems.at[place, step])

    def arrivals(step):
        return [copy(place, step) for place in range(in_count) if places[place](step) is not None]

    for step in range(steps):
        for arrival in arrivals(step):
            arrival.start()
    for step in range(steps):
        for arrival in arrivals(step):
            arrival.wait()
        for idx in range(step * per_step, (step + 1) * per_step):
            exts = scratch[idx % 2 :: 2]
            work(idx, held[:in_count], held[in_count:] + kept_refs, exts)
        for place in range(in_count, moved):
            copy(place, step).start()
    for step in range(steps):
        for place in range(in_count, moved):
            copy(place, step).wait()


def stream_call(work, steps, per_step, operands, results, scratch=(), after=(), kept=(), vmem_bytes=VMEM_BYTES):
    arrays = [operand[0] for operand in operands]
    shapes = [jax.ShapeDtypeStruct(array.shape, array.dtype) for array in arrays] + [result[0] for result in results]
    cuts = [entry[1] for entry in list(operands) + list(results)]
    held = [pltpu.VMEM(shape.shape, shape.dtype) for shape in shapes]
    extra = list(after)
    kernel = functools.partial(streamed, work, steps, per_step, cuts, len(arrays), len(results), len(kept))

    def without_extra(*refs):
        kernel(*refs[: len(arrays)], *refs[len(arrays) + len(extra) :])

    return call(
        without_extra,
        tuple(result[0] for result in results) + tuple(kept),
        held + list(scratch) + [pltpu.SemaphoreType.DMA((len(shapes), steps))],
        *arrays, *extra,
        vmem_bytes=vmem_bytes,
        in_specs=[ANYWHERE] * (len(arrays) + len(extra)),
        out_specs=(ANYWHERE,) * len(results) + (IN_VMEM,) * len(kept),
    )


def cut_lanes(width, rank):
    def place(step):
        return (slice(None),) * (rank - 1) + (pl.ds(step * width, width),)

    return place


def cut_groups(per_step):
    def place(step):
        return (pl.ds(step * per_step, per_step),)

    return place


def cut_none(step):
    return None if step else (slice(None),)


def row_blocks(rows_here):
    return [slice(start, start + ROWS) for start in range(0, rows_here, ROWS)]


def extend_rows(lead, in_ref, lanes, ext_ref):
    ext_ref[PAD - lead.shape[0] : PAD, :] = lead
    ext_ref[PAD:, :] = in_ref[:, lanes].astype(f32)


def short_conv(ext_ref, taps, rows):
    result = None
    for shift_idx in range(taps.shape[0]):
        term = taps[shift_idx : shift_idx + 1] * ext_ref[PAD + rows.start - shift_idx : PAD + rows.stop - shift_idx, :]
        result = term if result is None else result + term
    return result


def signals_work(idx, operands, results, exts):
    q_ref, k_ref, v_ref, grad_ref, kernel_ref, taps_ref = operands
    lanes = group(idx)
    taps = taps_ref[:, lanes]
    halo_rows = taps.shape[0] - 1
    rows_here = q_ref.shape[0]
    for ext, in_ref in zip(exts, operands):
        extend_rows(jnp.zeros((halo_rows, LANES), f32), in_ref, lanes, ext)
    for rows in row_blocks(rows_here):
        q_short, k_short, v_short = (short_conv(ext, taps, rows) for ext in exts)
        below = [slice(kind * rows_here + rows.start, kind * rows_here + rows.stop) for kind in range(3)]
        results[0][idx, below[0], :] = (k_short * v_short).astype(bf16)
        results[0][idx, below[1], :] = (grad_ref[rows, lanes].astype(f32) * q_short).astype(bf16)
        results[0][idx, below[2], :] = kernel_ref[rows, lanes].astype(bf16)
    top = grad_ref[0:TILE_ROWS, lanes].astype(f32)[:halo_rows]
    extra = [ext[ext.shape[0] - halo_rows :, :] for ext in exts] + [ext[PAD : PAD + halo_rows, :] for ext in exts]
    extra_count = results[0].shape[1] - 3 * rows_here
    blank = jnp.zeros((extra_count - 7 * halo_rows, LANES), f32)
    results[0][idx, 3 * rows_here :, :] = jnp.concatenate(extra + [top, blank], axis=0).astype(bf16)


def short_work(idx, operands, results, exts):
    lanes = group(idx)
    taps = operands[3][:, lanes]
    for ext, in_ref in zip(exts, operands):
        extend_rows(jnp.zeros((taps.shape[0] - 1, LANES), f32), in_ref, lanes, ext)
    for rows in row_blocks(operands[0].shape[0]):
        for place, ext in enumerate(exts):
            results[0][place, rows, lanes] = short_conv(ext, taps, rows)


def fold(value):
    return jnp.sum(value.reshape(-1, 8, LANES), axis=0)


def finish_work(idx, operands, results, exts):
    q_ref, k_ref, v_ref, grad_ref, short_ref, taps_ref, skip_ref, long_ref, squares_ref = operands
    mixed_ref, grad_q_ref, grad_k_ref, grad_v_ref, sums_ref = results
    lanes = group(idx)
    taps = taps_ref[:, lanes]
    skip = skip_ref[:, lanes]
    taps_count = taps.shape[0]
    halo_rows = taps_count - 1
    rows_here = q_ref.shape[0]
    sums = [jnp.zeros((8, LANES), f32) for _ in range(taps_count + 1)]
    edge = long_ref[idx, 2 * rows_here :, :].astype(f32)
    for place, ext in enumerate(exts):
        at = (3 + place) * halo_rows
        ext[rows_here : rows_here + halo_rows, :] = edge[at : at + halo_rows]
    row_idx = lax.broadcasted_iota(jnp.int32, (ROWS, LANES), 0)

    def short(place, rows):
        value = short_ref[place, rows, lanes]
        if rows.start == 0:
            for shift_idx in range(1, taps_count):
                terms = jnp.zeros((ROWS, LANES), f32)
                for row in range(shift_idx):
                    at = place * halo_rows + halo_rows + row - shift_idx
                    term = taps[shift_idx : shift_idx + 1] * edge[at : at + 1]
                    terms = jnp.where(row_idx == row, term, terms)
                value = value + terms
        return value

    for rows in row_blocks(rows_here):
        q_short, k_short, v_short = (short(place, rows) for place in range(3))
        product = (k_short * v_short).astype(bf16).astype(f32)
        filtered = long_ref[idx, rows, :].astype(f32) + skip * product
        mixed_ref[rows, lanes] = (q_short * filtered).astype(bf16)
        upstream = grad_ref[rows, lanes].astype(f32)
        back_mix = upstream * q_short
        below = slice(rows_here + rows.start, rows_here + rows.stop)
        back_prod = long_ref[idx, below, :].astype(f32) + skip * back_mix
        sums[taps_count] = sums[taps_count] + fold(back_mix * product)
        exts[0][rows, :] = upstream * filtered
        exts[1][rows, :] = back_prod * v_short
        exts[2][rows, :] = back_prod * k_short
    for ext, in_ref, out_ref in zip(exts, (q_ref, k_ref, v_ref), (grad_q_ref, grad_k_ref, grad_v_ref)):
        for rows in row_blocks(rows_here):
            signal = in_ref[rows, lanes].astype(f32)
            grad = None
            for shift_idx in range(taps_count):
                ahead = ext[rows.start + shift_idx : rows.stop + shift_idx, :]
                term = taps[shift_idx : shift_idx + 1] * ahead
                grad = term if grad is None else grad + term
                sums[shift_idx] = sums[shift_idx] + fold(ahead * signal)
            out_ref[rows, lanes] = grad.astype(bf16)
    if idx == 0:
        extra = slice(sums_ref.shape[1] - LANES, sums_ref.shape[1])
        sums_ref[:, extra] = jnp.zeros((taps_count + 1, LANES), f32)
        sums_ref[0:1, extra] = squares_ref[...]
    for shift_idx in range(taps_count + 1):
        sums_ref[shift_idx : shift_idx + 1, lanes] = jnp.sum(sums[shift_idx], axis=0, keepdims=True)


def norm_kernel(*refs):
    values, totals_ref, square_ref = refs[:-2], refs[-2], refs[-1]
    channels = totals_ref.shape[1] - LANES
    totals = add_up([value[...] for value in values]) if len(values) > 1 else values[0][...]
    totals_ref[...] = totals
    square = jnp.sum(totals[:, :channels] * totals[:, :channels]) + jnp.sum(totals[0:1, channels:])
    square_ref[...] = jnp.full(square_ref.shape, square)


def add_kernel(*refs):
    refs[-1][...] = add_up([ref[...] for ref in refs[:-1]])


def halves_kernel(odd_ref, own_ref, one_ref, two_ref, three_ref, four_ref, total_ref):
    even_sum = (own_ref[...] + one_ref[...]) + (two_ref[...] + three_ref[...])
    odd_sum = (one_ref[...] + two_ref[...]) + (three_ref[...] + four_ref[...])
    total_ref[...] = jnp.where(odd_ref[0] == 1, odd_sum, even_sum)


def same_kernel(value_ref, same_ref):
    same_ref[...] = value_ref[...]


def scale_kernel(limit, totals_ref, norm_ref, lag_ref, taps_out, skip_out, kernel_out):
    taps_count, channels = taps_out.shape
    factor = limit / jnp.maximum(jnp.sqrt(norm_ref[...]), limit)
    for idx in range(channels // LANES):
        lanes = slice(idx * LANES, (idx + 1) * LANES)
        taps_out[:, lanes] = totals_ref[0:taps_count, lanes] * factor
        skip_out[:, lanes] = totals_ref[taps_count : taps_count + 1, lanes] * factor
        kernel_out[:, lanes] = lag_ref[idx].astype(f32) * factor


def exchange(pieces_first):
    return lax.all_to_all(pieces_first, "ctx", split_axis=0, concat_axis=0, tiled=True)


def to_pieces(groups, pieces):
    count, rows, lanes = groups.shape
    if count == pieces:
        return groups
    share = count * lanes // pieces
    split = groups.reshape(count, rows, lanes // share, share)
    return split.transpose(0, 2, 1, 3).reshape(pieces, rows, share)


def to_groups(parts):
    pieces, rows, share = parts.shape
    if share == LANES:
        return parts
    joined = parts.reshape(pieces * share // LANES, LANES // share, rows, share)
    return joined.transpose(0, 2, 1, 3).reshape(-1, rows, LANES)


def partners(value, axis, steps):
    size = lax.axis_size(axis)
    return [value] + [lax.ppermute(value, axis, [(i, i ^ step) for i in range(size)]) for step in steps]


def rounds_of(size):
    rounds = []
    step = 1
    while step < size:
        rounds.append((step, 2 * step, 3 * step) if size // step >= 4 else (step,))
        step *= 4 if size // step >= 4 else 2
    return rounds


def halved_partners(value, axis):
    size = lax.axis_size(axis)
    heard = [value]
    for idx in range(1, 4):
        heard.append(lax.ppermute(value, axis, [(i, i ^ 2 * (idx + 3 * (i % 2))) for i in range(size)]))
    heard.append(lax.ppermute(value, axis, [(i, i ^ 14) for i in range(1, size, 2)]))
    return heard


def add_up(values):
    if len(values) == 2:
        return values[0] + values[1]
    return (values[0] + values[1]) + (values[2] + values[3])


def body(q_in, k_in, v_in, grad_out, short_filter, kernel, skip):
    pieces = lax.axis_size("ctx")
    sides = lax.axis_size("ch")
    rows_here, channels = q_in.shape
    seq_len = pieces * rows_here
    taps_count = short_filter.shape[0]
    halo_rows = taps_count - 1
    groups = channels // LANES
    share = channels // pieces
    per_step = min(groups, 4)
    steps = groups // per_step
    lanes2 = cut_lanes(per_step * LANES, 2)
    lanes3 = cut_lanes(per_step * LANES, 3)
    skip_row = skip.reshape(1, channels)
    transforms = (Transforms if share == LANES else PlainTransforms)(pieces, rows_here)
    stream = functools.partial(stream_call, steps=steps, per_step=per_step)

    flat = jax.ShapeDtypeStruct((rows_here, channels), bf16)
    extra_rows = -(-7 * halo_rows // TILE_ROWS) * TILE_ROWS
    sent = jax.ShapeDtypeStruct((groups, 3 * rows_here + extra_rows, LANES), bf16)
    exts = [pltpu.VMEM((rows_here + PAD, LANES), f32)] * 6

    (signals,) = stream(
        signals_work,
        operands=[(x, lanes2) for x in (q_in, k_in, v_in, grad_out, kernel, short_filter)],
        results=[(sent, cut_groups(per_step))],
        scratch=exts,
        vmem_bytes=MOST_VMEM_BYTES,
    )
    signals_here = exchange(to_pieces(signals, pieces))
    (short,) = stream(
        short_work,
        operands=[(x, lanes2) for x in (q_in, k_in, v_in, short_filter)],
        results=[(jax.ShapeDtypeStruct((3, rows_here, channels), f32), lanes3)],
        scratch=exts,
        after=[signals],
    )
    taps_and_skip = jnp.concatenate([short_filter, skip_row], axis=0)
    taps_here = lax.dynamic_slice_in_dim(taps_and_skip, lax.axis_index("ctx") * share, share, axis=1)
    long_here, lag_spec = transforms.products(signals_here, taps_here, short)
    long = to_groups(exchange(long_here))
    lag_here, lag_squares = transforms.lag(lag_spec)
    lag = to_groups(exchange(lag_here))

    mixed, grad_q, grad_k, grad_v, sums = stream(
        finish_work,
        operands=[(x, lanes2) for x in (q_in, k_in, v_in, grad_out)]
        + [(short, lanes3), (short_filter, lanes2), (skip_row, lanes2)]
        + [(long, cut_groups(per_step)), (lag_squares, cut_none)],
        results=[(flat, lanes2)] * 4,
        scratch=exts,
        kept=[jax.ShapeDtypeStruct((taps_count + 1, channels + LANES), f32)],
    )

    total_shape = jax.ShapeDtypeStruct(sums.shape, f32)

    def add(values):
        return call(
            add_kernel, total_shape, [], *values,
            vmem_bytes=SMALL_VMEM_BYTES, in_specs=[IN_VMEM] * len(values), out_specs=IN_VMEM,
        )

    if pieces >= 16:
        values = partners(sums, "ctx", (1,))
        values[0] = call(
            same_kernel, total_shape, [], sums,
            vmem_bytes=SMALL_VMEM_BYTES, in_specs=[IN_VMEM], out_specs=IN_VMEM,
        )
        odd = (lax.axis_index("ctx") % 2).reshape(1)
        halves = call(
            halves_kernel, total_shape, [], odd, *halved_partners(add(values), "ctx"),
            vmem_bytes=SMALL_VMEM_BYTES, in_specs=[IN_SMEM] + [IN_VMEM] * 5, out_specs=IN_VMEM,
        )
        last = partners(halves, "ctx", (1,))
        rounds = [tuple(16 * step for step in steps_of) for steps_of in rounds_of(pieces // 16)]
    else:
        last = [sums]
        rounds = rounds_of(pieces)
    for steps_of in rounds:
        last = partners(add(last) if len(last) > 1 else last[0], "ctx", steps_of)

    totals, norm_sq = call(
        norm_kernel,
        (total_shape, jax.ShapeDtypeStruct((1, LANES), f32)),
        [], *last,
        vmem_bytes=SMALL_VMEM_BYTES,
        in_specs=[IN_VMEM] * len(last), out_specs=(IN_VMEM, IN_VMEM),
    )
    for steps_of in rounds_of(sides):
        norm_sq = add_up(partners(norm_sq, "ch", steps_of))

    limit = math.sqrt(float(seq_len * channels * sides))
    grad_short, grad_skip, grad_kernel = call(
        functools.partial(scale_kernel, limit),
        (
            jax.ShapeDtypeStruct((taps_count, channels), f32),
            jax.ShapeDtypeStruct((1, channels), f32),
            jax.ShapeDtypeStruct((rows_here, channels), f32),
        ),
        [],
        totals, norm_sq, lag,
        vmem_bytes=SMALL_VMEM_BYTES,
        in_specs=[IN_VMEM] * 3,
        out_specs=(IN_VMEM,) * 3,
    )
    return mixed, grad_q, grad_k, grad_v, grad_short, grad_skip.reshape(channels), grad_kernel


def solution(mesh):
    in_specs = (
        P("ctx", "ch"),
        P("ctx", "ch"),
        P("ctx", "ch"),
        P("ctx", "ch"),
        P(None, "ch"),
        P("ctx", "ch"),
        P("ch"),
    )
    out_specs = (
        P("ctx", "ch"),
        P("ctx", "ch"),
        P("ctx", "ch"),
        P("ctx", "ch"),
        P(None, "ch"),
        P("ch"),
        P("ctx", "ch"),
    )
    return jax.shard_map(body, mesh=mesh, in_specs=in_specs, out_specs=out_specs, check_vma=False)
```

```python
import functools
import math

import jax
import jax.numpy as jnp
import ml_dtypes
import numpy as np
from jax import lax
from jax.experimental import pallas as pl
from jax.experimental.pallas import tpu as pltpu
from jax.sharding import PartitionSpec as P

LANES = 128
SPAN = 256
BOTH = 2 * SPAN
CHUNK = 16
CHUNKS = SPAN // CHUNK
PAD = 8
ROWS = 32
CUTS = 1
PASSES = 1
TILE_ROWS = 16
VMEM_BYTES = 60 * 1024 * 1024
MOST_VMEM_BYTES = 251 * 256 * 1024
SMALL_VMEM_BYTES = 8 * 1024 * 1024

f32 = jnp.float32
bf16 = jnp.bfloat16

IN_VMEM = pl.BlockSpec(memory_space=pltpu.VMEM)
IN_SMEM = pl.BlockSpec(memory_space=pltpu.SMEM)
ANYWHERE = pl.BlockSpec(memory_space=pl.ANY)


def call(kernel, outs, scratch, *args, vmem_bytes=VMEM_BYTES, **options):
    return pl.pallas_call(
        kernel,
        out_shape=outs,
        scratch_shapes=scratch,
        compiler_params=pltpu.CompilerParams(vmem_limit_bytes=vmem_bytes),
        **options,
    )(*args)


def leaf_phases(count):
    return [(4 * leaf + 1) / (4 * count) for leaf in range(count)]


def root_times(re, im, num, den, sign):
    if num == 0:
        return re, im
    if 4 * num == den:
        return (im, -re) if sign < 0 else (-im, re)
    cosine = math.cos(2.0 * math.pi * num / den)
    sine = sign * math.sin(2.0 * math.pi * num / den)
    if 8 * num == den:
        return ((re + im) * cosine, (im - re) * cosine) if sign < 0 else ((re - im) * cosine, (re + im) * cosine)
    if 8 * num == 3 * den:
        return ((re - im) * cosine, (re + im) * cosine) if sign < 0 else ((re + im) * cosine, (im - re) * cosine)
    return re * cosine - im * sine, im * cosine + re * sine


def short_fft(values, sign):
    count = len(values)
    if count == 1:
        return values
    even = short_fft(values[0::2], sign)
    odd = short_fft(values[1::2], sign)
    first = []
    second = []
    for num in range(count // 2):
        re, im = root_times(*odd[num], num, count, sign)
        first.append((even[num][0] + re, even[num][1] + im))
        second.append((even[num][0] - re, even[num][1] - im))
    return first + second


def to_leaves(parts):
    count = len(parts)
    turned = []
    for idx, part in enumerate(parts):
        angle = 2.0 * math.pi * idx / (4 * count)
        turned.append((part * math.cos(angle), part * (-math.sin(angle))) if idx else (part, jnp.zeros_like(part)))
    return short_fft(turned, -1)


def from_leaves(leaves, scale):
    count = len(leaves)
    parts = []
    for idx, (re, im) in enumerate(short_fft(leaves, 1)):
        angle = 2.0 * math.pi * idx / (4 * count)
        if idx == 0:
            parts.append(re * scale)
        else:
            parts.append(re * (math.cos(angle) * scale) - im * (math.sin(angle) * scale))
    return parts


def dft_matrix():
    idx = np.arange(SPAN)
    angle = (idx[:, None] * idx[None, :] % SPAN) * (2.0 * np.pi / SPAN)
    cosine, sine = np.cos(angle), np.sin(angle)
    return np.block([[cosine, sine], [-sine, cosine]])


def twist_angles(outer, inner):
    return np.asarray(leaf_phases(outer))[:, None] * np.asarray(inner)[None, :] * (2.0 * np.pi / SPAN)


def matrix_blocks():
    matrix = dft_matrix()
    high = matrix.astype(ml_dtypes.bfloat16)
    low = (matrix - high.astype(np.float64)).astype(ml_dtypes.bfloat16)
    return np.concatenate([high, low, high][:PASSES], axis=1)


def leaf_place(leaf):
    return leaf // 2, slice((leaf % 2) * LANES, (leaf % 2 + 1) * LANES)


def split_store(ref, leaf, below, here, value):
    pair, lanes = leaf_place(leaf)
    high = value.astype(bf16)
    for block in range(PASSES):
        part = high
        if PASSES == 3 and block == 2:
            part = (value - high.astype(f32)).astype(bf16)
        ref[pair, shifted_rows(here, block * BOTH + below), lanes] = part


def run_all(stages, rows_here, matmul=None, carry=0):
    tiles = matmul[2].shape[0] if matmul else 4
    per_tile = CHUNKS // tiles
    in_part = rows_here // CHUNK
    for tile in range(tiles):
        if matmul:
            matrix_ref, split_ref, result_ref = matmul
            result_ref[tile] = jnp.dot(matrix_ref[...], split_ref[tile], preferred_element_type=f32)
        for chunk in range(tile * per_tile, (tile + 1) * per_tile):
            for stage in stages:
                carry = stage(chunk // in_part, chunk % in_part * CHUNK, carry)
    return carry


def in_span(part, row, rows_here):
    return pl.ds(part * rows_here + row, CHUNK)


def twist_stage(coarse_ref, fine_ref, twist_ref, rows_here):
    outer = twist_ref.shape[1]

    def stage(part, row, carry):
        here = in_span(part, row, rows_here)
        idx = part * (rows_here // CHUNK) + row // CHUNK
        for leaf in range(outer):
            far_cosine = coarse_ref[idx, leaf]
            far_sine = coarse_ref[idx, outer + leaf]
            cosine = fine_ref[0, leaf]
            sine = fine_ref[1, leaf]
            twist_ref[0, leaf, here, :] = far_cosine * cosine - far_sine * sine
            twist_ref[1, leaf, here, :] = far_sine * cosine + far_cosine * sine
        return carry

    return stage


def leaves_stage(signals_ref, first_row, heads_ref, rows_here, twist_ref, split_ref):
    outer = twist_ref.shape[1]
    ratio = SPAN // rows_here

    def stage(part, row, carry):
        here = in_span(part, row, rows_here)
        rows = pl.ds(first_row + row, CHUNK)
        parts = [signals_ref[place * ratio + part, rows, :] for place in range(outer)]
        if heads_ref is not None and row == 0:
            parts = [heads_ref[place * ratio + part] for place in range(outer)]
        parts = [value.astype(f32) for value in parts]
        for leaf, (re, im) in enumerate(to_leaves(parts)):
            cosine = twist_ref[0, leaf, here, :]
            sine = twist_ref[1, leaf, here, :]
            split_store(split_ref, leaf, 0, here, re * cosine + im * sine)
            split_store(split_ref, leaf, SPAN, here, im * cosine - re * sine)
        return carry

    return stage


def shifted_rows(here, by):
    return pl.ds(here.start + by, here.size)


def combine_stage(left_ref, right_ref, split_ref, rows_here, conjugate):
    def stage(part, row, carry):
        here = in_span(part, row, rows_here)
        below = shifted_rows(here, SPAN)
        for leaf in range(2 * left_ref.shape[0]):
            pair, lanes = leaf_place(leaf)
            left_re = left_ref[pair, here, lanes]
            left_im = left_ref[pair, below, lanes]
            right_re = right_ref[pair, here, lanes]
            right_im = right_ref[pair, below, lanes]
            if conjugate:
                re = left_re * right_re + left_im * right_im
                minus_im = left_im * right_re - left_re * right_im
            else:
                re = left_re * right_re - left_im * right_im
                minus_im = -(left_re * right_im + left_im * right_re)
            split_store(split_ref, leaf, 0, here, re)
            split_store(split_ref, leaf, SPAN, here, minus_im)
        return carry

    return stage


def signal_stage(time_ref, twist_ref, rows_here, write):
    outer = twist_ref.shape[1]
    ratio = SPAN // rows_here
    scale = 1.0 / (SPAN * outer)

    def stage(part, row, carry):
        here = in_span(part, row, rows_here)
        below = shifted_rows(here, SPAN)
        leaves = []
        for leaf in range(outer):
            pair, lanes = leaf_place(leaf)
            cosine = twist_ref[0, leaf, here, :]
            sine = twist_ref[1, leaf, here, :]
            re = time_ref[pair, here, lanes]
            minus_im = time_ref[pair, below, lanes]
            leaves.append((re * cosine + minus_im * sine, re * sine - minus_im * cosine))
        for place, value in enumerate(from_leaves(leaves, scale)):
            carry = write(place * ratio + part, pl.ds(row, CHUNK), value, carry)
        return carry

    return stage


def first_rows(lead, first, taps):
    count = len(lead)
    rows = lead + first
    return [
        functools.reduce(lambda x, y: x + y, [taps[shift] * rows[count + row - shift] for shift in range(count + 1)])
        for row in range(count)
    ]


def first_signals(ahead, own, taps):
    count = len(taps) - 1

    def kind(rows, idx):
        return rows[idx * count : (idx + 1) * count]

    shorts = [first_rows(kind(ahead, idx), kind(own, 3 + idx), taps) for idx in range(3)]
    product = [(k_row * v_row).astype(bf16) for k_row, v_row in zip(shorts[1], shorts[2])]
    back_mix = [grad_row * q_row for grad_row, q_row in zip(kind(own, 6), shorts[0])]
    return shorts, product, back_mix


def first_backs(ahead, own, taps, skip, conv, corr):
    count = len(taps) - 1
    shorts, product, back_mix = first_signals(ahead, own, taps)
    back_q = []
    back_k = []
    back_v = []
    for row in range(count):
        filtered = conv[row] + skip * product[row].astype(f32)
        back_prod = corr[row] + skip * back_mix[row]
        back_q.append(own[6 * count + row] * filtered)
        back_k.append(back_prod * shorts[2][row])
        back_v.append(back_prod * shorts[1][row])
    return back_q + back_k + back_v


def extra_of(signals_ref, piece, rows_here, used):
    rows = signals_ref[piece, 3 * rows_here :, :].astype(f32)
    return [rows[idx : idx + 1] for idx in range(used)]


def tap_rows(taps_ref):
    return [taps_ref[shift : shift + 1, :] for shift in range(taps_ref.shape[0])]


def patch_first_rows(signals_ref, heads_ref, taps_ref, rows_here):
    pieces = signals_ref.shape[0]
    taps = tap_rows(taps_ref)[:-1]
    used = 7 * (len(taps) - 1)
    row_idx = lax.broadcasted_iota(jnp.int32, (TILE_ROWS, LANES), 0)
    ahead = [jnp.zeros((1, LANES), f32)] * used
    for piece in range(pieces):
        own = extra_of(signals_ref, piece, rows_here, used)
        for kind, rows in enumerate(first_signals(ahead, own, taps)[1:]):
            tile = signals_ref[piece, kind * rows_here : kind * rows_here + TILE_ROWS, :].astype(f32)
            for row, value in enumerate(rows):
                tile = jnp.where(row_idx == row, value.astype(f32), tile)
            heads_ref[kind, piece] = tile.astype(bf16)
        ahead = own


def write_edges(signals_ref, results_ref, taps_ref, rows_here):
    pieces = signals_ref.shape[0]
    *taps, skip = tap_rows(taps_ref)
    count = len(taps) - 1
    nothing = jnp.zeros((1, LANES), f32)
    extras = [extra_of(signals_ref, piece, rows_here, 7 * count) for piece in range(pieces)]
    for piece in range(pieces):
        rows = extras[piece - 1][: 3 * count] if piece else [nothing] * (3 * count)
        if piece + 1 < pieces:
            conv, corr = (
                results_ref[piece + 1, kind * rows_here : kind * rows_here + TILE_ROWS, :].astype(f32)
                for kind in range(2)
            )
            rows = rows + first_backs(
                extras[piece], extras[piece + 1], taps, skip,
                [conv[row : row + 1] for row in range(count)], [corr[row : row + 1] for row in range(count)],
            )
        spare = results_ref.shape[1] - 3 * rows_here - len(rows)
        rows.append(jnp.zeros((spare, LANES), f32))
        results_ref[piece, 3 * rows_here :, :] = jnp.concatenate(rows, axis=0).astype(bf16)


def products_kernel(
    rows_here, signals_hbm, taps_ref, coarse_ref, fine_ref, matrix_hbm, after_ref, results_hbm, square_ref,
    signals_ref, twist_ref, matrix_ref, heads_ref, results_ref, one_split, two_split, lag_split,
    filter_ref, product_ref, cotan_ref, time_ref, sems,
):
    all_rows = signals_ref.shape[1]
    back_rows = results_ref.shape[1]
    sem_idx = iter(range(sems.shape[0]))

    def cut_copies(source, target, rows):
        each = source.shape[0] // CUTS
        places = [(pl.ds(cut * each, each), pl.ds(*rows)) for cut in range(CUTS)]
        return [pltpu.make_async_copy(source.at[at], target.at[at], sems.at[next(sem_idx)]) for at in places]

    filter_copies = cut_copies(signals_hbm, signals_ref, (2 * rows_here, all_rows - 2 * rows_here))
    matrix_copies = [
        pltpu.make_async_copy(
            matrix_hbm.at[pl.ds(cut * BOTH // CUTS, BOTH // CUTS)],
            matrix_ref.at[pl.ds(cut * BOTH // CUTS, BOTH // CUTS)],
            sems.at[next(sem_idx)],
        )
        for cut in range(CUTS)
    ]
    signal_copies = [cut_copies(signals_hbm, signals_ref, (kind * rows_here, rows_here)) for kind in range(2)]
    return_copies = [
        cut_copies(results_ref, results_hbm, rows)
        for rows in ((0, rows_here), (rows_here, rows_here), (2 * rows_here, back_rows - 2 * rows_here))
    ]

    def start_all(copies):
        for copy in copies:
            copy.start()

    def wait_all(copies):
        for copy in copies:
            copy.wait()

    def leaves(kind, split_ref):
        heads = heads_ref.at[kind] if kind < 2 else None
        return leaves_stage(signals_ref, kind * rows_here, heads, rows_here, twist_ref, split_ref)

    def combine(left_ref, right_ref, split_ref, conjugate):
        return combine_stage(left_ref, right_ref, split_ref, rows_here, conjugate)

    def result(kind, from_ref):
        def write(piece, rows, value, carry):
            place = pl.ds(kind * rows_here + rows.start, CHUNK)
            results_ref[piece, place, :] = value.astype(bf16)
            return carry + value * value if kind == 2 else carry

        return signal_stage(from_ref, twist_ref, rows_here, write)

    start_all(filter_copies + matrix_copies + signal_copies[0] + signal_copies[1])
    run_all([twist_stage(coarse_ref, fine_ref, twist_ref, rows_here)], rows_here)
    wait_all(filter_copies)
    run_all([leaves(2, one_split)], rows_here)
    wait_all(signal_copies[0] + signal_copies[1] + matrix_copies)
    patch_first_rows(signals_ref, heads_ref, taps_ref, rows_here)
    run_all([leaves(0, two_split)], rows_here, (matrix_ref, one_split, filter_ref))
    run_all([leaves(1, one_split)], rows_here, (matrix_ref, two_split, product_ref))
    run_all([combine(filter_ref, product_ref, two_split, False)], rows_here, (matrix_ref, one_split, cotan_ref))
    run_all([combine(filter_ref, cotan_ref, one_split, True)], rows_here, (matrix_ref, two_split, time_ref))
    run_all(
        [combine(product_ref, cotan_ref, lag_split, True), result(0, time_ref)],
        rows_here, (matrix_ref, one_split, filter_ref),
    )
    start_all(return_copies[0])
    run_all([result(1, filter_ref)], rows_here, (matrix_ref, lag_split, time_ref))
    start_all(return_copies[1])
    write_edges(signals_ref, results_ref, taps_ref, rows_here)
    square = run_all([result(2, time_ref)], rows_here, None, jnp.zeros((CHUNK, LANES), f32))
    start_all(return_copies[2])
    square_ref[...] = jnp.sum(square, axis=0, keepdims=True)
    wait_all(return_copies[0] + return_copies[1] + return_copies[2])


class Transforms:
    def __init__(self, pieces, rows_here):
        outer = pieces * rows_here // SPAN
        pairs = outer // 2
        coarse = twist_angles(outer, CHUNK * np.arange(CHUNKS)).T
        fine = twist_angles(outer, np.arange(CHUNK))[..., None] * np.ones(LANES)
        self.tables = [
            jnp.asarray(np.concatenate([np.cos(coarse), np.sin(coarse)], axis=1).astype(np.float32)),
            jnp.asarray(np.stack([np.cos(fine), np.sin(fine)]).astype(np.float32)),
            jnp.asarray(matrix_blocks()),
        ]
        self.split = jax.ShapeDtypeStruct((pairs, PASSES * BOTH, 2 * LANES), bf16)
        self.signal = jax.ShapeDtypeStruct((pieces, rows_here, LANES), bf16)
        self.result = jax.ShapeDtypeStruct((pieces, 3 * rows_here + TILE_ROWS, LANES), bf16)
        self.square = jax.ShapeDtypeStruct((1, LANES), f32)
        self.result_work = pltpu.VMEM(self.result.shape, bf16)
        self.work = pltpu.VMEM((pairs, BOTH, 2 * LANES), f32)
        self.split_work = pltpu.VMEM(self.split.shape, bf16)
        self.twist_work = pltpu.VMEM((2, outer, SPAN, LANES), f32)
        self.matrix_work = pltpu.VMEM(self.tables[2].shape, bf16)

    def products(self, signals, taps, after):
        return call(
            functools.partial(products_kernel, self.signal.shape[1]), (self.result, self.square),
            [pltpu.VMEM(signals.shape, bf16), self.twist_work, self.matrix_work]
            + [pltpu.VMEM((2, signals.shape[0], TILE_ROWS, LANES), bf16), self.result_work]
            + [self.split_work] * 3
            + [self.work] * 4
            + [pltpu.SemaphoreType.DMA((7 * CUTS,))],
            signals, taps, *self.tables, after,
            vmem_bytes=MOST_VMEM_BYTES,
            in_specs=[ANYWHERE, IN_VMEM, IN_SMEM, IN_VMEM, ANYWHERE, ANYWHERE],
            out_specs=(ANYWHERE, IN_VMEM),
        )


class PlainTransforms:
    def __init__(self, pieces, rows_here):
        self.seq_len = pieces * rows_here
        self.pieces = pieces
        self.outer = self.seq_len // SPAN
        idx = np.arange(SPAN)
        angle = (idx[:, None] * idx[None, :] % SPAN) * (2.0 * np.pi / SPAN)
        self.cosine = jnp.asarray(np.cos(angle), f32)
        self.sine = jnp.asarray(np.sin(angle), f32)
        twist = twist_angles(self.outer, idx)
        self.twist = jnp.asarray(np.stack([np.cos(twist), np.sin(twist)]), f32)[..., None]

    def dot(self, matrix, signal):
        return jnp.einsum("fs,tsc->tfc", matrix, signal, precision=lax.Precision.HIGHEST)

    def spectrum(self, signal):
        parts = signal.astype(f32).reshape(self.outer, SPAN, -1)
        leaves = to_leaves([parts[part] for part in range(self.outer)])
        re = jnp.stack([leaf[0] for leaf in leaves])
        im = jnp.stack([leaf[1] for leaf in leaves])
        twist_re = re * self.twist[0] + im * self.twist[1]
        twist_im = im * self.twist[0] - re * self.twist[1]
        return (
            self.dot(self.cosine, twist_re) + self.dot(self.sine, twist_im),
            self.dot(self.cosine, twist_im) - self.dot(self.sine, twist_re),
        )

    def back(self, re, im):
        time_re = self.dot(self.cosine, re) - self.dot(self.sine, im)
        time_im = self.dot(self.cosine, im) + self.dot(self.sine, re)
        leaf_re = time_re * self.twist[0] - time_im * self.twist[1]
        leaf_im = time_im * self.twist[0] + time_re * self.twist[1]
        parts = from_leaves([(leaf_re[leaf], leaf_im[leaf]) for leaf in range(self.outer)], 1.0 / self.seq_len)
        return jnp.stack(parts).reshape(self.pieces, self.seq_len // self.pieces, -1)

    def products(self, signals, taps_and_skip, after):
        rows_here = self.seq_len // self.pieces
        parts = [signals[:, kind * rows_here : (kind + 1) * rows_here] for kind in range(3)]
        extra = signals[:, 3 * rows_here :].astype(f32)
        rows = [extra[:, idx : idx + 1] for idx in range(extra.shape[1])]
        ahead = [jnp.concatenate([jnp.zeros_like(row[:1]), row[:-1]], axis=0) for row in rows]
        *taps, skip = [taps_and_skip[row][None, None, :] for row in range(taps_and_skip.shape[0])]
        count = len(taps) - 1
        for kind, first in enumerate(first_signals(ahead, rows, taps)[1:]):
            first = jnp.concatenate(first, axis=1)
            parts[kind] = jnp.concatenate([first.astype(bf16), parts[kind][:, first.shape[1] :]], axis=1)
        product, cotan, taps_spec = (self.spectrum(part) for part in parts)
        conv = self.back(
            taps_spec[0] * product[0] - taps_spec[1] * product[1], taps_spec[0] * product[1] + taps_spec[1] * product[0]
        ).astype(bf16)
        corr = self.back(
            taps_spec[0] * cotan[0] + taps_spec[1] * cotan[1], taps_spec[0] * cotan[1] - taps_spec[1] * cotan[0]
        ).astype(bf16)
        lag = self.back(
            product[0] * cotan[0] + product[1] * cotan[1], product[0] * cotan[1] - product[1] * cotan[0]
        )
        squares = jnp.sum(lag * lag, axis=(0, 1))
        squares = jnp.zeros((1, LANES), f32).at[0, : squares.shape[0]].set(squares)
        backs = first_backs(
            ahead, rows, taps, skip,
            [conv[:, row : row + 1].astype(f32) for row in range(count)],
            [corr[:, row : row + 1].astype(f32) for row in range(count)],
        )
        behind = [jnp.concatenate([row[1:], jnp.zeros_like(row[:1])], axis=0) for row in backs]
        edge = jnp.concatenate(ahead[: 3 * count] + behind, axis=1).astype(bf16)
        edge = jnp.pad(edge, ((0, 0), (0, TILE_ROWS - edge.shape[1]), (0, 0)))
        return jnp.concatenate([conv, corr, lag.astype(bf16), edge], axis=1), squares


def group(idx):
    return slice(idx * LANES, (idx + 1) * LANES)


def streamed(work, steps, per_step, places, in_count, out_count, kept, *refs):
    moved = in_count + out_count
    hbm = refs[:moved]
    kept_refs = refs[moved : moved + kept]
    held = refs[moved + kept : 2 * moved + kept]
    scratch = refs[2 * moved + kept : -1]
    sems = refs[-1]

    def copy(place, step):
        outside = hbm[place].at[places[place](step)]
        inside = held[place].at[places[place](step)]
        ends = (outside, inside) if place < in_count else (inside, outside)
        return pltpu.make_async_copy(*ends, sems.at[place, step])

    def arrivals(step):
        return [copy(place, step) for place in range(in_count) if places[place](step) is not None]

    for step in range(steps):
        for arrival in arrivals(step):
            arrival.start()
    for step in range(steps):
        for arrival in arrivals(step):
            arrival.wait()
        for idx in range(step * per_step, (step + 1) * per_step):
            exts = scratch[idx % 2 :: 2]
            work(idx, held[:in_count], held[in_count:] + kept_refs, exts)
        for place in range(in_count, moved):
            copy(place, step).start()
    for step in range(steps):
        for place in range(in_count, moved):
            copy(place, step).wait()


def stream_call(work, steps, per_step, operands, results, scratch=(), after=(), kept=(), vmem_bytes=VMEM_BYTES):
    arrays = [operand[0] for operand in operands]
    shapes = [jax.ShapeDtypeStruct(array.shape, array.dtype) for array in arrays] + [result[0] for result in results]
    cuts = [entry[1] for entry in list(operands) + list(results)]
    held = [pltpu.VMEM(shape.shape, shape.dtype) for shape in shapes]
    extra = list(after)
    kernel = functools.partial(streamed, work, steps, per_step, cuts, len(arrays), len(results), len(kept))

    def without_extra(*refs):
        kernel(*refs[: len(arrays)], *refs[len(arrays) + len(extra) :])

    return call(
        without_extra,
        tuple(result[0] for result in results) + tuple(kept),
        held + list(scratch) + [pltpu.SemaphoreType.DMA((len(shapes), steps))],
        *arrays, *extra,
        vmem_bytes=vmem_bytes,
        in_specs=[ANYWHERE] * (len(arrays) + len(extra)),
        out_specs=(ANYWHERE,) * len(results) + (IN_VMEM,) * len(kept),
    )


def cut_lanes(width, rank):
    def place(step):
        return (slice(None),) * (rank - 1) + (pl.ds(step * width, width),)

    return place


def cut_groups(per_step, first_row, rows):
    def place(step):
        return (pl.ds(step * per_step, per_step), pl.ds(first_row, rows))

    return place


def cut_none(step):
    return None if step else (slice(None),)


def row_blocks(rows_here):
    return [slice(start, start + ROWS) for start in range(0, rows_here, ROWS)]


def extend_rows(lead, in_ref, lanes, ext_ref):
    ext_ref[PAD - lead.shape[0] : PAD, :] = lead
    ext_ref[PAD:, :] = in_ref[:, lanes].astype(f32)


def short_conv(ext_ref, taps, rows):
    result = None
    for shift_idx in range(taps.shape[0]):
        term = taps[shift_idx : shift_idx + 1] * ext_ref[PAD + rows.start - shift_idx : PAD + rows.stop - shift_idx, :]
        result = term if result is None else result + term
    return result


def signals_work(idx, operands, results, exts):
    q_ref, k_ref, v_ref, grad_ref, kernel_ref, taps_ref = operands
    lanes = group(idx)
    taps = taps_ref[:, lanes]
    halo_rows = taps.shape[0] - 1
    rows_here = q_ref.shape[0]
    for ext, in_ref in zip(exts, operands):
        extend_rows(jnp.zeros((halo_rows, LANES), f32), in_ref, lanes, ext)
    for rows in row_blocks(rows_here):
        q_short, k_short, v_short = (short_conv(ext, taps, rows) for ext in exts)
        below = [slice(kind * rows_here + rows.start, kind * rows_here + rows.stop) for kind in range(3)]
        results[0][idx, below[0], :] = (k_short * v_short).astype(bf16)
        results[0][idx, below[1], :] = (grad_ref[rows, lanes].astype(f32) * q_short).astype(bf16)
        results[0][idx, below[2], :] = kernel_ref[rows, lanes].astype(bf16)
    top = grad_ref[0:TILE_ROWS, lanes].astype(f32)[:halo_rows]
    extra = [ext[ext.shape[0] - halo_rows :, :] for ext in exts] + [ext[PAD : PAD + halo_rows, :] for ext in exts]
    extra_count = results[0].shape[1] - 3 * rows_here
    blank = jnp.zeros((extra_count - 7 * halo_rows, LANES), f32)
    results[0][idx, 3 * rows_here :, :] = jnp.concatenate(extra + [top, blank], axis=0).astype(bf16)


def short_work(idx, operands, results, exts):
    lanes = group(idx)
    taps = operands[3][:, lanes]
    for ext, in_ref in zip(exts, operands):
        extend_rows(jnp.zeros((taps.shape[0] - 1, LANES), f32), in_ref, lanes, ext)
    for rows in row_blocks(operands[0].shape[0]):
        for place, ext in enumerate(exts):
            results[0][place, rows, lanes] = short_conv(ext, taps, rows)


def fold(value):
    return jnp.sum(value.reshape(-1, 8, LANES), axis=0)


def finish_work(idx, operands, results, exts):
    q_ref, k_ref, v_ref, grad_ref, short_ref, taps_ref, skip_ref, long_ref, edge_ref, squares_ref = operands
    mixed_ref, grad_q_ref, grad_k_ref, grad_v_ref, sums_ref = results
    lanes = group(idx)
    taps = taps_ref[:, lanes]
    skip = skip_ref[:, lanes]
    taps_count = taps.shape[0]
    halo_rows = taps_count - 1
    rows_here = q_ref.shape[0]
    sums = [jnp.zeros((8, LANES), f32) for _ in range(taps_count + 1)]
    edge = edge_ref[idx, 3 * rows_here :, :].astype(f32)
    for place, ext in enumerate(exts):
        at = (3 + place) * halo_rows
        ext[rows_here : rows_here + halo_rows, :] = edge[at : at + halo_rows]
    row_idx = lax.broadcasted_iota(jnp.int32, (ROWS, LANES), 0)

    def short(place, rows):
        value = short_ref[place, rows, lanes]
        if rows.start == 0:
            for shift_idx in range(1, taps_count):
                terms = jnp.zeros((ROWS, LANES), f32)
                for row in range(shift_idx):
                    at = place * halo_rows + halo_rows + row - shift_idx
                    term = taps[shift_idx : shift_idx + 1] * edge[at : at + 1]
                    terms = jnp.where(row_idx == row, term, terms)
                value = value + terms
        return value

    for rows in row_blocks(rows_here):
        q_short, k_short, v_short = (short(place, rows) for place in range(3))
        product = (k_short * v_short).astype(bf16).astype(f32)
        filtered = long_ref[idx, rows, :].astype(f32) + skip * product
        mixed_ref[rows, lanes] = (q_short * filtered).astype(bf16)
        upstream = grad_ref[rows, lanes].astype(f32)
        back_mix = upstream * q_short
        below = slice(rows_here + rows.start, rows_here + rows.stop)
        back_prod = long_ref[idx, below, :].astype(f32) + skip * back_mix
        sums[taps_count] = sums[taps_count] + fold(back_mix * product)
        exts[0][rows, :] = upstream * filtered
        exts[1][rows, :] = back_prod * v_short
        exts[2][rows, :] = back_prod * k_short
    for ext, in_ref, out_ref in zip(exts, (q_ref, k_ref, v_ref), (grad_q_ref, grad_k_ref, grad_v_ref)):
        for rows in row_blocks(rows_here):
            signal = in_ref[rows, lanes].astype(f32)
            grad = None
            for shift_idx in range(taps_count):
                ahead = ext[rows.start + shift_idx : rows.stop + shift_idx, :]
                term = taps[shift_idx : shift_idx + 1] * ahead
                grad = term if grad is None else grad + term
                sums[shift_idx] = sums[shift_idx] + fold(ahead * signal)
            out_ref[rows, lanes] = grad.astype(bf16)
    if idx == 0:
        extra = slice(sums_ref.shape[1] - LANES, sums_ref.shape[1])
        sums_ref[:, extra] = jnp.zeros((taps_count + 1, LANES), f32)
        sums_ref[0:1, extra] = squares_ref[...]
    for shift_idx in range(taps_count + 1):
        sums_ref[shift_idx : shift_idx + 1, lanes] = jnp.sum(sums[shift_idx], axis=0, keepdims=True)


def norm_kernel(*refs):
    values, totals_ref, square_ref = refs[:-2], refs[-2], refs[-1]
    channels = totals_ref.shape[1] - LANES
    totals = add_up([value[...] for value in values]) if len(values) > 1 else values[0][...]
    totals_ref[...] = totals
    square = jnp.sum(totals[:, :channels] * totals[:, :channels]) + jnp.sum(totals[0:1, channels:])
    square_ref[...] = jnp.full(square_ref.shape, square)


def add_kernel(*refs):
    refs[-1][...] = add_up([ref[...] for ref in refs[:-1]])


def halves_kernel(odd_ref, own_ref, one_ref, two_ref, three_ref, four_ref, total_ref):
    even_sum = (own_ref[...] + one_ref[...]) + (two_ref[...] + three_ref[...])
    odd_sum = (one_ref[...] + two_ref[...]) + (three_ref[...] + four_ref[...])
    total_ref[...] = jnp.where(odd_ref[0] == 1, odd_sum, even_sum)


def same_kernel(value_ref, same_ref):
    same_ref[...] = value_ref[...]


def scale_kernel(limit, totals_ref, norm_ref, lag_ref, taps_out, skip_out, kernel_out):
    taps_count, channels = taps_out.shape
    factor = limit / jnp.maximum(jnp.sqrt(norm_ref[...]), limit)
    for idx in range(channels // LANES):
        lanes = slice(idx * LANES, (idx + 1) * LANES)
        taps_out[:, lanes] = totals_ref[0:taps_count, lanes] * factor
        skip_out[:, lanes] = totals_ref[taps_count : taps_count + 1, lanes] * factor
        kernel_out[:, lanes] = lag_ref[idx].astype(f32) * factor


def exchange(pieces_first):
    return lax.all_to_all(pieces_first, "ctx", split_axis=0, concat_axis=0, tiled=True)


def to_pieces(groups, pieces):
    count, rows, lanes = groups.shape
    if count == pieces:
        return groups
    share = count * lanes // pieces
    split = groups.reshape(count, rows, lanes // share, share)
    return split.transpose(0, 2, 1, 3).reshape(pieces, rows, share)


def to_groups(parts):
    pieces, rows, share = parts.shape
    if share == LANES:
        return parts
    joined = parts.reshape(pieces * share // LANES, LANES // share, rows, share)
    return joined.transpose(0, 2, 1, 3).reshape(-1, rows, LANES)


def partners(value, axis, steps):
    size = lax.axis_size(axis)
    return [value] + [lax.ppermute(value, axis, [(i, i ^ step) for i in range(size)]) for step in steps]


def rounds_of(size):
    rounds = []
    step = 1
    while step < size:
        rounds.append((step, 2 * step, 3 * step) if size // step >= 4 else (step,))
        step *= 4 if size // step >= 4 else 2
    return rounds


def halved_partners(value, axis):
    size = lax.axis_size(axis)
    heard = [value]
    for idx in range(1, 4):
        heard.append(lax.ppermute(value, axis, [(i, i ^ 2 * (idx + 3 * (i % 2))) for i in range(size)]))
    heard.append(lax.ppermute(value, axis, [(i, i ^ 14) for i in range(1, size, 2)]))
    return heard


def add_up(values):
    if len(values) == 2:
        return values[0] + values[1]
    return (values[0] + values[1]) + (values[2] + values[3])


def body(q_in, k_in, v_in, grad_out, short_filter, kernel, skip):
    pieces = lax.axis_size("ctx")
    sides = lax.axis_size("ch")
    rows_here, channels = q_in.shape
    seq_len = pieces * rows_here
    taps_count = short_filter.shape[0]
    halo_rows = taps_count - 1
    groups = channels // LANES
    share = channels // pieces
    per_step = min(groups, 4)
    steps = groups // per_step
    lanes2 = cut_lanes(per_step * LANES, 2)
    lanes3 = cut_lanes(per_step * LANES, 3)
    skip_row = skip.reshape(1, channels)
    transforms = (Transforms if share == LANES else PlainTransforms)(pieces, rows_here)
    stream = functools.partial(stream_call, steps=steps, per_step=per_step)

    flat = jax.ShapeDtypeStruct((rows_here, channels), bf16)
    extra_rows = -(-7 * halo_rows // TILE_ROWS) * TILE_ROWS
    sent = jax.ShapeDtypeStruct((groups, 3 * rows_here + extra_rows, LANES), bf16)
    exts = [pltpu.VMEM((rows_here + PAD, LANES), f32)] * 6

    (signals,) = stream(
        signals_work,
        operands=[(x, lanes2) for x in (q_in, k_in, v_in, grad_out, kernel, short_filter)],
        results=[(sent, cut_groups(per_step, 0, sent.shape[1]))],
        scratch=exts,
        vmem_bytes=MOST_VMEM_BYTES,
    )
    signals_here = exchange(to_pieces(signals, pieces))
    (short,) = stream(
        short_work,
        operands=[(x, lanes2) for x in (q_in, k_in, v_in, short_filter)],
        results=[(jax.ShapeDtypeStruct((3, rows_here, channels), f32), lanes3)],
        scratch=exts,
        after=[signals],
    )
    taps_and_skip = jnp.concatenate([short_filter, skip_row], axis=0)
    taps_here = lax.dynamic_slice_in_dim(taps_and_skip, lax.axis_index("ctx") * share, share, axis=1)
    long_here, lag_squares = transforms.products(signals_here, taps_here, short)
    long = to_groups(exchange(long_here))
    lag = long[:, 2 * rows_here : 3 * rows_here]

    mixed, grad_q, grad_k, grad_v, sums = stream(
        finish_work,
        operands=[(x, lanes2) for x in (q_in, k_in, v_in, grad_out)]
        + [(short, lanes3), (short_filter, lanes2), (skip_row, lanes2)]
        + [(long, cut_groups(per_step, 0, 2 * rows_here)), (long, cut_groups(per_step, 3 * rows_here, TILE_ROWS))]
        + [(lag_squares, cut_none)],
        results=[(flat, lanes2)] * 4,
        scratch=exts,
        kept=[jax.ShapeDtypeStruct((taps_count + 1, channels + LANES), f32)],
        vmem_bytes=MOST_VMEM_BYTES,
    )

    total_shape = jax.ShapeDtypeStruct(sums.shape, f32)

    def add(values):
        return call(
            add_kernel, total_shape, [], *values,
            vmem_bytes=SMALL_VMEM_BYTES, in_specs=[IN_VMEM] * len(values), out_specs=IN_VMEM,
        )

    if pieces >= 16:
        values = partners(sums, "ctx", (1,))
        values[0] = call(
            same_kernel, total_shape, [], sums,
            vmem_bytes=SMALL_VMEM_BYTES, in_specs=[IN_VMEM], out_specs=IN_VMEM,
        )
        odd = (lax.axis_index("ctx") % 2).reshape(1)
        halves = call(
            halves_kernel, total_shape, [], odd, *halved_partners(add(values), "ctx"),
            vmem_bytes=SMALL_VMEM_BYTES, in_specs=[IN_SMEM] + [IN_VMEM] * 5, out_specs=IN_VMEM,
        )
        last = partners(halves, "ctx", (1,))
        rounds = [tuple(16 * step for step in steps_of) for steps_of in rounds_of(pieces // 16)]
    else:
        last = [sums]
        rounds = rounds_of(pieces)
    for steps_of in rounds:
        last = partners(add(last) if len(last) > 1 else last[0], "ctx", steps_of)

    totals, norm_sq = call(
        norm_kernel,
        (total_shape, jax.ShapeDtypeStruct((1, LANES), f32)),
        [], *last,
        vmem_bytes=SMALL_VMEM_BYTES,
        in_specs=[IN_VMEM] * len(last), out_specs=(IN_VMEM, IN_VMEM),
    )
    for steps_of in rounds_of(sides):
        norm_sq = add_up(partners(norm_sq, "ch", steps_of))

    limit = math.sqrt(float(seq_len * channels * sides))
    grad_short, grad_skip, grad_kernel = call(
        functools.partial(scale_kernel, limit),
        (
            jax.ShapeDtypeStruct((taps_count, channels), f32),
            jax.ShapeDtypeStruct((1, channels), f32),
            jax.ShapeDtypeStruct((rows_here, channels), f32),
        ),
        [],
        totals, norm_sq, lag,
        vmem_bytes=SMALL_VMEM_BYTES,
        in_specs=[IN_VMEM] * 3,
        out_specs=(IN_VMEM,) * 3,
    )
    return mixed, grad_q, grad_k, grad_v, grad_short, grad_skip.reshape(channels), grad_kernel


def solution(mesh):
    in_specs = (
        P("ctx", "ch"),
        P("ctx", "ch"),
        P("ctx", "ch"),
        P("ctx", "ch"),
        P(None, "ch"),
        P("ctx", "ch"),
        P("ch"),
    )
    out_specs = (
        P("ctx", "ch"),
        P("ctx", "ch"),
        P("ctx", "ch"),
        P("ctx", "ch"),
        P(None, "ch"),
        P("ch"),
        P("ctx", "ch"),
    )
    return jax.shard_map(body, mesh=mesh, in_specs=in_specs, out_specs=out_specs, check_vma=False)
```

```python
import functools
import math

import jax
import jax.numpy as jnp
import ml_dtypes
import numpy as np
from jax import lax
from jax.experimental import pallas as pl
from jax.experimental.pallas import tpu as pltpu
from jax.sharding import PartitionSpec as P

LANES = 128
SPAN = 256
BOTH = 2 * SPAN
CHUNK = 16
CHUNKS = SPAN // CHUNK
PAD = 8
ROWS = 32
CUTS = 1
PASSES = 1
TILE_ROWS = 16
VMEM_BYTES = 60 * 1024 * 1024
MOST_VMEM_BYTES = 251 * 256 * 1024
SMALL_VMEM_BYTES = 8 * 1024 * 1024

f32 = jnp.float32
bf16 = jnp.bfloat16

IN_VMEM = pl.BlockSpec(memory_space=pltpu.VMEM)
IN_SMEM = pl.BlockSpec(memory_space=pltpu.SMEM)
ANYWHERE = pl.BlockSpec(memory_space=pl.ANY)


def call(kernel, outs, scratch, *args, vmem_bytes=VMEM_BYTES, **options):
    return pl.pallas_call(
        kernel,
        out_shape=outs,
        scratch_shapes=scratch,
        compiler_params=pltpu.CompilerParams(vmem_limit_bytes=vmem_bytes),
        **options,
    )(*args)


def leaf_phases(count):
    return [(4 * leaf + 1) / (4 * count) for leaf in range(count)]


def root_times(re, im, num, den, sign):
    if num == 0:
        return re, im
    if 4 * num == den:
        return (im, -re) if sign < 0 else (-im, re)
    cosine = math.cos(2.0 * math.pi * num / den)
    sine = sign * math.sin(2.0 * math.pi * num / den)
    if 8 * num == den:
        return ((re + im) * cosine, (im - re) * cosine) if sign < 0 else ((re - im) * cosine, (re + im) * cosine)
    if 8 * num == 3 * den:
        return ((re - im) * cosine, (re + im) * cosine) if sign < 0 else ((re + im) * cosine, (im - re) * cosine)
    return re * cosine - im * sine, im * cosine + re * sine


def short_fft(values, sign):
    count = len(values)
    if count == 1:
        return values
    even = short_fft(values[0::2], sign)
    odd = short_fft(values[1::2], sign)
    first = []
    second = []
    for num in range(count // 2):
        re, im = root_times(*odd[num], num, count, sign)
        first.append((even[num][0] + re, even[num][1] + im))
        second.append((even[num][0] - re, even[num][1] - im))
    return first + second


def to_leaves(parts):
    count = len(parts)
    turned = []
    for idx, part in enumerate(parts):
        angle = 2.0 * math.pi * idx / (4 * count)
        turned.append((part * math.cos(angle), part * (-math.sin(angle))) if idx else (part, jnp.zeros_like(part)))
    return short_fft(turned, -1)


def from_leaves(leaves, scale):
    count = len(leaves)
    parts = []
    for idx, (re, im) in enumerate(short_fft(leaves, 1)):
        angle = 2.0 * math.pi * idx / (4 * count)
        if idx == 0:
            parts.append(re * scale)
        else:
            parts.append(re * (math.cos(angle) * scale) - im * (math.sin(angle) * scale))
    return parts


def dft_matrix():
    idx = np.arange(SPAN)
    angle = (idx[:, None] * idx[None, :] % SPAN) * (2.0 * np.pi / SPAN)
    cosine, sine = np.cos(angle), np.sin(angle)
    return np.block([[cosine, sine], [-sine, cosine]])


def twist_angles(outer, inner):
    return np.asarray(leaf_phases(outer))[:, None] * np.asarray(inner)[None, :] * (2.0 * np.pi / SPAN)


def matrix_blocks():
    matrix = dft_matrix()
    high = matrix.astype(ml_dtypes.bfloat16)
    low = (matrix - high.astype(np.float64)).astype(ml_dtypes.bfloat16)
    return np.concatenate([high, low, high][:PASSES], axis=1)


def leaf_place(leaf):
    return leaf // 2, slice((leaf % 2) * LANES, (leaf % 2 + 1) * LANES)


def split_store(ref, leaf, below, here, value):
    pair, lanes = leaf_place(leaf)
    high = value.astype(bf16)
    for block in range(PASSES):
        part = high
        if PASSES == 3 and block == 2:
            part = (value - high.astype(f32)).astype(bf16)
        ref[pair, shifted_rows(here, block * BOTH + below), lanes] = part


def run_all(stages, rows_here, matmul=None, carry=0):
    tiles = matmul[2].shape[0] if matmul else 4
    per_tile = CHUNKS // tiles
    in_part = rows_here // CHUNK
    for tile in range(tiles):
        if matmul:
            matrix_ref, split_ref, result_ref = matmul
            result_ref[tile] = jnp.dot(matrix_ref[...], split_ref[tile], preferred_element_type=f32)
        for chunk in range(tile * per_tile, (tile + 1) * per_tile):
            for stage in stages:
                carry = stage(chunk // in_part, chunk % in_part * CHUNK, carry)
    return carry


def in_span(part, row, rows_here):
    return pl.ds(part * rows_here + row, CHUNK)


def twist_stage(coarse_ref, fine_ref, twist_ref, rows_here):
    outer = twist_ref.shape[1]

    def stage(part, row, carry):
        here = in_span(part, row, rows_here)
        idx = part * (rows_here // CHUNK) + row // CHUNK
        for leaf in range(outer):
            far_cosine = coarse_ref[idx, leaf]
            far_sine = coarse_ref[idx, outer + leaf]
            cosine = fine_ref[0, leaf]
            sine = fine_ref[1, leaf]
            twist_ref[0, leaf, here, :] = far_cosine * cosine - far_sine * sine
            twist_ref[1, leaf, here, :] = far_sine * cosine + far_cosine * sine
        return carry

    return stage


def leaves_stage(signals_ref, first_row, heads_ref, rows_here, twist_ref, split_ref):
    outer = twist_ref.shape[1]
    ratio = SPAN // rows_here

    def stage(part, row, carry):
        here = in_span(part, row, rows_here)
        rows = pl.ds(first_row + row, CHUNK)
        parts = [signals_ref[place * ratio + part, rows, :] for place in range(outer)]
        if heads_ref is not None and row == 0:
            parts = [heads_ref[place * ratio + part] for place in range(outer)]
        parts = [value.astype(f32) for value in parts]
        for leaf, (re, im) in enumerate(to_leaves(parts)):
            cosine = twist_ref[0, leaf, here, :]
            sine = twist_ref[1, leaf, here, :]
            split_store(split_ref, leaf, 0, here, re * cosine + im * sine)
            split_store(split_ref, leaf, SPAN, here, im * cosine - re * sine)
        return carry

    return stage


def shifted_rows(here, by):
    return pl.ds(here.start + by, here.size)


def combine_stage(left_ref, right_ref, split_ref, rows_here, conjugate):
    def stage(part, row, carry):
        here = in_span(part, row, rows_here)
        below = shifted_rows(here, SPAN)
        for leaf in range(2 * left_ref.shape[0]):
            pair, lanes = leaf_place(leaf)
            left_re = left_ref[pair, here, lanes]
            left_im = left_ref[pair, below, lanes]
            right_re = right_ref[pair, here, lanes]
            right_im = right_ref[pair, below, lanes]
            if conjugate:
                re = left_re * right_re + left_im * right_im
                minus_im = left_im * right_re - left_re * right_im
            else:
                re = left_re * right_re - left_im * right_im
                minus_im = -(left_re * right_im + left_im * right_re)
            split_store(split_ref, leaf, 0, here, re)
            split_store(split_ref, leaf, SPAN, here, minus_im)
        return carry

    return stage


def signal_stage(time_ref, twist_ref, rows_here, write):
    outer = twist_ref.shape[1]
    ratio = SPAN // rows_here
    scale = 1.0 / (SPAN * outer)

    def stage(part, row, carry):
        here = in_span(part, row, rows_here)
        below = shifted_rows(here, SPAN)
        leaves = []
        for leaf in range(outer):
            pair, lanes = leaf_place(leaf)
            cosine = twist_ref[0, leaf, here, :]
            sine = twist_ref[1, leaf, here, :]
            re = time_ref[pair, here, lanes]
            minus_im = time_ref[pair, below, lanes]
            leaves.append((re * cosine + minus_im * sine, re * sine - minus_im * cosine))
        for place, value in enumerate(from_leaves(leaves, scale)):
            carry = write(place * ratio + part, pl.ds(row, CHUNK), value, carry)
        return carry

    return stage


def first_rows(lead, first, taps):
    count = len(lead)
    rows = lead + first
    return [
        functools.reduce(lambda x, y: x + y, [taps[shift] * rows[count + row - shift] for shift in range(count + 1)])
        for row in range(count)
    ]


def first_signals(ahead, own, taps):
    count = len(taps) - 1

    def kind(rows, idx):
        return rows[idx * count : (idx + 1) * count]

    shorts = [first_rows(kind(ahead, idx), kind(own, 3 + idx), taps) for idx in range(3)]
    product = [(k_row * v_row).astype(bf16) for k_row, v_row in zip(shorts[1], shorts[2])]
    back_mix = [grad_row * q_row for grad_row, q_row in zip(kind(own, 6), shorts[0])]
    return shorts, product, back_mix


def first_backs(ahead, own, taps, skip, conv, corr):
    count = len(taps) - 1
    shorts, product, back_mix = first_signals(ahead, own, taps)
    back_q = []
    back_k = []
    back_v = []
    for row in range(count):
        filtered = conv[row] + skip * product[row].astype(f32)
        back_prod = corr[row] + skip * back_mix[row]
        back_q.append(own[6 * count + row] * filtered)
        back_k.append(back_prod * shorts[2][row])
        back_v.append(back_prod * shorts[1][row])
    return back_q + back_k + back_v


def extra_of(signals_ref, piece, rows_here, used):
    rows = signals_ref[piece, 3 * rows_here :, :].astype(f32)
    return [rows[idx : idx + 1] for idx in range(used)]


def tap_rows(taps_ref):
    return [taps_ref[shift : shift + 1, :] for shift in range(taps_ref.shape[0])]


def patch_first_rows(signals_ref, heads_ref, taps_ref, rows_here):
    pieces = signals_ref.shape[0]
    taps = tap_rows(taps_ref)[:-1]
    used = 7 * (len(taps) - 1)
    row_idx = lax.broadcasted_iota(jnp.int32, (TILE_ROWS, LANES), 0)
    ahead = [jnp.zeros((1, LANES), f32)] * used
    for piece in range(pieces):
        own = extra_of(signals_ref, piece, rows_here, used)
        for kind, rows in enumerate(first_signals(ahead, own, taps)[1:]):
            tile = signals_ref[piece, kind * rows_here : kind * rows_here + TILE_ROWS, :].astype(f32)
            for row, value in enumerate(rows):
                tile = jnp.where(row_idx == row, value.astype(f32), tile)
            heads_ref[kind, piece] = tile.astype(bf16)
        ahead = own


def write_edges(signals_ref, results_ref, taps_ref, rows_here):
    pieces = signals_ref.shape[0]
    *taps, skip = tap_rows(taps_ref)
    count = len(taps) - 1
    nothing = jnp.zeros((1, LANES), f32)
    extras = [extra_of(signals_ref, piece, rows_here, 7 * count) for piece in range(pieces)]
    for piece in range(pieces):
        rows = extras[piece - 1][: 3 * count] if piece else [nothing] * (3 * count)
        if piece + 1 < pieces:
            conv, corr = (
                results_ref[piece + 1, kind * rows_here : kind * rows_here + TILE_ROWS, :].astype(f32)
                for kind in range(2)
            )
            rows = rows + first_backs(
                extras[piece], extras[piece + 1], taps, skip,
                [conv[row : row + 1] for row in range(count)], [corr[row : row + 1] for row in range(count)],
            )
        spare = results_ref.shape[1] - 2 * rows_here - len(rows)
        rows.append(jnp.zeros((spare, LANES), f32))
        results_ref[piece, 2 * rows_here :, :] = jnp.concatenate(rows, axis=0).astype(bf16)


def products_kernel(
    rows_here, signals_hbm, taps_ref, coarse_ref, fine_ref, matrix_hbm, after_ref, results_hbm, lag_hbm,
    signals_ref, twist_ref, matrix_ref, heads_ref, results_ref, one_split, two_split, lag_split,
    filter_ref, product_ref, cotan_ref, time_ref, sems,
):
    all_rows = signals_ref.shape[1]
    back_rows = results_ref.shape[1]
    sem_idx = iter(range(sems.shape[0]))

    def cut_copies(source, target, rows):
        each = source.shape[0] // CUTS
        places = [(pl.ds(cut * each, each), pl.ds(*rows)) for cut in range(CUTS)]
        return [pltpu.make_async_copy(source.at[at], target.at[at], sems.at[next(sem_idx)]) for at in places]

    filter_copies = cut_copies(signals_hbm, signals_ref, (2 * rows_here, all_rows - 2 * rows_here))
    matrix_copies = [
        pltpu.make_async_copy(
            matrix_hbm.at[pl.ds(cut * BOTH // CUTS, BOTH // CUTS)],
            matrix_ref.at[pl.ds(cut * BOTH // CUTS, BOTH // CUTS)],
            sems.at[next(sem_idx)],
        )
        for cut in range(CUTS)
    ]
    signal_copies = [cut_copies(signals_hbm, signals_ref, (kind * rows_here, rows_here)) for kind in range(2)]
    lag_copies = [
        pltpu.make_async_copy(lag_split.at[pair], lag_hbm.at[pair], sems.at[next(sem_idx)])
        for pair in range(lag_split.shape[0])
    ]
    return_copies = [
        cut_copies(results_ref, results_hbm, rows)
        for rows in ((0, rows_here), (rows_here, back_rows - rows_here))
    ]

    def start_all(copies):
        for copy in copies:
            copy.start()

    def wait_all(copies):
        for copy in copies:
            copy.wait()

    def leaves(kind, split_ref):
        heads = heads_ref.at[kind] if kind < 2 else None
        return leaves_stage(signals_ref, kind * rows_here, heads, rows_here, twist_ref, split_ref)

    def combine(left_ref, right_ref, split_ref, conjugate):
        return combine_stage(left_ref, right_ref, split_ref, rows_here, conjugate)

    def result(kind, from_ref):
        def write(piece, rows, value, carry):
            place = pl.ds(kind * rows_here + rows.start, CHUNK)
            results_ref[piece, place, :] = value.astype(bf16)
            return carry

        return signal_stage(from_ref, twist_ref, rows_here, write)

    start_all(filter_copies + matrix_copies + signal_copies[0] + signal_copies[1])
    run_all([twist_stage(coarse_ref, fine_ref, twist_ref, rows_here)], rows_here)
    wait_all(filter_copies)
    run_all([leaves(2, one_split)], rows_here)
    wait_all(signal_copies[0] + signal_copies[1] + matrix_copies)
    patch_first_rows(signals_ref, heads_ref, taps_ref, rows_here)
    run_all([leaves(0, two_split)], rows_here, (matrix_ref, one_split, filter_ref))
    run_all([leaves(1, one_split)], rows_here, (matrix_ref, two_split, product_ref))
    run_all([combine(filter_ref, product_ref, two_split, False)], rows_here, (matrix_ref, one_split, cotan_ref))
    run_all([combine(filter_ref, cotan_ref, one_split, True)], rows_here, (matrix_ref, two_split, time_ref))
    run_all(
        [combine(product_ref, cotan_ref, lag_split, True), result(0, time_ref)],
        rows_here, (matrix_ref, one_split, filter_ref),
    )
    start_all(return_copies[0] + lag_copies)
    run_all([result(1, filter_ref)], rows_here)
    write_edges(signals_ref, results_ref, taps_ref, rows_here)
    start_all(return_copies[1])
    wait_all(lag_copies + return_copies[0] + return_copies[1])


def lag_kernel(
    split_hbm, coarse_ref, fine_ref, matrix_hbm, lag_ref, square_ref, twist_ref, matrix_ref, split_ref, time_ref, sems
):
    rows_here = lag_ref.shape[1]
    copies = [
        pltpu.make_async_copy(matrix_hbm, matrix_ref, sems.at[0]),
        pltpu.make_async_copy(split_hbm, split_ref, sems.at[1]),
    ]
    for copy in copies:
        copy.start()
    run_all([twist_stage(coarse_ref, fine_ref, twist_ref, rows_here)], rows_here)
    for copy in copies:
        copy.wait()
    run_all([], rows_here, (matrix_ref, split_ref, time_ref))

    def write(piece, rows, value, carry):
        lag_ref[piece, rows, :] = value.astype(bf16)
        return carry + value * value

    square = run_all(
        [signal_stage(time_ref, twist_ref, rows_here, write)], rows_here, None, jnp.zeros((CHUNK, LANES), f32)
    )
    square_ref[...] = jnp.sum(square, axis=0, keepdims=True)


class Transforms:
    def __init__(self, pieces, rows_here):
        outer = pieces * rows_here // SPAN
        pairs = outer // 2
        coarse = twist_angles(outer, CHUNK * np.arange(CHUNKS)).T
        fine = twist_angles(outer, np.arange(CHUNK))[..., None] * np.ones(LANES)
        self.tables = [
            jnp.asarray(np.concatenate([np.cos(coarse), np.sin(coarse)], axis=1).astype(np.float32)),
            jnp.asarray(np.stack([np.cos(fine), np.sin(fine)]).astype(np.float32)),
            jnp.asarray(matrix_blocks()),
        ]
        self.split = jax.ShapeDtypeStruct((pairs, PASSES * BOTH, 2 * LANES), bf16)
        self.signal = jax.ShapeDtypeStruct((pieces, rows_here, LANES), bf16)
        self.result = jax.ShapeDtypeStruct((pieces, 2 * rows_here + TILE_ROWS, LANES), bf16)
        self.square = jax.ShapeDtypeStruct((1, LANES), f32)
        self.result_work = pltpu.VMEM(self.result.shape, bf16)
        self.work = pltpu.VMEM((pairs, BOTH, 2 * LANES), f32)
        self.split_work = pltpu.VMEM(self.split.shape, bf16)
        self.twist_work = pltpu.VMEM((2, outer, SPAN, LANES), f32)
        self.matrix_work = pltpu.VMEM(self.tables[2].shape, bf16)

    def products(self, signals, taps, after):
        return call(
            functools.partial(products_kernel, self.signal.shape[1]), (self.result, self.split),
            [pltpu.VMEM(signals.shape, bf16), self.twist_work, self.matrix_work]
            + [pltpu.VMEM((2, signals.shape[0], TILE_ROWS, LANES), bf16), self.result_work]
            + [self.split_work] * 3
            + [self.work] * 4
            + [pltpu.SemaphoreType.DMA((6 * CUTS + self.split.shape[0],))],
            signals, taps, *self.tables, after,
            vmem_bytes=MOST_VMEM_BYTES,
            in_specs=[ANYWHERE, IN_VMEM, IN_SMEM, IN_VMEM, ANYWHERE, ANYWHERE],
            out_specs=(ANYWHERE, ANYWHERE),
        )

    def lag(self, lag_split):
        return call(
            lag_kernel, (self.signal, self.square),
            [self.twist_work, self.matrix_work, self.split_work, self.work, pltpu.SemaphoreType.DMA((2,))],
            lag_split, *self.tables,
            in_specs=[ANYWHERE, IN_SMEM, IN_VMEM, ANYWHERE],
            out_specs=(IN_VMEM, IN_VMEM),
        )


class PlainTransforms:
    def __init__(self, pieces, rows_here):
        self.seq_len = pieces * rows_here
        self.pieces = pieces
        self.outer = self.seq_len // SPAN
        idx = np.arange(SPAN)
        angle = (idx[:, None] * idx[None, :] % SPAN) * (2.0 * np.pi / SPAN)
        self.cosine = jnp.asarray(np.cos(angle), f32)
        self.sine = jnp.asarray(np.sin(angle), f32)
        twist = twist_angles(self.outer, idx)
        self.twist = jnp.asarray(np.stack([np.cos(twist), np.sin(twist)]), f32)[..., None]

    def dot(self, matrix, signal):
        return jnp.einsum("fs,tsc->tfc", matrix, signal, precision=lax.Precision.HIGHEST)

    def spectrum(self, signal):
        parts = signal.astype(f32).reshape(self.outer, SPAN, -1)
        leaves = to_leaves([parts[part] for part in range(self.outer)])
        re = jnp.stack([leaf[0] for leaf in leaves])
        im = jnp.stack([leaf[1] for leaf in leaves])
        twist_re = re * self.twist[0] + im * self.twist[1]
        twist_im = im * self.twist[0] - re * self.twist[1]
        return (
            self.dot(self.cosine, twist_re) + self.dot(self.sine, twist_im),
            self.dot(self.cosine, twist_im) - self.dot(self.sine, twist_re),
        )

    def back(self, re, im):
        time_re = self.dot(self.cosine, re) - self.dot(self.sine, im)
        time_im = self.dot(self.cosine, im) + self.dot(self.sine, re)
        leaf_re = time_re * self.twist[0] - time_im * self.twist[1]
        leaf_im = time_im * self.twist[0] + time_re * self.twist[1]
        parts = from_leaves([(leaf_re[leaf], leaf_im[leaf]) for leaf in range(self.outer)], 1.0 / self.seq_len)
        return jnp.stack(parts).reshape(self.pieces, self.seq_len // self.pieces, -1)

    def products(self, signals, taps_and_skip, after):
        rows_here = self.seq_len // self.pieces
        parts = [signals[:, kind * rows_here : (kind + 1) * rows_here] for kind in range(3)]
        extra = signals[:, 3 * rows_here :].astype(f32)
        rows = [extra[:, idx : idx + 1] for idx in range(extra.shape[1])]
        ahead = [jnp.concatenate([jnp.zeros_like(row[:1]), row[:-1]], axis=0) for row in rows]
        *taps, skip = [taps_and_skip[row][None, None, :] for row in range(taps_and_skip.shape[0])]
        count = len(taps) - 1
        for kind, first in enumerate(first_signals(ahead, rows, taps)[1:]):
            first = jnp.concatenate(first, axis=1)
            parts[kind] = jnp.concatenate([first.astype(bf16), parts[kind][:, first.shape[1] :]], axis=1)
        product, cotan, taps_spec = (self.spectrum(part) for part in parts)
        conv = self.back(
            taps_spec[0] * product[0] - taps_spec[1] * product[1], taps_spec[0] * product[1] + taps_spec[1] * product[0]
        ).astype(bf16)
        corr = self.back(
            taps_spec[0] * cotan[0] + taps_spec[1] * cotan[1], taps_spec[0] * cotan[1] - taps_spec[1] * cotan[0]
        ).astype(bf16)
        lag = (
            product[0] * cotan[0] + product[1] * cotan[1],
            product[0] * cotan[1] - product[1] * cotan[0],
        )
        backs = first_backs(
            ahead, rows, taps, skip,
            [conv[:, row : row + 1].astype(f32) for row in range(count)],
            [corr[:, row : row + 1].astype(f32) for row in range(count)],
        )
        behind = [jnp.concatenate([row[1:], jnp.zeros_like(row[:1])], axis=0) for row in backs]
        edge = jnp.concatenate(ahead[: 3 * count] + behind, axis=1).astype(bf16)
        edge = jnp.pad(edge, ((0, 0), (0, TILE_ROWS - edge.shape[1]), (0, 0)))
        return jnp.concatenate([conv, corr, edge], axis=1), lag

    def lag(self, lag_spec):
        lag = self.back(*lag_spec)
        squares = jnp.sum(lag * lag, axis=(0, 1))
        return lag.astype(bf16), jnp.zeros((1, LANES), f32).at[0, : squares.shape[0]].set(squares)


def group(idx):
    return slice(idx * LANES, (idx + 1) * LANES)


def streamed(work, steps, per_step, places, in_count, out_count, kept, *refs):
    moved = in_count + out_count
    hbm = refs[:moved]
    kept_refs = refs[moved : moved + kept]
    held = refs[moved + kept : 2 * moved + kept]
    scratch = refs[2 * moved + kept : -1]
    sems = refs[-1]

    def copy(place, step):
        outside = hbm[place].at[places[place](step)]
        inside = held[place].at[places[place](step)]
        ends = (outside, inside) if place < in_count else (inside, outside)
        return pltpu.make_async_copy(*ends, sems.at[place, step])

    def arrivals(step):
        return [copy(place, step) for place in range(in_count) if places[place](step) is not None]

    for step in range(steps):
        for arrival in arrivals(step):
            arrival.start()
    for step in range(steps):
        for arrival in arrivals(step):
            arrival.wait()
        for idx in range(step * per_step, (step + 1) * per_step):
            exts = scratch[idx % 2 :: 2]
            work(idx, held[:in_count], held[in_count:] + kept_refs, exts)
        for place in range(in_count, moved):
            copy(place, step).start()
    for step in range(steps):
        for place in range(in_count, moved):
            copy(place, step).wait()


def stream_call(work, steps, per_step, operands, results, scratch=(), after=(), kept=(), vmem_bytes=VMEM_BYTES):
    arrays = [operand[0] for operand in operands]
    shapes = [jax.ShapeDtypeStruct(array.shape, array.dtype) for array in arrays] + [result[0] for result in results]
    cuts = [entry[1] for entry in list(operands) + list(results)]
    held = [pltpu.VMEM(shape.shape, shape.dtype) for shape in shapes]
    extra = list(after)
    kernel = functools.partial(streamed, work, steps, per_step, cuts, len(arrays), len(results), len(kept))

    def without_extra(*refs):
        kernel(*refs[: len(arrays)], *refs[len(arrays) + len(extra) :])

    return call(
        without_extra,
        tuple(result[0] for result in results) + tuple(kept),
        held + list(scratch) + [pltpu.SemaphoreType.DMA((len(shapes), steps))],
        *arrays, *extra,
        vmem_bytes=vmem_bytes,
        in_specs=[ANYWHERE] * (len(arrays) + len(extra)),
        out_specs=(ANYWHERE,) * len(results) + (IN_VMEM,) * len(kept),
    )


def cut_lanes(width, rank):
    def place(step):
        return (slice(None),) * (rank - 1) + (pl.ds(step * width, width),)

    return place


def cut_groups(per_step):
    def place(step):
        return (pl.ds(step * per_step, per_step),)

    return place


def cut_none(step):
    return None if step else (slice(None),)


def row_blocks(rows_here):
    return [slice(start, start + ROWS) for start in range(0, rows_here, ROWS)]


def extend_rows(lead, in_ref, lanes, ext_ref):
    ext_ref[PAD - lead.shape[0] : PAD, :] = lead
    ext_ref[PAD:, :] = in_ref[:, lanes].astype(f32)


def short_conv(ext_ref, taps, rows):
    result = None
    for shift_idx in range(taps.shape[0]):
        term = taps[shift_idx : shift_idx + 1] * ext_ref[PAD + rows.start - shift_idx : PAD + rows.stop - shift_idx, :]
        result = term if result is None else result + term
    return result


def signals_work(idx, operands, results, exts):
    q_ref, k_ref, v_ref, grad_ref, kernel_ref, taps_ref = operands
    lanes = group(idx)
    taps = taps_ref[:, lanes]
    halo_rows = taps.shape[0] - 1
    rows_here = q_ref.shape[0]
    for ext, in_ref in zip(exts, operands):
        extend_rows(jnp.zeros((halo_rows, LANES), f32), in_ref, lanes, ext)
    for rows in row_blocks(rows_here):
        q_short, k_short, v_short = (short_conv(ext, taps, rows) for ext in exts)
        below = [slice(kind * rows_here + rows.start, kind * rows_here + rows.stop) for kind in range(3)]
        results[0][idx, below[0], :] = (k_short * v_short).astype(bf16)
        results[0][idx, below[1], :] = (grad_ref[rows, lanes].astype(f32) * q_short).astype(bf16)
        results[0][idx, below[2], :] = kernel_ref[rows, lanes].astype(bf16)
    top = grad_ref[0:TILE_ROWS, lanes].astype(f32)[:halo_rows]
    extra = [ext[ext.shape[0] - halo_rows :, :] for ext in exts] + [ext[PAD : PAD + halo_rows, :] for ext in exts]
    extra_count = results[0].shape[1] - 3 * rows_here
    blank = jnp.zeros((extra_count - 7 * halo_rows, LANES), f32)
    results[0][idx, 3 * rows_here :, :] = jnp.concatenate(extra + [top, blank], axis=0).astype(bf16)


def short_work(idx, operands, results, exts):
    lanes = group(idx)
    taps = operands[3][:, lanes]
    for ext, in_ref in zip(exts, operands):
        extend_rows(jnp.zeros((taps.shape[0] - 1, LANES), f32), in_ref, lanes, ext)
    for rows in row_blocks(operands[0].shape[0]):
        for place, ext in enumerate(exts):
            results[0][place, rows, lanes] = short_conv(ext, taps, rows)


def fold(value):
    return jnp.sum(value.reshape(-1, 8, LANES), axis=0)


def finish_work(idx, operands, results, exts):
    q_ref, k_ref, v_ref, grad_ref, short_ref, taps_ref, skip_ref, long_ref, squares_ref = operands
    mixed_ref, grad_q_ref, grad_k_ref, grad_v_ref, sums_ref = results
    lanes = group(idx)
    taps = taps_ref[:, lanes]
    skip = skip_ref[:, lanes]
    taps_count = taps.shape[0]
    halo_rows = taps_count - 1
    rows_here = q_ref.shape[0]
    sums = [jnp.zeros((8, LANES), f32) for _ in range(taps_count + 1)]
    edge = long_ref[idx, 2 * rows_here :, :].astype(f32)
    for place, ext in enumerate(exts):
        at = (3 + place) * halo_rows
        ext[rows_here : rows_here + halo_rows, :] = edge[at : at + halo_rows]
    row_idx = lax.broadcasted_iota(jnp.int32, (ROWS, LANES), 0)

    def short(place, rows):
        value = short_ref[place, rows, lanes]
        if rows.start == 0:
            for shift_idx in range(1, taps_count):
                terms = jnp.zeros((ROWS, LANES), f32)
                for row in range(shift_idx):
                    at = place * halo_rows + halo_rows + row - shift_idx
                    term = taps[shift_idx : shift_idx + 1] * edge[at : at + 1]
                    terms = jnp.where(row_idx == row, term, terms)
                value = value + terms
        return value

    for rows in row_blocks(rows_here):
        q_short, k_short, v_short = (short(place, rows) for place in range(3))
        product = (k_short * v_short).astype(bf16).astype(f32)
        filtered = long_ref[idx, rows, :].astype(f32) + skip * product
        mixed_ref[rows, lanes] = (q_short * filtered).astype(bf16)
        upstream = grad_ref[rows, lanes].astype(f32)
        back_mix = upstream * q_short
        below = slice(rows_here + rows.start, rows_here + rows.stop)
        back_prod = long_ref[idx, below, :].astype(f32) + skip * back_mix
        sums[taps_count] = sums[taps_count] + fold(back_mix * product)
        exts[0][rows, :] = upstream * filtered
        exts[1][rows, :] = back_prod * v_short
        exts[2][rows, :] = back_prod * k_short
    for ext, in_ref, out_ref in zip(exts, (q_ref, k_ref, v_ref), (grad_q_ref, grad_k_ref, grad_v_ref)):
        for rows in row_blocks(rows_here):
            signal = in_ref[rows, lanes].astype(f32)
            grad = None
            for shift_idx in range(taps_count):
                ahead = ext[rows.start + shift_idx : rows.stop + shift_idx, :]
                term = taps[shift_idx : shift_idx + 1] * ahead
                grad = term if grad is None else grad + term
                sums[shift_idx] = sums[shift_idx] + fold(ahead * signal)
            out_ref[rows, lanes] = grad.astype(bf16)
    if idx == 0:
        extra = slice(sums_ref.shape[1] - LANES, sums_ref.shape[1])
        sums_ref[:, extra] = jnp.zeros((taps_count + 1, LANES), f32)
        sums_ref[0:1, extra] = squares_ref[...]
    for shift_idx in range(taps_count + 1):
        sums_ref[shift_idx : shift_idx + 1, lanes] = jnp.sum(sums[shift_idx], axis=0, keepdims=True)


def norm_kernel(*refs):
    values, totals_ref, square_ref = refs[:-2], refs[-2], refs[-1]
    channels = totals_ref.shape[1] - LANES
    totals = add_up([value[...] for value in values]) if len(values) > 1 else values[0][...]
    totals_ref[...] = totals
    square = jnp.sum(totals[:, :channels] * totals[:, :channels]) + jnp.sum(totals[0:1, channels:])
    square_ref[...] = jnp.full(square_ref.shape, square)


def add_kernel(*refs):
    refs[-1][...] = add_up([ref[...] for ref in refs[:-1]])


def same_kernel(value_ref, same_ref):
    same_ref[...] = value_ref[...]


def scale_kernel(limit, totals_ref, norm_ref, lag_ref, taps_out, skip_out, kernel_out):
    taps_count, channels = taps_out.shape
    factor = limit / jnp.maximum(jnp.sqrt(norm_ref[...]), limit)
    for idx in range(channels // LANES):
        lanes = slice(idx * LANES, (idx + 1) * LANES)
        taps_out[:, lanes] = totals_ref[0:taps_count, lanes] * factor
        skip_out[:, lanes] = totals_ref[taps_count : taps_count + 1, lanes] * factor
        kernel_out[:, lanes] = lag_ref[idx].astype(f32) * factor


def exchange(pieces_first):
    return lax.all_to_all(pieces_first, "ctx", split_axis=0, concat_axis=0, tiled=True)


def to_pieces(groups, pieces):
    count, rows, lanes = groups.shape
    if count == pieces:
        return groups
    share = count * lanes // pieces
    split = groups.reshape(count, rows, lanes // share, share)
    return split.transpose(0, 2, 1, 3).reshape(pieces, rows, share)


def to_groups(parts):
    pieces, rows, share = parts.shape
    if share == LANES:
        return parts
    joined = parts.reshape(pieces * share // LANES, LANES // share, rows, share)
    return joined.transpose(0, 2, 1, 3).reshape(-1, rows, LANES)


def partners(value, axis, steps):
    size = lax.axis_size(axis)
    return [value] + [lax.ppermute(value, axis, [(i, i ^ step) for i in range(size)]) for step in steps]


def rounds_of(size):
    rounds = [(1,)] if size > 1 else []
    step = 2
    while step < size:
        rounds.append((step, 2 * step, 3 * step) if size // step >= 4 else (step,))
        step *= 4 if size // step >= 4 else 2
    return rounds


def add_up(values):
    if len(values) == 2:
        return values[0] + values[1]
    return (values[0] + values[1]) + (values[2] + values[3])


def body(q_in, k_in, v_in, grad_out, short_filter, kernel, skip):
    pieces = lax.axis_size("ctx")
    sides = lax.axis_size("ch")
    rows_here, channels = q_in.shape
    seq_len = pieces * rows_here
    taps_count = short_filter.shape[0]
    halo_rows = taps_count - 1
    groups = channels // LANES
    share = channels // pieces
    per_step = min(groups, 4)
    steps = groups // per_step
    lanes2 = cut_lanes(per_step * LANES, 2)
    lanes3 = cut_lanes(per_step * LANES, 3)
    skip_row = skip.reshape(1, channels)
    transforms = (Transforms if share == LANES else PlainTransforms)(pieces, rows_here)
    stream = functools.partial(stream_call, steps=steps, per_step=per_step)

    flat = jax.ShapeDtypeStruct((rows_here, channels), bf16)
    extra_rows = -(-7 * halo_rows // TILE_ROWS) * TILE_ROWS
    sent = jax.ShapeDtypeStruct((groups, 3 * rows_here + extra_rows, LANES), bf16)
    exts = [pltpu.VMEM((rows_here + PAD, LANES), f32)] * 6

    (signals,) = stream(
        signals_work,
        operands=[(x, lanes2) for x in (q_in, k_in, v_in, grad_out, kernel, short_filter)],
        results=[(sent, cut_groups(per_step))],
        scratch=exts,
        vmem_bytes=MOST_VMEM_BYTES,
    )
    signals_here = exchange(to_pieces(signals, pieces))
    (short,) = stream(
        short_work,
        operands=[(x, lanes2) for x in (q_in, k_in, v_in, short_filter)],
        results=[(jax.ShapeDtypeStruct((3, rows_here, channels), f32), lanes3)],
        scratch=exts,
        after=[signals],
    )
    taps_and_skip = jnp.concatenate([short_filter, skip_row], axis=0)
    taps_here = lax.dynamic_slice_in_dim(taps_and_skip, lax.axis_index("ctx") * share, share, axis=1)
    long_here, lag_spec = transforms.products(signals_here, taps_here, short)
    long = to_groups(exchange(long_here))
    lag_here, lag_squares = transforms.lag(lag_spec)
    lag = to_groups(exchange(lag_here))

    mixed, grad_q, grad_k, grad_v, sums = stream(
        finish_work,
        operands=[(x, lanes2) for x in (q_in, k_in, v_in, grad_out)]
        + [(short, lanes3), (short_filter, lanes2), (skip_row, lanes2)]
        + [(long, cut_groups(per_step)), (lag_squares, cut_none)],
        results=[(flat, lanes2)] * 4,
        scratch=exts,
        kept=[jax.ShapeDtypeStruct((taps_count + 1, channels + LANES), f32)],
    )

    total_shape = jax.ShapeDtypeStruct(sums.shape, f32)

    def add(values):
        return call(
            add_kernel, total_shape, [], *values,
            vmem_bytes=SMALL_VMEM_BYTES, in_specs=[IN_VMEM] * len(values), out_specs=IN_VMEM,
        )

    last = [sums]
    for idx, steps_of in enumerate(rounds_of(pieces)):
        last = partners(add(last) if idx else sums, "ctx", steps_of)
        if idx == 0:
            last[0] = call(
                same_kernel, total_shape, [], sums,
                vmem_bytes=SMALL_VMEM_BYTES, in_specs=[IN_VMEM], out_specs=IN_VMEM,
            )

    totals, norm_sq = call(
        norm_kernel,
        (total_shape, jax.ShapeDtypeStruct((1, LANES), f32)),
        [], *last,
        vmem_bytes=SMALL_VMEM_BYTES,
        in_specs=[IN_VMEM] * len(last), out_specs=(IN_VMEM, IN_VMEM),
    )
    for steps_of in rounds_of(sides):
        norm_sq = add_up(partners(norm_sq, "ch", steps_of))

    limit = math.sqrt(float(seq_len * channels * sides))
    grad_short, grad_skip, grad_kernel = call(
        functools.partial(scale_kernel, limit),
        (
            jax.ShapeDtypeStruct((taps_count, channels), f32),
            jax.ShapeDtypeStruct((1, channels), f32),
            jax.ShapeDtypeStruct((rows_here, channels), f32),
        ),
        [],
        totals, norm_sq, lag,
        vmem_bytes=SMALL_VMEM_BYTES,
        in_specs=[IN_VMEM] * 3,
        out_specs=(IN_VMEM,) * 3,
    )
    return mixed, grad_q, grad_k, grad_v, grad_short, grad_skip.reshape(channels), grad_kernel


def solution(mesh):
    in_specs = (
        P("ctx", "ch"),
        P("ctx", "ch"),
        P("ctx", "ch"),
        P("ctx", "ch"),
        P(None, "ch"),
        P("ctx", "ch"),
        P("ch"),
    )
    out_specs = (
        P("ctx", "ch"),
        P("ctx", "ch"),
        P("ctx", "ch"),
        P("ctx", "ch"),
        P(None, "ch"),
        P("ch"),
        P("ctx", "ch"),
    )
    return jax.shard_map(body, mesh=mesh, in_specs=in_specs, out_specs=out_specs, check_vma=False)
```
